32 devices in a mesh: dp: 2 (over x), pass: 16 (over z, y, core).
Axes of the slice: x: 2, y: 2, z: 4, core: 2. Of those that a mesh axis runs over, the one named last changes fastest.
Arguments:
- tokens: bfloat16 [6144, 768], P(('dp', 'pass')), may hold values from -6 to 6
- cotangent: bfloat16 [6144, 768], P(('dp', 'pass')), may hold values from -6 to 6
- passages: bfloat16 [640, 384, 768], P(('dp', 'pass')), may hold values from -6 to 6
- refresh: int32 [640], P(('dp', 'pass')), may hold values 0 or 1
- passage_ids: int32 [32, 20], P('dp'), may hold values from 0 to 639, as said below
- self_query: bfloat16 [768, 768], P(('dp', 'pass')), may hold values from -0.0546875 to 0.0546875
- self_key: bfloat16 [768, 768], P(('dp', 'pass')), may hold values from -0.21875 to 0.21875
- self_value: bfloat16 [768, 768], P(('dp', 'pass')), may hold values from -0.21875 to 0.21875
- self_out: bfloat16 [768, 768], P(('dp', 'pass')), may hold values from -0.4375 to 0.4375
- cross_query: bfloat16 [768, 768], P(('dp', 'pass')), may hold values from -0.0546875 to 0.0546875
- cross_key: bfloat16 [768, 768], P(('dp', 'pass')), may hold values from -0.21875 to 0.21875
- cross_value: bfloat16 [768, 768], P(('dp', 'pass')), may hold values from -0.21875 to 0.21875
- cross_out: bfloat16 [768, 768], P(('dp', 'pass')), may hold values from -1.75 to 1.75
- up_weight: bfloat16 [768, 3072], P(('dp', 'pass')), may hold values from -0.21875 to 0.21875
- down_weight: bfloat16 [3072, 768], P(('dp', 'pass')), may hold values from -0.15625 to 0.15625
- gains: bfloat16 [768, 3], P(('dp', 'pass')), may hold values from 0.5 to 1.5
- rel_table: bfloat16 [32, 12], replicated, may hold values from -4 to 4
Outputs:
- block_out: bfloat16 [6144, 768], P(('dp', 'pass'))
- input_grad: float32 [6144, 768], P(('dp', 'pass'))
- passage_grad: bfloat16 [640, 384, 768], P(('dp', 'pass'))
- grad_self_query: float32 [768, 768], P(('dp', 'pass'))
- grad_self_key: float32 [768, 768], P(('dp', 'pass'))
- grad_self_value: float32 [768, 768], P(('dp', 'pass'))
- grad_self_out: float32 [768, 768], P(('dp', 'pass'))
- grad_cross_query: float32 [768, 768], P(('dp', 'pass'))
- grad_cross_key: float32 [768, 768], P(('dp', 'pass'))
- grad_cross_value: float32 [768, 768], P(('dp', 'pass'))
- grad_cross_out: float32 [768, 768], P(('dp', 'pass'))
- grad_up: float32 [768, 3072], P(('dp', 'pass'))
- grad_down: float32 [3072, 768], P(('dp', 'pass'))
- grad_gains: float32 [768, 3], P(('dp', 'pass'))
- grad_table: float32 [32, 12], replicated
The draws below stay inside these ranges and needn't reach their ends.
Inputs may be any that keep to these rules, and one draw needn't show every extreme that they name: `passage_ids`: the 16 queries of one index of dp (consecutive rows) name every pool row of that index's pool devices exactly once; a pool device holds the 20 consecutive pool rows of its own index, and at most 2 of them belong to one query, exactly 2 for some query.
All inputs are finite; a program needn't handle non-finite values. No bound on the sum of `refresh` on one device may be relied on, other than what follows from the above.
Results may differ from the reference program's by a relative error of at most 0.03.
The reference program's roundings to bfloat16 on the way count: a program that leaves them out, or rounds other values in their place, can miss the bound.
Values may be sent and summed in bfloat16 or wider, within the bound.
No kernel may reach another device: no remote copies, remote signals or barrier semaphores. Data moves between devices by JAX's collectives and lax.ppermute only.
A program may use at most 256 MiB of HBM per device.

```python
import jax
import jax.numpy as jnp
from jax import lax

D = 768
HEADS = 12
FF = 3072
BUCKETS = 32
ANS = 192
PASSAGES = 20
PLEN = 384
QUERIES = 32
TOKENS = 6144
POOL = 640
CAP = 2
N_DP = 2
N_PASS = 16


def permute_slots(subkey):
    return jax.random.permutation(subkey, PASSAGES)


def choose_slots(subkey):
    return jax.random.permutation(subkey, N_PASS * CAP)[:PASSAGES]


def draw_passage_ids(key, part):
    key = jax.random.fold_in(key, 7)
    key_pick, key_rows, key_order = jax.random.split(key, 3)
    groups = N_DP
    chosen = jax.vmap(choose_slots)(jax.random.split(key_pick, groups))
    holder = (jnp.arange(N_PASS)[None, :, None] + chosen[:, None, :]) % N_PASS
    row_order = jax.vmap(permute_slots)(jax.random.split(key_rows, groups * N_PASS)).reshape(groups, N_PASS, PASSAGES)
    local_row = row_order[jnp.arange(groups)[:, None, None], holder, jnp.arange(PASSAGES)[None, None, :]]
    passage_id = (jnp.arange(groups)[:, None, None] * N_PASS + holder) * PASSAGES + local_row
    slot_order = jax.vmap(permute_slots)(jax.random.split(key_order, groups * N_PASS)).reshape(groups, N_PASS, PASSAGES)
    return jnp.take_along_axis(passage_id, slot_order, axis=2).reshape(groups * N_PASS, PASSAGES).astype(jnp.int32)


def touch_ends(drawn, key, least, largest):
    index_at = [jax.random.randint(jax.random.fold_in(key, axis), (), 0, length) for axis, length in enumerate(drawn.shape)]
    widest = drawn.shape.index(max(drawn.shape))
    neighbour = index_at[:widest] + [(index_at[widest] + 1) % drawn.shape[widest]] + index_at[widest + 1:]
    return drawn.at[tuple(index_at)].set(least).at[tuple(neighbour)].set(largest)


def spiked(values, own_key, source, target, blocks, factor):
    def block_of(axis_at):
        return (jnp.arange(values.shape[axis_at]) // (values.shape[axis_at] // blocks)).reshape((-1,) + (1,) * (values.ndim - 1 - axis_at))

    first = jax.random.permutation(own_key, blocks)[block_of(target)]
    other_side = (block_of(target) + blocks // 2) % blocks
    return jnp.where((block_of(source) == first) | (block_of(source) == other_side), factor * values, values)


def block_scale(rng, dims, cuts, low, largest):
    factor_of, own = 1.0, jax.random.fold_in(rng, 6)
    for position, parts in cuts:
        draws = jnp.exp(jax.random.uniform(jax.random.fold_in(own, position), (parts,), jnp.float32, low / len(cuts), largest / len(cuts)))
        factor_of = factor_of * jnp.repeat(draws, dims[position] // parts).reshape([-1 if axis == position else 1 for axis in range(len(dims))])
    return factor_of


def scatter_about(rng, extent, width, bound, cuts=(), kind=jnp.bfloat16):
    entries = width * jax.random.normal(rng, extent, jnp.float32)
    if cuts:
        entries = entries * block_scale(rng, extent, cuts, -0.22, 0.18)
    return jnp.clip(entries, -bound, bound).astype(kind)


def gaussian_with(key, shape, scale, bound, pieces, heavy, kind=jnp.bfloat16):
    values = scale * jax.random.normal(key, shape, jnp.float32)
    if pieces:
        values = values * block_scale(key, shape, pieces, -0.22, 0.18)
    return jnp.clip(spiked(values, jax.random.fold_in(key, 3), *heavy), -bound, bound).astype(kind)


def setup_inputs(seed: int = 0) -> dict:
    keys = jax.random.split(jax.random.key(seed), 18)
    return {
        "tokens": gaussian_with(keys[0], (TOKENS, D), 1.0, 6.0, ((0, 32),), (0, 1, 32, 2.75)),
        "cotangent": scatter_about(keys[1], (TOKENS, D), 1.0, 6.0, ((0, 32),)),
        "passages": scatter_about(keys[2], (POOL, PLEN, D), 1.0, 6.0, ((0, 32),)),
        "refresh": touch_ends((jax.random.randint(keys[3], (POOL,), 0, 2) < 1).astype(jnp.int32), jax.random.fold_in(keys[3], 1), 0, 1),
        "passage_ids": draw_passage_ids(jax.random.fold_in(keys[17], 71), 0),
        "self_query": scatter_about(keys[5], (D, D), (16 * D) ** -0.5, 0.0546875, ((0, 32),)),
        "self_key": scatter_about(keys[6], (D, D), D ** -0.5, 0.21875, ((0, 32),)),
        "self_value": scatter_about(keys[7], (D, D), D ** -0.5, 0.21875, ((0, 32),)),
        "self_out": scatter_about(keys[8], (D, D), (D // 4) ** -0.5, 0.4375, ((0, 32),)),
        "cross_query": scatter_about(keys[9], (D, D), (16 * D) ** -0.5, 0.0546875, ((0, 32),)),
        "cross_key": scatter_about(keys[10], (D, D), D ** -0.5, 0.21875, ((0, 32),)),
        "cross_value": scatter_about(keys[11], (D, D), D ** -0.5, 0.21875, ((0, 32),)),
        "cross_out": scatter_about(keys[12], (D, D), (D // 64) ** -0.5, 1.75, ((0, 32),)),
        "up_weight": scatter_about(keys[13], (D, FF), D ** -0.5, 0.21875, ((0, 32),)),
        "down_weight": scatter_about(keys[14], (FF, D), (FF // 2) ** -0.5, 0.15625, ((0, 32),)),
        "gains": jnp.clip(1.0 + 0.1 * jax.random.normal(keys[15], (D, 3), jnp.float32), 0.5, 1.5).astype(jnp.bfloat16),
        "rel_table": scatter_about(keys[16], (BUCKETS, HEADS), 1.0, 4.0),
    }


@jax.custom_vjp
def low(v):
    return lax.optimization_barrier(v.astype(jnp.bfloat16)).astype(jnp.float32)

@jax.custom_vjp
def low_back(v):
    return v

def low_keep(v):
    return (low(v), None)

def low_pass(kept, grad):
    return (grad,)

def back_keep(v):
    return (v, None)

def back_low(kept, grad):
    return (low(grad),)
low.defvjp(low_keep, low_pass)
low_back.defvjp(back_keep, back_low)

def product(left, right):
    return jnp.dot(left, right, precision=lax.Precision.HIGHEST)

def both_ways(value):
    return low_back(low(value))

def norm_rows(value, gain):
    return value * lax.rsqrt(lax.optimization_barrier(jnp.mean(value * value, axis=-1, keepdims=True)) + 1e-06) * gain

def softmax_rows(scores):
    row_max = lax.optimization_barrier(jnp.max(scores, axis=-1, keepdims=True))
    raised = jnp.exp(scores - row_max)
    return raised / lax.optimization_barrier(jnp.sum(raised, axis=-1, keepdims=True))

def bucket_table(length, buckets):
    near_count = buckets // 2
    positions = jnp.arange(length)
    spread = jnp.maximum(positions[:, None] - positions[None, :], 0).astype(jnp.float32)
    bounds = near_count * 8.0 ** (jnp.arange(1, near_count, dtype=jnp.float32) / near_count)
    far_bucket = near_count + lax.optimization_barrier(jnp.sum((spread[:, :, None] >= bounds[None, None, :]).astype(jnp.int32), axis=-1))
    return jnp.where(spread < near_count, spread.astype(jnp.int32), far_bucket)

def one_query(params, tokens, slots):
    query_self, key_self, value_self, out_self, query_cross, key_cross, value_cross, out_cross, up_weight, down_weight, gains, rel_table = params
    head_count = rel_table.shape[1]
    answer_len = tokens.shape[0]
    model_width = tokens.shape[1]
    highest = lax.Precision.HIGHEST
    positions = jnp.arange(answer_len)
    onehot = (bucket_table(answer_len, rel_table.shape[0])[:, :, None] == jnp.arange(rel_table.shape[0])[None, None, :]).astype(jnp.float32)
    bias = jnp.einsum('qkb,bh->hqk', onehot, rel_table, precision=highest)
    normed = low(norm_rows(tokens, gains[:, 0]))
    query_one = both_ways(product(normed, query_self)).reshape(answer_len, head_count, -1)
    key_one = both_ways(product(normed, key_self)).reshape(answer_len, head_count, -1)
    value_one = both_ways(product(normed, value_self)).reshape(answer_len, head_count, -1)
    scores = low_back(jnp.einsum('qhe,khe->hqk', query_one, key_one, precision=highest) + bias)
    scores = jnp.where(positions[:, None] >= positions[None, :], scores, -1e+30)
    weights_one = low(softmax_rows(scores))
    mixed = both_ways(jnp.einsum('hqk,khe->qhe', weights_one, value_one, precision=highest).reshape(answer_len, model_width))
    stream_one = tokens + low_back(product(mixed, out_self))
    normed = low(norm_rows(stream_one, gains[:, 1]))
    query_two = both_ways(product(normed, query_cross)).reshape(answer_len, head_count, -1)
    encoded = low_back(slots)
    key_two = both_ways(product(encoded, key_cross)).reshape(encoded.shape[0], head_count, -1)
    value_two = both_ways(product(encoded, value_cross)).reshape(encoded.shape[0], head_count, -1)
    scores = low_back(jnp.einsum('qhe,khe->hqk', query_two, key_two, precision=highest))
    weights_two = low(softmax_rows(scores))
    mixed = both_ways(jnp.einsum('hqk,khe->qhe', weights_two, value_two, precision=highest).reshape(answer_len, model_width))
    stream_two = stream_one + low_back(product(mixed, out_cross))
    normed = low(norm_rows(stream_two, gains[:, 2]))
    inner = low_back(product(normed, up_weight))
    active = low(jax.nn.gelu(inner, approximate=True))
    return stream_two + low_back(product(active, down_weight))

def reference(tokens, cotangent, passages, refresh, passage_ids, self_query, self_key, self_value, self_out, cross_query, cross_key, cross_value, cross_out, up_weight, down_weight, gains, rel_table):
    params = tuple((weight_arg.astype(jnp.float32) for weight_arg in (self_query, self_key, self_value, self_out, cross_query, cross_key, cross_value, cross_out, up_weight, down_weight, gains, rel_table)))
    states = tokens.astype(jnp.float32).reshape(QUERIES, ANS, D)
    slots = passages.astype(jnp.float32)[passage_ids].reshape(QUERIES, PASSAGES * PLEN, D)

    def whole_layer(states, slots, params):

        def query_step(carried, query_items):
            return (carried, one_query(params, query_items[0], query_items[1]))
        carried, result = lax.scan(jax.checkpoint(query_step), jnp.zeros((), jnp.float32), (states, slots))
        return result
    result, pullback = jax.vjp(whole_layer, states, slots, params)
    d_states, d_slots, d_params = pullback(cotangent.astype(jnp.float32).reshape(QUERIES, ANS, D))
    d_pool = jnp.zeros((POOL, PLEN, D), jnp.float32).at[passage_ids.reshape(-1)].add(d_slots.reshape(QUERIES * PASSAGES, PLEN, D))
    passage_grad = (d_pool * refresh.astype(jnp.float32)[:, None, None]).astype(jnp.bfloat16)
    return (result.reshape(TOKENS, D).astype(jnp.bfloat16), d_states.reshape(TOKENS, D), passage_grad, d_params[0], d_params[1], d_params[2], d_params[3], d_params[4], d_params[5], d_params[6], d_params[7], d_params[8], d_params[9], d_params[10], d_params[11])
```

```python
from functools import partial

import jax
import jax.numpy as jnp
from jax import lax
from jax.experimental import pallas as pl
from jax.experimental.pallas import tpu as pltpu
from jax.sharding import PartitionSpec as P

F32 = jnp.float32
BF16 = jnp.bfloat16
GROUP = 4
BLOCK = 4
STAT_ROWS = 16
BACK_ROWS = 32
FLOOR = -1e30


def norm_rows(value, gain):
    return value * lax.rsqrt(jnp.mean(value * value, axis=-1, keepdims=True) + 1e-06) * gain


def bucket_table(length, buckets):
    near_count = buckets // 2
    positions = jnp.arange(length)
    spread = jnp.maximum(positions[:, None] - positions[None, :], 0).astype(F32)
    bounds = near_count * 8.0 ** (jnp.arange(1, near_count, dtype=F32) / near_count)
    far_bucket = near_count + jnp.sum(
        (spread[:, :, None] >= bounds[None, None, :]).astype(jnp.int32), axis=-1
    )
    return jnp.where(spread < near_count, spread.astype(jnp.int32), far_bucket)


def matmul(left, right):
    return jnp.dot(left, right, preferred_element_type=F32)


def left_t(left, right):
    return jnp.einsum("td,te->de", left, right, preferred_element_type=F32)


def right_t(left, right):
    return jnp.einsum("te,de->td", left, right, preferred_element_type=F32)


def dot(left, right, dims):
    return lax.dot_general(left, right, (dims, ((), ())), preferred_element_type=F32)


def split_parts(value, count):
    parts = []
    for _ in range(count):
        part = value.astype(BF16).astype(F32)
        parts.append(part)
        value = value - part
    return parts


def spread_heads(rows, head):
    column = lax.broadcasted_iota(jnp.int32, rows.shape, 1) // head
    return jnp.concatenate(
        [jnp.where(column == h, rows, jnp.zeros_like(rows)) for h in range(GROUP)], axis=0
    )


def pick_heads(full, head, rows):
    lane = lax.broadcasted_iota(jnp.int32, (head, GROUP * rows), 1) // rows
    out = jnp.zeros((head, GROUP * rows), F32)
    for h in range(GROUP):
        out = out + jnp.where(lane == h, full[h * head : (h + 1) * head, :], 0.0)
    return out


def attend_kernel(plen, head, rows, asker_ref, owner_ref, core_ref, q_ref, kv_ref, out_ref, acc, top, total, stat):
    group, step = pl.program_id(0), pl.program_id(1)
    queries = q_ref.shape[0]
    width = GROUP * head

    @pl.when(step == 0)
    def _():
        acc[...] = jnp.zeros_like(acc)
        top[...] = jnp.full_like(top, FLOOR)
        total[...] = jnp.zeros_like(total)

    @pl.when((step == 0) & (group == 0))
    def _():
        stat[...] = jnp.zeros_like(stat)

    for p in range(BLOCK):
        slot = step * BLOCK + p
        owner = owner_ref[slot]
        spread = spread_heads(q_ref[asker_ref[slot]], head)
        keys = kv_ref[p * plen : (p + 1) * plen, :width]
        values = kv_ref[p * plen : (p + 1) * plen, width:]
        scores = dot(keys, spread, ((1,), (1,)))
        old = top[owner]
        new = jnp.maximum(old, jnp.max(scores, axis=0, keepdims=True))
        raised = jnp.exp(scores - new)
        scale = jnp.exp(old - new)
        top[owner] = new
        total[owner] = total[owner] * scale + jnp.sum(raised, axis=0, keepdims=True)
        mixed = dot(values, raised.astype(BF16), ((0,), (0,)))
        acc[owner] = acc[owner] * scale + pick_heads(mixed, head, rows)

    @pl.when(step == pl.num_programs(1) - 1)
    def _():
        def flush(j, carry):
            half = jnp.bitwise_xor(jnp.bitwise_and(j, 1), core_ref[0])
            place = pl.multiple_of(group * head, head)
            out_ref[half, j // 2, pl.ds(place, head), :] = acc[j].astype(BF16)
            parts = split_parts(top[j], 3) + split_parts(total[j], 2)
            for t, part in enumerate(parts):
                stat[j, pl.ds(group * len(parts) + t, 1), :] = part
            return carry

        lax.fori_loop(0, queries, flush, 0)

    @pl.when((step == pl.num_programs(1) - 1) & (group == pl.num_programs(0) - 1))
    def _():
        base = pl.num_programs(0) * head

        def flush(j, carry):
            half = jnp.bitwise_xor(jnp.bitwise_and(j, 1), core_ref[0])
            out_ref[half, j // 2, out_ref.shape[2] - STAT_ROWS :, :] = stat[j].astype(BF16)
            return carry

        lax.fori_loop(0, queries, flush, 0)


def attend(asker, owner, core, q_all, kv, plen, head):
    queries, rows, width = q_all.shape
    groups = width // (GROUP * head)
    slots = kv.shape[0] // plen
    lanes = GROUP * rows
    out_rows = groups * head + STAT_ROWS
    return pl.pallas_call(
        partial(attend_kernel, plen, head, rows),
        out_shape=jax.ShapeDtypeStruct((2, queries // 2, out_rows, lanes), BF16),
        grid_spec=pltpu.PrefetchScalarGridSpec(
            num_scalar_prefetch=3,
            grid=(groups, slots // BLOCK),
            in_specs=[
                pl.BlockSpec((queries, rows, GROUP * head), lambda g, b, *_: (0, 0, g)),
                pl.BlockSpec((BLOCK * plen, 2 * GROUP * head), lambda g, b, *_: (b, g)),
            ],
            out_specs=pl.BlockSpec((2, queries // 2, out_rows, lanes), lambda g, b, *_: (0, 0, 0, 0)),
            scratch_shapes=[
                pltpu.VMEM((queries, head, lanes), F32),
                pltpu.VMEM((queries, 1, lanes), F32),
                pltpu.VMEM((queries, 1, lanes), F32),
                pltpu.VMEM((queries, STAT_ROWS, lanes), F32),
            ],
        ),
        compiler_params=pltpu.CompilerParams(vmem_limit_bytes=56 * 2**20),
        cost_estimate=pl.CostEstimate(
            flops=16 * rows * kv.shape[0] * width,
            bytes_accessed=4 * kv.size,
            transcendentals=rows * kv.shape[0] * width // head,
        ),
        name="attend",
    )(asker, owner, core, q_all, kv)


def read_stats(stat, groups):
    found = []
    for g in range(groups):
        at = g * 5
        found.append(
            (
                stat[at : at + 1] + stat[at + 1 : at + 2] + stat[at + 2 : at + 3],
                stat[at + 3 : at + 4] + stat[at + 4 : at + 5],
            )
        )
    return found


def pair_kernel(groups, head, a_ref, b_ref, out_ref):
    body = groups * head
    stats = [read_stats(ref[0, body:, :].astype(F32), groups) for ref in (a_ref, b_ref)]
    rows = []
    for g in range(groups):
        (top_a, sum_a), (top_b, sum_b) = stats[0][g], stats[1][g]
        top = jnp.maximum(top_a, top_b)
        w_a, w_b = jnp.exp(top_a - top), jnp.exp(top_b - top)
        at = slice(g * head, (g + 1) * head)
        out_ref[0, at, :] = (
            a_ref[0, at, :].astype(F32) * w_a + b_ref[0, at, :].astype(F32) * w_b
        ).astype(BF16)
        rows += split_parts(top, 3) + split_parts(sum_a * w_a + sum_b * w_b, 2)
    rows.append(jnp.zeros((STAT_ROWS - len(rows), rows[0].shape[1]), F32))
    out_ref[0, body:, :] = jnp.concatenate(rows, axis=0).astype(BF16)


def pair_merge(kept, came, groups, head):
    count, rows, lanes = kept.shape
    spec = pl.BlockSpec((1, rows, lanes), lambda i: (i, 0, 0))
    return pl.pallas_call(
        partial(pair_kernel, groups, head),
        out_shape=jax.ShapeDtypeStruct(kept.shape, BF16),
        grid=(count,),
        in_specs=[spec, spec],
        out_specs=spec,
        cost_estimate=pl.CostEstimate(flops=4 * kept.size, bytes_accessed=6 * kept.size, transcendentals=0),
        name="pair_merge",
    )(kept, came)


def final_kernel(groups, head, in_ref, out_ref, log_ref):
    body = groups * head
    count = in_ref.shape[0]
    stats = [read_stats(in_ref[i, body:, :].astype(F32), groups) for i in range(count)]
    logs = []
    for g in range(groups):
        top = stats[0][g][0]
        for i in range(1, count):
            top = jnp.maximum(top, stats[i][g][0])
        weights = [jnp.exp(stats[i][g][0] - top) for i in range(count)]
        whole = stats[0][g][1] * weights[0]
        at = slice(g * head, (g + 1) * head)
        mixed = in_ref[0, at, :].astype(F32) * weights[0]
        for i in range(1, count):
            whole = whole + stats[i][g][1] * weights[i]
            mixed = mixed + in_ref[i, at, :].astype(F32) * weights[i]
        out_ref[at, :] = mixed / whole
        logs.append(top + jnp.log(whole))
    log_ref[...] = jnp.concatenate(logs, axis=0)


def final_merge(parts, groups, head):
    lanes = parts.shape[2]
    return pl.pallas_call(
        partial(final_kernel, groups, head),
        out_shape=(
            jax.ShapeDtypeStruct((groups * head, lanes), F32),
            jax.ShapeDtypeStruct((groups, lanes), F32),
        ),
        compiler_params=pltpu.CompilerParams(vmem_limit_bytes=56 * 2**20),
        name="final_merge",
    )(parts)


def attend_back_kernel(plen, head, rows, asker_ref, owner_ref, core_ref, q_ref, do_ref, stat_ref, kv_ref, dkv_ref, out_ref, acc, log, delta):
    group, step = pl.program_id(0), pl.program_id(1)
    groups = pl.num_programs(0)
    queries = q_ref.shape[0]
    width = GROUP * head

    @pl.when(step == 0)
    def _():
        acc[...] = jnp.zeros_like(acc)

        def fill(j, carry):
            stat = stat_ref[j].astype(F32)
            row = lax.broadcasted_iota(jnp.int32, stat.shape, 0) // 3
            log[j] = jnp.sum(jnp.where(row == group, stat, 0.0), axis=0, keepdims=True)
            delta[j] = jnp.sum(jnp.where(row == group + groups, stat, 0.0), axis=0, keepdims=True)
            return carry

        lax.fori_loop(0, queries, fill, 0)

    for p in range(BLOCK):
        slot = step * BLOCK + p
        owner, asker = owner_ref[slot], asker_ref[slot]
        q_spread = spread_heads(q_ref[asker], head)
        do_spread = spread_heads(do_ref[asker], head)
        at = slice(p * plen, (p + 1) * plen)
        keys = kv_ref[at, :width]
        values = kv_ref[at, width:]
        soft = jnp.exp(dot(keys, q_spread, ((1,), (1,))) - log[asker])
        d_soft = dot(values, do_spread, ((1,), (1,)))
        d_score = (soft * (d_soft - delta[asker])).astype(BF16)
        dkv_ref[at, width:] = dot(soft.astype(BF16), do_spread, ((1,), (0,))).astype(BF16)
        dkv_ref[at, :width] = dot(d_score, q_spread, ((1,), (0,))).astype(BF16)
        acc[owner] += pick_heads(dot(keys, d_score, ((0,), (0,))), head, rows)

    @pl.when(step == pl.num_programs(1) - 1)
    def _():
        def flush(j, carry):
            half = jnp.bitwise_xor(jnp.bitwise_and(j, 1), core_ref[0])
            place = pl.multiple_of(group * head, head)
            out_ref[half, j // 2, pl.ds(place, head), :] = acc[j].astype(BF16)
            return carry

        lax.fori_loop(0, queries, flush, 0)


def attend_back(asker, owner, core, q_all, do_all, kv, plen, head):
    queries, rows, width = q_all.shape
    groups = width // (GROUP * head)
    slots = kv.shape[0] // plen
    lanes = GROUP * rows
    out_rows = groups * head
    return pl.pallas_call(
        partial(attend_back_kernel, plen, head, rows),
        out_shape=(
            jax.ShapeDtypeStruct(kv.shape, BF16),
            jax.ShapeDtypeStruct((2, queries // 2, out_rows, lanes), BF16),
        ),
        grid_spec=pltpu.PrefetchScalarGridSpec(
            num_scalar_prefetch=3,
            grid=(groups, slots // BLOCK),
            in_specs=[
                pl.BlockSpec((queries, rows, GROUP * head), lambda g, b, *_: (0, 0, g)),
                pl.BlockSpec((queries, rows, GROUP * head), lambda g, b, *_: (0, 0, g)),
                pl.BlockSpec((queries, BACK_ROWS, lanes), lambda g, b, *_: (0, rows // BACK_ROWS, 0)),
                pl.BlockSpec((BLOCK * plen, 2 * GROUP * head), lambda g, b, *_: (b, g)),
            ],
            out_specs=(
                pl.BlockSpec((BLOCK * plen, 2 * GROUP * head), lambda g, b, *_: (b, g)),
                pl.BlockSpec((2, queries // 2, out_rows, lanes), lambda g, b, *_: (0, 0, 0, 0)),
            ),
            scratch_shapes=[
                pltpu.VMEM((queries, head, lanes), F32),
                pltpu.VMEM((queries, 1, lanes), F32),
                pltpu.VMEM((queries, 1, lanes), F32),
            ],
        ),
        compiler_params=pltpu.CompilerParams(vmem_limit_bytes=60 * 2**20),
        cost_estimate=pl.CostEstimate(
            flops=40 * rows * kv.shape[0] * width,
            bytes_accessed=8 * kv.size,
            transcendentals=rows * kv.shape[0] * width // head,
        ),
        name="attend_back",
    )(asker, owner, core, q_all, do_all, do_all, kv)


def pass_gather(block, count):
    major = count // 4
    ring = [(i, (i + 4) % count) for i in range(count)]
    pieces = [block]
    for _ in range(major - 1):
        pieces.append(lax.ppermute(pieces[-1], "pass", ring))
    across = [lax.ppermute(piece, "pass", [(i, i ^ 2) for i in range(count)]) for piece in pieces]
    pieces = pieces + across
    return jnp.stack(
        pieces + [lax.ppermute(piece, "pass", [(i, i ^ 1) for i in range(count)]) for piece in pieces]
    )


def gather_place(query, own, count):
    major = count // 4
    turn = jnp.mod(own // 4 - query // 4, major)
    return turn + major * ((own // 2) % 2 != (query // 2) % 2) + 2 * major * (own % 2 != query % 2)


def chip_exchange(parts, count):
    groups = [[c + 2 * k for k in range(count // 2)] for c in range(2)]
    return lax.all_to_all(
        parts, "pass", split_axis=0, concat_axis=0, tiled=True, axis_index_groups=groups
    )


def core_swap(value, count):
    return lax.ppermute(value, "pass", [(i, i ^ 1) for i in range(count)])


def on_device(
    tokens,
    cotangent,
    passages,
    refresh,
    passage_ids,
    self_query,
    self_key,
    self_value,
    self_out,
    cross_query,
    cross_key,
    cross_value,
    cross_out,
    up_weight,
    down_weight,
    gains,
    rel_table,
):
    both = ("dp", "pass")
    pass_count = lax.axis_size("pass")
    device_id = lax.axis_index(both)
    own_pass = lax.axis_index("pass")
    per_query, plen, model_width = passages.shape
    head_count = rel_table.shape[1]
    head = model_width // head_count
    rows = tokens.shape[0]
    groups = head_count // GROUP
    wide = GROUP * head
    shard = self_query.shape[0]

    def gather(value):
        return lax.all_gather(value, both, axis=0, tiled=True)

    kv_shard = jnp.stack(
        [cross_key.reshape(shard, groups, wide), cross_value.reshape(shard, groups, wide)], axis=2
    ).reshape(shard, 2 * model_width)
    gain_pad = jnp.pad(gains, ((0, 0), (0, 128 - gains.shape[1])))
    first = gather(
        jnp.concatenate(
            [self_query, self_key, self_value, self_out, cross_query, kv_shard, gain_pad], axis=1
        )
    )
    first, more = lax.optimization_barrier((first, (cross_out, up_weight, down_weight)))
    second = gather(jnp.concatenate([more[0], more[1]], axis=1))
    down_full = gather(more[2])
    cuts = [first[:, i * model_width : (i + 1) * model_width] for i in range(5)]
    query_self, key_self, value_self, out_self, query_cross = cuts
    kv_weight = first[:, 5 * model_width : 7 * model_width]
    gain_all = first[:, 7 * model_width : 7 * model_width + 3].astype(F32)
    out_cross, up_full = second[:, :model_width], second[:, model_width:]

    row_ids = device_id * per_query + jnp.arange(per_query)
    owned = jnp.any(passage_ids[:, :, None] == row_ids[None, None, :], axis=1)
    owner = jnp.sum(
        jnp.where(owned, jnp.arange(passage_ids.shape[0])[:, None], 0), axis=0
    ).astype(jnp.int32)
    asker = gather_place(owner, own_pass, pass_count).astype(jnp.int32)
    core = (own_pass % 2).astype(jnp.int32).reshape(1)

    inputs = tokens.astype(F32)
    positions = jnp.arange(rows)
    causal = positions[:, None] >= positions[None, :]
    onehot_low = (
        bucket_table(rows, rel_table.shape[0])[:, :, None]
        == jnp.arange(rel_table.shape[0])[None, None, :]
    ).astype(BF16)
    bias = jnp.einsum("qkb,bh->hqk", onehot_low, rel_table, preferred_element_type=F32)
    normed_self = norm_rows(inputs, gain_all[:, 0]).astype(BF16)
    query_one = matmul(normed_self, query_self).astype(BF16).reshape(rows, head_count, head)
    key_one = matmul(normed_self, key_self).astype(BF16).reshape(rows, head_count, head)
    value_one = matmul(normed_self, value_self).astype(BF16).reshape(rows, head_count, head)
    scores = jnp.einsum("qhe,khe->hqk", query_one, key_one, preferred_element_type=F32) + bias
    scores = jnp.where(causal[None, :, :], scores, FLOOR)
    raised = jnp.exp(scores - jnp.max(scores, axis=-1, keepdims=True))
    weights_one = raised / jnp.sum(raised, axis=-1, keepdims=True)
    weights_low = weights_one.astype(BF16)
    mixed_one = (
        jnp.einsum("hqk,khe->qhe", weights_low, value_one, preferred_element_type=F32)
        .reshape(rows, model_width)
        .astype(BF16)
    )
    stream_one = inputs + matmul(mixed_one, out_self)
    normed_cross = norm_rows(stream_one, gain_all[:, 1]).astype(BF16)
    query_two = matmul(normed_cross, query_cross).astype(BF16)

    encoded = passages.reshape(per_query * plen, model_width)
    q_all = pass_gather(query_two, pass_count)
    kv = matmul(encoded, kv_weight).astype(BF16)
    partials = attend(asker, owner, core, q_all, kv, plen, head)
    merged = pair_merge(partials[0], core_swap(partials[1], pass_count), groups, head)
    mixed_t, log_total = final_merge(chip_exchange(merged, pass_count), groups, head)

    def rows_first(value):
        return (
            value.reshape(groups, head, GROUP, rows).transpose(3, 0, 2, 1).reshape(rows, model_width)
        )

    mixed_full = rows_first(mixed_t)
    mixed_two = mixed_full.astype(BF16)
    stream_two = stream_one + matmul(mixed_two, out_cross)
    normed_ffn = norm_rows(stream_two, gain_all[:, 2]).astype(BF16)
    inner = matmul(normed_ffn, up_full)
    active = jax.nn.gelu(inner, approximate=True).astype(BF16)
    block_out = (stream_two + matmul(active, down_full)).astype(BF16)
    d_active = right_t(cotangent, down_full)
    unused, gelu_back = jax.vjp(partial(jax.nn.gelu, approximate=True), inner)
    d_inner = gelu_back(d_active)[0].astype(BF16)
    d_normed_ffn = right_t(d_inner, up_full)
    unused, norm_back = jax.vjp(norm_rows, stream_two, gain_all[:, 2])
    d_stream_two, d_gain_ffn = norm_back(d_normed_ffn)
    d_stream_two = d_stream_two + cotangent.astype(F32)
    grad_two = d_stream_two.astype(BF16)
    d_mixed_two = right_t(grad_two, out_cross).astype(BF16)
    delta = jnp.sum(
        (d_mixed_two.astype(F32) * mixed_full).reshape(rows, groups, GROUP, head), axis=-1
    )
    delta = delta.transpose(1, 2, 0).reshape(groups, GROUP * rows)

    def three(value):
        high = lax.reduce_precision(value, 8, 7)
        middle = lax.reduce_precision(value - high, 8, 7)
        return jnp.stack([high, middle, value - high - middle], axis=1).reshape(3 * groups, -1)

    stats = jnp.concatenate([three(log_total), three(delta)], axis=0).astype(BF16)
    stats = jnp.pad(stats, ((0, BACK_ROWS - stats.shape[0]), (0, 0)))
    do_all = pass_gather(jnp.concatenate([d_mixed_two, stats], axis=0), pass_count)

    d_down = left_t(active, cotangent).astype(BF16)
    d_up = left_t(normed_ffn, d_inner).astype(BF16)
    d_out_cross = left_t(mixed_two, grad_two).astype(BF16)

    def scatter(value):
        return lax.psum_scatter(value, both, scatter_dimension=0, tiled=True).astype(F32)

    grad_down = scatter(d_down)
    grad_second = scatter(jnp.concatenate([d_out_cross, d_up], axis=1))

    dkv, dq_parts = attend_back(asker, owner, core, q_all, do_all, kv, plen, head)
    dq_merged = (
        dq_parts[0].astype(F32) + core_swap(dq_parts[1], pass_count).astype(F32)
    ).astype(BF16)
    dq_t = jnp.sum(chip_exchange(dq_merged, pass_count).astype(F32), axis=0)
    d_query_two = rows_first(dq_t).astype(BF16)

    d_encoded = right_t(dkv, kv_weight).astype(BF16).astype(F32)
    keep = refresh.astype(F32)[:, None, None]
    passage_grad = (d_encoded.reshape(per_query, plen, model_width) * keep).astype(BF16)
    d_kv = left_t(encoded, dkv).astype(BF16)

    d_query_cross = left_t(normed_cross, d_query_two)
    d_normed_cross = right_t(d_query_two, query_cross)
    unused, norm_back = jax.vjp(norm_rows, stream_one, gain_all[:, 1])
    d_stream_one, d_gain_cross = norm_back(d_normed_cross)
    d_stream_one = d_stream_one + d_stream_two
    grad_one = d_stream_one.astype(BF16)
    d_out_self = left_t(mixed_one, grad_one)
    d_mixed_one = right_t(grad_one, out_self).astype(BF16).reshape(rows, head_count, head)
    d_value_one = (
        jnp.einsum("hqk,qhe->khe", weights_low, d_mixed_one, preferred_element_type=F32)
        .reshape(rows, model_width)
        .astype(BF16)
    )
    d_weights = jnp.einsum("qhe,khe->hqk", d_mixed_one, value_one, preferred_element_type=F32)
    d_score = (
        weights_one * (d_weights - jnp.sum(weights_one * d_weights, axis=-1, keepdims=True))
    ).astype(BF16)
    d_table = jnp.einsum("hqk,qkb->bh", d_score, onehot_low, preferred_element_type=F32)
    d_query_one = (
        jnp.einsum("hqk,khe->qhe", d_score, key_one, preferred_element_type=F32)
        .reshape(rows, model_width)
        .astype(BF16)
    )
    d_key_one = (
        jnp.einsum("hqk,qhe->khe", d_score, query_one, preferred_element_type=F32)
        .reshape(rows, model_width)
        .astype(BF16)
    )
    d_query_self = left_t(normed_self, d_query_one)
    d_key_self = left_t(normed_self, d_key_one)
    d_value_self = left_t(normed_self, d_value_one)
    d_normed_self = (
        right_t(d_query_one, query_self)
        + right_t(d_key_one, key_self)
        + right_t(d_value_one, value_self)
    )
    unused, norm_back = jax.vjp(norm_rows, inputs, gain_all[:, 0])
    d_inputs, d_gain_self = norm_back(d_normed_self)
    d_inputs = d_inputs + d_stream_one
    d_gains = jnp.stack([d_gain_self, d_gain_cross, d_gain_ffn], axis=1)
    d_gains = jnp.pad(d_gains, ((0, 0), (0, 128 - d_gains.shape[1])))
    grad_kv = scatter(d_kv)
    last = scatter(
        jnp.concatenate(
            [
                d_query_self.astype(BF16),
                d_key_self.astype(BF16),
                d_value_self.astype(BF16),
                d_out_self.astype(BF16),
                d_query_cross.astype(BF16),
                d_gains.astype(BF16),
            ],
            axis=1,
        )
    )
    table_grad = lax.psum(d_table, both)
    grad_kv = grad_kv.reshape(shard, groups, 2, wide)
    mine = [last[:, i * model_width : (i + 1) * model_width] for i in range(5)]
    return (
        block_out,
        d_inputs,
        passage_grad,
        mine[0],
        mine[1],
        mine[2],
        mine[3],
        mine[4],
        grad_kv[:, :, 0].reshape(shard, model_width),
        grad_kv[:, :, 1].reshape(shard, model_width),
        grad_second[:, :model_width],
        grad_second[:, model_width:],
        grad_down,
        last[:, 5 * model_width : 5 * model_width + gains.shape[1]],
        table_grad,
    )


def solution(mesh):
    split = P(("dp", "pass"), None)
    cube = P(("dp", "pass"), None, None)
    in_specs = (split, split, cube, P(("dp", "pass")), P("dp", None)) + (split,) * 11 + (P(),)
    out_specs = (split, split, cube) + (split,) * 11 + (P(),)
    return jax.shard_map(
        on_device, mesh=mesh, in_specs=in_specs, out_specs=out_specs, check_vma=False
    )
```

```python
from functools import partial

import jax
import jax.numpy as jnp
from jax import lax
from jax.experimental import pallas as pl
from jax.experimental.pallas import tpu as pltpu
from jax.sharding import PartitionSpec as P

F32 = jnp.float32
BF16 = jnp.bfloat16
GROUP = 4
BLOCK = 4
STAT_ROWS = 16
FLOOR = -1e30


def norm_rows(value, gain):
    return value * lax.rsqrt(jnp.mean(value * value, axis=-1, keepdims=True) + 1e-06) * gain


def bucket_table(length, buckets):
    near_count = buckets // 2
    positions = jnp.arange(length)
    spread = jnp.maximum(positions[:, None] - positions[None, :], 0).astype(F32)
    bounds = near_count * 8.0 ** (jnp.arange(1, near_count, dtype=F32) / near_count)
    far_bucket = near_count + jnp.sum(
        (spread[:, :, None] >= bounds[None, None, :]).astype(jnp.int32), axis=-1
    )
    return jnp.where(spread < near_count, spread.astype(jnp.int32), far_bucket)


def matmul(left, right):
    return jnp.dot(left, right, preferred_element_type=F32)


def left_t(left, right):
    return jnp.einsum("td,te->de", left, right, preferred_element_type=F32)


def right_t(left, right):
    return jnp.einsum("te,de->td", left, right, preferred_element_type=F32)


def dot(left, right, dims):
    return lax.dot_general(left, right, (dims, ((), ())), preferred_element_type=F32)


def split_parts(value, count):
    parts = []
    for _ in range(count):
        part = value.astype(BF16).astype(F32)
        parts.append(part)
        value = value - part
    return parts


def spread_heads(rows, head):
    column = lax.broadcasted_iota(jnp.int32, rows.shape, 1) // head
    return jnp.concatenate(
        [jnp.where(column == h, rows, jnp.zeros_like(rows)) for h in range(GROUP)], axis=0
    )


def pick_heads(full, head, rows):
    lane = lax.broadcasted_iota(jnp.int32, (head, GROUP * rows), 1) // rows
    out = jnp.zeros((head, GROUP * rows), F32)
    for h in range(GROUP):
        out = out + jnp.where(lane == h, full[h * head : (h + 1) * head, :], 0.0)
    return out


def attend_kernel(plen, head, rows, asker_ref, owner_ref, core_ref, q_ref, kv_ref, out_ref, acc, top, total):
    step = pl.program_id(0)
    queries = q_ref.shape[0]
    width = GROUP * head

    @pl.when(step == 0)
    def _():
        acc[...] = jnp.zeros_like(acc)
        top[...] = jnp.full_like(top, FLOOR)
        total[...] = jnp.zeros_like(total)

    for p in range(BLOCK):
        slot = step * BLOCK + p
        owner = owner_ref[slot]
        spread = spread_heads(q_ref[asker_ref[slot]], head)
        keys = kv_ref[p * plen : (p + 1) * plen, :width]
        values = kv_ref[p * plen : (p + 1) * plen, width:]
        scores = dot(keys, spread, ((1,), (1,)))
        here = jnp.max(scores, axis=0, keepdims=True)
        raised = jnp.exp(scores - here)
        here_total = jnp.sum(raised, axis=0, keepdims=True)
        mixed = pick_heads(dot(values, raised.astype(BF16), ((0,), (0,))), head, rows)
        old = top[owner]
        new = jnp.maximum(old, here)
        old_scale, here_scale = jnp.exp(old - new), jnp.exp(here - new)
        top[owner] = new
        total[owner] = total[owner] * old_scale + here_total * here_scale
        acc[owner] = acc[owner] * old_scale + mixed * here_scale

    @pl.when(step == pl.num_programs(0) - 1)
    def _():
        def flush(j, carry):
            half = jnp.bitwise_xor(jnp.bitwise_and(j, 1), core_ref[0])
            out_ref[half, j // 2, :head, :] = acc[j].astype(BF16)
            parts = split_parts(top[j], 3) + split_parts(total[j], 2)
            parts.append(jnp.zeros((STAT_ROWS - len(parts), parts[0].shape[1]), F32))
            out_ref[half, j // 2, head:, :] = jnp.concatenate(parts, axis=0).astype(BF16)
            return carry

        lax.fori_loop(0, queries, flush, 0)


def attend(asker, owner, core, q_part, kv, group, plen, head):
    queries, rows, width = q_part.shape
    slots = kv.shape[0] // plen
    lanes = GROUP * rows
    shape = (2, queries // 2, head + STAT_ROWS, lanes)
    return pl.pallas_call(
        partial(attend_kernel, plen, head, rows),
        out_shape=jax.ShapeDtypeStruct(shape, BF16),
        grid_spec=pltpu.PrefetchScalarGridSpec(
            num_scalar_prefetch=3,
            grid=(slots // BLOCK,),
            in_specs=[
                pl.BlockSpec((queries, rows, width), lambda b, *_: (0, 0, 0)),
                pl.BlockSpec((BLOCK * plen, 2 * width), lambda b, *_: (b, group)),
            ],
            out_specs=pl.BlockSpec(shape, lambda b, *_: (0, 0, 0, 0)),
            scratch_shapes=[
                pltpu.VMEM((queries, head, lanes), F32),
                pltpu.VMEM((queries, 1, lanes), F32),
                pltpu.VMEM((queries, 1, lanes), F32),
            ],
        ),
        compiler_params=pltpu.CompilerParams(vmem_limit_bytes=56 * 2**20),
        cost_estimate=pl.CostEstimate(
            flops=16 * rows * kv.shape[0] * width,
            bytes_accessed=4 * kv.shape[0] * width,
            transcendentals=rows * kv.shape[0] * GROUP,
        ),
        name="attend",
    )(asker, owner, core, q_part, kv)


def read_stats(stat, at):
    return (
        stat[at : at + 1] + stat[at + 1 : at + 2] + stat[at + 2 : at + 3],
        stat[at + 3 : at + 4] + stat[at + 4 : at + 5],
    )


def pair_kernel(head, place, a_ref, b_ref, out_ref, stat_ref):
    top_a, sum_a = read_stats(a_ref[0, head:, :].astype(F32), 0)
    top_b, sum_b = read_stats(b_ref[0, head:, :].astype(F32), 0)
    top = jnp.maximum(top_a, top_b)
    w_a, w_b = jnp.exp(top_a - top), jnp.exp(top_b - top)
    out_ref[0] = (
        a_ref[0, :head, :].astype(F32) * w_a + b_ref[0, :head, :].astype(F32) * w_b
    ).astype(BF16)
    rows = split_parts(top, 3) + split_parts(sum_a * w_a + sum_b * w_b, 2)
    lanes = top.shape[1]
    if place:
        rows.insert(0, jnp.zeros((place, lanes), F32))
    rows.append(jnp.zeros((STAT_ROWS - 5 - place, lanes), F32))
    stat_ref[0] = jnp.concatenate(rows, axis=0).astype(BF16)


def pair_merge(kept, came, head, place):
    count, rows, lanes = kept.shape

    def spec(size):
        return pl.BlockSpec((1, size, lanes), lambda i: (i, 0, 0))

    return pl.pallas_call(
        partial(pair_kernel, head, place),
        out_shape=(
            jax.ShapeDtypeStruct((count, head, lanes), BF16),
            jax.ShapeDtypeStruct((count, STAT_ROWS, lanes), BF16),
        ),
        grid=(count,),
        in_specs=[spec(rows), spec(rows)],
        out_specs=(spec(head), spec(STAT_ROWS)),
        cost_estimate=pl.CostEstimate(flops=4 * kept.size, bytes_accessed=6 * kept.size, transcendentals=0),
        name="pair_merge",
    )(kept, came)


def final_kernel(head, *refs):
    groups = len(refs) - 2
    out_ref, log_ref = refs[groups:]
    last = refs[groups - 1]
    count = last.shape[0]
    stat = [last[i, head:, :].astype(F32) for i in range(count)]
    for g in range(groups):
        found = [read_stats(stat[i], 5 * g) for i in range(count)]
        top = found[0][0]
        for i in range(1, count):
            top = jnp.maximum(top, found[i][0])
        weights = [jnp.exp(found[i][0] - top) for i in range(count)]
        whole = found[0][1] * weights[0]
        mixed = refs[g][0, :head, :].astype(F32) * weights[0]
        for i in range(1, count):
            whole = whole + found[i][1] * weights[i]
            mixed = mixed + refs[g][i, :head, :].astype(F32) * weights[i]
        out_ref[g * head : (g + 1) * head, :] = mixed / whole
        log_ref[g : g + 1, :] = top + jnp.log(whole)


def final_merge(parts, head):
    lanes = parts[0].shape[2]
    return pl.pallas_call(
        partial(final_kernel, head),
        out_shape=(
            jax.ShapeDtypeStruct((len(parts) * head, lanes), F32),
            jax.ShapeDtypeStruct((len(parts), lanes), F32),
        ),
        compiler_params=pltpu.CompilerParams(vmem_limit_bytes=56 * 2**20),
        name="final_merge",
    )(*parts)


def attend_back_kernel(plen, head, rows, asker_ref, owner_ref, core_ref, q_ref, do_ref, stat_ref, kv_ref, held_ref, dkv_ref, out_ref, acc, log, delta):
    step = pl.program_id(0)
    queries = q_ref.shape[0]
    width = GROUP * head

    @pl.when(step == 0)
    def _():
        acc[...] = jnp.zeros_like(acc)
        third = (GROUP * rows) // width

        def fill(j, carry):
            stat = stat_ref[j].astype(F32)
            row = lax.broadcasted_iota(jnp.int32, stat.shape, 0)
            for at, ref, count in ((0, log, 3), (3 * third, delta, 2)):
                pieces = []
                for t in range(third):
                    wanted = row == at + t
                    for k in range(1, count):
                        wanted = wanted | (row == at + k * third + t)
                    pieces.append(jnp.sum(jnp.where(wanted, stat, 0.0), axis=0, keepdims=True))
                ref[j] = jnp.concatenate(pieces, axis=1)
            return carry

        lax.fori_loop(0, queries, fill, 0)

    for p in range(BLOCK):
        slot = step * BLOCK + p
        owner, asker = owner_ref[slot], asker_ref[slot]
        q_spread = spread_heads(q_ref[asker], head)
        do_spread = spread_heads(do_ref[asker], head)
        at = slice(p * plen, (p + 1) * plen)
        keys = kv_ref[at, :width]
        values = kv_ref[at, width:]
        soft = jnp.exp(dot(keys, q_spread, ((1,), (1,))) - log[asker])
        d_soft = dot(values, do_spread, ((1,), (1,)))
        d_score = (soft * (d_soft - delta[asker])).astype(BF16)
        dkv_ref[at, width:] = dot(soft.astype(BF16), do_spread, ((1,), (0,))).astype(BF16)
        dkv_ref[at, :width] = dot(d_score, q_spread, ((1,), (0,))).astype(BF16)
        acc[owner] += pick_heads(dot(keys, d_score, ((0,), (0,))), head, rows)

    @pl.when(step == pl.num_programs(0) - 1)
    def _():
        def flush(j, carry):
            half = jnp.bitwise_xor(jnp.bitwise_and(j, 1), core_ref[0])
            out_ref[half, j // 2] = acc[j].astype(BF16)
            return carry

        lax.fori_loop(0, queries, flush, 0)


def attend_back(asker, owner, core, q_part, do_part, kv, held, group, plen, head):
    queries, rows, width = q_part.shape
    slots = kv.shape[0] // plen
    lanes = GROUP * rows
    shape = (2, queries // 2, head, lanes)
    return pl.pallas_call(
        partial(attend_back_kernel, plen, head, rows),
        out_shape=(jax.ShapeDtypeStruct(kv.shape, BF16), jax.ShapeDtypeStruct(shape, BF16)),
        grid_spec=pltpu.PrefetchScalarGridSpec(
            num_scalar_prefetch=3,
            grid=(slots // BLOCK,),
            in_specs=[
                pl.BlockSpec((queries, rows, width), lambda b, *_: (0, 0, 0)),
                pl.BlockSpec((queries, rows, width), lambda b, *_: (0, 0, 0)),
                pl.BlockSpec((queries, STAT_ROWS, width), lambda b, *_: (0, rows // STAT_ROWS, 0)),
                pl.BlockSpec((BLOCK * plen, 2 * width), lambda b, *_: (b, group)),
                pl.BlockSpec(memory_space=pl.ANY),
            ],
            out_specs=(
                pl.BlockSpec((BLOCK * plen, 2 * width), lambda b, *_: (b, group)),
                pl.BlockSpec(shape, lambda b, *_: (0, 0, 0, 0)),
            ),
            scratch_shapes=[
                pltpu.VMEM((queries, head, lanes), F32),
                pltpu.VMEM((queries, 1, lanes), F32),
                pltpu.VMEM((queries, 1, lanes), F32),
            ],
        ),
        input_output_aliases={7: 0} if held is not kv else {},
        compiler_params=pltpu.CompilerParams(vmem_limit_bytes=60 * 2**20),
        cost_estimate=pl.CostEstimate(
            flops=40 * rows * kv.shape[0] * width,
            bytes_accessed=8 * kv.shape[0] * width,
            transcendentals=rows * kv.shape[0] * GROUP,
        ),
        name="attend_back",
    )(asker, owner, core, q_part, do_part, do_part, kv, held)


def flip(value, bit):
    count = lax.axis_size("pass")
    return lax.ppermute(value, "pass", [(i, i ^ bit) for i in range(count)])


def pass_gather(block):
    count = lax.axis_size("pass")
    pieces = [block]
    for k in range(1, count // 4):
        ring = [(i, (i + 4 * k) % count) for i in range(count)]
        pieces.append(lax.ppermute(block, "pass", ring))
    line = jnp.stack(pieces)
    plane = jnp.concatenate([line, flip(line, 2)])
    return jnp.concatenate([plane, flip(plane, 1)])


def gather_place(query, own, count):
    major = count // 4
    turn = jnp.mod(own // 4 - query // 4, major)
    return turn + major * ((own // 2) % 2 != (query // 2) % 2) + 2 * major * (own % 2 != query % 2)


def chip_exchange(parts):
    count = lax.axis_size("pass")
    groups = [[c + 2 * k for k in range(count // 2)] for c in range(2)]
    return lax.all_to_all(
        parts, "pass", split_axis=0, concat_axis=0, tiled=True, axis_index_groups=groups
    )


def line_exchange(parts):
    count = lax.axis_size("pass")
    groups = [[r + 4 * k for k in range(count // 4)] for r in range(4)]
    return lax.all_to_all(
        parts, "pass", split_axis=0, concat_axis=0, tiled=True, axis_index_groups=groups
    )


def swap_half(value, place, axis, send):
    kept = lax.dynamic_index_in_dim(value, place, axis, keepdims=False)
    sent = lax.dynamic_index_in_dim(value, 1 - place, axis, keepdims=False)
    return (kept.astype(F32) + send(sent).astype(F32)).astype(BF16)


def scatter_sum(value):
    n_dp, count = lax.axis_size("dp"), lax.axis_size("pass")
    own_dp, own = lax.axis_index("dp"), lax.axis_index("pass")
    rows, columns = value.shape
    part = value.reshape(n_dp, count // 4, 2, 2, rows // (n_dp * count), columns)
    part = swap_half(part, own % 2, 3, lambda v: flip(v, 1))

    def over_dp(v):
        if n_dp == 2:
            return swap_half(v, own_dp, 0, lambda u: lax.ppermute(u, "dp", [(0, 1), (1, 0)]))
        return lax.psum_scatter(v, "dp", scatter_dimension=0, tiled=False)

    def over_near(v, axis):
        return swap_half(v, (own // 2) % 2, axis, lambda u: flip(u, 2))

    cut = columns // 256 * 128
    left = over_near(over_dp(part[..., :cut]), 1)
    right = over_dp(over_near(part[..., cut:], 2))
    line = line_exchange(jnp.concatenate([left, right], axis=-1))
    return jnp.sum(line.astype(F32), axis=0)


def total_sum(value):
    for bit in range((lax.axis_size("pass") - 1).bit_length()):
        value = value + flip(value, 1 << bit)
    n_dp = lax.axis_size("dp")
    for bit in range((n_dp - 1).bit_length()):
        pairs = [(i, i ^ (1 << bit)) for i in range(n_dp)]
        value = value + lax.ppermute(value, "dp", pairs)
    return value


def on_device(
    tokens,
    cotangent,
    passages,
    refresh,
    passage_ids,
    self_query,
    self_key,
    self_value,
    self_out,
    cross_query,
    cross_key,
    cross_value,
    cross_out,
    up_weight,
    down_weight,
    gains,
    rel_table,
):
    both = ("dp", "pass")
    pass_count = lax.axis_size("pass")
    device_id = lax.axis_index(both)
    own_pass = lax.axis_index("pass")
    per_query, plen, model_width = passages.shape
    head_count = rel_table.shape[1]
    head = model_width // head_count
    rows = tokens.shape[0]
    groups = head_count // GROUP
    wide = GROUP * head
    shard = self_query.shape[0]

    def gather(value):
        return lax.all_gather(value, both, axis=0, tiled=True)

    kv_shard = jnp.stack(
        [cross_key.reshape(shard, groups, wide), cross_value.reshape(shard, groups, wide)], axis=2
    ).reshape(shard, 2 * model_width)
    gain_pad = jnp.pad(gains, ((0, 0), (0, 128 - gains.shape[1])))
    first = gather(
        jnp.concatenate(
            [self_query, self_key, self_value, self_out, cross_query, kv_shard, gain_pad], axis=1
        )
    )
    first, more = lax.optimization_barrier((first, (cross_out, up_weight, down_weight)))
    second = gather(jnp.concatenate([more[0], more[1]], axis=1))
    down_full = gather(more[2])
    cuts = [first[:, i * model_width : (i + 1) * model_width] for i in range(5)]
    query_self, key_self, value_self, out_self, query_cross = cuts
    kv_weight = first[:, 5 * model_width : 7 * model_width]
    gain_all = first[:, 7 * model_width : 7 * model_width + 3].astype(F32)
    out_cross, up_full = second[:, :model_width], second[:, model_width:]

    row_ids = device_id * per_query + jnp.arange(per_query)
    owned = jnp.any(passage_ids[:, :, None] == row_ids[None, None, :], axis=1)
    owner = jnp.sum(
        jnp.where(owned, jnp.arange(passage_ids.shape[0])[:, None], 0), axis=0
    ).astype(jnp.int32)
    asker = gather_place(owner, own_pass, pass_count).astype(jnp.int32)
    core = (own_pass % 2).astype(jnp.int32).reshape(1)

    inputs = tokens.astype(F32)
    positions = jnp.arange(rows)
    causal = positions[:, None] >= positions[None, :]
    onehot_low = (
        bucket_table(rows, rel_table.shape[0])[:, :, None]
        == jnp.arange(rel_table.shape[0])[None, None, :]
    ).astype(BF16)
    bias = jnp.einsum("qkb,bh->hqk", onehot_low, rel_table, preferred_element_type=F32)
    normed_self = norm_rows(inputs, gain_all[:, 0]).astype(BF16)
    query_one = matmul(normed_self, query_self).astype(BF16).reshape(rows, head_count, head)
    key_one = matmul(normed_self, key_self).astype(BF16).reshape(rows, head_count, head)
    value_one = matmul(normed_self, value_self).astype(BF16).reshape(rows, head_count, head)
    scores = jnp.einsum("qhe,khe->hqk", query_one, key_one, preferred_element_type=F32) + bias
    scores = jnp.where(causal[None, :, :], scores, FLOOR)
    raised = jnp.exp(scores - jnp.max(scores, axis=-1, keepdims=True))
    weights_one = raised / jnp.sum(raised, axis=-1, keepdims=True)
    weights_low = weights_one.astype(BF16)
    mixed_one = (
        jnp.einsum("hqk,khe->qhe", weights_low, value_one, preferred_element_type=F32)
        .reshape(rows, model_width)
        .astype(BF16)
    )
    stream_one = inputs + matmul(mixed_one, out_self)
    normed_cross = norm_rows(stream_one, gain_all[:, 1]).astype(BF16)
    query_two = matmul(normed_cross, query_cross).astype(BF16)

    encoded = passages.reshape(per_query * plen, model_width)
    q_parts = [pass_gather(query_two[:, g * wide : (g + 1) * wide]) for g in range(groups)]
    kv = matmul(encoded, kv_weight).astype(BF16)
    arrived, stat_rows = [], None
    for g in range(groups):
        mine, other = attend(asker, owner, core, q_parts[g], kv, g, plen, head)
        body, stat = pair_merge(mine, flip(other, 1), head, 5 * g)
        stat_rows = stat if stat_rows is None else stat_rows + stat
        if g == groups - 1:
            body = jnp.concatenate([body, stat_rows], axis=1)
        arrived.append(chip_exchange(body))
    mixed_t, log_total = final_merge(arrived, head)

    def rows_first(value):
        return (
            value.reshape(groups, head, GROUP, rows).transpose(3, 0, 2, 1).reshape(rows, model_width)
        )

    mixed_full = rows_first(mixed_t)
    mixed_two = mixed_full.astype(BF16)
    stream_two = stream_one + matmul(mixed_two, out_cross)
    normed_ffn = norm_rows(stream_two, gain_all[:, 2]).astype(BF16)
    inner = matmul(normed_ffn, up_full)
    active = jax.nn.gelu(inner, approximate=True).astype(BF16)
    block_out = (stream_two + matmul(active, down_full)).astype(BF16)
    d_active = right_t(cotangent, down_full)
    unused, gelu_back = jax.vjp(partial(jax.nn.gelu, approximate=True), inner)
    d_inner = gelu_back(d_active)[0].astype(BF16)
    d_normed_ffn = right_t(d_inner, up_full)
    unused, norm_back = jax.vjp(norm_rows, stream_two, gain_all[:, 2])
    d_stream_two, d_gain_ffn = norm_back(d_normed_ffn)
    d_stream_two = d_stream_two + cotangent.astype(F32)
    grad_two = d_stream_two.astype(BF16)
    d_mixed_two = right_t(grad_two, out_cross).astype(BF16)
    delta = jnp.sum(
        (d_mixed_two.astype(F32) * mixed_full).reshape(rows, groups, GROUP, head), axis=-1
    )
    delta = delta.transpose(1, 2, 0).reshape(groups, GROUP * rows)

    def pieces_of(value, parts):
        found = []
        for _ in range(parts - 1):
            found.append(lax.reduce_precision(value, 8, 7))
            value = value - found[-1]
        return jnp.stack(found + [value], axis=1)

    stats = jnp.concatenate([pieces_of(log_total, 3), pieces_of(delta, 2)], axis=1).astype(BF16)
    stats = stats.reshape(groups, -1, wide)
    stats = jnp.pad(stats, ((0, 0), (0, STAT_ROWS - stats.shape[1]), (0, 0)))
    do_parts = [
        pass_gather(jnp.concatenate([d_mixed_two[:, g * wide : (g + 1) * wide], stats[g]], axis=0))
        for g in range(groups)
    ]

    d_down = left_t(active, cotangent).astype(BF16)
    d_second = jnp.concatenate([left_t(mixed_two, grad_two), left_t(normed_ffn, d_inner)], axis=1).astype(BF16)

    def scatter(value):
        return lax.psum_scatter(value, both, scatter_dimension=0, tiled=True).astype(F32)

    do_parts[0], d_down, d_second = lax.optimization_barrier((do_parts[0], d_down, d_second))
    grad_down = scatter(d_down)
    grad_second = scatter(d_second)

    dkv, dq_parts = kv, []
    for g in range(groups):
        dkv, (mine, other) = attend_back(
            asker, owner, core, q_parts[g], do_parts[g], kv, dkv, g, plen, head
        )
        merged = (mine.astype(F32) + flip(other, 1).astype(F32)).astype(BF16)
        dq_parts.append(jnp.sum(chip_exchange(merged).astype(F32), axis=0))
    d_query_two = rows_first(jnp.concatenate(dq_parts, axis=0)).astype(BF16)
    d_kv = left_t(encoded, dkv).astype(BF16)
    d_query_two, d_kv = lax.optimization_barrier((d_query_two, d_kv))

    d_query_cross = left_t(normed_cross, d_query_two)
    d_normed_cross = right_t(d_query_two, query_cross)
    unused, norm_back = jax.vjp(norm_rows, stream_one, gain_all[:, 1])
    d_stream_one, d_gain_cross = norm_back(d_normed_cross)
    d_stream_one = d_stream_one + d_stream_two
    grad_one = d_stream_one.astype(BF16)
    d_out_self = left_t(mixed_one, grad_one)
    early = scatter_sum(jnp.concatenate([d_out_self.astype(BF16), d_query_cross.astype(BF16), d_kv], axis=1))
    d_mixed_one = right_t(grad_one, out_self).astype(BF16).reshape(rows, head_count, head)
    d_value_one = (
        jnp.einsum("hqk,qhe->khe", weights_low, d_mixed_one, preferred_element_type=F32)
        .reshape(rows, model_width)
        .astype(BF16)
    )
    d_weights = jnp.einsum("qhe,khe->hqk", d_mixed_one, value_one, preferred_element_type=F32)
    d_score = (
        weights_one * (d_weights - jnp.sum(weights_one * d_weights, axis=-1, keepdims=True))
    ).astype(BF16)
    d_table = jnp.einsum("hqk,qkb->bh", d_score, onehot_low, preferred_element_type=F32)
    d_query_one = (
        jnp.einsum("hqk,khe->qhe", d_score, key_one, preferred_element_type=F32)
        .reshape(rows, model_width)
        .astype(BF16)
    )
    d_key_one = (
        jnp.einsum("hqk,qhe->khe", d_score, query_one, preferred_element_type=F32)
        .reshape(rows, model_width)
        .astype(BF16)
    )
    d_query_self = left_t(normed_self, d_query_one)
    d_key_self = left_t(normed_self, d_key_one)
    d_value_self = left_t(normed_self, d_value_one)
    d_normed_self = (
        right_t(d_query_one, query_self)
        + right_t(d_key_one, key_self)
        + right_t(d_value_one, value_self)
    )
    unused, norm_back = jax.vjp(norm_rows, inputs, gain_all[:, 0])
    d_inputs, d_gain_self = norm_back(d_normed_self)
    d_inputs = d_inputs + d_stream_one
    d_gains = jnp.stack([d_gain_self, d_gain_cross, d_gain_ffn], axis=1)
    d_gains = jnp.pad(d_gains, ((0, 0), (0, 128 - d_gains.shape[1])))
    late = jnp.concatenate([d_query_self, d_key_self, d_value_self, d_gains], axis=1).astype(BF16)
    late, dkv_late = lax.optimization_barrier((late, dkv))
    last = scatter_sum(late)
    table_grad = total_sum(d_table)
    d_encoded = right_t(dkv_late, kv_weight).astype(BF16).astype(F32)
    keep = refresh.astype(F32)[:, None, None]
    passage_grad = (d_encoded.reshape(per_query, plen, model_width) * keep).astype(BF16)

    def cut_columns(value, at):
        return value[:, at * model_width : (at + 1) * model_width]

    grad_kv = early[:, 2 * model_width :]
    grad_kv = grad_kv.reshape(shard, groups, 2, wide)
    return (
        block_out,
        d_inputs,
        passage_grad,
        cut_columns(last, 0),
        cut_columns(last, 1),
        cut_columns(last, 2),
        cut_columns(early, 0),
        cut_columns(early, 1),
        grad_kv[:, :, 0].reshape(shard, model_width),
        grad_kv[:, :, 1].reshape(shard, model_width),
        grad_second[:, :model_width],
        grad_second[:, model_width:],
        grad_down,
        last[:, 3 * model_width : 3 * model_width + gains.shape[1]],
        table_grad,
    )


def solution(mesh):
    split = P(("dp", "pass"), None)
    cube = P(("dp", "pass"), None, None)
    in_specs = (split, split, cube, P(("dp", "pass")), P("dp", None)) + (split,) * 11 + (P(),)
    out_specs = (split, split, cube) + (split,) * 11 + (P(),)
    return jax.shard_map(
        on_device, mesh=mesh, in_specs=in_specs, out_specs=out_specs, check_vma=False
    )
```

```python
from functools import partial

import jax
import jax.numpy as jnp
from jax import lax
from jax.experimental import pallas as pl
from jax.experimental.pallas import tpu as pltpu
from jax.sharding import PartitionSpec as P

F32 = jnp.float32
BF16 = jnp.bfloat16
GROUP = 4
BLOCK = 4
STAT_ROWS = 16
CHUNK = 256
AHEAD = 2
FLOOR = -1e30


def norm_rows(value, gain):
    return value * lax.rsqrt(jnp.mean(value * value, axis=-1, keepdims=True) + 1e-06) * gain


def bucket_table(length, buckets):
    near_count = buckets // 2
    positions = jnp.arange(length)
    spread = jnp.maximum(positions[:, None] - positions[None, :], 0).astype(F32)
    bounds = near_count * 8.0 ** (jnp.arange(1, near_count, dtype=F32) / near_count)
    far_bucket = near_count + jnp.sum(
        (spread[:, :, None] >= bounds[None, None, :]).astype(jnp.int32), axis=-1
    )
    return jnp.where(spread < near_count, spread.astype(jnp.int32), far_bucket)


def matmul(left, right):
    return jnp.dot(left, right, preferred_element_type=F32)


def left_t(left, right):
    return jnp.einsum("td,te->de", left, right, preferred_element_type=F32)


def right_t(left, right):
    return jnp.einsum("te,de->td", left, right, preferred_element_type=F32)


def dot(left, right, dims):
    return lax.dot_general(left, right, (dims, ((), ())), preferred_element_type=F32)


def split_parts(value, count):
    parts = []
    for _ in range(count):
        part = value.astype(BF16).astype(F32)
        parts.append(part)
        value = value - part
    return parts


def spread_heads(rows, head):
    column = lax.broadcasted_iota(jnp.int32, rows.shape, 1) // head
    return jnp.concatenate(
        [jnp.where(column == h, rows, jnp.zeros_like(rows)) for h in range(GROUP)], axis=0
    )


def pick_chunk(full, head, rows, start):
    chunk = full.shape[1]
    first = start // rows
    lane = (lax.broadcasted_iota(jnp.int32, (head, chunk), 1) + start) // rows - first
    out = full[:head]
    for h in range(1, full.shape[0] // head):
        out = jnp.where(lane == h, full[h * head : (h + 1) * head], out)
    return out


def flush_queries(core_ref, queries, pack, mine_ref, other_ref):
    def flush(chip, carry):
        mine_ref[chip, 0] = pack(2 * chip + core_ref[0])
        other_ref[chip, 0] = pack(2 * chip + 1 - core_ref[0])
        return carry

    lax.fori_loop(0, queries // 2, flush, 0)


def attend_kernel(plen, head, rows, asker_ref, owner_ref, core_ref, q_ref, kv_ref, mine_ref, other_ref, acc, top, total):
    step = pl.program_id(1)
    queries = q_ref.shape[0]
    width = GROUP * head

    @pl.when(step == 0)
    def _():
        acc[...] = jnp.zeros_like(acc)
        top[...] = jnp.full_like(top, FLOOR)
        total[...] = jnp.zeros_like(total)

    lanes = GROUP * rows
    chunk = min(CHUNK, lanes)

    def begin(unit):
        p, c = divmod(unit, lanes // chunk)
        if c == 0:
            spreads[p] = spread_heads(q_ref[asker_ref[step * BLOCK + p]], head)
            turned[p] = kv_ref[p * plen : (p + 1) * plen, width:].T
        keys = kv_ref[p * plen : (p + 1) * plen, :width]
        return dot(keys, spreads[p][c * chunk : (c + 1) * chunk], ((1,), (1,)))

    def finish(unit, scores):
        p, c = divmod(unit, lanes // chunk)
        owner = owner_ref[step * BLOCK + p]
        at = pl.ds(c * chunk, chunk)
        first, last = c * chunk // rows, ((c + 1) * chunk - 1) // rows
        here = jnp.max(scores, axis=0, keepdims=True)
        raised = jnp.exp(scores - here)
        here_total = jnp.sum(raised, axis=0, keepdims=True)
        full = dot(turned[p][first * head : (last + 1) * head], raised.astype(BF16), ((1,), (0,)))
        mixed = pick_chunk(full, head, rows, c * chunk)
        old = top[owner, :, at]
        new = jnp.maximum(old, here)
        old_scale, here_scale = jnp.exp(old - new), jnp.exp(here - new)
        top[owner, :, at] = new
        total[owner, :, at] = total[owner, :, at] * old_scale + here_total * here_scale
        acc[owner, :, at] = acc[owner, :, at] * old_scale + mixed * here_scale

    spreads, turned = {}, {}
    units = BLOCK * (lanes // chunk)
    waiting = [begin(u) for u in range(min(AHEAD, units))]
    for unit in range(units):
        if unit + AHEAD < units:
            waiting.append(begin(unit + AHEAD))
        finish(unit, waiting.pop(0))

    @pl.when(step == pl.num_programs(1) - 1)
    def _():
        def pack(j):
            parts = split_parts(top[j], 3) + split_parts(total[j], 2)
            parts.append(jnp.zeros((STAT_ROWS - len(parts), parts[0].shape[1]), F32))
            return jnp.concatenate([acc[j]] + parts, axis=0).astype(BF16)

        flush_queries(core_ref, queries, pack, mine_ref, other_ref)


def attend(asker, owner, core, q_part, kv, first, plen, head):
    queries, rows, columns = q_part.shape
    width = GROUP * head
    slots = kv.shape[0] // plen
    lanes = GROUP * rows
    groups = columns // width
    block = (queries // 2, 1, head + STAT_ROWS, lanes)
    out = jax.ShapeDtypeStruct((queries // 2, groups, head + STAT_ROWS, lanes), BF16)
    return pl.pallas_call(
        partial(attend_kernel, plen, head, rows),
        out_shape=(out, out),
        grid_spec=pltpu.PrefetchScalarGridSpec(
            num_scalar_prefetch=3,
            grid=(groups, slots // BLOCK),
            in_specs=[
                pl.BlockSpec((queries, rows, width), lambda g, b, *_: (0, 0, g)),
                pl.BlockSpec((BLOCK * plen, 2 * width), lambda g, b, *_: (b, g + first)),
            ],
            out_specs=(pl.BlockSpec(block, lambda g, b, *_: (0, g, 0, 0)),) * 2,
            scratch_shapes=[
                pltpu.VMEM((queries, head, lanes), F32),
                pltpu.VMEM((queries, 1, lanes), F32),
                pltpu.VMEM((queries, 1, lanes), F32),
            ],
        ),
        compiler_params=pltpu.CompilerParams(vmem_limit_bytes=60 * 2**20),
        cost_estimate=pl.CostEstimate(
            flops=16 * rows * kv.shape[0] * columns,
            bytes_accessed=4 * kv.shape[0] * columns,
            transcendentals=rows * kv.shape[0] * GROUP * groups,
        ),
        name="attend",
    )(asker, owner, core, q_part, kv)


def read_stats(stat):
    return stat[0:1] + stat[1:2] + stat[2:3], stat[3:4] + stat[4:5]


def merge_kernel(head, a_ref, b_ref, out_ref):
    for i in range(a_ref.shape[0]):
        for g in range(a_ref.shape[1]):
            top_a, sum_a = read_stats(a_ref[i, g, head:, :].astype(F32))
            top_b, sum_b = read_stats(b_ref[i, g, head:, :].astype(F32))
            top = jnp.maximum(top_a, top_b)
            w_a, w_b = jnp.exp(top_a - top), jnp.exp(top_b - top)
            body = a_ref[i, g, :head, :].astype(F32) * w_a + b_ref[i, g, :head, :].astype(F32) * w_b
            rows = split_parts(top, 3) + split_parts(sum_a * w_a + sum_b * w_b, 2)
            rows.append(jnp.zeros((STAT_ROWS - 5, top.shape[1]), F32))
            out_ref[i, g] = jnp.concatenate([body] + rows, axis=0).astype(BF16)


def core_merge(kept, came, head):
    spec = pl.BlockSpec((kept.shape[0] // 4,) + kept.shape[1:], lambda i: (i, 0, 0, 0))
    return pl.pallas_call(
        partial(merge_kernel, head),
        out_shape=jax.ShapeDtypeStruct(kept.shape, BF16),
        grid=(4,),
        in_specs=[spec, spec],
        out_specs=spec,
        cost_estimate=pl.CostEstimate(flops=4 * kept.size, bytes_accessed=6 * kept.size, transcendentals=0),
        name="core_merge",
    )(kept, came)


def final_kernel(head, *refs):
    out_ref, log_ref = refs[-2:]
    at = 0
    for ref in refs[:-2]:
        count = ref.shape[0]
        for g in range(ref.shape[1]):
            found = [read_stats(ref[i, g, head:, :].astype(F32)) for i in range(count)]
            top = found[0][0]
            for i in range(1, count):
                top = jnp.maximum(top, found[i][0])
            weights = [jnp.exp(found[i][0] - top) for i in range(count)]
            whole = found[0][1] * weights[0]
            mixed = ref[0, g, :head, :].astype(F32) * weights[0]
            for i in range(1, count):
                whole = whole + found[i][1] * weights[i]
                mixed = mixed + ref[i, g, :head, :].astype(F32) * weights[i]
            out_ref[at * head : (at + 1) * head, :] = mixed / whole
            log_ref[at : at + 1, :] = top + jnp.log(whole)
            at += 1


def final_merge(parts, head):
    lanes = parts[0].shape[3]
    groups = sum(part.shape[1] for part in parts)
    return pl.pallas_call(
        partial(final_kernel, head),
        out_shape=(
            jax.ShapeDtypeStruct((groups * head, lanes), F32),
            jax.ShapeDtypeStruct((groups, lanes), F32),
        ),
        compiler_params=pltpu.CompilerParams(vmem_limit_bytes=56 * 2**20),
        name="final_merge",
    )(*parts)


def attend_back_kernel(plen, head, rows, asker_ref, owner_ref, core_ref, q_ref, do_ref, stat_ref, kv_ref, held_ref, dkv_ref, mine_ref, other_ref, acc, log, delta):
    step = pl.program_id(1)
    queries = q_ref.shape[0]
    width = GROUP * head

    @pl.when(step == 0)
    def _():
        acc[...] = jnp.zeros_like(acc)
        third = (GROUP * rows) // width

        def fill(j, carry):
            stat = stat_ref[j].astype(F32)
            row = lax.broadcasted_iota(jnp.int32, stat.shape, 0)
            for at, ref, count in ((0, log, 3), (3 * third, delta, 2)):
                pieces = []
                for t in range(third):
                    wanted = row == at + t
                    for k in range(1, count):
                        wanted = wanted | (row == at + k * third + t)
                    pieces.append(jnp.sum(jnp.where(wanted, stat, 0.0), axis=0, keepdims=True))
                ref[j] = jnp.concatenate(pieces, axis=1)
            return carry

        lax.fori_loop(0, queries, fill, 0)

    lanes = GROUP * rows
    chunk = min(CHUNK, lanes)

    def begin(unit):
        p, c = divmod(unit, lanes // chunk)
        rows_at = slice(p * plen, (p + 1) * plen)
        if c == 0:
            asker = asker_ref[step * BLOCK + p]
            q_spread[p] = spread_heads(q_ref[asker], head)
            do_spread[p] = spread_heads(do_ref[asker], head)
            turned[p] = kv_ref[rows_at, :width].T
        at = slice(c * chunk, (c + 1) * chunk)
        return (
            dot(kv_ref[rows_at, :width], q_spread[p][at], ((1,), (1,))),
            dot(kv_ref[rows_at, width:], do_spread[p][at], ((1,), (1,))),
        )

    def finish(unit, found):
        scores, d_soft = found
        p, c = divmod(unit, lanes // chunk)
        owner, asker = owner_ref[step * BLOCK + p], asker_ref[step * BLOCK + p]
        at = pl.ds(c * chunk, chunk)
        cut = slice(c * chunk, (c + 1) * chunk)
        first, last = c * chunk // rows, ((c + 1) * chunk - 1) // rows
        soft = jnp.exp(scores - log[asker, :, at])
        d_score = (soft * (d_soft - delta[asker, :, at])).astype(BF16)
        d_value = dot(soft.astype(BF16), do_spread[p][cut], ((1,), (0,)))
        d_key = dot(d_score, q_spread[p][cut], ((1,), (0,)))
        sums[p] = (d_key, d_value) if c == 0 else (sums[p][0] + d_key, sums[p][1] + d_value)
        full = dot(turned[p][first * head : (last + 1) * head], d_score, ((1,), (0,)))
        acc[owner, :, at] += pick_chunk(full, head, rows, c * chunk)
        if c == lanes // chunk - 1:
            rows_at = slice(p * plen, (p + 1) * plen)
            dkv_ref[rows_at, :width] = sums[p][0].astype(BF16)
            dkv_ref[rows_at, width:] = sums[p][1].astype(BF16)

    q_spread, do_spread, turned, sums = {}, {}, {}, {}
    units = BLOCK * (lanes // chunk)
    waiting = [begin(u) for u in range(min(AHEAD, units))]
    for unit in range(units):
        if unit + AHEAD < units:
            waiting.append(begin(unit + AHEAD))
        finish(unit, waiting.pop(0))

    @pl.when(step == pl.num_programs(1) - 1)
    def _():
        flush_queries(core_ref, queries, lambda j: acc[j].astype(BF16), mine_ref, other_ref)


def attend_back(asker, owner, core, q_part, do_part, kv, held, first, plen, head):
    queries, rows, columns = q_part.shape
    width = GROUP * head
    slots = kv.shape[0] // plen
    lanes = GROUP * rows
    groups = columns // width
    block = (queries // 2, 1, head, lanes)
    out = jax.ShapeDtypeStruct((queries // 2, groups, head, lanes), BF16)
    return pl.pallas_call(
        partial(attend_back_kernel, plen, head, rows),
        out_shape=(jax.ShapeDtypeStruct(kv.shape, BF16), out, out),
        grid_spec=pltpu.PrefetchScalarGridSpec(
            num_scalar_prefetch=3,
            grid=(groups, slots // BLOCK),
            in_specs=[
                pl.BlockSpec((queries, rows, width), lambda g, b, *_: (0, 0, g)),
                pl.BlockSpec((queries, rows, width), lambda g, b, *_: (0, 0, g)),
                pl.BlockSpec((queries, STAT_ROWS, width), lambda g, b, *_: (0, rows // STAT_ROWS, g)),
                pl.BlockSpec((BLOCK * plen, 2 * width), lambda g, b, *_: (b, g + first)),
                pl.BlockSpec(memory_space=pl.ANY),
            ],
            out_specs=(
                pl.BlockSpec((BLOCK * plen, 2 * width), lambda g, b, *_: (b, g + first)),
                pl.BlockSpec(block, lambda g, b, *_: (0, g, 0, 0)),
                pl.BlockSpec(block, lambda g, b, *_: (0, g, 0, 0)),
            ),
            scratch_shapes=[
                pltpu.VMEM((queries, head, lanes), F32),
                pltpu.VMEM((queries, 1, lanes), F32),
                pltpu.VMEM((queries, 1, lanes), F32),
            ],
        ),
        input_output_aliases={} if held is kv else {7: 0},
        compiler_params=pltpu.CompilerParams(vmem_limit_bytes=60 * 2**20),
        cost_estimate=pl.CostEstimate(
            flops=40 * rows * kv.shape[0] * columns,
            bytes_accessed=8 * kv.shape[0] * columns,
            transcendentals=rows * kv.shape[0] * GROUP * groups,
        ),
        name="attend_back",
    )(asker, owner, core, q_part, do_part, do_part, kv, held)


def source_kernel(keep_ref, fetch_ref, dkv_ref, weight_ref, out_ref):
    kept = keep_ref[pl.program_id(0)]

    @pl.when(kept == 0)
    def _():
        out_ref[...] = jnp.zeros_like(out_ref)

    @pl.when(kept != 0)
    def _():
        out_ref[0] = dot(dkv_ref[...], weight_ref[...], ((1,), (1,))).astype(BF16)


def source_grads(refresh, dkv, weight, plen):
    slots = refresh.shape[0]
    model_width = weight.shape[0]
    fetch = lax.cummax(jnp.where(refresh != 0, jnp.arange(slots), 0), axis=0).astype(jnp.int32)
    return pl.pallas_call(
        source_kernel,
        out_shape=jax.ShapeDtypeStruct((slots, plen, model_width), BF16),
        grid_spec=pltpu.PrefetchScalarGridSpec(
            num_scalar_prefetch=2,
            grid=(slots,),
            in_specs=[
                pl.BlockSpec((plen, dkv.shape[1]), lambda r, keep, fetch: (fetch[r], 0)),
                pl.BlockSpec(weight.shape, lambda r, *_: (0, 0)),
            ],
            out_specs=pl.BlockSpec((1, plen, model_width), lambda r, *_: (r, 0, 0)),
        ),
        compiler_params=pltpu.CompilerParams(vmem_limit_bytes=40 * 2**20),
        cost_estimate=pl.CostEstimate(
            flops=slots * plen * model_width * 2 * model_width,
            bytes_accessed=4 * slots * plen * model_width,
            transcendentals=0,
        ),
        name="source_grads",
    )(refresh, fetch, dkv, weight)


def outer_kernel(starts, added, half_ref, *refs):
    out_ref = refs[-1]
    tile = pl.program_id(1)
    for k in range(len(starts) - 1):

        @pl.when((tile >= starts[k]) & (tile < starts[k + 1]))
        def _(k=k):
            found = dot(refs[2 * k][...], refs[2 * k + 1][...], ((0,), (0,)))
            if added:
                found = found + refs[-2][...].astype(F32)
            out_ref[...] = found.astype(BF16)


def outer(half, pairs, came=None):
    rows = pairs[0][0].shape[0]
    height = min(left.shape[1] for left, _ in pairs)
    height = height if height <= 1024 else height // 4
    total_rows = pairs[0][0].shape[1]
    width = min(right.shape[1] for _, right in pairs) // 2
    counts = [right.shape[1] // 2 // width for _, right in pairs]
    starts = [sum(counts[:k]) for k in range(len(counts) + 1)]
    operands, specs = [], []
    for k, (left, right) in enumerate(pairs):

        def right_map(r, t, half_ref, start=starts[k], count=counts[k]):
            return (0, half_ref[0] * count + jnp.clip(t - start, 0, count - 1))

        operands += [left, right]
        specs += [
            pl.BlockSpec((rows, height), lambda r, t, half_ref: (0, r)),
            pl.BlockSpec((rows, width), right_map),
        ]
    out_spec = pl.BlockSpec((height, width), lambda r, t, half_ref: (r, t))
    if came is not None:
        operands.append(came)
        specs.append(out_spec)
    size = total_rows * starts[-1] * width
    return pl.pallas_call(
        partial(outer_kernel, starts, came is not None),
        out_shape=jax.ShapeDtypeStruct((total_rows, starts[-1] * width), BF16),
        grid_spec=pltpu.PrefetchScalarGridSpec(
            num_scalar_prefetch=1,
            grid=(total_rows // height, starts[-1]),
            in_specs=specs,
            out_specs=out_spec,
        ),
        compiler_params=pltpu.CompilerParams(vmem_limit_bytes=32 * 2**20),
        cost_estimate=pl.CostEstimate(flops=2 * rows * size, bytes_accessed=4 * size, transcendentals=0),
        name="outer",
    )(half, *operands)


def flip(value, bit):
    count = lax.axis_size("pass")
    return lax.ppermute(value, "pass", [(i, i ^ bit) for i in range(count)])


def after(value, *others):
    return lax.optimization_barrier((value,) + others)


def chip_exchange(parts):
    count = lax.axis_size("pass")
    groups = [[c + 2 * k for k in range(count // 2)] for c in range(2)]
    return lax.all_to_all(
        parts, "pass", split_axis=0, concat_axis=0, tiled=True, axis_index_groups=groups
    )


def near_gather(block):
    chips = lax.axis_size("pass") // 2
    return chip_exchange(jnp.broadcast_to(block[None], (chips,) + block.shape))


def add_other(own):
    return jnp.concatenate([own, flip(own, 1)])


def line_exchange(parts):
    count = lax.axis_size("pass")
    groups = [[r + 4 * k for k in range(count // 4)] for r in range(4)]
    return lax.all_to_all(
        parts, "pass", split_axis=0, concat_axis=0, tiled=True, axis_index_groups=groups
    )


def swap_half(value, place, axis, send):
    kept = lax.dynamic_index_in_dim(value, place, axis, keepdims=False)
    sent = lax.dynamic_index_in_dim(value, 1 - place, axis, keepdims=False)
    return (kept.astype(F32) + send(sent).astype(F32)).astype(BF16)


def core_sum(half, pairs):
    sent = outer(1 - half, pairs)
    return rows_by_owner(outer(half, pairs, flip(sent, 1)))


def rows_by_owner(value):
    n_dp, count = lax.axis_size("dp"), lax.axis_size("pass")
    rows, columns = value.shape
    return value.reshape(n_dp, count // 4, 2, rows // (n_dp * count // 2), columns)


def over_dp(value):
    n_dp = lax.axis_size("dp")
    if n_dp == 2:
        pairs = [(0, 1), (1, 0)]
        return swap_half(value, lax.axis_index("dp"), 0, lambda v: lax.ppermute(v, "dp", pairs))
    return lax.psum_scatter(value, "dp", scatter_dimension=0, tiled=False)


def over_near(value, axis):
    return swap_half(value, lax.axis_index("pass") // 2 % 2, axis, lambda v: flip(v, 2))


def over_line(value):
    return jnp.sum(line_exchange(value).astype(F32), axis=0)


def own_rows(value, core):
    shard = value.shape[0] // 2
    parts = value.reshape(2, shard, value.shape[1])
    kept = lax.dynamic_index_in_dim(parts, core, 0, keepdims=False)
    came = flip(lax.dynamic_index_in_dim(parts, 1 - core, 0, keepdims=False), 1)
    return jnp.where(core == 0, kept, came), jnp.where(core == 0, came, kept)


def total_sum(value):
    for bit in range((lax.axis_size("pass") - 1).bit_length()):
        value = value + flip(value, 1 << bit)
    n_dp = lax.axis_size("dp")
    for bit in range((n_dp - 1).bit_length()):
        pairs = [(i, i ^ (1 << bit)) for i in range(n_dp)]
        value = value + lax.ppermute(value, "dp", pairs)
    return value


def on_device(
    tokens,
    cotangent,
    passages,
    refresh,
    passage_ids,
    self_query,
    self_key,
    self_value,
    self_out,
    cross_query,
    cross_key,
    cross_value,
    cross_out,
    up_weight,
    down_weight,
    gains,
    rel_table,
):
    both = ("dp", "pass")
    pass_count = lax.axis_size("pass")
    device_id = lax.axis_index(both)
    own_pass = lax.axis_index("pass")
    per_query, plen, model_width = passages.shape
    head_count = rel_table.shape[1]
    head = model_width // head_count
    rows = tokens.shape[0]
    groups = head_count // GROUP
    wide = GROUP * head
    shard = self_query.shape[0]

    def gather(value):
        return lax.all_gather(value, both, axis=0, tiled=True)

    kv_shard = jnp.stack(
        [cross_key.reshape(shard, groups, wide), cross_value.reshape(shard, groups, wide)], axis=2
    ).reshape(shard, 2 * model_width)
    gain_pad = jnp.pad(gains, ((0, 0), (0, 128 - gains.shape[1])))
    first = gather(
        jnp.concatenate(
            [self_query, self_key, self_value, self_out, cross_query, kv_shard, gain_pad], axis=1
        )
    )
    first, more = lax.optimization_barrier((first, (cross_out, up_weight, down_weight)))
    second = gather(jnp.concatenate([more[0], more[1]], axis=1))
    down_full = gather(more[2])
    cuts = [first[:, i * model_width : (i + 1) * model_width] for i in range(5)]
    query_self, key_self, value_self, out_self, query_cross = cuts
    kv_weight = first[:, 5 * model_width : 7 * model_width]
    gain_all = first[:, 7 * model_width : 7 * model_width + 3].astype(F32)
    out_cross, up_full = second[:, :model_width], second[:, model_width:]

    row_ids = device_id * per_query + jnp.arange(per_query)
    owned = jnp.any(passage_ids[:, :, None] == row_ids[None, None, :], axis=1)
    owner = jnp.sum(
        jnp.where(owned, jnp.arange(passage_ids.shape[0])[:, None], 0), axis=0
    ).astype(jnp.int32)
    core = own_pass % 2
    half = core.astype(jnp.int32).reshape(1)
    asker = (owner // 2 + (owner % 2 != core) * (pass_count // 2)).astype(jnp.int32)

    inputs = tokens.astype(F32)
    positions = jnp.arange(rows)
    causal = positions[:, None] >= positions[None, :]
    onehot_low = (
        bucket_table(rows, rel_table.shape[0])[:, :, None]
        == jnp.arange(rel_table.shape[0])[None, None, :]
    ).astype(BF16)
    bias = jnp.einsum("qkb,bh->hqk", onehot_low, rel_table, preferred_element_type=F32)
    normed_self = norm_rows(inputs, gain_all[:, 0]).astype(BF16)
    query_one = matmul(normed_self, query_self).astype(BF16).reshape(rows, head_count, head)
    key_one = matmul(normed_self, key_self).astype(BF16).reshape(rows, head_count, head)
    value_one = matmul(normed_self, value_self).astype(BF16).reshape(rows, head_count, head)
    scores = jnp.einsum("qhe,khe->hqk", query_one, key_one, preferred_element_type=F32) + bias
    scores = jnp.where(causal[None, :, :], scores, FLOOR)
    raised = jnp.exp(scores - jnp.max(scores, axis=-1, keepdims=True))
    weights_one = raised / jnp.sum(raised, axis=-1, keepdims=True)
    weights_low = weights_one.astype(BF16)
    mixed_one = (
        jnp.einsum("hqk,khe->qhe", weights_low, value_one, preferred_element_type=F32)
        .reshape(rows, model_width)
        .astype(BF16)
    )
    stream_one = inputs + matmul(mixed_one, out_self)
    normed_cross = norm_rows(stream_one, gain_all[:, 1]).astype(BF16)
    query_two = matmul(normed_cross, query_cross).astype(BF16)

    encoded = passages.reshape(per_query * plen, model_width)
    kv = matmul(encoded, kv_weight).astype(BF16)
    cut = (groups + 1) // 2
    chunks = [(0, cut), (cut, groups)]
    blocks = [query_two[:, low * wide : high * wide] for low, high in chunks]
    own, kv = after(near_gather(blocks[0]), kv)
    own, block = after(own, blocks[1])
    q_parts = [add_other(own)]
    own = near_gather(block)
    mine, other = attend(asker, owner, half, q_parts[0], kv, 0, plen, head)
    own, mine, other = after(own, mine, other)
    merged = core_merge(mine, flip(other, 1), head)
    merged, own = after(merged, own)
    arrived = chip_exchange(merged)
    q_parts.append(add_other(own))
    mine, other = attend(asker, owner, half, q_parts[1], kv, cut, plen, head)
    merged = core_merge(mine, flip(other, 1), head)
    arrived, merged = after(arrived, merged)
    mixed_t, log_total = final_merge([arrived, chip_exchange(merged)], head)

    def rows_first(value):
        return (
            value.reshape(groups, head, GROUP, rows).transpose(3, 0, 2, 1).reshape(rows, model_width)
        )

    mixed_full = rows_first(mixed_t)
    mixed_two = mixed_full.astype(BF16)
    stream_two = stream_one + matmul(mixed_two, out_cross)
    normed_ffn = norm_rows(stream_two, gain_all[:, 2]).astype(BF16)
    inner = matmul(normed_ffn, up_full)
    active = jax.nn.gelu(inner, approximate=True).astype(BF16)
    block_out = (stream_two + matmul(active, down_full)).astype(BF16)
    d_active = right_t(cotangent, down_full)
    unused, gelu_back = jax.vjp(partial(jax.nn.gelu, approximate=True), inner)
    d_inner = gelu_back(d_active)[0].astype(BF16)
    d_normed_ffn = right_t(d_inner, up_full)
    unused, norm_back = jax.vjp(norm_rows, stream_two, gain_all[:, 2])
    d_stream_two, d_gain_ffn = norm_back(d_normed_ffn)
    d_stream_two = d_stream_two + cotangent.astype(F32)
    grad_two = d_stream_two.astype(BF16)
    d_mixed_two = right_t(grad_two, out_cross).astype(BF16)
    delta = jnp.sum(
        (d_mixed_two.astype(F32) * mixed_full).reshape(rows, groups, GROUP, head), axis=-1
    )
    delta = delta.transpose(1, 2, 0).reshape(groups, GROUP * rows)

    def pieces_of(value, parts):
        found = []
        for _ in range(parts - 1):
            found.append(lax.reduce_precision(value, 8, 7))
            value = value - found[-1]
        return jnp.stack(found + [value], axis=1)

    stats = jnp.concatenate([pieces_of(log_total, 3), pieces_of(delta, 2)], axis=1).astype(BF16)
    stats = stats.reshape(groups, -1, wide)
    stats = jnp.pad(stats, ((0, 0), (0, STAT_ROWS - stats.shape[1]), (0, 0)))
    stats = stats.transpose(1, 0, 2).reshape(STAT_ROWS, model_width)
    payload = jnp.concatenate([d_mixed_two, stats], axis=0)
    d_down = left_t(active, cotangent).astype(BF16)
    folds = d_down.shape[0] // model_width
    d_down = d_down.reshape(-1, folds, shard, model_width).transpose(0, 2, 1, 3)
    ffn_terms = jnp.concatenate(
        [
            left_t(mixed_two, grad_two).astype(BF16),
            left_t(normed_ffn, d_inner).astype(BF16),
            d_down.reshape(model_width, folds * model_width),
        ],
        axis=1,
    )
    blocks = [payload[:, low * wide : high * wide] for low, high in chunks]
    own, ffn_terms = after(near_gather(blocks[0]), ffn_terms)
    ffn_sums = lax.psum_scatter(ffn_terms, both, scatter_dimension=0, tiled=True)
    own, block = after(own, blocks[1])
    do_part = add_other(own)
    own = near_gather(block)
    dkv, mine, other = attend_back(asker, owner, half, q_parts[0], do_part, kv, kv, 0, plen, head)
    own, dkv, mine, other = after(own, dkv, mine, other)
    do_part = add_other(own)
    merged = (mine.astype(F32) + flip(other, 1).astype(F32)).astype(BF16)
    merged, do_part = after(merged, do_part)
    arrived = chip_exchange(merged)
    dkv, mine, other = attend_back(asker, owner, half, q_parts[1], do_part, kv, dkv, cut, plen, head)
    merged = (mine.astype(F32) + flip(other, 1).astype(F32)).astype(BF16)
    arrived, merged, dkv = after(arrived, merged, dkv)
    last, d_kv = after(chip_exchange(merged), left_t(encoded, dkv).astype(BF16))
    dq_parts = [jnp.sum(part.astype(F32), axis=0) for part in (arrived, last)]
    d_query_two = rows_first(jnp.concatenate(dq_parts, axis=0)).astype(BF16)

    def kv_half(at):
        cube = d_kv.reshape(model_width, groups, 2, wide)
        return lax.dynamic_index_in_dim(cube, at, 2, keepdims=False).reshape(model_width, -1)

    kv_part = kv_half(core).astype(F32) + flip(kv_half(1 - core), 1).astype(F32)
    kv_part = over_near(rows_by_owner(kv_part.astype(BF16)), 2)

    d_normed_cross = right_t(d_query_two, query_cross)
    unused, norm_back = jax.vjp(norm_rows, stream_one, gain_all[:, 1])
    d_stream_one, d_gain_cross = norm_back(d_normed_cross)
    d_stream_one = d_stream_one + d_stream_two
    grad_one = d_stream_one.astype(BF16)
    d_mixed_one = right_t(grad_one, out_self).astype(BF16).reshape(rows, head_count, head)
    d_value_one = (
        jnp.einsum("hqk,qhe->khe", weights_low, d_mixed_one, preferred_element_type=F32)
        .reshape(rows, model_width)
        .astype(BF16)
    )
    d_weights = jnp.einsum("qhe,khe->hqk", d_mixed_one, value_one, preferred_element_type=F32)
    d_score = (
        weights_one * (d_weights - jnp.sum(weights_one * d_weights, axis=-1, keepdims=True))
    ).astype(BF16)
    d_table = jnp.einsum("hqk,qkb->bh", d_score, onehot_low, preferred_element_type=F32)
    d_query_one = (
        jnp.einsum("hqk,khe->qhe", d_score, key_one, preferred_element_type=F32)
        .reshape(rows, model_width)
        .astype(BF16)
    )
    d_key_one = (
        jnp.einsum("hqk,qhe->khe", d_score, query_one, preferred_element_type=F32)
        .reshape(rows, model_width)
        .astype(BF16)
    )
    kv_part = over_dp(kv_part)
    late_pairs = [(normed_self, d_query_one), (normed_self, d_key_one), (normed_self, d_value_one)]
    more_pairs = [(mixed_one, grad_one), (normed_cross, d_query_two)]
    more_part, late_part = core_sum(half, more_pairs), core_sum(half, late_pairs)
    d_normed_self = (
        right_t(d_query_one, query_self)
        + right_t(d_key_one, key_self)
        + right_t(d_value_one, value_self)
    )
    unused, norm_back = jax.vjp(norm_rows, inputs, gain_all[:, 0])
    d_inputs, d_gain_self = norm_back(d_normed_self)
    d_inputs = d_inputs + d_stream_one
    small = jnp.concatenate([d_table.reshape(-1), d_gain_self, d_gain_cross, d_gain_ffn])
    small = total_sum(small.reshape(-1, 128)).reshape(-1)
    table_grad = small[: d_table.size].reshape(d_table.shape)
    d_gains = lax.dynamic_slice_in_dim(small[d_table.size :].reshape(3, -1), device_id * shard, shard, 1)

    more_part, late_part, kv_part, dkv_late, ffn_sums = after(
        more_part, late_part, kv_part, dkv, ffn_sums
    )
    passage_grad = source_grads(refresh, dkv_late, kv_weight, plen)
    late_part, more_part = over_dp(late_part), over_near(more_part, 2)
    late_part, more_part, passage_grad = after(late_part, more_part, passage_grad)
    late_part, more_part = over_near(late_part, 1), over_dp(more_part)
    line = over_line(jnp.concatenate([late_part, more_part, kv_part], axis=-1))

    left, right = own_rows(line, core)
    half_width = model_width // 2

    def whole(at):
        cut = slice(at * half_width, (at + 1) * half_width)
        return jnp.concatenate([left[:, cut], right[:, cut]], axis=1)

    d_query_self, d_key_self, d_value_self, d_out_self, d_query_cross = [whole(k) for k in range(5)]
    d_key_cross, d_value_cross = left[:, 5 * half_width :], right[:, 5 * half_width :]
    ffn_sums = ffn_sums.astype(F32)
    d_out_cross = ffn_sums[:, :model_width]
    d_up = ffn_sums[:, model_width : model_width + up_weight.shape[1]]
    d_down = ffn_sums[:, model_width + up_weight.shape[1] :].reshape(shard, folds, model_width)
    d_down = d_down.transpose(1, 0, 2).reshape(down_weight.shape)
    return (
        block_out,
        d_inputs,
        passage_grad,
        d_query_self,
        d_key_self,
        d_value_self,
        d_out_self,
        d_query_cross,
        d_key_cross,
        d_value_cross,
        d_out_cross,
        d_up,
        d_down,
        d_gains.T,
        table_grad,
    )


def solution(mesh):
    split = P(("dp", "pass"), None)
    cube = P(("dp", "pass"), None, None)
    in_specs = (split, split, cube, P(("dp", "pass")), P("dp", None)) + (split,) * 11 + (P(),)
    out_specs = (split, split, cube) + (split,) * 11 + (P(),)
    return jax.shard_map(
        on_device, mesh=mesh, in_specs=in_specs, out_specs=out_specs, check_vma=False
    )
```

```python
from functools import partial

import jax
import jax.numpy as jnp
from jax import lax
from jax.experimental import pallas as pl
from jax.experimental.pallas import tpu as pltpu
from jax.sharding import PartitionSpec as P

F32 = jnp.float32
BF16 = jnp.bfloat16
GROUP = 4
BLOCK = 4
STAT_ROWS = 16
CHUNK = 256
AHEAD = 2
FLOOR = -1e30


def norm_rows(value, gain):
    return value * lax.rsqrt(jnp.mean(value * value, axis=-1, keepdims=True) + 1e-06) * gain


def bucket_table(length, buckets):
    near_count = buckets // 2
    positions = jnp.arange(length)
    spread = jnp.maximum(positions[:, None] - positions[None, :], 0).astype(F32)
    bounds = near_count * 8.0 ** (jnp.arange(1, near_count, dtype=F32) / near_count)
    far_bucket = near_count + jnp.sum(
        (spread[:, :, None] >= bounds[None, None, :]).astype(jnp.int32), axis=-1
    )
    return jnp.where(spread < near_count, spread.astype(jnp.int32), far_bucket)


def matmul(left, right):
    return jnp.dot(left, right, preferred_element_type=F32)


def left_t(left, right):
    return jnp.einsum("td,te->de", left, right, preferred_element_type=F32)


def right_t(left, right):
    return jnp.einsum("te,de->td", left, right, preferred_element_type=F32)


def dot(left, right, dims):
    return lax.dot_general(left, right, (dims, ((), ())), preferred_element_type=F32)


def split_parts(value, count):
    parts = []
    for _ in range(count):
        part = value.astype(BF16).astype(F32)
        parts.append(part)
        value = value - part
    return parts


def spread_heads(rows, head):
    column = lax.broadcasted_iota(jnp.int32, rows.shape, 1) // head
    return jnp.concatenate(
        [jnp.where(column == h, rows, jnp.zeros_like(rows)) for h in range(GROUP)], axis=0
    )


def scale_rows(value):
    return lax.rsqrt(jnp.mean(value * value, axis=-1, keepdims=True) + 1e-06)


def norm_gradient(value, gain, grad):
    scale = scale_rows(value)
    unit = value * scale
    inner = grad * gain
    mean = jnp.mean(inner * unit, axis=-1, keepdims=True)
    return scale * (inner - unit * mean), jnp.sum(grad * unit, axis=0, keepdims=True)


def pair_spread(rows, head):
    first = lax.broadcasted_iota(jnp.int32, rows.shape, 1) < head
    zero = jnp.zeros_like(rows)
    return jnp.concatenate([jnp.where(first, rows, zero), jnp.where(first, zero, rows)], axis=0)


def pair_pick(full, head):
    rows = full.shape[0] // 2
    first = lax.broadcasted_iota(jnp.int32, (rows, full.shape[1]), 1) < head
    return jnp.where(first, full[:rows], full[rows:])


def pair_weights(qkv_ref, bias_ref, pair, head, width):
    at = slice(pair * 2 * head, (pair + 1) * 2 * head)
    query = pair_spread(qkv_ref[:, at], head)
    key = qkv_ref[:, width + at.start : width + at.stop]
    value = qkv_ref[:, 2 * width + at.start : 2 * width + at.stop]
    rows = key.shape[0]
    bias = bias_ref[2 * pair : 2 * pair + 2].reshape(2 * rows, rows)
    scores = dot(query, key, ((1,), (1,))) + bias
    raised = jnp.exp(scores - jnp.max(scores, axis=-1, keepdims=True))
    return query, key, value, raised / jnp.sum(raised, axis=-1, keepdims=True)


def self_kernel(head, tokens_ref, gain_ref, bias_ref, weight_ref, qkv_ref, mixed_ref, normed_ref, stream_ref, cross_ref, query_ref):
    width = tokens_ref.shape[1]
    inputs = tokens_ref[...].astype(F32)
    normed = (inputs * scale_rows(inputs) * gain_ref[0:1, :]).astype(BF16)
    normed_ref[...] = normed
    for k in range(3):
        at = slice(k * width, (k + 1) * width)
        qkv_ref[:, at] = dot(normed, weight_ref[:, at], ((1,), (0,))).astype(BF16)
    for pair in range(width // (2 * head)):
        _, _, value, weights = pair_weights(qkv_ref, bias_ref, pair, head, width)
        full = dot(weights.astype(BF16), value, ((1,), (0,)))
        mixed_ref[:, pair * 2 * head : (pair + 1) * 2 * head] = pair_pick(full, head).astype(BF16)
    stream = inputs + dot(mixed_ref[...], weight_ref[:, 3 * width : 4 * width], ((1,), (0,)))
    stream_ref[...] = stream
    cross = (stream * scale_rows(stream) * gain_ref[1:2, :]).astype(BF16)
    cross_ref[...] = cross
    query_ref[...] = dot(cross, weight_ref[:, 4 * width : 5 * width], ((1,), (0,))).astype(BF16)


def self_attend(tokens, gain_rows, bias, weight, head):
    rows, width = tokens.shape
    low = jax.ShapeDtypeStruct((rows, width), BF16)
    weight_spec = pl.BlockSpec((width, 5 * width), lambda i: (0, 0))
    return pl.pallas_call(
        partial(self_kernel, head),
        out_shape=(
            jax.ShapeDtypeStruct((rows, 3 * width), BF16),
            low,
            low,
            jax.ShapeDtypeStruct((rows, width), F32),
            low,
            low,
        ),
        grid=(1,),
        in_specs=[
            pl.BlockSpec(tokens.shape, lambda i: (0, 0)),
            pl.BlockSpec(gain_rows.shape, lambda i: (0, 0)),
            pl.BlockSpec(bias.shape, lambda i: (0, 0, 0)),
            weight_spec,
        ],
        out_specs=(pl.BlockSpec((rows, 3 * width), lambda i: (0, 0)),)
        + (pl.BlockSpec((rows, width), lambda i: (0, 0)),) * 5,
        compiler_params=pltpu.CompilerParams(vmem_limit_bytes=56 * 2**20),
        name="self_attend",
    )(tokens, gain_rows, bias, weight)


def self_back_kernel(head, tokens_ref, gain_ref, bias_ref, weight_ref, qkv_ref, stream_ref, dq_ref, dstream_ref, dqkv_ref, low_ref, dinput_ref, score_ref, dgain_ref):
    width = tokens_ref.shape[1]
    rows = tokens_ref.shape[0]
    d_cross = dot(dq_ref[...], weight_ref[:, 4 * width : 5 * width], ((1,), (1,)))
    d_stream, gain_cross = norm_gradient(stream_ref[...], gain_ref[1:2, :], d_cross)
    d_stream = d_stream + dstream_ref[...]
    low = d_stream.astype(BF16)
    low_ref[...] = low
    d_mixed = dot(low, weight_ref[:, 3 * width : 4 * width], ((1,), (1,))).astype(BF16)
    for pair in range(width // (2 * head)):
        query, key, value, weights = pair_weights(qkv_ref, bias_ref, pair, head, width)
        at = slice(pair * 2 * head, (pair + 1) * 2 * head)
        spread = pair_spread(d_mixed[:, at], head)
        d_value = dot(weights.astype(BF16), spread, ((0,), (0,)))
        d_weights = dot(spread, value, ((1,), (1,)))
        inner = jnp.sum(weights * d_weights, axis=-1, keepdims=True)
        d_score = (weights * (d_weights - inner)).astype(BF16)
        score_ref[2 * pair : 2 * pair + 2] = d_score.reshape(2, rows, rows)
        d_query = pair_pick(dot(d_score, key, ((1,), (0,))), head)
        d_key = dot(d_score, query, ((0,), (0,)))
        dqkv_ref[:, at] = d_query.astype(BF16)
        dqkv_ref[:, width + at.start : width + at.stop] = d_key.astype(BF16)
        dqkv_ref[:, 2 * width + at.start : 2 * width + at.stop] = d_value.astype(BF16)
    d_normed = jnp.zeros((rows, width), F32)
    for k in range(3):
        at = slice(k * width, (k + 1) * width)
        d_normed = d_normed + dot(dqkv_ref[:, at], weight_ref[:, at], ((1,), (1,)))
    d_input, gain_self = norm_gradient(tokens_ref[...].astype(F32), gain_ref[0:1, :], d_normed)
    dinput_ref[...] = d_input + d_stream
    dgain_ref[...] = jnp.concatenate([gain_self, gain_cross, jnp.zeros((6, width), F32)], axis=0)


def self_back(tokens, gain_rows, bias, weight, qkv, stream, d_query, d_stream, head):
    rows, width = tokens.shape

    def whole(shape):
        return pl.BlockSpec(shape, lambda i: (0,) * len(shape))

    shapes = (
        jax.ShapeDtypeStruct(qkv.shape, BF16),
        jax.ShapeDtypeStruct(tokens.shape, BF16),
        jax.ShapeDtypeStruct(tokens.shape, F32),
        jax.ShapeDtypeStruct(bias.shape, BF16),
        jax.ShapeDtypeStruct((8, width), F32),
    )
    return pl.pallas_call(
        partial(self_back_kernel, head),
        out_shape=shapes,
        grid=(1,),
        in_specs=[
            whole(tokens.shape),
            whole(gain_rows.shape),
            whole(bias.shape),
            whole((width, 5 * width)),
            whole(qkv.shape),
            whole(tokens.shape),
            whole(tokens.shape),
            whole(tokens.shape),
        ],
        out_specs=tuple(whole(shape.shape) for shape in shapes),
        compiler_params=pltpu.CompilerParams(vmem_limit_bytes=56 * 2**20),
        name="self_back",
    )(tokens, gain_rows, bias, weight, qkv, stream, d_query, d_stream)


def pick_chunk(full, head, rows, start):
    chunk = full.shape[1]
    first = start // rows
    lane = (lax.broadcasted_iota(jnp.int32, (head, chunk), 1) + start) // rows - first
    out = full[:head]
    for h in range(1, full.shape[0] // head):
        out = jnp.where(lane == h, full[h * head : (h + 1) * head], out)
    return out


def flush_queries(here_ref, queries, pack, mine_ref, other_ref):
    near = queries // 4

    def flush(at, carry):
        y = jnp.bitwise_xor(here_ref[1], at // near)
        j = at % near * 4 + 2 * y
        mine_ref[at, 0] = pack(j + here_ref[0])
        other_ref[at, 0] = pack(j + 1 - here_ref[0])
        return carry

    lax.fori_loop(0, queries // 2, flush, 0)


def either(index, a_ref, b_ref):
    count = a_ref.shape[0]
    return jnp.where(index < count, a_ref[index % count], b_ref[index % count])


def attend_kernel(plen, head, rows, asker_ref, owner_ref, here_ref, qa_ref, qb_ref, kv_ref, mine_ref, other_ref, acc, top, total):
    step = pl.program_id(1)
    queries = 2 * qa_ref.shape[0]
    width = GROUP * head

    @pl.when(step == 0)
    def _():
        acc[...] = jnp.zeros_like(acc)
        top[...] = jnp.full_like(top, FLOOR)
        total[...] = jnp.zeros_like(total)

    lanes = GROUP * rows
    chunk = min(CHUNK, lanes)

    def begin(unit):
        p, c = divmod(unit, lanes // chunk)
        if c == 0:
            spreads[p] = spread_heads(either(asker_ref[step * BLOCK + p], qa_ref, qb_ref), head)
            turned[p] = kv_ref[p * plen : (p + 1) * plen, width:].T
        keys = kv_ref[p * plen : (p + 1) * plen, :width]
        return dot(keys, spreads[p][c * chunk : (c + 1) * chunk], ((1,), (1,)))

    def finish(unit, scores):
        p, c = divmod(unit, lanes // chunk)
        owner = owner_ref[step * BLOCK + p]
        at = pl.ds(c * chunk, chunk)
        first, last = c * chunk // rows, ((c + 1) * chunk - 1) // rows
        here = jnp.max(scores, axis=0, keepdims=True)
        raised = jnp.exp(scores - here)
        here_total = jnp.sum(raised, axis=0, keepdims=True)
        full = dot(turned[p][first * head : (last + 1) * head], raised.astype(BF16), ((1,), (0,)))
        mixed = pick_chunk(full, head, rows, c * chunk)
        old = top[owner, :, at]
        new = jnp.maximum(old, here)
        old_scale, here_scale = jnp.exp(old - new), jnp.exp(here - new)
        top[owner, :, at] = new
        total[owner, :, at] = total[owner, :, at] * old_scale + here_total * here_scale
        acc[owner, :, at] = acc[owner, :, at] * old_scale + mixed * here_scale

    spreads, turned = {}, {}
    units = BLOCK * (lanes // chunk)
    waiting = [begin(u) for u in range(min(AHEAD, units))]
    for unit in range(units):
        if unit + AHEAD < units:
            waiting.append(begin(unit + AHEAD))
        finish(unit, waiting.pop(0))

    @pl.when(step == pl.num_programs(1) - 1)
    def _():
        def pack(j):
            parts = split_parts(top[j], 3) + split_parts(total[j], 2)
            parts.append(jnp.zeros((STAT_ROWS - len(parts), parts[0].shape[1]), F32))
            return jnp.concatenate([acc[j]] + parts, axis=0).astype(BF16)

        flush_queries(here_ref, queries, pack, mine_ref, other_ref)


def attend(asker, owner, here, plane, across, kv, plen, head):
    near, rows, columns = plane.shape
    queries = 2 * near
    width = GROUP * head
    slots = kv.shape[0] // plen
    lanes = GROUP * rows
    groups = columns // width
    block = (near, 1, head + STAT_ROWS, lanes)
    out = jax.ShapeDtypeStruct((near, groups, head + STAT_ROWS, lanes), BF16)
    q_spec = pl.BlockSpec((near, rows, width), lambda g, b, *_: (0, 0, g))
    return pl.pallas_call(
        partial(attend_kernel, plen, head, rows),
        out_shape=(out, out),
        grid_spec=pltpu.PrefetchScalarGridSpec(
            num_scalar_prefetch=3,
            grid=(groups, slots // BLOCK),
            in_specs=[
                q_spec,
                q_spec,
                pl.BlockSpec((BLOCK * plen, 2 * width), lambda g, b, *_: (b, g)),
            ],
            out_specs=(pl.BlockSpec(block, lambda g, b, *_: (0, g, 0, 0)),) * 2,
            scratch_shapes=[
                pltpu.VMEM((queries, head, lanes), F32),
                pltpu.VMEM((queries, 1, lanes), F32),
                pltpu.VMEM((queries, 1, lanes), F32),
            ],
        ),
        compiler_params=pltpu.CompilerParams(vmem_limit_bytes=60 * 2**20),
        cost_estimate=pl.CostEstimate(
            flops=16 * rows * kv.shape[0] * columns,
            bytes_accessed=4 * kv.shape[0] * columns,
            transcendentals=rows * kv.shape[0] * GROUP * groups,
        ),
        name="attend",
    )(asker, owner, here, plane, across, kv)


def read_stats(stat):
    return stat[0:1] + stat[1:2] + stat[2:3], stat[3:4] + stat[4:5]


def merge_kernel(head, a_ref, b_ref, out_ref):
    for i in range(a_ref.shape[0]):
        for g in range(a_ref.shape[1]):
            top_a, sum_a = read_stats(a_ref[i, g, head:, :].astype(F32))
            top_b, sum_b = read_stats(b_ref[i, g, head:, :].astype(F32))
            top = jnp.maximum(top_a, top_b)
            w_a, w_b = jnp.exp(top_a - top), jnp.exp(top_b - top)
            body = a_ref[i, g, :head, :].astype(F32) * w_a + b_ref[i, g, :head, :].astype(F32) * w_b
            rows = split_parts(top, 3) + split_parts(sum_a * w_a + sum_b * w_b, 2)
            rows.append(jnp.zeros((STAT_ROWS - 5, top.shape[1]), F32))
            out_ref[i, g] = jnp.concatenate([body] + rows, axis=0).astype(BF16)


def core_kernel(head, a_ref, b_ref, near_ref, far_ref):
    @pl.when(pl.program_id(0) < 2)
    def _():
        merge_kernel(head, a_ref, b_ref, far_ref)

    @pl.when(pl.program_id(0) >= 2)
    def _():
        merge_kernel(head, a_ref, b_ref, near_ref)


def core_merge(kept, came, head):
    block = (kept.shape[0] // 4,) + kept.shape[1:]
    out = jax.ShapeDtypeStruct((kept.shape[0] // 2,) + kept.shape[1:], BF16)
    return pl.pallas_call(
        partial(core_kernel, head),
        out_shape=(out, out),
        grid=(4,),
        in_specs=[pl.BlockSpec(block, lambda i: ((i + 2) % 4, 0, 0, 0))] * 2,
        out_specs=(
            pl.BlockSpec(block, lambda i: (jnp.maximum(i - 2, 0), 0, 0, 0)),
            pl.BlockSpec(block, lambda i: (jnp.minimum(i, 1), 0, 0, 0)),
        ),
        cost_estimate=pl.CostEstimate(flops=4 * kept.size, bytes_accessed=6 * kept.size, transcendentals=0),
        name="core_merge",
    )(kept, came)


def near_merge(kept, came, head):
    spec = pl.BlockSpec((kept.shape[0] // 2,) + kept.shape[1:], lambda i: (i, 0, 0, 0))
    return pl.pallas_call(
        partial(merge_kernel, head),
        out_shape=jax.ShapeDtypeStruct(kept.shape, BF16),
        grid=(2,),
        in_specs=[spec, spec],
        out_specs=spec,
        cost_estimate=pl.CostEstimate(flops=4 * kept.size, bytes_accessed=6 * kept.size, transcendentals=0),
        name="near_merge",
    )(kept, came)


def final_kernel(head, *refs):
    out_ref, log_ref = refs[-2:]
    at = 0
    for ref in refs[:-2]:
        count = ref.shape[0]
        for g in range(ref.shape[1]):
            found = [read_stats(ref[i, g, head:, :].astype(F32)) for i in range(count)]
            top = found[0][0]
            for i in range(1, count):
                top = jnp.maximum(top, found[i][0])
            weights = [jnp.exp(found[i][0] - top) for i in range(count)]
            whole = found[0][1] * weights[0]
            mixed = ref[0, g, :head, :].astype(F32) * weights[0]
            for i in range(1, count):
                whole = whole + found[i][1] * weights[i]
                mixed = mixed + ref[i, g, :head, :].astype(F32) * weights[i]
            out_ref[at * head : (at + 1) * head, :] = mixed / whole
            log_ref[at : at + 1, :] = top + jnp.log(whole)
            at += 1


def final_merge(parts, head):
    lanes = parts[0].shape[3]
    groups = sum(part.shape[1] for part in parts)
    return pl.pallas_call(
        partial(final_kernel, head),
        out_shape=(
            jax.ShapeDtypeStruct((groups * head, lanes), F32),
            jax.ShapeDtypeStruct((groups, lanes), F32),
        ),
        compiler_params=pltpu.CompilerParams(vmem_limit_bytes=56 * 2**20),
        name="final_merge",
    )(*parts)


def attend_back_kernel(plen, head, rows, asker_ref, owner_ref, here_ref, qa_ref, qb_ref, doa_ref, dob_ref, sa_ref, sb_ref, kv_ref, *refs):
    step = pl.program_id(1)
    dkv_ref, mine_ref, other_ref, acc, log, delta = refs[-6:]
    held_ref = refs[0] if len(refs) > 6 else None
    near = qa_ref.shape[0]
    queries = 2 * near
    width = GROUP * head

    @pl.when(step == 0)
    def _():
        acc[...] = jnp.zeros_like(acc)
        third = (GROUP * rows) // width

        def fill(j, carry):
            stat = either(j, sa_ref, sb_ref).astype(F32)
            row = lax.broadcasted_iota(jnp.int32, stat.shape, 0)
            for at, ref, count in ((0, log, 3), (3 * third, delta, 2)):
                pieces = []
                for t in range(third):
                    wanted = row == at + t
                    for k in range(1, count):
                        wanted = wanted | (row == at + k * third + t)
                    pieces.append(jnp.sum(jnp.where(wanted, stat, 0.0), axis=0, keepdims=True))
                ref[j] = jnp.concatenate(pieces, axis=1)
            return carry

        lax.fori_loop(0, queries, fill, 0)

    lanes = GROUP * rows
    chunk = min(CHUNK, lanes)

    def begin(unit):
        p, c = divmod(unit, lanes // chunk)
        rows_at = slice(p * plen, (p + 1) * plen)
        if c == 0:
            asker = asker_ref[step * BLOCK + p]
            q_spread[p] = spread_heads(either(asker, qa_ref, qb_ref), head)
            do_spread[p] = spread_heads(either(asker, doa_ref, dob_ref), head)
            turned[p] = kv_ref[rows_at, :width].T
        at = slice(c * chunk, (c + 1) * chunk)
        return (
            dot(kv_ref[rows_at, :width], q_spread[p][at], ((1,), (1,))),
            dot(kv_ref[rows_at, width:], do_spread[p][at], ((1,), (1,))),
        )

    def finish(unit, found):
        scores, d_soft = found
        p, c = divmod(unit, lanes // chunk)
        owner, asker = owner_ref[step * BLOCK + p], asker_ref[step * BLOCK + p]
        at = pl.ds(c * chunk, chunk)
        cut = slice(c * chunk, (c + 1) * chunk)
        first, last = c * chunk // rows, ((c + 1) * chunk - 1) // rows
        soft = jnp.exp(scores - log[asker, :, at])
        d_score = (soft * (d_soft - delta[asker, :, at])).astype(BF16)
        d_value = dot(soft.astype(BF16), do_spread[p][cut], ((1,), (0,)))
        d_key = dot(d_score, q_spread[p][cut], ((1,), (0,)))
        sums[p] = (d_key, d_value) if c == 0 else (sums[p][0] + d_key, sums[p][1] + d_value)
        full = dot(turned[p][first * head : (last + 1) * head], d_score, ((1,), (0,)))
        acc[owner, :, at] += pick_chunk(full, head, rows, c * chunk)
        if c == lanes // chunk - 1:
            rows_at = slice(p * plen, (p + 1) * plen)
            for found, columns in zip(sums[p], (slice(0, width), slice(width, 2 * width))):
                if held_ref is not None:
                    found = found + held_ref[rows_at, columns].astype(F32)
                dkv_ref[rows_at, columns] = found.astype(BF16)

    q_spread, do_spread, turned, sums = {}, {}, {}, {}
    units = BLOCK * (lanes // chunk)
    waiting = [begin(u) for u in range(min(AHEAD, units))]
    for unit in range(units):
        if unit + AHEAD < units:
            waiting.append(begin(unit + AHEAD))
        finish(unit, waiting.pop(0))

    @pl.when(step == pl.num_programs(1) - 1)
    def _():
        flush_queries(here_ref, queries, lambda j: acc[j].astype(BF16), mine_ref, other_ref)


def attend_back(asker, owner, here, queries_in, grads_in, kv, held, plen, head):
    near, rows, columns = queries_in[0].shape
    queries = 2 * near
    width = GROUP * head
    slots = kv.shape[0] // plen
    lanes = GROUP * rows
    groups = columns // width
    block = (near, 1, head, lanes)
    out = jax.ShapeDtypeStruct((near, groups, head, lanes), BF16)
    q_spec = pl.BlockSpec((near, rows, width), lambda g, b, *_: (0, 0, g))
    stat_spec = pl.BlockSpec((near, STAT_ROWS, width), lambda g, b, *_: (0, rows // STAT_ROWS, g))
    kv_spec = pl.BlockSpec((BLOCK * plen, 2 * width), lambda g, b, *_: (b, g))
    operands = [*queries_in, *grads_in, *grads_in, kv]
    specs = [q_spec] * 4 + [stat_spec] * 2 + [kv_spec]
    if held is not None:
        operands.append(held)
        specs.append(kv_spec)
    return pl.pallas_call(
        partial(attend_back_kernel, plen, head, rows),
        out_shape=(jax.ShapeDtypeStruct(kv.shape, BF16), out, out),
        grid_spec=pltpu.PrefetchScalarGridSpec(
            num_scalar_prefetch=3,
            grid=(groups, slots // BLOCK),
            in_specs=specs,
            out_specs=(
                kv_spec,
                pl.BlockSpec(block, lambda g, b, *_: (0, g, 0, 0)),
                pl.BlockSpec(block, lambda g, b, *_: (0, g, 0, 0)),
            ),
            scratch_shapes=[
                pltpu.VMEM((queries, head, lanes), F32),
                pltpu.VMEM((queries, 1, lanes), F32),
                pltpu.VMEM((queries, 1, lanes), F32),
            ],
        ),
        input_output_aliases={} if held is None else {3 + len(operands) - 1: 0},
        compiler_params=pltpu.CompilerParams(vmem_limit_bytes=60 * 2**20),
        cost_estimate=pl.CostEstimate(
            flops=40 * rows * kv.shape[0] * columns,
            bytes_accessed=8 * kv.shape[0] * columns,
            transcendentals=rows * kv.shape[0] * GROUP * groups,
        ),
        name="attend_back",
    )(asker, owner, here, *operands)


def source_kernel(keep_ref, fetch_ref, dkv_ref, weight_ref, out_ref):
    kept = keep_ref[pl.program_id(0)]

    @pl.when(kept == 0)
    def _():
        out_ref[...] = jnp.zeros_like(out_ref)

    @pl.when(kept != 0)
    def _():
        out_ref[0] = dot(dkv_ref[...], weight_ref[...], ((1,), (1,))).astype(BF16)


def source_grads(refresh, dkv, weight, plen):
    slots = refresh.shape[0]
    model_width = weight.shape[0]
    fetch = lax.cummax(jnp.where(refresh != 0, jnp.arange(slots), 0), axis=0).astype(jnp.int32)
    return pl.pallas_call(
        source_kernel,
        out_shape=jax.ShapeDtypeStruct((slots, plen, model_width), BF16),
        grid_spec=pltpu.PrefetchScalarGridSpec(
            num_scalar_prefetch=2,
            grid=(slots,),
            in_specs=[
                pl.BlockSpec((plen, dkv.shape[1]), lambda r, keep, fetch: (fetch[r], 0)),
                pl.BlockSpec(weight.shape, lambda r, *_: (0, 0)),
            ],
            out_specs=pl.BlockSpec((1, plen, model_width), lambda r, *_: (r, 0, 0)),
        ),
        compiler_params=pltpu.CompilerParams(vmem_limit_bytes=40 * 2**20),
        cost_estimate=pl.CostEstimate(
            flops=slots * plen * model_width * 2 * model_width,
            bytes_accessed=4 * slots * plen * model_width,
            transcendentals=0,
        ),
        name="source_grads",
    )(refresh, fetch, dkv, weight)


def outer_kernel(starts, added, half_ref, *refs):
    out_ref = refs[-1]
    tile = pl.program_id(1)
    for k in range(len(starts) - 1):

        @pl.when((tile >= starts[k]) & (tile < starts[k + 1]))
        def _(k=k):
            found = dot(refs[2 * k][...], refs[2 * k + 1][...], ((0,), (0,)))
            if added:
                found = found + refs[-2][...].astype(F32)
            out_ref[...] = found.astype(BF16)


def outer(half, pairs, came=None):
    rows = pairs[0][0].shape[0]
    height = min(left.shape[1] for left, _ in pairs)
    height = height if height <= 1024 else height // 4
    total_rows = pairs[0][0].shape[1]
    width = min(right.shape[1] for _, right in pairs) // 2
    counts = [right.shape[1] // 2 // width for _, right in pairs]
    starts = [sum(counts[:k]) for k in range(len(counts) + 1)]
    operands, specs = [], []
    for k, (left, right) in enumerate(pairs):

        def right_map(r, t, half_ref, start=starts[k], count=counts[k]):
            return (0, half_ref[0] * count + jnp.clip(t - start, 0, count - 1))

        operands += [left, right]
        specs += [
            pl.BlockSpec((rows, height), lambda r, t, half_ref: (0, r)),
            pl.BlockSpec((rows, width), right_map),
        ]
    out_spec = pl.BlockSpec((height, width), lambda r, t, half_ref: (r, t))
    if came is not None:
        operands.append(came)
        specs.append(out_spec)
    size = total_rows * starts[-1] * width
    return pl.pallas_call(
        partial(outer_kernel, starts, came is not None),
        out_shape=jax.ShapeDtypeStruct((total_rows, starts[-1] * width), BF16),
        grid_spec=pltpu.PrefetchScalarGridSpec(
            num_scalar_prefetch=1,
            grid=(total_rows // height, starts[-1]),
            in_specs=specs,
            out_specs=out_spec,
        ),
        compiler_params=pltpu.CompilerParams(vmem_limit_bytes=32 * 2**20),
        cost_estimate=pl.CostEstimate(flops=2 * rows * size, bytes_accessed=4 * size, transcendentals=0),
        name="outer",
    )(half, *operands)


def flip(value, bit):
    count = lax.axis_size("pass")
    return lax.ppermute(value, "pass", [(i, i ^ bit) for i in range(count)])


def after(value, *others):
    return lax.optimization_barrier((value,) + others)


def line_sends(block):
    count = lax.axis_size("pass")
    rings = [[(i, (i + 4 * k) % count) for i in range(count)] for k in range(1, count // 4)]
    return [lax.ppermute(block, "pass", ring) for ring in rings]


def gather_place(query, own, count):
    major = count // 4
    turn = jnp.mod(own // 4 - query // 4, major)
    return turn + major * ((own // 2) % 2 != (query // 2) % 2) + 2 * major * (own % 2 != query % 2)


def line_exchange(parts):
    count = lax.axis_size("pass")
    groups = [[r + 4 * k for k in range(count // 4)] for r in range(4)]
    return lax.all_to_all(
        parts, "pass", split_axis=0, concat_axis=0, tiled=True, axis_index_groups=groups
    )


def swap_send(value, place, axis, send):
    kept = lax.dynamic_index_in_dim(value, place, axis, keepdims=False)
    return kept, send(lax.dynamic_index_in_dim(value, 1 - place, axis, keepdims=False))


def add_low(kept, came):
    return (kept.astype(F32) + came.astype(F32)).astype(BF16)


def rows_by_owner(value):
    n_dp, count = lax.axis_size("dp"), lax.axis_size("pass")
    rows, columns = value.shape
    return value.reshape(n_dp, count // 4, 2, rows // (n_dp * count // 2), columns)


def dp_step(value, bit):
    pairs = [(i, i ^ bit) for i in range(lax.axis_size("dp"))]
    return lax.ppermute(value, "dp", pairs)


def dp_flip(value):
    return lax.ppermute(value, "dp", [(0, 1), (1, 0)])


def dp_send(value):
    if lax.axis_size("dp") == 2:
        return swap_send(value, lax.axis_index("dp"), 0, dp_flip)
    total = lax.psum_scatter(value, "dp", scatter_dimension=0, tiled=False)
    return total, jnp.zeros_like(total)


def near_send(value, axis):
    return swap_send(value, lax.axis_index("pass") // 2 % 2, axis, lambda v: flip(v, 2))


def over_line(value):
    return jnp.sum(line_exchange(value).astype(F32), axis=0)


def own_rows(value, core):
    shard = value.shape[0] // 2
    parts = value.reshape(2, shard, value.shape[1])
    kept = lax.dynamic_index_in_dim(parts, core, 0, keepdims=False)
    came = flip(lax.dynamic_index_in_dim(parts, 1 - core, 0, keepdims=False), 1)
    return jnp.where(core == 0, kept, came), jnp.where(core == 0, came, kept)


def on_device(
    tokens,
    cotangent,
    passages,
    refresh,
    passage_ids,
    self_query,
    self_key,
    self_value,
    self_out,
    cross_query,
    cross_key,
    cross_value,
    cross_out,
    up_weight,
    down_weight,
    gains,
    rel_table,
):
    both = ("dp", "pass")
    pass_count = lax.axis_size("pass")
    device_id = lax.axis_index(both)
    own_pass = lax.axis_index("pass")
    per_query, plen, model_width = passages.shape
    head_count = rel_table.shape[1]
    head = model_width // head_count
    rows = tokens.shape[0]
    groups = head_count // GROUP
    wide = GROUP * head
    shard = self_query.shape[0]

    def gather(value):
        return lax.all_gather(value, both, axis=0, tiled=True)

    kv_shard = jnp.stack(
        [cross_key.reshape(shard, groups, wide), cross_value.reshape(shard, groups, wide)], axis=2
    ).reshape(shard, 2 * model_width)
    gain_pad = jnp.pad(gains, ((0, 0), (0, 128 - gains.shape[1])))
    first = gather(
        jnp.concatenate(
            [self_query, self_key, self_value, self_out, cross_query, kv_shard, gain_pad], axis=1
        )
    )
    positions = jnp.arange(rows)
    causal = positions[:, None] >= positions[None, :]
    onehot_low = (
        bucket_table(rows, rel_table.shape[0])[:, :, None]
        == jnp.arange(rel_table.shape[0])[None, None, :]
    ).astype(BF16)
    bias = jnp.einsum("qkb,bh->hqk", onehot_low, rel_table, preferred_element_type=F32)
    bias = jnp.where(causal[None, :, :], bias, FLOOR)
    first, bias = after(first, bias)
    first, more = lax.optimization_barrier((first, (cross_out, up_weight, down_weight)))
    second = gather(jnp.concatenate([more[0], more[1]], axis=1))
    down_full = gather(more[2])
    kv_weight = first[:, 5 * model_width : 7 * model_width]
    gain_all = first[:, 7 * model_width : 7 * model_width + 3].astype(F32)
    out_cross, up_full = second[:, :model_width], second[:, model_width:]

    row_ids = device_id * per_query + jnp.arange(per_query)
    owned = jnp.any(passage_ids[:, :, None] == row_ids[None, None, :], axis=1)
    owner = jnp.sum(
        jnp.where(owned, jnp.arange(passage_ids.shape[0])[:, None], 0), axis=0
    ).astype(jnp.int32)
    core = own_pass % 2
    half = core.astype(jnp.int32).reshape(1)
    here = jnp.stack([core, own_pass // 2 % 2]).astype(jnp.int32)
    asker = gather_place(owner, own_pass, pass_count).astype(jnp.int32)

    gain_rows = jnp.pad(gain_all.T, ((0, 5), (0, 0)))
    qkv, mixed_one, normed_self, stream_one, normed_cross, query_two = self_attend(
        tokens, gain_rows, bias, first, head
    )

    encoded = passages.reshape(per_query * plen, model_width)
    kv = matmul(encoded, kv_weight).astype(BF16)
    cut = rows // 192 * 64

    def merge_send(mine, came):
        near, far = core_merge(mine, came, head)
        return near, flip(far, 2)

    def rows_first(value):
        cube = value.reshape(groups, head, GROUP, -1).transpose(3, 0, 2, 1)
        return cube.reshape(-1, model_width)

    def pieces_of(value, parts):
        found = []
        for _ in range(parts - 1):
            found.append(lax.reduce_precision(value, 8, 7))
            value = value - found[-1]
        return jnp.stack(found + [value], axis=1)

    def feed_forward(part, part_t, log_total):
        at = slice(0, cut) if part == 0 else slice(cut, rows)
        stream, grads = stream_one[at], cotangent[at]
        mixed_full = rows_first(part_t)
        mixed = mixed_full.astype(BF16)
        stream = stream + matmul(mixed, out_cross)
        normed = norm_rows(stream, gain_all[:, 2]).astype(BF16)
        inner = matmul(normed, up_full)
        active, gelu_back = jax.vjp(partial(jax.nn.gelu, approximate=True), inner)
        active = active.astype(BF16)
        out = (stream + matmul(active, down_full)).astype(BF16)
        d_inner = gelu_back(right_t(grads, down_full))[0].astype(BF16)
        unused, norm_back = jax.vjp(norm_rows, stream, gain_all[:, 2])
        d_stream, d_gain = norm_back(right_t(d_inner, up_full))
        d_stream = d_stream + grads.astype(F32)
        low = d_stream.astype(BF16)
        d_mixed = right_t(low, out_cross).astype(BF16)
        delta = jnp.sum(
            (d_mixed.astype(F32) * mixed_full).reshape(-1, groups, GROUP, head), axis=-1
        )
        delta = delta.transpose(1, 2, 0).reshape(groups, -1)
        stats = jnp.concatenate([pieces_of(log_total, 3), pieces_of(delta, 2)], axis=1)
        stats = stats.astype(BF16).reshape(groups, -1, wide)
        stats = jnp.pad(stats, ((0, 0), (0, STAT_ROWS - stats.shape[1]), (0, 0)))
        stats = stats.transpose(1, 0, 2).reshape(STAT_ROWS, model_width)
        payload = jnp.concatenate([d_mixed, stats], axis=0)
        return payload, out, d_stream, d_gain, (mixed, low, normed, d_inner, active)

    kv, *sends = after(kv, *line_sends(query_two))
    line = jnp.stack([value[:cut] for value in (query_two, *sends)])
    across = flip(line, 2)
    plane = jnp.concatenate([line, across])
    q_first = (plane, flip(plane, 1))
    line = jnp.stack([value[cut:] for value in (query_two, *sends)])
    across = flip(line, 2)
    mine, other = attend(asker, owner, here, *q_first, kv, plen, head)
    across, mine, other = after(across, mine, other)
    came = flip(other, 1)
    plane = jnp.concatenate([line, across])
    q_second = (plane, flip(plane, 1))
    near, came = merge_send(mine, came)
    q_second, near = after(q_second, near)
    mine, other = attend(asker, owner, here, *q_second, kv, plen, head)
    came, mine, other = after(came, mine, other)
    came_next = flip(other, 1)
    arrived = line_exchange(near_merge(near, came, head))
    near, came = merge_send(mine, came_next)
    arrived, near = after(arrived, near)
    first_t, first_log = final_merge([arrived], head)
    payload, out_first, ds_first, gain_first, terms_first = feed_forward(0, first_t, first_log)
    came, payload = after(came, payload)
    merged, *sends = after(near_merge(near, came, head), *line_sends(payload))
    arrived = line_exchange(merged)
    line = jnp.stack([payload, *sends])
    across = flip(line, 2)
    last_t, last_log = final_merge([arrived], head)
    payload, out_last, ds_last, gain_last, terms_last = feed_forward(1, last_t, last_log)
    across, payload = after(across, payload)
    plane = jnp.concatenate([line, across])
    do_first = (plane, flip(plane, 1))
    sends = line_sends(payload)

    block_out = jnp.concatenate([out_first, out_last])
    d_stream_two = jnp.concatenate([ds_first, ds_last])
    d_gain_ffn = gain_first + gain_last
    mixed_two, grad_two, normed_ffn, d_inner, active = [
        jnp.concatenate(pair) for pair in zip(terms_first, terms_last)
    ]
    d_down = left_t(active, cotangent).astype(BF16)
    folds = d_down.shape[0] // model_width
    d_down = d_down.reshape(-1, folds, shard, model_width).transpose(0, 2, 1, 3)
    ffn_terms = jnp.concatenate(
        [
            left_t(mixed_two, grad_two).astype(BF16),
            left_t(normed_ffn, d_inner).astype(BF16),
            d_down.reshape(model_width, folds * model_width),
        ],
        axis=1,
    )
    ffn_terms, *sends = after(ffn_terms, *sends)
    ffn_sums = lax.psum_scatter(ffn_terms, both, scatter_dimension=0, tiled=True)
    line = jnp.stack([payload, *sends])
    across = flip(line, 2)

    def half_of(value, came):
        value = (value.astype(F32) + came.astype(F32)).astype(BF16)
        return value[: value.shape[0] // 2], value[value.shape[0] // 2 :]

    dkv, mine, other = attend_back(asker, owner, here, q_first, do_first, kv, None, plen, head)
    across, dkv, mine, other = after(across, dkv, mine, other)
    came = flip(other, 1)
    plane = jnp.concatenate([line, across])
    do_last = (plane, flip(plane, 1))
    near, far = half_of(mine, came)
    came = flip(far, 2)
    do_last, near = after(do_last, near)
    dkv, mine, other = attend_back(asker, owner, here, q_second, do_last, kv, dkv, plen, head)
    came, dkv, mine, other = after(came, dkv, mine, other)
    came_next = flip(other, 1)
    arrived = line_exchange((near.astype(F32) + came.astype(F32)).astype(BF16))
    near, far = half_of(mine, came_next)
    came, arrived = after(flip(far, 2), arrived)
    last = line_exchange((near.astype(F32) + came.astype(F32)).astype(BF16))
    last, d_kv = after(last, left_t(encoded, dkv).astype(BF16))
    dq_parts = [rows_first(jnp.sum(part.astype(F32), axis=0)) for part in (arrived, last)]
    d_query_two = jnp.concatenate(dq_parts).astype(BF16)
    def kv_half(at):
        cube = d_kv.reshape(model_width, groups, 2, wide)
        return lax.dynamic_index_in_dim(cube, at, 2, keepdims=False).reshape(model_width, -1)

    kv_came = flip(kv_half(1 - core), 1)
    found = self_back(
        tokens, gain_rows, bias, first, qkv, stream_one, d_query_two, d_stream_two, head
    )
    kv_came, *found = after(kv_came, *found)
    d_qkv, grad_one, d_inputs, d_score, gain_terms = found
    kv_kept, kv_came = near_send(rows_by_owner(add_low(kv_half(core), kv_came)), 2)
    late_pairs = [(normed_self, d_qkv)]
    more_pairs = [(mixed_one, grad_one), (normed_cross, d_query_two)]
    late_sent, more_sent = outer(1 - half, late_pairs), outer(1 - half, more_pairs)
    d_table = jnp.einsum("hqk,qkb->bh", d_score, onehot_low, preferred_element_type=F32)
    small = jnp.concatenate([d_table.reshape(-1), gain_terms[0], gain_terms[1], d_gain_ffn])
    small = small.reshape(-1, 128)
    steps = [partial(flip, bit=1 << k) for k in range((pass_count - 1).bit_length())]
    steps += [partial(dp_step, bit=1 << k) for k in range((lax.axis_size("dp") - 1).bit_length())]
    late_came, more_came, small_came = after(flip(late_sent, 1), flip(more_sent, 1), steps[0](small))
    small = small + small_came

    late, more = outer(half, late_pairs, late_came), outer(half, more_pairs, more_came)
    kv_came, late, more, small_came = after(kv_came, late, more, steps[1](small))
    small = small + small_came
    late_kept, late_came = dp_send(rows_by_owner(late))
    more_kept, more_came = near_send(rows_by_owner(more), 2)
    kv_kept, kv_came = dp_send(add_low(kv_kept, kv_came))
    passage_grad = source_grads(refresh, dkv, kv_weight, plen)
    kv_came, late_came, more_came, passage_grad, ffn_sums, small_came = after(
        kv_came, late_came, more_came, passage_grad, ffn_sums, steps[2](small)
    )
    small = small + small_came
    late_kept, late_came = near_send(add_low(late_kept, late_came), 1)
    more_kept, more_came = dp_send(add_low(more_kept, more_came))
    late_came, more_came, small_came = after(late_came, more_came, steps[3](small))
    small = small + small_came
    parts = [(late_kept, late_came), (more_kept, more_came), (kv_kept, kv_came)]
    line = line_exchange(jnp.concatenate([add_low(*part) for part in parts], axis=-1))
    for step in steps[4:]:
        line, small_came = after(line, step(small))
        small = small + small_came
    line = jnp.sum(line.astype(F32), axis=0)
    table_grad = small.reshape(-1)[: d_table.size].reshape(d_table.shape)
    d_gains = small.reshape(-1)[d_table.size :].reshape(3, -1)
    d_gains = lax.dynamic_slice_in_dim(d_gains, device_id * shard, shard, 1)

    left, right = own_rows(line, core)
    half_width = model_width // 2

    def whole(start, stop):
        cut = slice(start * half_width, stop * half_width)
        return jnp.concatenate([left[:, cut], right[:, cut]], axis=1)

    d_first, d_out_self, d_query_cross = whole(0, 3), whole(3, 4), whole(4, 5)
    d_query_self, d_key_self, d_value_self = jnp.split(d_first, 3, axis=1)
    d_key_cross, d_value_cross = left[:, 5 * half_width :], right[:, 5 * half_width :]
    ffn_sums = ffn_sums.astype(F32)
    d_out_cross = ffn_sums[:, :model_width]
    d_up = ffn_sums[:, model_width : model_width + up_weight.shape[1]]
    d_down = ffn_sums[:, model_width + up_weight.shape[1] :].reshape(shard, folds, model_width)
    d_down = d_down.transpose(1, 0, 2).reshape(down_weight.shape)
    return (
        block_out,
        d_inputs,
        passage_grad,
        d_query_self,
        d_key_self,
        d_value_self,
        d_out_self,
        d_query_cross,
        d_key_cross,
        d_value_cross,
        d_out_cross,
        d_up,
        d_down,
        d_gains.T,
        table_grad,
    )


def solution(mesh):
    split = P(("dp", "pass"), None)
    cube = P(("dp", "pass"), None, None)
    in_specs = (split, split, cube, P(("dp", "pass")), P("dp", None)) + (split,) * 11 + (P(),)
    out_specs = (split, split, cube) + (split,) * 11 + (P(),)
    return jax.shard_map(
        on_device, mesh=mesh, in_specs=in_specs, out_specs=out_specs, check_vma=False
    )
```

```python
from functools import partial

import jax
import jax.numpy as jnp
from jax import lax
from jax.experimental import pallas as pl
from jax.experimental.pallas import tpu as pltpu
from jax.sharding import PartitionSpec as P

F32 = jnp.float32
BF16 = jnp.bfloat16
GROUP = 4
BLOCK = 10
STAT_ROWS = 16
CHUNK = 256
AHEAD = 2
FLOOR = -1e30


def norm_rows(value, gain):
    return value * lax.rsqrt(jnp.mean(value * value, axis=-1, keepdims=True) + 1e-06) * gain


def bucket_table(length, buckets):
    near_count = buckets // 2
    positions = jnp.arange(length)
    spread = jnp.maximum(positions[:, None] - positions[None, :], 0).astype(F32)
    bounds = near_count * 8.0 ** (jnp.arange(1, near_count, dtype=F32) / near_count)
    far_bucket = near_count + jnp.sum(
        (spread[:, :, None] >= bounds[None, None, :]).astype(jnp.int32), axis=-1
    )
    return jnp.where(spread < near_count, spread.astype(jnp.int32), far_bucket)


def matmul(left, right):
    return jnp.dot(left, right, preferred_element_type=F32)


def left_t(left, right):
    return jnp.einsum("td,te->de", left, right, preferred_element_type=F32)


def right_t(left, right):
    return jnp.einsum("te,de->td", left, right, preferred_element_type=F32)


def dot(left, right, dims):
    return lax.dot_general(left, right, (dims, ((), ())), preferred_element_type=F32)


def split_parts(value, count):
    parts = []
    for _ in range(count):
        part = value.astype(BF16).astype(F32)
        parts.append(part)
        value = value - part
    return parts


def spread_heads(rows, head):
    column = lax.broadcasted_iota(jnp.int32, rows.shape, 1) // head
    return jnp.concatenate(
        [jnp.where(column == h, rows, jnp.zeros_like(rows)) for h in range(GROUP)], axis=0
    )


def scale_rows(value):
    return lax.rsqrt(jnp.mean(value * value, axis=-1, keepdims=True) + 1e-06)


def norm_gradient(value, gain, grad):
    scale = scale_rows(value)
    unit = value * scale
    inner = grad * gain
    mean = jnp.mean(inner * unit, axis=-1, keepdims=True)
    return scale * (inner - unit * mean), jnp.sum(grad * unit, axis=0, keepdims=True)


def pair_spread(rows, head):
    first = lax.broadcasted_iota(jnp.int32, rows.shape, 1) < head
    zero = jnp.zeros_like(rows)
    return jnp.concatenate([jnp.where(first, rows, zero), jnp.where(first, zero, rows)], axis=0)


def pair_pick(full, head):
    rows = full.shape[0] // 2
    first = lax.broadcasted_iota(jnp.int32, (rows, full.shape[1]), 1) < head
    return jnp.where(first, full[:rows], full[rows:])


def pair_weights(qkv_ref, bias_ref, pair, head, width):
    at = slice(pair * 2 * head, (pair + 1) * 2 * head)
    query = pair_spread(qkv_ref[:, at], head)
    key = qkv_ref[:, width + at.start : width + at.stop]
    value = qkv_ref[:, 2 * width + at.start : 2 * width + at.stop]
    rows = key.shape[0]
    bias = bias_ref[2 * pair : 2 * pair + 2].reshape(2 * rows, rows)
    scores = dot(query, key, ((1,), (1,))) + bias
    raised = jnp.exp(scores - jnp.max(scores, axis=-1, keepdims=True))
    return query, key, value, raised / jnp.sum(raised, axis=-1, keepdims=True)


def self_kernel(head, tokens_ref, gain_ref, bias_ref, weight_ref, qkv_ref, mixed_ref, normed_ref, stream_ref, cross_ref, query_ref):
    width = tokens_ref.shape[1]
    inputs = tokens_ref[...].astype(F32)
    normed = (inputs * scale_rows(inputs) * gain_ref[0:1, :]).astype(BF16)
    normed_ref[...] = normed
    for k in range(3):
        at = slice(k * width, (k + 1) * width)
        qkv_ref[:, at] = dot(normed, weight_ref[:, at], ((1,), (0,))).astype(BF16)
    for pair in range(width // (2 * head)):
        _, _, value, weights = pair_weights(qkv_ref, bias_ref, pair, head, width)
        full = dot(weights.astype(BF16), value, ((1,), (0,)))
        mixed_ref[:, pair * 2 * head : (pair + 1) * 2 * head] = pair_pick(full, head).astype(BF16)
    stream = inputs + dot(mixed_ref[...], weight_ref[:, 3 * width : 4 * width], ((1,), (0,)))
    stream_ref[...] = stream
    cross = (stream * scale_rows(stream) * gain_ref[1:2, :]).astype(BF16)
    cross_ref[...] = cross
    query_ref[...] = dot(cross, weight_ref[:, 4 * width : 5 * width], ((1,), (0,))).astype(BF16)


def self_attend(tokens, gain_rows, bias, weight, head):
    rows, width = tokens.shape
    low = jax.ShapeDtypeStruct((rows, width), BF16)
    weight_spec = pl.BlockSpec((width, 5 * width), lambda i: (0, 0))
    return pl.pallas_call(
        partial(self_kernel, head),
        out_shape=(
            jax.ShapeDtypeStruct((rows, 3 * width), BF16),
            low,
            low,
            jax.ShapeDtypeStruct((rows, width), F32),
            low,
            low,
        ),
        grid=(1,),
        in_specs=[
            pl.BlockSpec(tokens.shape, lambda i: (0, 0)),
            pl.BlockSpec(gain_rows.shape, lambda i: (0, 0)),
            pl.BlockSpec(bias.shape, lambda i: (0, 0, 0)),
            weight_spec,
        ],
        out_specs=(pl.BlockSpec((rows, 3 * width), lambda i: (0, 0)),)
        + (pl.BlockSpec((rows, width), lambda i: (0, 0)),) * 5,
        compiler_params=pltpu.CompilerParams(vmem_limit_bytes=56 * 2**20),
        name="self_attend",
    )(tokens, gain_rows, bias, weight)


def self_back_kernel(head, tokens_ref, gain_ref, bias_ref, weight_ref, qkv_ref, stream_ref, dq_ref, dstream_ref, dqkv_ref, low_ref, dinput_ref, score_ref, dgain_ref):
    width = tokens_ref.shape[1]
    rows = tokens_ref.shape[0]
    d_cross = dot(dq_ref[...], weight_ref[:, 4 * width : 5 * width], ((1,), (1,)))
    d_stream, gain_cross = norm_gradient(stream_ref[...], gain_ref[1:2, :], d_cross)
    d_stream = d_stream + dstream_ref[...]
    low = d_stream.astype(BF16)
    low_ref[...] = low
    d_mixed = dot(low, weight_ref[:, 3 * width : 4 * width], ((1,), (1,))).astype(BF16)
    lanes = score_ref.shape[1]
    place = lax.broadcasted_iota(jnp.int32, (rows, lanes), 0) + lax.broadcasted_iota(
        jnp.int32, (rows, lanes), 1
    )
    mirror = (place == rows - 1).astype(F32).astype(BF16)
    sums = []
    for pair in range(width // (2 * head)):
        query, key, value, weights = pair_weights(qkv_ref, bias_ref, pair, head, width)
        at = slice(pair * 2 * head, (pair + 1) * 2 * head)
        spread = pair_spread(d_mixed[:, at], head)
        d_value = dot(weights.astype(BF16), spread, ((0,), (0,)))
        d_weights = dot(spread, value, ((1,), (1,)))
        inner = jnp.sum(weights * d_weights, axis=-1, keepdims=True)
        d_score = (weights * (d_weights - inner)).astype(BF16)
        reverse = dot(d_score, mirror, ((1,), (0,)))
        for h in range(2):
            turned = pltpu.roll(reverse[h * rows : (h + 1) * rows], 0, 1, stride=1, stride_axis=0)
            sums.append(jnp.sum(turned, axis=0, keepdims=True))
        d_query = pair_pick(dot(d_score, key, ((1,), (0,))), head)
        d_key = dot(d_score, query, ((0,), (0,)))
        dqkv_ref[:, at] = d_query.astype(BF16)
        dqkv_ref[:, width + at.start : width + at.stop] = d_key.astype(BF16)
        dqkv_ref[:, 2 * width + at.start : 2 * width + at.stop] = d_value.astype(BF16)
    d_normed = jnp.zeros((rows, width), F32)
    for k in range(3):
        at = slice(k * width, (k + 1) * width)
        d_normed = d_normed + dot(dqkv_ref[:, at], weight_ref[:, at], ((1,), (1,)))
    d_input, gain_self = norm_gradient(tokens_ref[...].astype(F32), gain_ref[0:1, :], d_normed)
    dinput_ref[...] = d_input + d_stream
    sums.append(jnp.zeros((score_ref.shape[0] - len(sums), lanes), F32))
    score_ref[...] = jnp.concatenate(sums, axis=0)
    dgain_ref[...] = jnp.concatenate([gain_self, gain_cross, jnp.zeros((6, width), F32)], axis=0)


def self_back(tokens, gain_rows, bias, weight, qkv, stream, d_query, d_stream, head):
    rows, width = tokens.shape

    def whole(shape):
        return pl.BlockSpec(shape, lambda i: (0,) * len(shape))

    shapes = (
        jax.ShapeDtypeStruct(qkv.shape, BF16),
        jax.ShapeDtypeStruct(tokens.shape, BF16),
        jax.ShapeDtypeStruct(tokens.shape, F32),
        jax.ShapeDtypeStruct((-(-bias.shape[0] // 8) * 8, -(-rows // 128) * 128), F32),
        jax.ShapeDtypeStruct((8, width), F32),
    )
    return pl.pallas_call(
        partial(self_back_kernel, head),
        out_shape=shapes,
        grid=(1,),
        in_specs=[
            whole(tokens.shape),
            whole(gain_rows.shape),
            whole(bias.shape),
            whole((width, 5 * width)),
            whole(qkv.shape),
            whole(tokens.shape),
            whole(tokens.shape),
            whole(tokens.shape),
        ],
        out_specs=tuple(whole(shape.shape) for shape in shapes),
        compiler_params=pltpu.CompilerParams(vmem_limit_bytes=56 * 2**20),
        name="self_back",
    )(tokens, gain_rows, bias, weight, qkv, stream, d_query, d_stream)


def pick_chunk(full, head, rows, start):
    chunk = full.shape[1]
    first = start // rows
    lane = (lax.broadcasted_iota(jnp.int32, (head, chunk), 1) + start) // rows - first
    out = full[:head]
    for h in range(1, full.shape[0] // head):
        out = jnp.where(lane == h, full[h * head : (h + 1) * head], out)
    return out


def flush_queries(here_ref, queries, pack, mine_ref, other_ref):
    near = queries // 4

    def flush(at, carry):
        y = jnp.bitwise_xor(here_ref[1], at // near)
        j = at % near * 4 + 2 * y
        mine_ref[at, 0] = pack(j + here_ref[0])
        other_ref[at, 0] = pack(j + 1 - here_ref[0])
        return carry

    lax.fori_loop(0, queries // 2, flush, 0)


def either(index, a_ref, b_ref):
    count = a_ref.shape[0]
    return jnp.where(index < count, a_ref[index % count], b_ref[index % count])


def attend_kernel(plen, head, rows, asker_ref, owner_ref, here_ref, qa_ref, qb_ref, kv_ref, mine_ref, other_ref, acc, top, total):
    step = pl.program_id(1)
    queries = 2 * qa_ref.shape[0]
    width = GROUP * head

    @pl.when(step == 0)
    def _():
        acc[...] = jnp.zeros_like(acc)
        top[...] = jnp.full_like(top, FLOOR)
        total[...] = jnp.zeros_like(total)

    lanes = GROUP * rows
    chunk = min(CHUNK, lanes)

    def begin(unit):
        p, c = divmod(unit, lanes // chunk)
        if c == 0:
            spreads[p] = spread_heads(either(asker_ref[step * BLOCK + p], qa_ref, qb_ref), head)
            turned[p] = kv_ref[p * plen : (p + 1) * plen, width:].T
        keys = kv_ref[p * plen : (p + 1) * plen, :width]
        return dot(keys, spreads[p][c * chunk : (c + 1) * chunk], ((1,), (1,)))

    def finish(unit, scores):
        p, c = divmod(unit, lanes // chunk)
        owner = owner_ref[step * BLOCK + p]
        at = pl.ds(c * chunk, chunk)
        first, last = c * chunk // rows, ((c + 1) * chunk - 1) // rows
        here = jnp.max(scores, axis=0, keepdims=True)
        raised = jnp.exp(scores - here)
        here_total = jnp.sum(raised, axis=0, keepdims=True)
        full = dot(turned[p][first * head : (last + 1) * head], raised.astype(BF16), ((1,), (0,)))
        mixed = pick_chunk(full, head, rows, c * chunk)
        old = top[owner, :, at]
        new = jnp.maximum(old, here)
        old_scale, here_scale = jnp.exp(old - new), jnp.exp(here - new)
        top[owner, :, at] = new
        total[owner, :, at] = total[owner, :, at] * old_scale + here_total * here_scale
        acc[owner, :, at] = acc[owner, :, at] * old_scale + mixed * here_scale

    spreads, turned = {}, {}
    units = BLOCK * (lanes // chunk)
    waiting = [begin(u) for u in range(min(AHEAD, units))]
    for unit in range(units):
        if unit + AHEAD < units:
            waiting.append(begin(unit + AHEAD))
        finish(unit, waiting.pop(0))

    @pl.when(step == pl.num_programs(1) - 1)
    def _():
        def pack(j):
            parts = split_parts(top[j], 3) + split_parts(total[j], 2)
            parts.append(jnp.zeros((STAT_ROWS - len(parts), parts[0].shape[1]), F32))
            return jnp.concatenate([acc[j]] + parts, axis=0).astype(BF16)

        flush_queries(here_ref, queries, pack, mine_ref, other_ref)


def attend(asker, owner, here, plane, across, kv, plen, head):
    near, rows, columns = plane.shape
    queries = 2 * near
    width = GROUP * head
    slots = kv.shape[0] // plen
    lanes = GROUP * rows
    groups = columns // width
    block = (near, 1, head + STAT_ROWS, lanes)
    out = jax.ShapeDtypeStruct((near, groups, head + STAT_ROWS, lanes), BF16)
    q_spec = pl.BlockSpec((near, rows, width), lambda g, b, *_: (0, 0, g))
    return pl.pallas_call(
        partial(attend_kernel, plen, head, rows),
        out_shape=(out, out),
        grid_spec=pltpu.PrefetchScalarGridSpec(
            num_scalar_prefetch=3,
            grid=(groups, slots // BLOCK),
            in_specs=[
                q_spec,
                q_spec,
                pl.BlockSpec((BLOCK * plen, 2 * width), lambda g, b, *_: (b, g)),
            ],
            out_specs=(pl.BlockSpec(block, lambda g, b, *_: (0, g, 0, 0)),) * 2,
            scratch_shapes=[
                pltpu.VMEM((queries, head, lanes), F32),
                pltpu.VMEM((queries, 1, lanes), F32),
                pltpu.VMEM((queries, 1, lanes), F32),
            ],
        ),
        compiler_params=pltpu.CompilerParams(vmem_limit_bytes=60 * 2**20),
        cost_estimate=pl.CostEstimate(
            flops=16 * rows * kv.shape[0] * columns,
            bytes_accessed=4 * kv.shape[0] * columns,
            transcendentals=rows * kv.shape[0] * GROUP * groups,
        ),
        name="attend",
    )(asker, owner, here, plane, across, kv)


def read_stats(stat):
    return stat[0:1] + stat[1:2] + stat[2:3], stat[3:4] + stat[4:5]


def merge_kernel(head, a_ref, b_ref, out_ref):
    for i in range(a_ref.shape[0]):
        for g in range(a_ref.shape[1]):
            top_a, sum_a = read_stats(a_ref[i, g, head:, :].astype(F32))
            top_b, sum_b = read_stats(b_ref[i, g, head:, :].astype(F32))
            top = jnp.maximum(top_a, top_b)
            w_a, w_b = jnp.exp(top_a - top), jnp.exp(top_b - top)
            body = a_ref[i, g, :head, :].astype(F32) * w_a + b_ref[i, g, :head, :].astype(F32) * w_b
            rows = split_parts(top, 3) + split_parts(sum_a * w_a + sum_b * w_b, 2)
            rows.append(jnp.zeros((STAT_ROWS - 5, top.shape[1]), F32))
            out_ref[i, g] = jnp.concatenate([body] + rows, axis=0).astype(BF16)


def core_kernel(head, a_ref, b_ref, near_ref, far_ref):
    @pl.when(pl.program_id(0) < 2)
    def _():
        merge_kernel(head, a_ref, b_ref, far_ref)

    @pl.when(pl.program_id(0) >= 2)
    def _():
        merge_kernel(head, a_ref, b_ref, near_ref)


def core_merge(kept, came, head):
    block = (kept.shape[0] // 4,) + kept.shape[1:]
    out = jax.ShapeDtypeStruct((kept.shape[0] // 2,) + kept.shape[1:], BF16)
    return pl.pallas_call(
        partial(core_kernel, head),
        out_shape=(out, out),
        grid=(4,),
        in_specs=[pl.BlockSpec(block, lambda i: ((i + 2) % 4, 0, 0, 0))] * 2,
        out_specs=(
            pl.BlockSpec(block, lambda i: (jnp.maximum(i - 2, 0), 0, 0, 0)),
            pl.BlockSpec(block, lambda i: (jnp.minimum(i, 1), 0, 0, 0)),
        ),
        cost_estimate=pl.CostEstimate(flops=4 * kept.size, bytes_accessed=6 * kept.size, transcendentals=0),
        name="core_merge",
    )(kept, came)


def near_merge(kept, came, head):
    spec = pl.BlockSpec((kept.shape[0] // 2,) + kept.shape[1:], lambda i: (i, 0, 0, 0))
    return pl.pallas_call(
        partial(merge_kernel, head),
        out_shape=jax.ShapeDtypeStruct(kept.shape, BF16),
        grid=(2,),
        in_specs=[spec, spec],
        out_specs=spec,
        cost_estimate=pl.CostEstimate(flops=4 * kept.size, bytes_accessed=6 * kept.size, transcendentals=0),
        name="near_merge",
    )(kept, came)


def join_parts(ref, g, head):
    count = ref.shape[0]
    found = [read_stats(ref[i, g, head:, :].astype(F32)) for i in range(count)]
    top = found[0][0]
    for i in range(1, count):
        top = jnp.maximum(top, found[i][0])
    weights = [jnp.exp(found[i][0] - top) for i in range(count)]
    whole = found[0][1] * weights[0]
    mixed = ref[0, g, :head, :].astype(F32) * weights[0]
    for i in range(1, count):
        whole = whole + found[i][1] * weights[i]
        mixed = mixed + ref[i, g, :head, :].astype(F32) * weights[i]
    return mixed / whole, top + jnp.log(whole)


def ffn_kernel(head, arrived_ref, stream_ref, cot_ref, gain_ref, weight_ref, payload_ref, out_ref, dstream_ref, dgain_ref, mixed_ref, low_ref, normed_ref, dinner_ref, active_ref, full_ref):
    rows, width = stream_ref.shape
    groups = arrived_ref.shape[1]
    wide = GROUP * head
    logs = []
    for g in range(groups):
        part, log = join_parts(arrived_ref, g, head)
        logs.append(log)
        turned = part.T
        heads = [turned[h * rows : (h + 1) * rows] for h in range(GROUP)]
        full_ref[:, g * wide : (g + 1) * wide] = jnp.concatenate(heads, axis=1)
    mixed = full_ref[...].astype(BF16)
    mixed_ref[...] = mixed
    stream = stream_ref[...] + dot(mixed, weight_ref[:, :width], ((1,), (0,)))
    normed = (stream * scale_rows(stream) * gain_ref[2:3, :]).astype(BF16)
    normed_ref[...] = normed
    grads = cot_ref[...]
    out = stream
    d_normed = jnp.zeros((rows, width), F32)
    folds = dinner_ref.shape[1] // width
    for k in range(folds):
        up = weight_ref[:, (k + 1) * width : (k + 2) * width]
        down = weight_ref[:, (k + 1 + folds) * width : (k + 2 + folds) * width]
        at = slice(k * width, (k + 1) * width)
        inner = dot(normed, up, ((1,), (0,)))
        square = inner * inner
        bent = jnp.tanh(0.7978845608028654 * (inner + 0.044715 * square * inner))
        half = 0.5 * (1.0 + bent)
        active = (inner * half).astype(BF16)
        slope = half + 0.5 * inner * (1.0 - bent * bent) * (
            0.7978845608028654 * (1.0 + 0.134145 * square)
        )
        active_ref[:, at] = active
        out = out + dot(active, down, ((1,), (0,)))
        d_inner = (dot(grads, down, ((1,), (1,))) * slope).astype(BF16)
        dinner_ref[:, at] = d_inner
        d_normed = d_normed + dot(d_inner, up, ((1,), (1,)))
    out_ref[...] = out.astype(BF16)
    d_stream, gain = norm_gradient(stream, gain_ref[2:3, :], d_normed)
    d_stream = d_stream + grads.astype(F32)
    dstream_ref[...] = d_stream
    dgain_ref[...] = jnp.concatenate([gain, jnp.zeros((7, width), F32)], axis=0)
    low = d_stream.astype(BF16)
    low_ref[...] = low
    d_mixed = dot(low, weight_ref[:, :width], ((1,), (1,))).astype(BF16)
    payload_ref[:rows, :] = d_mixed
    for g in range(groups):
        columns = slice(g * wide, (g + 1) * wide)
        product = (d_mixed[:, columns].astype(F32) * full_ref[:, columns]).T
        delta = [
            jnp.sum(product[h * head : (h + 1) * head], axis=0, keepdims=True) for h in range(GROUP)
        ]
        parts = split_parts(logs[g], 3) + split_parts(jnp.concatenate(delta, axis=1), 2)
        lines = [
            part[:, t * wide : (t + 1) * wide]
            for part in parts
            for t in range(GROUP * rows // wide)
        ]
        lines.append(jnp.zeros((STAT_ROWS - len(lines), wide), F32))
        payload_ref[rows:, columns] = jnp.concatenate(lines, axis=0).astype(BF16)


def feed_forward(arrived, stream, grads, gain_rows, weight, head):
    rows, width = stream.shape
    hidden = (weight.shape[1] - width) // 2

    def whole(shape):
        return pl.BlockSpec(shape, lambda i: (0,) * len(shape))

    low = jax.ShapeDtypeStruct((rows, width), BF16)
    long = jax.ShapeDtypeStruct((rows, hidden), BF16)
    shapes = (
        jax.ShapeDtypeStruct((rows + STAT_ROWS, width), BF16),
        low,
        jax.ShapeDtypeStruct((rows, width), F32),
        jax.ShapeDtypeStruct((8, width), F32),
        low,
        low,
        low,
        long,
        long,
    )
    return pl.pallas_call(
        partial(ffn_kernel, head),
        out_shape=shapes,
        grid=(1,),
        in_specs=[whole(v.shape) for v in (arrived, stream, grads, gain_rows, weight)],
        out_specs=tuple(whole(shape.shape) for shape in shapes),
        scratch_shapes=[pltpu.VMEM((rows, width), F32)],
        compiler_params=pltpu.CompilerParams(vmem_limit_bytes=56 * 2**20),
        cost_estimate=pl.CostEstimate(
            flops=4 * rows * weight.size, bytes_accessed=2 * weight.size, transcendentals=rows * hidden
        ),
        name="feed_forward",
    )(arrived, stream, grads, gain_rows, weight)


def ffn_terms_kernel(folds, *refs):
    out_ref = refs[-1]
    tile = pl.program_id(0)
    for first, last, left, right in ((0, 1, 0, 1), (1, 1 + folds, 2, 3), (1 + folds, 1 + 2 * folds, 4, 5)):

        @pl.when((tile >= first) & (tile < last))
        def _(left=left, right=right):
            a, b = refs[2 * left : 2 * left + 2], refs[2 * right : 2 * right + 2]
            found = dot(a[0][...], b[0][...], ((0,), (0,))) + dot(a[1][...], b[1][...], ((0,), (0,)))
            out_ref[...] = found.astype(BF16)


def ffn_terms(parts, grads, hidden):
    width = grads[0].shape[1]
    folds = hidden // width

    def spec(value, start):
        if start is None:
            return pl.BlockSpec((value.shape[0], width), lambda t: (0, 0))
        return pl.BlockSpec((value.shape[0], width), lambda t: (0, jnp.clip(t - start, 0, folds - 1)))

    operands, specs = [], []
    for values, start in zip([*zip(*parts), grads], (None, None, None, 1, 1 + folds, None)):
        for value in values:
            operands.append(value)
            specs.append(spec(value, start))
    return pl.pallas_call(
        partial(ffn_terms_kernel, folds),
        out_shape=jax.ShapeDtypeStruct((width, width + 2 * hidden), BF16),
        grid=(1 + 2 * folds,),
        in_specs=specs,
        out_specs=pl.BlockSpec((width, width), lambda t: (0, t)),
        compiler_params=pltpu.CompilerParams(vmem_limit_bytes=32 * 2**20),
        cost_estimate=pl.CostEstimate(
            flops=6 * width * width * width, bytes_accessed=8 * width * hidden, transcendentals=0
        ),
        name="ffn_terms",
    )(*operands)


def attend_back_kernel(plen, head, rows, asker_ref, owner_ref, here_ref, qa_ref, qb_ref, doa_ref, dob_ref, sa_ref, sb_ref, kv_ref, *refs):
    step = pl.program_id(1)
    dkv_ref, mine_ref, other_ref, acc, log, delta = refs[-6:]
    held_ref = refs[0] if len(refs) > 6 else None
    near = qa_ref.shape[0]
    queries = 2 * near
    width = GROUP * head

    @pl.when(step == 0)
    def _():
        acc[...] = jnp.zeros_like(acc)
        third = (GROUP * rows) // width

        def fill(j, carry):
            stat = either(j, sa_ref, sb_ref).astype(F32)
            row = lax.broadcasted_iota(jnp.int32, stat.shape, 0)
            for at, ref, count in ((0, log, 3), (3 * third, delta, 2)):
                pieces = []
                for t in range(third):
                    wanted = row == at + t
                    for k in range(1, count):
                        wanted = wanted | (row == at + k * third + t)
                    pieces.append(jnp.sum(jnp.where(wanted, stat, 0.0), axis=0, keepdims=True))
                ref[j] = jnp.concatenate(pieces, axis=1)
            return carry

        lax.fori_loop(0, queries, fill, 0)

    lanes = GROUP * rows
    chunk = min(CHUNK, lanes)

    def begin(unit):
        p, c = divmod(unit, lanes // chunk)
        rows_at = slice(p * plen, (p + 1) * plen)
        if c == 0:
            asker = asker_ref[step * BLOCK + p]
            q_spread[p] = spread_heads(either(asker, qa_ref, qb_ref), head)
            do_spread[p] = spread_heads(either(asker, doa_ref, dob_ref), head)
            turned[p] = kv_ref[rows_at, :width].T
        at = slice(c * chunk, (c + 1) * chunk)
        return (
            dot(kv_ref[rows_at, :width], q_spread[p][at], ((1,), (1,))),
            dot(kv_ref[rows_at, width:], do_spread[p][at], ((1,), (1,))),
        )

    def finish(unit, found):
        scores, d_soft = found
        p, c = divmod(unit, lanes // chunk)
        owner, asker = owner_ref[step * BLOCK + p], asker_ref[step * BLOCK + p]
        at = pl.ds(c * chunk, chunk)
        cut = slice(c * chunk, (c + 1) * chunk)
        first, last = c * chunk // rows, ((c + 1) * chunk - 1) // rows
        soft = jnp.exp(scores - log[asker, :, at])
        d_score = (soft * (d_soft - delta[asker, :, at])).astype(BF16)
        d_value = dot(soft.astype(BF16), do_spread[p][cut], ((1,), (0,)))
        d_key = dot(d_score, q_spread[p][cut], ((1,), (0,)))
        sums[p] = (d_key, d_value) if c == 0 else (sums[p][0] + d_key, sums[p][1] + d_value)
        full = dot(turned[p][first * head : (last + 1) * head], d_score, ((1,), (0,)))
        acc[owner, :, at] += pick_chunk(full, head, rows, c * chunk)
        if c == lanes // chunk - 1:
            rows_at = slice(p * plen, (p + 1) * plen)
            for found, columns in zip(sums[p], (slice(0, width), slice(width, 2 * width))):
                if held_ref is not None:
                    found = found + held_ref[rows_at, columns].astype(F32)
                dkv_ref[rows_at, columns] = found.astype(BF16)

    q_spread, do_spread, turned, sums = {}, {}, {}, {}
    units = BLOCK * (lanes // chunk)
    waiting = [begin(u) for u in range(min(AHEAD, units))]
    for unit in range(units):
        if unit + AHEAD < units:
            waiting.append(begin(unit + AHEAD))
        finish(unit, waiting.pop(0))

    @pl.when(step == pl.num_programs(1) - 1)
    def _():
        flush_queries(here_ref, queries, lambda j: acc[j].astype(BF16), mine_ref, other_ref)


def attend_back(asker, owner, here, queries_in, grads_in, kv, held, plen, head):
    near, rows, columns = queries_in[0].shape
    queries = 2 * near
    width = GROUP * head
    slots = kv.shape[0] // plen
    lanes = GROUP * rows
    groups = columns // width
    block = (near, 1, head, lanes)
    out = jax.ShapeDtypeStruct((near, groups, head, lanes), BF16)
    q_spec = pl.BlockSpec((near, rows, width), lambda g, b, *_: (0, 0, g))
    stat_spec = pl.BlockSpec((near, STAT_ROWS, width), lambda g, b, *_: (0, rows // STAT_ROWS, g))
    kv_spec = pl.BlockSpec((BLOCK * plen, 2 * width), lambda g, b, *_: (b, g))
    operands = [*queries_in, *grads_in, *grads_in, kv]
    specs = [q_spec] * 4 + [stat_spec] * 2 + [kv_spec]
    if held is not None:
        operands.append(held)
        specs.append(kv_spec)
    return pl.pallas_call(
        partial(attend_back_kernel, plen, head, rows),
        out_shape=(jax.ShapeDtypeStruct(kv.shape, BF16), out, out),
        grid_spec=pltpu.PrefetchScalarGridSpec(
            num_scalar_prefetch=3,
            grid=(groups, slots // BLOCK),
            in_specs=specs,
            out_specs=(
                kv_spec,
                pl.BlockSpec(block, lambda g, b, *_: (0, g, 0, 0)),
                pl.BlockSpec(block, lambda g, b, *_: (0, g, 0, 0)),
            ),
            scratch_shapes=[
                pltpu.VMEM((queries, head, lanes), F32),
                pltpu.VMEM((queries, 1, lanes), F32),
                pltpu.VMEM((queries, 1, lanes), F32),
            ],
        ),
        input_output_aliases={} if held is None else {3 + len(operands) - 1: 0},
        compiler_params=pltpu.CompilerParams(vmem_limit_bytes=60 * 2**20),
        cost_estimate=pl.CostEstimate(
            flops=40 * rows * kv.shape[0] * columns,
            bytes_accessed=8 * kv.shape[0] * columns,
            transcendentals=rows * kv.shape[0] * GROUP * groups,
        ),
        name="attend_back",
    )(asker, owner, here, *operands)


def source_kernel(keep_ref, fetch_ref, dkv_ref, weight_ref, out_ref):
    kept = keep_ref[pl.program_id(0)]

    @pl.when(kept == 0)
    def _():
        out_ref[...] = jnp.zeros_like(out_ref)

    @pl.when(kept != 0)
    def _():
        out_ref[0] = dot(dkv_ref[...], weight_ref[...], ((1,), (1,))).astype(BF16)


def source_grads(refresh, dkv, weight, plen):
    slots = refresh.shape[0]
    model_width = weight.shape[0]
    fetch = lax.cummax(jnp.where(refresh != 0, jnp.arange(slots), 0), axis=0).astype(jnp.int32)
    return pl.pallas_call(
        source_kernel,
        out_shape=jax.ShapeDtypeStruct((slots, plen, model_width), BF16),
        grid_spec=pltpu.PrefetchScalarGridSpec(
            num_scalar_prefetch=2,
            grid=(slots,),
            in_specs=[
                pl.BlockSpec((plen, dkv.shape[1]), lambda r, keep, fetch: (fetch[r], 0)),
                pl.BlockSpec(weight.shape, lambda r, *_: (0, 0)),
            ],
            out_specs=pl.BlockSpec((1, plen, model_width), lambda r, *_: (r, 0, 0)),
        ),
        compiler_params=pltpu.CompilerParams(vmem_limit_bytes=40 * 2**20),
        cost_estimate=pl.CostEstimate(
            flops=slots * plen * model_width * 2 * model_width,
            bytes_accessed=4 * slots * plen * model_width,
            transcendentals=0,
        ),
        name="source_grads",
    )(refresh, fetch, dkv, weight)


def outer_kernel(starts, added, half_ref, *refs):
    out_ref = refs[-1]
    tile = pl.program_id(1)
    for k in range(len(starts) - 1):

        @pl.when((tile >= starts[k]) & (tile < starts[k + 1]))
        def _(k=k):
            found = dot(refs[2 * k][...], refs[2 * k + 1][...], ((0,), (0,)))
            if added:
                found = found + refs[-2][...].astype(F32)
            out_ref[...] = found.astype(BF16)


def outer(half, pairs, came=None):
    rows = pairs[0][0].shape[0]
    height = min(left.shape[1] for left, _ in pairs)
    height = height if height <= 1024 else height // 4
    total_rows = pairs[0][0].shape[1]
    width = min(right.shape[1] for _, right in pairs) // 2
    counts = [right.shape[1] // 2 // width for _, right in pairs]
    starts = [sum(counts[:k]) for k in range(len(counts) + 1)]
    operands, specs = [], []
    for k, (left, right) in enumerate(pairs):

        def right_map(r, t, half_ref, start=starts[k], count=counts[k]):
            return (0, half_ref[0] * count + jnp.clip(t - start, 0, count - 1))

        operands += [left, right]
        specs += [
            pl.BlockSpec((rows, height), lambda r, t, half_ref: (0, r)),
            pl.BlockSpec((rows, width), right_map),
        ]
    out_spec = pl.BlockSpec((height, width), lambda r, t, half_ref: (r, t))
    if came is not None:
        operands.append(came)
        specs.append(out_spec)
    size = total_rows * starts[-1] * width
    return pl.pallas_call(
        partial(outer_kernel, starts, came is not None),
        out_shape=jax.ShapeDtypeStruct((total_rows, starts[-1] * width), BF16),
        grid_spec=pltpu.PrefetchScalarGridSpec(
            num_scalar_prefetch=1,
            grid=(total_rows // height, starts[-1]),
            in_specs=specs,
            out_specs=out_spec,
        ),
        compiler_params=pltpu.CompilerParams(vmem_limit_bytes=32 * 2**20),
        cost_estimate=pl.CostEstimate(flops=2 * rows * size, bytes_accessed=4 * size, transcendentals=0),
        name="outer",
    )(half, *operands)


def flip(value, bit):
    count = lax.axis_size("pass")
    return lax.ppermute(value, "pass", [(i, i ^ bit) for i in range(count)])


def after(value, *others):
    return lax.optimization_barrier((value,) + others)


def line_sends(block):
    count = lax.axis_size("pass")
    rings = [[(i, (i + 4 * k) % count) for i in range(count)] for k in range(1, count // 4)]
    return [lax.ppermute(block, "pass", ring) for ring in rings]


def gather_place(query, own, count):
    major = count // 4
    turn = jnp.mod(own // 4 - query // 4, major)
    return turn + major * ((own // 2) % 2 != (query // 2) % 2) + 2 * major * (own % 2 != query % 2)


def line_exchange(parts):
    count = lax.axis_size("pass")
    groups = [[r + 4 * k for k in range(count // 4)] for r in range(4)]
    return lax.all_to_all(
        parts, "pass", split_axis=0, concat_axis=0, tiled=True, axis_index_groups=groups
    )


def in_order(own, came, place, axis):
    return jnp.stack([jnp.where(place == 0, own, came), jnp.where(place == 0, came, own)], axis=axis)


def gather_rows(block):
    n_dp, count = lax.axis_size("dp"), lax.axis_size("pass")
    if n_dp != 2:
        return lax.all_gather(block, ("dp", "pass"), axis=0, tiled=True)
    own, dp = lax.axis_index("pass"), lax.axis_index("dp")
    major, core, y = count // 4, own % 2, own // 2 % 2
    pieces = [block, *line_sends(block)]
    line = jnp.zeros((major,) + block.shape, block.dtype)
    for k, piece in enumerate(pieces):
        line = lax.dynamic_update_index_in_dim(line, piece, jnp.mod(own // 4 - k, major), 0)
    cut = block.shape[1] // 256 * 128
    left, right = line[..., :cut], line[..., cut:]
    left, right = in_order(left, flip(left, 2), y, 1), in_order(right, dp_flip(right), dp, 0)
    left, right = in_order(left, dp_flip(left), dp, 0), in_order(right, flip(right, 2), y, 2)
    full = [in_order(part, flip(part, 1), core, 3) for part in (left, right)]
    return jnp.concatenate([part.reshape(-1, part.shape[-1]) for part in full], axis=1)


def swap_send(value, place, axis, send):
    kept = lax.dynamic_index_in_dim(value, place, axis, keepdims=False)
    return kept, send(lax.dynamic_index_in_dim(value, 1 - place, axis, keepdims=False))


def add_low(kept, came):
    return (kept.astype(F32) + came.astype(F32)).astype(BF16)


def rows_by_owner(value):
    n_dp, count = lax.axis_size("dp"), lax.axis_size("pass")
    rows, columns = value.shape
    return value.reshape(n_dp, count // 4, 2, rows // (n_dp * count // 2), columns)


def dp_step(value, bit):
    pairs = [(i, i ^ bit) for i in range(lax.axis_size("dp"))]
    return lax.ppermute(value, "dp", pairs)


def dp_flip(value):
    return lax.ppermute(value, "dp", [(0, 1), (1, 0)])


def dp_send(value):
    if lax.axis_size("dp") == 2:
        return swap_send(value, lax.axis_index("dp"), 0, dp_flip)
    total = lax.psum_scatter(value, "dp", scatter_dimension=0, tiled=False)
    return total, jnp.zeros_like(total)


def near_send(value, axis):
    return swap_send(value, lax.axis_index("pass") // 2 % 2, axis, lambda v: flip(v, 2))


def over_line(value):
    return jnp.sum(line_exchange(value).astype(F32), axis=0)


def own_rows(value, core):
    shard = value.shape[0] // 2
    parts = value.reshape(2, shard, value.shape[1])
    kept = lax.dynamic_index_in_dim(parts, core, 0, keepdims=False)
    came = flip(lax.dynamic_index_in_dim(parts, 1 - core, 0, keepdims=False), 1)
    return jnp.where(core == 0, kept, came), jnp.where(core == 0, came, kept)


def on_device(
    tokens,
    cotangent,
    passages,
    refresh,
    passage_ids,
    self_query,
    self_key,
    self_value,
    self_out,
    cross_query,
    cross_key,
    cross_value,
    cross_out,
    up_weight,
    down_weight,
    gains,
    rel_table,
):
    both = ("dp", "pass")
    pass_count = lax.axis_size("pass")
    device_id = lax.axis_index(both)
    own_pass = lax.axis_index("pass")
    per_query, plen, model_width = passages.shape
    head_count = rel_table.shape[1]
    head = model_width // head_count
    rows = tokens.shape[0]
    groups = head_count // GROUP
    wide = GROUP * head
    shard = self_query.shape[0]

    def gather(value):
        return lax.all_gather(value, both, axis=0, tiled=True)

    kv_shard = jnp.stack(
        [cross_key.reshape(shard, groups, wide), cross_value.reshape(shard, groups, wide)], axis=2
    ).reshape(shard, 2 * model_width)
    gain_pad = jnp.pad(gains, ((0, 0), (0, 128 - gains.shape[1])))
    first = gather(
        jnp.concatenate([self_query, self_key, self_value, self_out, cross_query, gain_pad], axis=1)
    )
    kv_weight = gather_rows(kv_shard)
    encoded = passages.reshape(per_query * plen, model_width)
    kv = matmul(encoded, kv_weight).astype(BF16)
    positions = jnp.arange(rows)
    causal = positions[:, None] >= positions[None, :]
    onehot_low = (
        bucket_table(rows, rel_table.shape[0])[:, :, None]
        == jnp.arange(rel_table.shape[0])[None, None, :]
    ).astype(BF16)
    bias = jnp.einsum("qkb,bh->hqk", onehot_low, rel_table, preferred_element_type=F32)
    bias = jnp.where(causal[None, :, :], bias, FLOOR)
    first, kv, bias, *more = after(first, kv, bias, cross_out, up_weight, down_weight)
    folds = up_weight.shape[1] // model_width
    total = up_weight.shape[1] // (folds * shard)
    up_fold = more[1].reshape(shard, total, folds, shard).transpose(0, 2, 1, 3).reshape(shard, -1)
    down_fold = more[2].reshape(folds, shard, model_width).transpose(1, 0, 2).reshape(shard, -1)
    rest = gather(jnp.concatenate([more[0], up_fold, down_fold], axis=1))
    gain_all = first[:, 5 * model_width : 5 * model_width + 3].astype(F32)

    row_ids = device_id * per_query + jnp.arange(per_query)
    owned = jnp.any(passage_ids[:, :, None] == row_ids[None, None, :], axis=1)
    owner = jnp.sum(
        jnp.where(owned, jnp.arange(passage_ids.shape[0])[:, None], 0), axis=0
    ).astype(jnp.int32)
    core = own_pass % 2
    half = core.astype(jnp.int32).reshape(1)
    here = jnp.stack([core, own_pass // 2 % 2]).astype(jnp.int32)
    asker = gather_place(owner, own_pass, pass_count).astype(jnp.int32)

    gain_rows = jnp.pad(gain_all.T, ((0, 5), (0, 0)))
    qkv, mixed_one, normed_self, stream_one, normed_cross, query_two = self_attend(
        tokens, gain_rows, bias, first, head
    )

    cut = rows // 192 * 64

    def merge_send(mine, came):
        near, far = core_merge(mine, came, head)
        return near, flip(far, 2)

    def rows_first(value):
        cube = value.reshape(groups, head, GROUP, -1).transpose(3, 0, 2, 1)
        return cube.reshape(-1, model_width)

    block, last_block = query_two[:cut], query_two[cut:]
    last_block, *sends = after(last_block, *line_sends(block))
    line = jnp.stack([block, *sends])
    across = flip(line, 2)
    sends = line_sends(last_block)
    plane = jnp.concatenate([line, across])
    q_first = (plane, flip(plane, 1))
    mine, other = attend(asker, owner, here, *q_first, kv, plen, head)
    mine, other, *sends = after(mine, other, *sends)
    came = flip(other, 1)
    line = jnp.stack([last_block, *sends])
    across = flip(line, 2)
    near, far = core_merge(mine, came, head)
    across, near, far = after(across, near, far)
    came = flip(far, 2)
    plane = jnp.concatenate([line, across])
    q_second = (plane, flip(plane, 1))
    mine, other = attend(asker, owner, here, *q_second, kv, plen, head)
    came, mine, other = after(came, mine, other)
    came_next = flip(other, 1)
    merged, mine, came_next = after(near_merge(near, came, head), mine, came_next)
    arrived = line_exchange(merged)
    near, came = merge_send(mine, came_next)
    arrived, near = after(arrived, near)
    payload, out_first, ds_first, gain_first, *terms_first = feed_forward(
        arrived, stream_one[:cut], cotangent[:cut], gain_rows, rest, head
    )
    came, payload = after(came, payload)
    merged, *sends = after(near_merge(near, came, head), *line_sends(payload))
    arrived = line_exchange(merged)
    line = jnp.stack([payload, *sends])
    across = flip(line, 2)
    payload, out_last, ds_last, gain_last, *terms_last = feed_forward(
        arrived, stream_one[cut:], cotangent[cut:], gain_rows, rest, head
    )
    across, payload = after(across, payload)
    plane = jnp.concatenate([line, across])
    do_first = (plane, flip(plane, 1))
    sends = line_sends(payload)

    block_out = jnp.concatenate([out_first, out_last])
    d_stream_two = jnp.concatenate([ds_first, ds_last])
    d_gain_ffn = gain_first[0] + gain_last[0]
    terms = ffn_terms(
        (terms_first, terms_last), (cotangent[:cut], cotangent[cut:]), up_weight.shape[1]
    )
    terms, *sends = after(terms, *sends)
    ffn_sums = lax.psum_scatter(terms, both, scatter_dimension=0, tiled=True)
    line = jnp.stack([payload, *sends])
    across = flip(line, 2)

    def half_of(value, came):
        value = (value.astype(F32) + came.astype(F32)).astype(BF16)
        return value[: value.shape[0] // 2], value[value.shape[0] // 2 :]

    dkv, mine, other = attend_back(asker, owner, here, q_first, do_first, kv, None, plen, head)
    across, dkv, mine, other = after(across, dkv, mine, other)
    came = flip(other, 1)
    plane = jnp.concatenate([line, across])
    do_last = (plane, flip(plane, 1))
    near, far = half_of(mine, came)
    came = flip(far, 2)
    do_last, near = after(do_last, near)
    dkv, mine, other = attend_back(asker, owner, here, q_second, do_last, kv, dkv, plen, head)
    came, dkv, mine, other = after(came, dkv, mine, other)
    came_next = flip(other, 1)
    arrived = line_exchange((near.astype(F32) + came.astype(F32)).astype(BF16))
    near, far = half_of(mine, came_next)
    came, arrived = after(flip(far, 2), arrived)
    last = line_exchange((near.astype(F32) + came.astype(F32)).astype(BF16))
    last, d_kv = after(last, left_t(encoded, dkv).astype(BF16))
    dq_parts = [rows_first(jnp.sum(part.astype(F32), axis=0)) for part in (arrived, last)]
    d_query_two = jnp.concatenate(dq_parts).astype(BF16)
    def kv_half(at):
        cube = d_kv.reshape(model_width, groups, 2, wide)
        return lax.dynamic_index_in_dim(cube, at, 2, keepdims=False).reshape(model_width, -1)

    kv_came = flip(kv_half(1 - core), 1)
    found = self_back(
        tokens, gain_rows, bias, first, qkv, stream_one, d_query_two, d_stream_two, head
    )
    kv_came, ffn_sums, *found = after(kv_came, ffn_sums, *found)
    d_qkv, grad_one, d_inputs, d_score, gain_terms = found
    late_pairs = [(normed_self, d_qkv)]
    more_pairs = [(mixed_one, grad_one), (normed_cross, d_query_two)]
    late_sent, more_sent = outer(1 - half, late_pairs), outer(1 - half, more_pairs)
    distance = jnp.mod(jnp.arange(d_score.shape[1]) - (rows - 1), d_score.shape[1])
    of_distance = bucket_table(d_score.shape[1], rel_table.shape[0])[:, 0][distance]
    of_distance = (of_distance[:, None] == jnp.arange(rel_table.shape[0])[None, :]).astype(F32)
    d_table = jnp.dot(d_score, of_distance, precision=lax.Precision.HIGHEST)[:head_count].T
    small = jnp.concatenate([d_table.reshape(-1), gain_terms[0], gain_terms[1], d_gain_ffn])
    small = small.reshape(-1, 128)
    late_sent, more_sent, kv_came = after(late_sent, more_sent, kv_came)
    kv_part = jnp.moveaxis(rows_by_owner(add_low(kv_half(core), kv_came)), 1, 0)
    late_came, more_came, kv_part, came = after(
        flip(late_sent, 1), flip(more_sent, 1), kv_part, flip(small, 1)
    )
    small = small + came

    late, more = outer(half, late_pairs, late_came), outer(half, more_pairs, more_came)
    late, more, came = after(late, more, flip(small, 2))
    small = small + came
    late_kept, late_came = dp_send(rows_by_owner(late))
    more_kept, more_came = near_send(rows_by_owner(more), 2)
    kv_line = line_exchange(kv_part)
    passage_grad = source_grads(refresh, dkv, kv_weight, plen)
    for bit in range((lax.axis_size("dp") - 1).bit_length()):
        small = small + dp_step(small, 1 << bit)
    kv_line, late_came, more_came, passage_grad, small = after(
        kv_line, late_came, more_came, passage_grad, small
    )
    late_kept, late_came = near_send(add_low(late_kept, late_came), 1)
    more_kept, more_came = dp_send(add_low(more_kept, more_came))
    kv_kept, kv_came = dp_send(jnp.sum(kv_line.astype(F32), axis=0).astype(BF16))
    for bit in range(2, (pass_count - 1).bit_length()):
        small = small + flip(small, 1 << bit)
    late_came, more_came, kv_came, small = after(late_came, more_came, kv_came, small)
    kv_kept, kv_came = near_send(add_low(kv_kept, kv_came), 0)
    parts = [(late_kept, late_came), (more_kept, more_came)]
    line = line_exchange(jnp.concatenate([add_low(*part) for part in parts], axis=-1))
    ffn_sums = ffn_sums.astype(F32)
    d_up = ffn_sums[:, model_width : model_width + up_weight.shape[1]]
    d_up = d_up.reshape(shard, folds, total, shard).transpose(0, 2, 1, 3).reshape(up_weight.shape)
    d_down = ffn_sums[:, model_width + up_weight.shape[1] :].reshape(shard, folds, model_width)
    d_down = d_down.transpose(1, 0, 2).reshape(down_weight.shape)
    line, kv_came, d_up, d_down = after(line, kv_came, d_up, d_down)
    small = small.reshape(-1)
    line = jnp.sum(line.astype(F32), axis=0)
    line = jnp.concatenate([line, kv_kept.astype(F32) + kv_came.astype(F32)], axis=1)
    table_grad = small[: d_table.size].reshape(d_table.shape)
    d_gains = small[d_table.size :].reshape(3, -1)
    d_gains = lax.dynamic_slice_in_dim(d_gains, device_id * shard, shard, 1)

    left, right = own_rows(line, core)
    half_width = model_width // 2

    def whole(start, stop):
        cut = slice(start * half_width, stop * half_width)
        return jnp.concatenate([left[:, cut], right[:, cut]], axis=1)

    d_first, d_out_self, d_query_cross = whole(0, 3), whole(3, 4), whole(4, 5)
    d_query_self, d_key_self, d_value_self = jnp.split(d_first, 3, axis=1)
    d_key_cross, d_value_cross = left[:, 5 * half_width :], right[:, 5 * half_width :]
    d_out_cross = ffn_sums[:, :model_width]
    return (
        block_out,
        d_inputs,
        passage_grad,
        d_query_self,
        d_key_self,
        d_value_self,
        d_out_self,
        d_query_cross,
        d_key_cross,
        d_value_cross,
        d_out_cross,
        d_up,
        d_down,
        d_gains.T,
        table_grad,
    )


def solution(mesh):
    split = P(("dp", "pass"), None)
    cube = P(("dp", "pass"), None, None)
    in_specs = (split, split, cube, P(("dp", "pass")), P("dp", None)) + (split,) * 11 + (P(),)
    out_specs = (split, split, cube) + (split,) * 11 + (P(),)
    return jax.shard_map(
        on_device, mesh=mesh, in_specs=in_specs, out_specs=out_specs, check_vma=False
    )
```

```python
from functools import partial

import jax
import jax.numpy as jnp
from jax import lax
from jax.experimental import pallas as pl
from jax.experimental.pallas import tpu as pltpu
from jax.sharding import PartitionSpec as P

F32 = jnp.float32
BF16 = jnp.bfloat16
GROUP = 4
BLOCK = 10
STAT_ROWS = 16
CHUNK = 256
AHEAD = 2
FLOOR = -1e30


def norm_rows(value, gain):
    return value * lax.rsqrt(jnp.mean(value * value, axis=-1, keepdims=True) + 1e-06) * gain


def bucket_of(spread, buckets):
    near_count = buckets // 2
    spread = jnp.maximum(spread, 0).astype(F32)
    bounds = near_count * 8.0 ** (jnp.arange(1, near_count, dtype=F32) / near_count)
    far_bucket = near_count + jnp.sum((spread[..., None] >= bounds).astype(jnp.int32), axis=-1)
    return jnp.where(spread < near_count, spread.astype(jnp.int32), far_bucket)


def matmul(left, right):
    return jnp.dot(left, right, preferred_element_type=F32)


def left_t(left, right):
    return jnp.einsum("td,te->de", left, right, preferred_element_type=F32)


def right_t(left, right):
    return jnp.einsum("te,de->td", left, right, preferred_element_type=F32)


def dot(left, right, dims):
    return lax.dot_general(left, right, (dims, ((), ())), preferred_element_type=F32)


def split_parts(value, count):
    parts = []
    for _ in range(count):
        part = value.astype(BF16).astype(F32)
        parts.append(part)
        value = value - part
    return parts


def spread_heads(rows, head):
    column = lax.broadcasted_iota(jnp.int32, rows.shape, 1) // head
    return jnp.concatenate(
        [jnp.where(column == h, rows, jnp.zeros_like(rows)) for h in range(GROUP)], axis=0
    )


def scale_rows(value):
    return lax.rsqrt(jnp.mean(value * value, axis=-1, keepdims=True) + 1e-06)


def norm_gradient(value, gain, grad):
    scale = scale_rows(value)
    unit = value * scale
    inner = grad * gain
    mean = jnp.mean(inner * unit, axis=-1, keepdims=True)
    return scale * (inner - unit * mean), jnp.sum(grad * unit, axis=0, keepdims=True)


def pair_spread(rows, head):
    first = lax.broadcasted_iota(jnp.int32, rows.shape, 1) < head
    zero = jnp.zeros_like(rows)
    return jnp.concatenate([jnp.where(first, rows, zero), jnp.where(first, zero, rows)], axis=0)


def pair_pick(full, head):
    rows = full.shape[0] // 2
    first = lax.broadcasted_iota(jnp.int32, (rows, full.shape[1]), 1) < head
    return jnp.where(first, full[:rows], full[rows:])


def pair_weights(qkv_ref, bias_ref, pair, head, width):
    at = slice(pair * 2 * head, (pair + 1) * 2 * head)
    query = pair_spread(qkv_ref[:, at], head)
    key = qkv_ref[:, width + at.start : width + at.stop]
    value = qkv_ref[:, 2 * width + at.start : 2 * width + at.stop]
    rows = key.shape[0]
    bias = bias_ref[2 * pair : 2 * pair + 2].reshape(2 * rows, rows)
    scores = dot(query, key, ((1,), (1,))) + bias
    raised = jnp.exp(scores - jnp.max(scores, axis=-1, keepdims=True))
    return query, key, value, raised / jnp.sum(raised, axis=-1, keepdims=True)


def self_kernel(head, tokens_ref, gain_ref, bias_ref, weight_ref, qkv_ref, mixed_ref, normed_ref, stream_ref, cross_ref, query_ref):
    width = tokens_ref.shape[1]
    inputs = tokens_ref[...].astype(F32)
    normed = (inputs * scale_rows(inputs) * gain_ref[0:1, :]).astype(BF16)
    normed_ref[...] = normed
    for k in range(3):
        at = slice(k * width, (k + 1) * width)
        qkv_ref[:, at] = dot(normed, weight_ref[:, at], ((1,), (0,))).astype(BF16)
    for pair in range(width // (2 * head)):
        _, _, value, weights = pair_weights(qkv_ref, bias_ref, pair, head, width)
        full = dot(weights.astype(BF16), value, ((1,), (0,)))
        mixed_ref[:, pair * 2 * head : (pair + 1) * 2 * head] = pair_pick(full, head).astype(BF16)
    stream = inputs + dot(mixed_ref[...], weight_ref[:, 3 * width : 4 * width], ((1,), (0,)))
    stream_ref[...] = stream
    cross = (stream * scale_rows(stream) * gain_ref[1:2, :]).astype(BF16)
    cross_ref[...] = cross
    query_ref[...] = dot(cross, weight_ref[:, 4 * width : 5 * width], ((1,), (0,))).astype(BF16)


def self_attend(tokens, gain_rows, bias, weight, head):
    rows, width = tokens.shape
    low = jax.ShapeDtypeStruct((rows, width), BF16)
    weight_spec = pl.BlockSpec((width, 5 * width), lambda i: (0, 0))
    return pl.pallas_call(
        partial(self_kernel, head),
        out_shape=(
            jax.ShapeDtypeStruct((rows, 3 * width), BF16),
            low,
            low,
            jax.ShapeDtypeStruct((rows, width), F32),
            low,
            low,
        ),
        grid=(1,),
        in_specs=[
            pl.BlockSpec(tokens.shape, lambda i: (0, 0)),
            pl.BlockSpec(gain_rows.shape, lambda i: (0, 0)),
            pl.BlockSpec(bias.shape, lambda i: (0, 0, 0)),
            weight_spec,
        ],
        out_specs=(pl.BlockSpec((rows, 3 * width), lambda i: (0, 0)),)
        + (pl.BlockSpec((rows, width), lambda i: (0, 0)),) * 5,
        compiler_params=pltpu.CompilerParams(vmem_limit_bytes=56 * 2**20),
        name="self_attend",
    )(tokens, gain_rows, bias, weight)


def self_back_kernel(head, tokens_ref, gain_ref, bias_ref, weight_ref, qkv_ref, stream_ref, dq_ref, dstream_ref, dqkv_ref, low_ref, dinput_ref, score_ref, dgain_ref):
    width = tokens_ref.shape[1]
    rows = tokens_ref.shape[0]
    d_cross = dot(dq_ref[...], weight_ref[:, 4 * width : 5 * width], ((1,), (1,)))
    d_stream, gain_cross = norm_gradient(stream_ref[...], gain_ref[1:2, :], d_cross)
    d_stream = d_stream + dstream_ref[...]
    low = d_stream.astype(BF16)
    low_ref[...] = low
    d_mixed = dot(low, weight_ref[:, 3 * width : 4 * width], ((1,), (1,))).astype(BF16)
    lanes = score_ref.shape[1]
    place = lax.broadcasted_iota(jnp.int32, (rows, lanes), 0) + lax.broadcasted_iota(
        jnp.int32, (rows, lanes), 1
    )
    mirror = (place == rows - 1).astype(F32).astype(BF16)
    sums = []
    for pair in range(width // (2 * head)):
        query, key, value, weights = pair_weights(qkv_ref, bias_ref, pair, head, width)
        at = slice(pair * 2 * head, (pair + 1) * 2 * head)
        spread = pair_spread(d_mixed[:, at], head)
        d_value = dot(weights.astype(BF16), spread, ((0,), (0,)))
        d_weights = dot(spread, value, ((1,), (1,)))
        inner = jnp.sum(weights * d_weights, axis=-1, keepdims=True)
        d_score = (weights * (d_weights - inner)).astype(BF16)
        reverse = dot(d_score, mirror, ((1,), (0,)))
        for h in range(2):
            turned = pltpu.roll(reverse[h * rows : (h + 1) * rows], 0, 1, stride=1, stride_axis=0)
            sums.append(jnp.sum(turned, axis=0, keepdims=True))
        d_query = pair_pick(dot(d_score, key, ((1,), (0,))), head)
        d_key = dot(d_score, query, ((0,), (0,)))
        dqkv_ref[:, at] = d_query.astype(BF16)
        dqkv_ref[:, width + at.start : width + at.stop] = d_key.astype(BF16)
        dqkv_ref[:, 2 * width + at.start : 2 * width + at.stop] = d_value.astype(BF16)
    d_normed = jnp.zeros((rows, width), F32)
    for k in range(3):
        at = slice(k * width, (k + 1) * width)
        d_normed = d_normed + dot(dqkv_ref[:, at], weight_ref[:, at], ((1,), (1,)))
    d_input, gain_self = norm_gradient(tokens_ref[...].astype(F32), gain_ref[0:1, :], d_normed)
    dinput_ref[...] = d_input + d_stream
    sums.append(jnp.zeros((score_ref.shape[0] - len(sums), lanes), F32))
    score_ref[...] = jnp.concatenate(sums, axis=0)
    dgain_ref[...] = jnp.concatenate([gain_self, gain_cross, jnp.zeros((6, width), F32)], axis=0)


def self_back(tokens, gain_rows, bias, weight, qkv, stream, d_query, d_stream, head):
    rows, width = tokens.shape

    def whole(shape):
        return pl.BlockSpec(shape, lambda i: (0,) * len(shape))

    shapes = (
        jax.ShapeDtypeStruct(qkv.shape, BF16),
        jax.ShapeDtypeStruct(tokens.shape, BF16),
        jax.ShapeDtypeStruct(tokens.shape, F32),
        jax.ShapeDtypeStruct((-(-bias.shape[0] // 8) * 8, -(-rows // 128) * 128), F32),
        jax.ShapeDtypeStruct((8, width), F32),
    )
    return pl.pallas_call(
        partial(self_back_kernel, head),
        out_shape=shapes,
        grid=(1,),
        in_specs=[
            whole(tokens.shape),
            whole(gain_rows.shape),
            whole(bias.shape),
            whole((width, 5 * width)),
            whole(qkv.shape),
            whole(tokens.shape),
            whole(tokens.shape),
            whole(tokens.shape),
        ],
        out_specs=tuple(whole(shape.shape) for shape in shapes),
        compiler_params=pltpu.CompilerParams(vmem_limit_bytes=56 * 2**20),
        name="self_back",
    )(tokens, gain_rows, bias, weight, qkv, stream, d_query, d_stream)


def pick_chunk(full, head, rows, start):
    chunk = full.shape[1]
    first = start // rows
    lane = (lax.broadcasted_iota(jnp.int32, (head, chunk), 1) + start) // rows - first
    out = full[:head]
    for h in range(1, full.shape[0] // head):
        out = jnp.where(lane == h, full[h * head : (h + 1) * head], out)
    return out


def flush_queries(here_ref, queries, pack, mine_ref, other_ref):
    near = queries // 4

    def flush(at, carry):
        y = jnp.bitwise_xor(here_ref[1], at // near)
        j = at % near * 4 + 2 * y
        mine_ref[at, 0] = pack(j + here_ref[0])
        other_ref[at, 0] = pack(j + 1 - here_ref[0])
        return carry

    lax.fori_loop(0, queries // 2, flush, 0)


def either(index, a_ref, b_ref):
    count = a_ref.shape[0]
    return jnp.where(index < count, a_ref[index % count], b_ref[index % count])


def attend_kernel(plen, head, rows, asker_ref, owner_ref, here_ref, qa_ref, qb_ref, kv_ref, mine_ref, other_ref, acc, top, total):
    step = pl.program_id(1)
    queries = 2 * qa_ref.shape[0]
    width = GROUP * head

    @pl.when(step == 0)
    def _():
        acc[...] = jnp.zeros_like(acc)
        top[...] = jnp.full_like(top, FLOOR)
        total[...] = jnp.zeros_like(total)

    lanes = GROUP * rows
    chunk = min(CHUNK, lanes)

    def begin(unit):
        p, c = divmod(unit, lanes // chunk)
        if c == 0:
            spreads[p] = spread_heads(either(asker_ref[step * BLOCK + p], qa_ref, qb_ref), head)
            turned[p] = kv_ref[p * plen : (p + 1) * plen, width:].T
        keys = kv_ref[p * plen : (p + 1) * plen, :width]
        return dot(keys, spreads[p][c * chunk : (c + 1) * chunk], ((1,), (1,)))

    def finish(unit, scores):
        p, c = divmod(unit, lanes // chunk)
        owner = owner_ref[step * BLOCK + p]
        at = pl.ds(c * chunk, chunk)
        first, last = c * chunk // rows, ((c + 1) * chunk - 1) // rows
        here = jnp.max(scores, axis=0, keepdims=True)
        raised = jnp.exp(scores - here)
        here_total = jnp.sum(raised, axis=0, keepdims=True)
        full = dot(turned[p][first * head : (last + 1) * head], raised.astype(BF16), ((1,), (0,)))
        mixed = pick_chunk(full, head, rows, c * chunk)
        old = top[owner, :, at]
        new = jnp.maximum(old, here)
        old_scale, here_scale = jnp.exp(old - new), jnp.exp(here - new)
        top[owner, :, at] = new
        total[owner, :, at] = total[owner, :, at] * old_scale + here_total * here_scale
        acc[owner, :, at] = acc[owner, :, at] * old_scale + mixed * here_scale

    spreads, turned = {}, {}
    units = BLOCK * (lanes // chunk)
    waiting = [begin(u) for u in range(min(AHEAD, units))]
    for unit in range(units):
        if unit + AHEAD < units:
            waiting.append(begin(unit + AHEAD))
        finish(unit, waiting.pop(0))

    @pl.when(step == pl.num_programs(1) - 1)
    def _():
        def pack(j):
            parts = split_parts(top[j], 3) + split_parts(total[j], 2)
            parts.append(jnp.zeros((STAT_ROWS - len(parts), parts[0].shape[1]), F32))
            return jnp.concatenate([acc[j]] + parts, axis=0).astype(BF16)

        flush_queries(here_ref, queries, pack, mine_ref, other_ref)


def attend(asker, owner, here, plane, across, kv, plen, head):
    near, rows, columns = plane.shape
    queries = 2 * near
    width = GROUP * head
    slots = kv.shape[0] // plen
    lanes = GROUP * rows
    groups = columns // width
    block = (near, 1, head + STAT_ROWS, lanes)
    out = jax.ShapeDtypeStruct((near, groups, head + STAT_ROWS, lanes), BF16)
    q_spec = pl.BlockSpec((near, rows, width), lambda g, b, *_: (0, 0, g))
    return pl.pallas_call(
        partial(attend_kernel, plen, head, rows),
        out_shape=(out, out),
        grid_spec=pltpu.PrefetchScalarGridSpec(
            num_scalar_prefetch=3,
            grid=(groups, slots // BLOCK),
            in_specs=[
                q_spec,
                q_spec,
                pl.BlockSpec((BLOCK * plen, 2 * width), lambda g, b, *_: (b, g)),
            ],
            out_specs=(pl.BlockSpec(block, lambda g, b, *_: (0, g, 0, 0)),) * 2,
            scratch_shapes=[
                pltpu.VMEM((queries, head, lanes), F32),
                pltpu.VMEM((queries, 1, lanes), F32),
                pltpu.VMEM((queries, 1, lanes), F32),
            ],
        ),
        compiler_params=pltpu.CompilerParams(vmem_limit_bytes=60 * 2**20),
        cost_estimate=pl.CostEstimate(
            flops=16 * rows * kv.shape[0] * columns,
            bytes_accessed=4 * kv.shape[0] * columns,
            transcendentals=rows * kv.shape[0] * GROUP * groups,
        ),
        name="attend",
    )(asker, owner, here, plane, across, kv)


def read_stats(stat):
    return stat[0:1] + stat[1:2] + stat[2:3], stat[3:4] + stat[4:5]


def merge_kernel(head, a_ref, b_ref, out_ref):
    for i in range(a_ref.shape[0]):
        for g in range(a_ref.shape[1]):
            top_a, sum_a = read_stats(a_ref[i, g, head:, :].astype(F32))
            top_b, sum_b = read_stats(b_ref[i, g, head:, :].astype(F32))
            top = jnp.maximum(top_a, top_b)
            w_a, w_b = jnp.exp(top_a - top), jnp.exp(top_b - top)
            body = a_ref[i, g, :head, :].astype(F32) * w_a + b_ref[i, g, :head, :].astype(F32) * w_b
            rows = split_parts(top, 3) + split_parts(sum_a * w_a + sum_b * w_b, 2)
            rows.append(jnp.zeros((STAT_ROWS - 5, top.shape[1]), F32))
            out_ref[i, g] = jnp.concatenate([body] + rows, axis=0).astype(BF16)


def core_kernel(head, a_ref, b_ref, near_ref, far_ref):
    @pl.when(pl.program_id(0) < 2)
    def _():
        merge_kernel(head, a_ref, b_ref, far_ref)

    @pl.when(pl.program_id(0) >= 2)
    def _():
        merge_kernel(head, a_ref, b_ref, near_ref)


def core_merge(kept, came, head):
    block = (kept.shape[0] // 4,) + kept.shape[1:]
    out = jax.ShapeDtypeStruct((kept.shape[0] // 2,) + kept.shape[1:], BF16)
    return pl.pallas_call(
        partial(core_kernel, head),
        out_shape=(out, out),
        grid=(4,),
        in_specs=[pl.BlockSpec(block, lambda i: ((i + 2) % 4, 0, 0, 0))] * 2,
        out_specs=(
            pl.BlockSpec(block, lambda i: (jnp.maximum(i - 2, 0), 0, 0, 0)),
            pl.BlockSpec(block, lambda i: (jnp.minimum(i, 1), 0, 0, 0)),
        ),
        cost_estimate=pl.CostEstimate(flops=4 * kept.size, bytes_accessed=6 * kept.size, transcendentals=0),
        name="core_merge",
    )(kept, came)


def near_merge(kept, came, head):
    spec = pl.BlockSpec((kept.shape[0] // 2,) + kept.shape[1:], lambda i: (i, 0, 0, 0))
    return pl.pallas_call(
        partial(merge_kernel, head),
        out_shape=jax.ShapeDtypeStruct(kept.shape, BF16),
        grid=(2,),
        in_specs=[spec, spec],
        out_specs=spec,
        cost_estimate=pl.CostEstimate(flops=4 * kept.size, bytes_accessed=6 * kept.size, transcendentals=0),
        name="near_merge",
    )(kept, came)


def join_parts(ref, g, head):
    count = ref.shape[0]
    found = [read_stats(ref[i, g, head:, :].astype(F32)) for i in range(count)]
    top = found[0][0]
    for i in range(1, count):
        top = jnp.maximum(top, found[i][0])
    weights = [jnp.exp(found[i][0] - top) for i in range(count)]
    whole = found[0][1] * weights[0]
    mixed = ref[0, g, :head, :].astype(F32) * weights[0]
    for i in range(1, count):
        whole = whole + found[i][1] * weights[i]
        mixed = mixed + ref[i, g, :head, :].astype(F32) * weights[i]
    return mixed / whole, top + jnp.log(whole)


def ffn_kernel(head, arrived_ref, stream_ref, cot_ref, gain_ref, weight_ref, payload_ref, out_ref, dstream_ref, dgain_ref, mixed_ref, low_ref, normed_ref, dinner_ref, active_ref, full_ref):
    rows, width = stream_ref.shape
    groups = arrived_ref.shape[1]
    wide = GROUP * head
    logs = []
    for g in range(groups):
        part, log = join_parts(arrived_ref, g, head)
        logs.append(log)
        turned = part.T
        heads = [turned[h * rows : (h + 1) * rows] for h in range(GROUP)]
        full_ref[:, g * wide : (g + 1) * wide] = jnp.concatenate(heads, axis=1)
    mixed = full_ref[...].astype(BF16)
    mixed_ref[...] = mixed
    stream = stream_ref[...] + dot(mixed, weight_ref[:, :width], ((1,), (0,)))
    normed = (stream * scale_rows(stream) * gain_ref[2:3, :]).astype(BF16)
    normed_ref[...] = normed
    grads = cot_ref[...]
    out = stream
    d_normed = jnp.zeros((rows, width), F32)
    folds = dinner_ref.shape[1] // width
    for k in range(folds):
        up = weight_ref[:, (k + 1) * width : (k + 2) * width]
        down = weight_ref[:, (k + 1 + folds) * width : (k + 2 + folds) * width]
        at = slice(k * width, (k + 1) * width)
        inner = dot(normed, up, ((1,), (0,)))
        square = inner * inner
        bent = jnp.tanh(0.7978845608028654 * (inner + 0.044715 * square * inner))
        half = 0.5 * (1.0 + bent)
        active = (inner * half).astype(BF16)
        slope = half + 0.5 * inner * (1.0 - bent * bent) * (
            0.7978845608028654 * (1.0 + 0.134145 * square)
        )
        active_ref[:, at] = active
        out = out + dot(active, down, ((1,), (0,)))
        d_inner = (dot(grads, down, ((1,), (1,))) * slope).astype(BF16)
        dinner_ref[:, at] = d_inner
        d_normed = d_normed + dot(d_inner, up, ((1,), (1,)))
    out_ref[...] = out.astype(BF16)
    d_stream, gain = norm_gradient(stream, gain_ref[2:3, :], d_normed)
    d_stream = d_stream + grads.astype(F32)
    dstream_ref[...] = d_stream
    dgain_ref[...] = jnp.concatenate([gain, jnp.zeros((7, width), F32)], axis=0)
    low = d_stream.astype(BF16)
    low_ref[...] = low
    d_mixed = dot(low, weight_ref[:, :width], ((1,), (1,))).astype(BF16)
    payload_ref[:rows, :] = d_mixed
    for g in range(groups):
        columns = slice(g * wide, (g + 1) * wide)
        product = (d_mixed[:, columns].astype(F32) * full_ref[:, columns]).T
        delta = [
            jnp.sum(product[h * head : (h + 1) * head], axis=0, keepdims=True) for h in range(GROUP)
        ]
        parts = split_parts(logs[g], 3) + split_parts(jnp.concatenate(delta, axis=1), 2)
        lines = [
            part[:, t * wide : (t + 1) * wide]
            for part in parts
            for t in range(GROUP * rows // wide)
        ]
        lines.append(jnp.zeros((STAT_ROWS - len(lines), wide), F32))
        payload_ref[rows:, columns] = jnp.concatenate(lines, axis=0).astype(BF16)


def feed_forward(arrived, stream, grads, gain_rows, weight, head):
    rows, width = stream.shape
    hidden = (weight.shape[1] - width) // 2

    def whole(shape):
        return pl.BlockSpec(shape, lambda i: (0,) * len(shape))

    low = jax.ShapeDtypeStruct((rows, width), BF16)
    long = jax.ShapeDtypeStruct((rows, hidden), BF16)
    shapes = (
        jax.ShapeDtypeStruct((rows + STAT_ROWS, width), BF16),
        low,
        jax.ShapeDtypeStruct((rows, width), F32),
        jax.ShapeDtypeStruct((8, width), F32),
        low,
        low,
        low,
        long,
        long,
    )
    return pl.pallas_call(
        partial(ffn_kernel, head),
        out_shape=shapes,
        grid=(1,),
        in_specs=[whole(v.shape) for v in (arrived, stream, grads, gain_rows, weight)],
        out_specs=tuple(whole(shape.shape) for shape in shapes),
        scratch_shapes=[pltpu.VMEM((rows, width), F32)],
        compiler_params=pltpu.CompilerParams(vmem_limit_bytes=56 * 2**20),
        cost_estimate=pl.CostEstimate(
            flops=4 * rows * weight.size, bytes_accessed=2 * weight.size, transcendentals=rows * hidden
        ),
        name="feed_forward",
    )(arrived, stream, grads, gain_rows, weight)


def ffn_terms_kernel(folds, *refs):
    out_ref = refs[-1]
    tile = pl.program_id(0)
    for first, last, left, right in ((0, 1, 0, 1), (1, 1 + folds, 2, 3), (1 + folds, 1 + 2 * folds, 4, 5)):

        @pl.when((tile >= first) & (tile < last))
        def _(left=left, right=right):
            a, b = refs[2 * left : 2 * left + 2], refs[2 * right : 2 * right + 2]
            found = dot(a[0][...], b[0][...], ((0,), (0,))) + dot(a[1][...], b[1][...], ((0,), (0,)))
            out_ref[...] = found.astype(BF16)


def ffn_terms(parts, grads, hidden):
    width = grads[0].shape[1]
    folds = hidden // width

    def spec(value, start):
        if start is None:
            return pl.BlockSpec((value.shape[0], width), lambda t: (0, 0))
        return pl.BlockSpec((value.shape[0], width), lambda t: (0, jnp.clip(t - start, 0, folds - 1)))

    operands, specs = [], []
    for values, start in zip([*zip(*parts), grads], (None, None, None, 1, 1 + folds, None)):
        for value in values:
            operands.append(value)
            specs.append(spec(value, start))
    return pl.pallas_call(
        partial(ffn_terms_kernel, folds),
        out_shape=jax.ShapeDtypeStruct((width, width + 2 * hidden), BF16),
        grid=(1 + 2 * folds,),
        in_specs=specs,
        out_specs=pl.BlockSpec((width, width), lambda t: (0, t)),
        compiler_params=pltpu.CompilerParams(vmem_limit_bytes=60 * 2**20),
        cost_estimate=pl.CostEstimate(
            flops=6 * width * width * width, bytes_accessed=8 * width * hidden, transcendentals=0
        ),
        name="ffn_terms",
    )(*operands)


def attend_back_kernel(plen, head, rows, asker_ref, owner_ref, here_ref, qa_ref, qb_ref, doa_ref, dob_ref, sa_ref, sb_ref, kv_ref, *refs):
    step = pl.program_id(1)
    dkv_ref, mine_ref, other_ref, acc, log, delta = refs[-6:]
    held_ref = refs[0] if len(refs) > 6 else None
    near = qa_ref.shape[0]
    queries = 2 * near
    width = GROUP * head

    @pl.when(step == 0)
    def _():
        acc[...] = jnp.zeros_like(acc)
        third = (GROUP * rows) // width

        def fill(j, carry):
            stat = either(j, sa_ref, sb_ref).astype(F32)
            row = lax.broadcasted_iota(jnp.int32, stat.shape, 0)
            for at, ref, count in ((0, log, 3), (3 * third, delta, 2)):
                pieces = []
                for t in range(third):
                    wanted = row == at + t
                    for k in range(1, count):
                        wanted = wanted | (row == at + k * third + t)
                    pieces.append(jnp.sum(jnp.where(wanted, stat, 0.0), axis=0, keepdims=True))
                ref[j] = jnp.concatenate(pieces, axis=1)
            return carry

        lax.fori_loop(0, queries, fill, 0)

    lanes = GROUP * rows
    chunk = min(CHUNK, lanes)

    def begin(unit):
        p, c = divmod(unit, lanes // chunk)
        rows_at = slice(p * plen, (p + 1) * plen)
        if c == 0:
            asker = asker_ref[step * BLOCK + p]
            q_spread[p] = spread_heads(either(asker, qa_ref, qb_ref), head)
            do_spread[p] = spread_heads(either(asker, doa_ref, dob_ref), head)
            turned[p] = kv_ref[rows_at, :width].T
        at = slice(c * chunk, (c + 1) * chunk)
        return (
            dot(kv_ref[rows_at, :width], q_spread[p][at], ((1,), (1,))),
            dot(kv_ref[rows_at, width:], do_spread[p][at], ((1,), (1,))),
        )

    def finish(unit, found):
        scores, d_soft = found
        p, c = divmod(unit, lanes // chunk)
        owner, asker = owner_ref[step * BLOCK + p], asker_ref[step * BLOCK + p]
        at = pl.ds(c * chunk, chunk)
        cut = slice(c * chunk, (c + 1) * chunk)
        first, last = c * chunk // rows, ((c + 1) * chunk - 1) // rows
        soft = jnp.exp(scores - log[asker, :, at])
        d_score = (soft * (d_soft - delta[asker, :, at])).astype(BF16)
        d_value = dot(soft.astype(BF16), do_spread[p][cut], ((1,), (0,)))
        d_key = dot(d_score, q_spread[p][cut], ((1,), (0,)))
        sums[p] = (d_key, d_value) if c == 0 else (sums[p][0] + d_key, sums[p][1] + d_value)
        full = dot(turned[p][first * head : (last + 1) * head], d_score, ((1,), (0,)))
        acc[owner, :, at] += pick_chunk(full, head, rows, c * chunk)
        if c == lanes // chunk - 1:
            rows_at = slice(p * plen, (p + 1) * plen)
            for found, columns in zip(sums[p], (slice(0, width), slice(width, 2 * width))):
                if held_ref is not None:
                    found = found + held_ref[rows_at, columns].astype(F32)
                dkv_ref[rows_at, columns] = found.astype(BF16)

    q_spread, do_spread, turned, sums = {}, {}, {}, {}
    units = BLOCK * (lanes // chunk)
    waiting = [begin(u) for u in range(min(AHEAD, units))]
    for unit in range(units):
        if unit + AHEAD < units:
            waiting.append(begin(unit + AHEAD))
        finish(unit, waiting.pop(0))

    @pl.when(step == pl.num_programs(1) - 1)
    def _():
        flush_queries(here_ref, queries, lambda j: acc[j].astype(BF16), mine_ref, other_ref)


def attend_back(asker, owner, here, queries_in, grads_in, kv, held, plen, head):
    near, rows, columns = queries_in[0].shape
    queries = 2 * near
    width = GROUP * head
    slots = kv.shape[0] // plen
    lanes = GROUP * rows
    groups = columns // width
    block = (near, 1, head, lanes)
    out = jax.ShapeDtypeStruct((near, groups, head, lanes), BF16)
    q_spec = pl.BlockSpec((near, rows, width), lambda g, b, *_: (0, 0, g))
    stat_spec = pl.BlockSpec((near, STAT_ROWS, width), lambda g, b, *_: (0, rows // STAT_ROWS, g))
    kv_spec = pl.BlockSpec((BLOCK * plen, 2 * width), lambda g, b, *_: (b, g))
    operands = [*queries_in, *grads_in, *grads_in, kv]
    specs = [q_spec] * 4 + [stat_spec] * 2 + [kv_spec]
    if held is not None:
        operands.append(held)
        specs.append(kv_spec)
    return pl.pallas_call(
        partial(attend_back_kernel, plen, head, rows),
        out_shape=(jax.ShapeDtypeStruct(kv.shape, BF16), out, out),
        grid_spec=pltpu.PrefetchScalarGridSpec(
            num_scalar_prefetch=3,
            grid=(groups, slots // BLOCK),
            in_specs=specs,
            out_specs=(
                kv_spec,
                pl.BlockSpec(block, lambda g, b, *_: (0, g, 0, 0)),
                pl.BlockSpec(block, lambda g, b, *_: (0, g, 0, 0)),
            ),
            scratch_shapes=[
                pltpu.VMEM((queries, head, lanes), F32),
                pltpu.VMEM((queries, 1, lanes), F32),
                pltpu.VMEM((queries, 1, lanes), F32),
            ],
        ),
        input_output_aliases={} if held is None else {3 + len(operands) - 1: 0},
        compiler_params=pltpu.CompilerParams(vmem_limit_bytes=60 * 2**20),
        cost_estimate=pl.CostEstimate(
            flops=40 * rows * kv.shape[0] * columns,
            bytes_accessed=8 * kv.shape[0] * columns,
            transcendentals=rows * kv.shape[0] * GROUP * groups,
        ),
        name="attend_back",
    )(asker, owner, here, *operands)


def source_kernel(keep_ref, fetch_ref, dkv_ref, weight_ref, out_ref):
    kept = keep_ref[pl.program_id(0)]

    @pl.when(kept == 0)
    def _():
        out_ref[...] = jnp.zeros_like(out_ref)

    @pl.when(kept != 0)
    def _():
        out_ref[0] = dot(dkv_ref[...], weight_ref[...], ((1,), (1,))).astype(BF16)


def source_grads(refresh, dkv, weight, plen):
    slots = refresh.shape[0]
    model_width = weight.shape[0]
    fetch = lax.cummax(jnp.where(refresh != 0, jnp.arange(slots), 0), axis=0).astype(jnp.int32)
    return pl.pallas_call(
        source_kernel,
        out_shape=jax.ShapeDtypeStruct((slots, plen, model_width), BF16),
        grid_spec=pltpu.PrefetchScalarGridSpec(
            num_scalar_prefetch=2,
            grid=(slots,),
            in_specs=[
                pl.BlockSpec((plen, dkv.shape[1]), lambda r, keep, fetch: (fetch[r], 0)),
                pl.BlockSpec(weight.shape, lambda r, *_: (0, 0)),
            ],
            out_specs=pl.BlockSpec((1, plen, model_width), lambda r, *_: (r, 0, 0)),
        ),
        compiler_params=pltpu.CompilerParams(vmem_limit_bytes=60 * 2**20),
        cost_estimate=pl.CostEstimate(
            flops=slots * plen * model_width * 2 * model_width,
            bytes_accessed=4 * slots * plen * model_width,
            transcendentals=0,
        ),
        name="source_grads",
    )(refresh, fetch, dkv, weight)


def outer_kernel(starts, added, half_ref, *refs):
    out_ref = refs[-1]
    tile = pl.program_id(1)
    for k in range(len(starts) - 1):

        @pl.when((tile >= starts[k]) & (tile < starts[k + 1]))
        def _(k=k):
            found = dot(refs[2 * k][...], refs[2 * k + 1][...], ((0,), (0,)))
            if added:
                found = found + refs[-2][...].astype(F32)
            out_ref[...] = found.astype(BF16)


def outer(half, pairs, came=None):
    rows = pairs[0][0].shape[0]
    height = min(left.shape[1] for left, _ in pairs)
    height = height if height <= 1024 else height // 4
    total_rows = pairs[0][0].shape[1]
    width = total_rows // 2 if total_rows == height else height // 2
    counts = [right.shape[1] // 2 // width for _, right in pairs]
    starts = [sum(counts[:k]) for k in range(len(counts) + 1)]
    operands, specs = [], []
    for k, (left, right) in enumerate(pairs):

        def right_map(r, t, half_ref, start=starts[k], count=counts[k]):
            return (0, half_ref[0] * count + jnp.clip(t - start, 0, count - 1))

        operands += [left, right]
        specs += [
            pl.BlockSpec((rows, height), lambda r, t, half_ref: (0, r)),
            pl.BlockSpec((rows, width), right_map),
        ]
    out_spec = pl.BlockSpec((height, width), lambda r, t, half_ref: (r, t))
    if came is not None:
        operands.append(came)
        specs.append(out_spec)
    size = total_rows * starts[-1] * width
    return pl.pallas_call(
        partial(outer_kernel, starts, came is not None),
        out_shape=jax.ShapeDtypeStruct((total_rows, starts[-1] * width), BF16),
        grid_spec=pltpu.PrefetchScalarGridSpec(
            num_scalar_prefetch=1,
            grid=(total_rows // height, starts[-1]),
            in_specs=specs,
            out_specs=out_spec,
        ),
        compiler_params=pltpu.CompilerParams(vmem_limit_bytes=60 * 2**20),
        cost_estimate=pl.CostEstimate(flops=2 * rows * size, bytes_accessed=4 * size, transcendentals=0),
        name="outer",
    )(half, *operands)


def flip(value, bit):
    count = lax.axis_size("pass")
    return lax.ppermute(value, "pass", [(i, i ^ bit) for i in range(count)])


def after(value, *others):
    return lax.optimization_barrier((value,) + others)


def line_sends(block):
    count = lax.axis_size("pass")
    rings = [[(i, (i + 4 * k) % count) for i in range(count)] for k in range(1, count // 4)]
    return [lax.ppermute(block, "pass", ring) for ring in rings]


def gather_place(query, own, count):
    major = count // 4
    turn = jnp.mod(own // 4 - query // 4, major)
    return turn + major * ((own // 2) % 2 != (query // 2) % 2) + 2 * major * (own % 2 != query % 2)


def line_exchange(parts):
    count = lax.axis_size("pass")
    groups = [[r + 4 * k for k in range(count // 4)] for r in range(4)]
    return lax.all_to_all(
        parts, "pass", split_axis=0, concat_axis=0, tiled=True, axis_index_groups=groups
    )


def in_order(own, came, place, axis):
    return jnp.stack([jnp.where(place == 0, own, came), jnp.where(place == 0, came, own)], axis=axis)


def gather_rows(block):
    n_dp, count = lax.axis_size("dp"), lax.axis_size("pass")
    if n_dp != 2:
        return lax.all_gather(block, ("dp", "pass"), axis=0, tiled=True)
    own, dp = lax.axis_index("pass"), lax.axis_index("dp")
    major, core, y = count // 4, own % 2, own // 2 % 2
    pieces = [block, *line_sends(block)]
    line = jnp.zeros((major,) + block.shape, block.dtype)
    for k, piece in enumerate(pieces):
        line = lax.dynamic_update_index_in_dim(line, piece, jnp.mod(own // 4 - k, major), 0)
    cut = block.shape[1] // 256 * 128
    left, right = line[..., :cut], line[..., cut:]
    left, right = in_order(left, flip(left, 2), y, 1), in_order(right, dp_flip(right), dp, 0)
    left, right = in_order(left, dp_flip(left), dp, 0), in_order(right, flip(right, 2), y, 2)
    full = [in_order(part, flip(part, 1), core, 3) for part in (left, right)]
    return jnp.concatenate([part.reshape(-1, part.shape[-1]) for part in full], axis=1)


def line_scatter(parts):
    count = lax.axis_size("pass")
    major, place = count // 4, lax.axis_index("pass") // 4
    came = []
    for k in range(1, major):
        sent = lax.dynamic_index_in_dim(parts, jnp.mod(place + k, major), 0, keepdims=False)
        came.append(lax.ppermute(sent, "pass", [(i, (i + 4 * k) % count) for i in range(count)]))
    return lax.dynamic_index_in_dim(parts, place, 0, keepdims=False), came


def swap_send(value, place, axis, send):
    kept = lax.dynamic_index_in_dim(value, place, axis, keepdims=False)
    return kept, send(lax.dynamic_index_in_dim(value, 1 - place, axis, keepdims=False))


def add_low(kept, came):
    return (kept.astype(F32) + came.astype(F32)).astype(BF16)


def rows_by_owner(value):
    n_dp, count = lax.axis_size("dp"), lax.axis_size("pass")
    rows, columns = value.shape
    return value.reshape(n_dp, count // 4, 2, rows // (n_dp * count // 2), columns)


def dp_step(value, bit):
    pairs = [(i, i ^ bit) for i in range(lax.axis_size("dp"))]
    return lax.ppermute(value, "dp", pairs)


def dp_flip(value):
    return lax.ppermute(value, "dp", [(0, 1), (1, 0)])


def dp_send(value):
    if lax.axis_size("dp") == 2:
        return swap_send(value, lax.axis_index("dp"), 0, dp_flip)
    total = lax.psum_scatter(value, "dp", scatter_dimension=0, tiled=False)
    return total, jnp.zeros_like(total)


def near_send(value, axis):
    return swap_send(value, lax.axis_index("pass") // 2 % 2, axis, lambda v: flip(v, 2))


def over_line(value):
    return jnp.sum(line_exchange(value).astype(F32), axis=0)


def own_rows(value, core):
    shard = value.shape[0] // 2
    parts = value.reshape(2, shard, value.shape[1])
    kept = lax.dynamic_index_in_dim(parts, core, 0, keepdims=False)
    came = flip(lax.dynamic_index_in_dim(parts, 1 - core, 0, keepdims=False), 1)
    return jnp.where(core == 0, kept, came), jnp.where(core == 0, came, kept)


def on_device(
    tokens,
    cotangent,
    passages,
    refresh,
    passage_ids,
    self_query,
    self_key,
    self_value,
    self_out,
    cross_query,
    cross_key,
    cross_value,
    cross_out,
    up_weight,
    down_weight,
    gains,
    rel_table,
):
    both = ("dp", "pass")
    pass_count = lax.axis_size("pass")
    device_id = lax.axis_index(both)
    own_pass = lax.axis_index("pass")
    per_query, plen, model_width = passages.shape
    head_count = rel_table.shape[1]
    head = model_width // head_count
    rows = tokens.shape[0]
    groups = head_count // GROUP
    wide = GROUP * head
    shard = self_query.shape[0]

    def gather(value):
        return lax.all_gather(value, both, axis=0, tiled=True)

    kv_shard = jnp.stack(
        [cross_key.reshape(shard, groups, wide), cross_value.reshape(shard, groups, wide)], axis=2
    ).reshape(shard, 2 * model_width)
    gain_pad = jnp.pad(gains, ((0, 0), (0, 128 - gains.shape[1])))
    first = gather(
        jnp.concatenate([self_query, self_key, self_value, self_out, cross_query, gain_pad], axis=1)
    )
    kv_weight = lax.optimization_barrier(gather_rows(kv_shard))
    encoded = passages.reshape(per_query * plen, model_width)
    kv = matmul(encoded, kv_weight).astype(BF16)
    positions = jnp.arange(rows)
    causal = positions[:, None] >= positions[None, :]
    onehot_low = (
        bucket_of(positions[:, None] - positions[None, :], rel_table.shape[0])[:, :, None]
        == jnp.arange(rel_table.shape[0])[None, None, :]
    ).astype(BF16)
    bias = jnp.einsum("qkb,bh->hqk", onehot_low, rel_table, preferred_element_type=F32)
    bias = jnp.where(causal[None, :, :], bias, FLOOR)
    folds = up_weight.shape[1] // model_width
    total = up_weight.shape[1] // (folds * shard)
    up_fold = up_weight.reshape(shard, total, folds, shard).transpose(0, 2, 1, 3).reshape(shard, -1)
    down_fold = down_weight.reshape(folds, shard, model_width).transpose(1, 0, 2).reshape(shard, -1)
    rest = jnp.concatenate([cross_out, up_fold, down_fold], axis=1)
    first, kv, bias, rest = after(first, kv, bias, rest)
    gain_all = first[:, 5 * model_width : 5 * model_width + 3].astype(F32)

    row_ids = device_id * per_query + jnp.arange(per_query)
    owned = jnp.any(passage_ids[:, :, None] == row_ids[None, None, :], axis=1)
    owner = jnp.sum(
        jnp.where(owned, jnp.arange(passage_ids.shape[0])[:, None], 0), axis=0
    ).astype(jnp.int32)
    core = own_pass % 2
    half = core.astype(jnp.int32).reshape(1)
    here = jnp.stack([core, own_pass // 2 % 2]).astype(jnp.int32)
    asker = gather_place(owner, own_pass, pass_count).astype(jnp.int32)

    gain_rows = jnp.pad(gain_all.T, ((0, 5), (0, 0)))
    qkv, mixed_one, normed_self, stream_one, normed_cross, query_two = self_attend(
        tokens, gain_rows, bias, first, head
    )

    cut = rows // 192 * 128

    def merge_send(mine, came):
        near, far = core_merge(mine, came, head)
        return near, flip(far, 2)

    def rows_first(value):
        cube = value.reshape(groups, head, GROUP, -1).transpose(3, 0, 2, 1)
        return cube.reshape(-1, model_width)

    block, last_block = query_two[:cut], query_two[cut:]
    last_block, rest, *sends = after(last_block, rest, *line_sends(block))
    rest = gather(rest)
    line = jnp.stack([block, *sends])
    across, *sends = after(flip(line, 2), *line_sends(last_block))
    plane = jnp.concatenate([line, across])
    q_first = (plane, flip(plane, 1))
    line = jnp.stack([last_block, *sends])
    across = flip(line, 2)
    mine, other = attend(asker, owner, here, *q_first, kv, plen, head)
    across, mine, other = after(across, mine, other)
    came = flip(other, 1)
    plane = jnp.concatenate([line, across])
    q_second = (plane, flip(plane, 1))
    near, came = merge_send(mine, came)
    q_second, near = after(q_second, near)
    mine, other = attend(asker, owner, here, *q_second, kv, plen, head)
    came, mine, other = after(came, mine, other)
    merged, mine, other = after(near_merge(near, came, head), mine, other)
    came_next = flip(other, 1)
    arrived = line_exchange(merged)
    near, came = merge_send(mine, came_next)
    arrived, near, came = after(arrived, near, came)
    merged, arrived = after(near_merge(near, came, head), arrived)
    arrived_last = line_exchange(merged)
    payload_first, out_first, ds_first, gain_first, *terms_first = feed_forward(
        arrived, stream_one[:cut], cotangent[:cut], gain_rows, rest, head
    )
    arrived_last, payload_first = after(arrived_last, payload_first)
    sends = line_sends(payload_first)
    payload, out_last, ds_last, gain_last, *terms_last = feed_forward(
        arrived_last, stream_one[cut:], cotangent[cut:], gain_rows, rest, head
    )
    payload, *sends = after(payload, *sends)
    line_first = jnp.stack([payload_first, *sends])
    across = flip(line_first, 2)
    sends = line_sends(payload)

    block_out = jnp.concatenate([out_first, out_last])
    d_stream_two = jnp.concatenate([ds_first, ds_last])
    d_gain_ffn = gain_first[0] + gain_last[0]
    terms = ffn_terms(
        (terms_first, terms_last), (cotangent[:cut], cotangent[cut:]), up_weight.shape[1]
    )
    across, terms, *sends = after(across, terms, *sends)
    ffn_sums = lax.psum_scatter(terms, both, scatter_dimension=0, tiled=True)
    plane = jnp.concatenate([line_first, across])
    do_first = (plane, flip(plane, 1))
    line = jnp.stack([payload, *sends])
    across = flip(line, 2)

    def half_of(value, came):
        value = (value.astype(F32) + came.astype(F32)).astype(BF16)
        return value[: value.shape[0] // 2], value[value.shape[0] // 2 :]

    dkv, mine, other = attend_back(asker, owner, here, q_first, do_first, kv, None, plen, head)
    across, dkv, mine, other = after(across, dkv, mine, other)
    came = flip(other, 1)
    plane = jnp.concatenate([line, across])
    do_last = (plane, flip(plane, 1))
    near, far = half_of(mine, came)
    came = flip(far, 2)
    do_last, near = after(do_last, near)
    dkv, mine, other = attend_back(asker, owner, here, q_second, do_last, kv, dkv, plen, head)
    came, dkv, mine, other = after(came, dkv, mine, other)
    came_next = flip(other, 1)
    arrived = line_exchange((near.astype(F32) + came.astype(F32)).astype(BF16))
    near, far = half_of(mine, came_next)
    came, dkv = after(flip(far, 2), dkv)
    kept, last = line_scatter((near.astype(F32) + came.astype(F32)).astype(BF16))
    arrived, d_kv, *last = after(arrived, left_t(encoded, dkv).astype(BF16), *last)
    last = sum((part.astype(F32) for part in last), kept.astype(F32))
    dq_parts = [rows_first(jnp.sum(arrived.astype(F32), axis=0)), rows_first(last)]
    d_query_two = jnp.concatenate(dq_parts).astype(BF16)
    def kv_half(at):
        cube = d_kv.reshape(model_width, groups, 2, wide)
        return lax.dynamic_index_in_dim(cube, at, 2, keepdims=False).reshape(model_width, -1)

    kv_came = flip(kv_half(1 - core), 1)
    found = self_back(
        tokens, gain_rows, bias, first, qkv, stream_one, d_query_two, d_stream_two, head
    )
    kv_came, ffn_sums, *found = after(kv_came, ffn_sums, *found)
    d_qkv, grad_one, d_inputs, d_score, gain_terms = found
    late_pairs = [(normed_self, d_qkv)]
    more_pairs = [(mixed_one, grad_one), (normed_cross, d_query_two)]
    late_sent, more_sent = outer(1 - half, late_pairs), outer(1 - half, more_pairs)
    distance = jnp.mod(jnp.arange(d_score.shape[1]) - (rows - 1), d_score.shape[1])
    of_distance = bucket_of(distance, rel_table.shape[0])
    of_distance = (of_distance[:, None] == jnp.arange(rel_table.shape[0])[None, :]).astype(F32)
    d_table = jnp.dot(d_score, of_distance, precision=lax.Precision.HIGHEST)[:head_count].T
    small = jnp.concatenate([d_table.reshape(-1), gain_terms[0], gain_terms[1], d_gain_ffn])
    small = small.reshape(-1, 128)
    late_sent, more_sent, kv_came = after(late_sent, more_sent, kv_came)
    kv_part = jnp.moveaxis(rows_by_owner(add_low(kv_half(core), kv_came)), 1, 0)
    late_came, more_came, kv_part, came = after(
        flip(late_sent, 1), flip(more_sent, 1), kv_part, flip(small, 1)
    )
    small = small + came

    late, more = outer(half, late_pairs, late_came), outer(half, more_pairs, more_came)
    late, more, came = after(late, more, flip(small, 2))
    small = small + came
    late_kept, late_came = dp_send(rows_by_owner(late))
    more_kept, more_came = near_send(rows_by_owner(more), 2)
    kv_line = line_exchange(kv_part)
    passage_grad = source_grads(refresh, dkv, kv_weight, plen)
    for bit in range((lax.axis_size("dp") - 1).bit_length()):
        small = small + dp_step(small, 1 << bit)
    kv_line, late_came, more_came, passage_grad, small = after(
        kv_line, late_came, more_came, passage_grad, small
    )
    late_kept, late_came = near_send(add_low(late_kept, late_came), 1)
    more_kept, more_came = dp_send(add_low(more_kept, more_came))
    kv_kept, kv_came = dp_send(jnp.sum(kv_line.astype(F32), axis=0).astype(BF16))
    for bit in range(2, (pass_count - 1).bit_length() - 1):
        small = small + flip(small, 1 << bit)
    late_came, more_came, kv_came, small = after(late_came, more_came, kv_came, small)
    came = flip(small, pass_count // 2)
    kv_kept, kv_came = near_send(add_low(kv_kept, kv_came), 0)
    parts = [(late_kept, late_came), (more_kept, more_came)]
    line = line_exchange(jnp.concatenate([add_low(*part) for part in parts], axis=-1))
    ffn_sums = ffn_sums.astype(F32)
    d_up = ffn_sums[:, model_width : model_width + up_weight.shape[1]]
    d_up = d_up.reshape(shard, folds, total, shard).transpose(0, 2, 1, 3).reshape(up_weight.shape)
    d_down = ffn_sums[:, model_width + up_weight.shape[1] :].reshape(shard, folds, model_width)
    d_down = d_down.transpose(1, 0, 2).reshape(down_weight.shape)
    line, kv_came, came, d_up, d_down = after(line, kv_came, came, d_up, d_down)
    small = (small + came).reshape(-1)
    line = jnp.sum(line.astype(F32), axis=0)
    line = jnp.concatenate([line, kv_kept.astype(F32) + kv_came.astype(F32)], axis=1)
    table_grad = small[: d_table.size].reshape(d_table.shape)
    d_gains = small[d_table.size :].reshape(3, -1)
    d_gains = lax.dynamic_slice_in_dim(d_gains, device_id * shard, shard, 1)

    left, right = own_rows(line, core)
    half_width = model_width // 2

    def whole(start, stop):
        cut = slice(start * half_width, stop * half_width)
        return jnp.concatenate([left[:, cut], right[:, cut]], axis=1)

    d_first, d_out_self, d_query_cross = whole(0, 3), whole(3, 4), whole(4, 5)
    d_query_self, d_key_self, d_value_self = jnp.split(d_first, 3, axis=1)
    d_key_cross, d_value_cross = left[:, 5 * half_width :], right[:, 5 * half_width :]
    d_out_cross = ffn_sums[:, :model_width]
    return (
        block_out,
        d_inputs,
        passage_grad,
        d_query_self,
        d_key_self,
        d_value_self,
        d_out_self,
        d_query_cross,
        d_key_cross,
        d_value_cross,
        d_out_cross,
        d_up,
        d_down,
        d_gains.T,
        table_grad,
    )


def solution(mesh):
    split = P(("dp", "pass"), None)
    cube = P(("dp", "pass"), None, None)
    in_specs = (split, split, cube, P(("dp", "pass")), P("dp", None)) + (split,) * 11 + (P(),)
    out_specs = (split, split, cube) + (split,) * 11 + (P(),)
    return jax.shard_map(
        on_device, mesh=mesh, in_specs=in_specs, out_specs=out_specs, check_vma=False
    )
```

```python
from functools import partial

import jax
import jax.numpy as jnp
from jax import lax
from jax.experimental import pallas as pl
from jax.experimental.pallas import tpu as pltpu
from jax.sharding import PartitionSpec as P

F32 = jnp.float32
BF16 = jnp.bfloat16
GROUP = 4
BLOCK = 10
STAT_ROWS = 16
CHUNK = 256
AHEAD = 2
FLOOR = -1e30


def norm_rows(value, gain):
    return value * lax.rsqrt(jnp.mean(value * value, axis=-1, keepdims=True) + 1e-06) * gain


def bucket_of(spread, buckets):
    near_count = buckets // 2
    spread = jnp.maximum(spread, 0).astype(F32)
    bounds = near_count * 8.0 ** (jnp.arange(1, near_count, dtype=F32) / near_count)
    far_bucket = near_count + jnp.sum((spread[..., None] >= bounds).astype(jnp.int32), axis=-1)
    return jnp.where(spread < near_count, spread.astype(jnp.int32), far_bucket)


def matmul(left, right):
    return jnp.dot(left, right, preferred_element_type=F32)


def left_t(left, right):
    return jnp.einsum("td,te->de", left, right, preferred_element_type=F32)


def right_t(left, right):
    return jnp.einsum("te,de->td", left, right, preferred_element_type=F32)


def dot(left, right, dims):
    return lax.dot_general(left, right, (dims, ((), ())), preferred_element_type=F32)


def split_parts(value, count):
    parts = []
    for _ in range(count):
        part = value.astype(BF16).astype(F32)
        parts.append(part)
        value = value - part
    return parts


def spread_heads(rows, head):
    column = lax.broadcasted_iota(jnp.int32, rows.shape, 1) // head
    return jnp.concatenate(
        [jnp.where(column == h, rows, jnp.zeros_like(rows)) for h in range(GROUP)], axis=0
    )


def scale_rows(value):
    return lax.rsqrt(jnp.mean(value * value, axis=-1, keepdims=True) + 1e-06)


def norm_gradient(value, gain, grad):
    scale = scale_rows(value)
    unit = value * scale
    inner = grad * gain
    mean = jnp.mean(inner * unit, axis=-1, keepdims=True)
    return scale * (inner - unit * mean), jnp.sum(grad * unit, axis=0, keepdims=True)


def pair_spread(rows, head):
    first = lax.broadcasted_iota(jnp.int32, rows.shape, 1) < head
    zero = jnp.zeros_like(rows)
    return jnp.concatenate([jnp.where(first, rows, zero), jnp.where(first, zero, rows)], axis=0)


def pair_pick(full, head):
    rows = full.shape[0] // 2
    first = lax.broadcasted_iota(jnp.int32, (rows, full.shape[1]), 1) < head
    return jnp.where(first, full[:rows], full[rows:])


def pair_weights(qkv_ref, bias_ref, pair, head, width):
    at = slice(pair * 2 * head, (pair + 1) * 2 * head)
    query = pair_spread(qkv_ref[:, at], head)
    key = qkv_ref[:, width + at.start : width + at.stop]
    value = qkv_ref[:, 2 * width + at.start : 2 * width + at.stop]
    rows = key.shape[0]
    bias = bias_ref[2 * pair : 2 * pair + 2].reshape(2 * rows, rows)
    scores = dot(query, key, ((1,), (1,))) + bias
    raised = jnp.exp(scores - jnp.max(scores, axis=-1, keepdims=True))
    return query, key, value, raised / jnp.sum(raised, axis=-1, keepdims=True)


def self_kernel(head, tokens_ref, gain_ref, bias_ref, weight_ref, qkv_ref, mixed_ref, normed_ref, stream_ref, cross_ref, query_ref):
    width = tokens_ref.shape[1]
    inputs = tokens_ref[...].astype(F32)
    normed = (inputs * scale_rows(inputs) * gain_ref[0:1, :]).astype(BF16)
    normed_ref[...] = normed
    for k in range(3):
        at = slice(k * width, (k + 1) * width)
        qkv_ref[:, at] = dot(normed, weight_ref[:, at], ((1,), (0,))).astype(BF16)
    for pair in range(width // (2 * head)):
        _, _, value, weights = pair_weights(qkv_ref, bias_ref, pair, head, width)
        full = dot(weights.astype(BF16), value, ((1,), (0,)))
        mixed_ref[:, pair * 2 * head : (pair + 1) * 2 * head] = pair_pick(full, head).astype(BF16)
    stream = inputs + dot(mixed_ref[...], weight_ref[:, 3 * width : 4 * width], ((1,), (0,)))
    stream_ref[...] = stream
    cross = (stream * scale_rows(stream) * gain_ref[1:2, :]).astype(BF16)
    cross_ref[...] = cross
    query_ref[...] = dot(cross, weight_ref[:, 4 * width : 5 * width], ((1,), (0,))).astype(BF16)


def self_attend(tokens, gain_rows, bias, weight, head):
    rows, width = tokens.shape
    low = jax.ShapeDtypeStruct((rows, width), BF16)
    weight_spec = pl.BlockSpec((width, 5 * width), lambda i: (0, 0))
    return pl.pallas_call(
        partial(self_kernel, head),
        out_shape=(
            jax.ShapeDtypeStruct((rows, 3 * width), BF16),
            low,
            low,
            jax.ShapeDtypeStruct((rows, width), F32),
            low,
            low,
        ),
        grid=(1,),
        in_specs=[
            pl.BlockSpec(tokens.shape, lambda i: (0, 0)),
            pl.BlockSpec(gain_rows.shape, lambda i: (0, 0)),
            pl.BlockSpec(bias.shape, lambda i: (0, 0, 0)),
            weight_spec,
        ],
        out_specs=(pl.BlockSpec((rows, 3 * width), lambda i: (0, 0)),)
        + (pl.BlockSpec((rows, width), lambda i: (0, 0)),) * 5,
        compiler_params=pltpu.CompilerParams(vmem_limit_bytes=56 * 2**20),
        name="self_attend",
    )(tokens, gain_rows, bias, weight)


def self_back_kernel(head, tokens_ref, gain_ref, bias_ref, weight_ref, qkv_ref, stream_ref, dq_ref, dstream_ref, dqkv_ref, low_ref, dinput_ref, score_ref, dgain_ref):
    width = tokens_ref.shape[1]
    rows = tokens_ref.shape[0]
    d_cross = dot(dq_ref[...], weight_ref[:, 4 * width : 5 * width], ((1,), (1,)))
    d_stream, gain_cross = norm_gradient(stream_ref[...], gain_ref[1:2, :], d_cross)
    d_stream = d_stream + dstream_ref[...]
    low = d_stream.astype(BF16)
    low_ref[...] = low
    d_mixed = dot(low, weight_ref[:, 3 * width : 4 * width], ((1,), (1,))).astype(BF16)
    lanes = score_ref.shape[1]
    place = lax.broadcasted_iota(jnp.int32, (rows, lanes), 0) + lax.broadcasted_iota(
        jnp.int32, (rows, lanes), 1
    )
    mirror = (place == rows - 1).astype(F32).astype(BF16)
    sums = []
    for pair in range(width // (2 * head)):
        query, key, value, weights = pair_weights(qkv_ref, bias_ref, pair, head, width)
        at = slice(pair * 2 * head, (pair + 1) * 2 * head)
        spread = pair_spread(d_mixed[:, at], head)
        d_value = dot(weights.astype(BF16), spread, ((0,), (0,)))
        d_weights = dot(spread, value, ((1,), (1,)))
        inner = jnp.sum(weights * d_weights, axis=-1, keepdims=True)
        d_score = (weights * (d_weights - inner)).astype(BF16)
        reverse = dot(d_score, mirror, ((1,), (0,)))
        for h in range(2):
            turned = pltpu.roll(reverse[h * rows : (h + 1) * rows], 0, 1, stride=1, stride_axis=0)
            sums.append(jnp.sum(turned, axis=0, keepdims=True))
        d_query = pair_pick(dot(d_score, key, ((1,), (0,))), head)
        d_key = dot(d_score, query, ((0,), (0,)))
        dqkv_ref[:, at] = d_query.astype(BF16)
        dqkv_ref[:, width + at.start : width + at.stop] = d_key.astype(BF16)
        dqkv_ref[:, 2 * width + at.start : 2 * width + at.stop] = d_value.astype(BF16)
    d_normed = jnp.zeros((rows, width), F32)
    for k in range(3):
        at = slice(k * width, (k + 1) * width)
        d_normed = d_normed + dot(dqkv_ref[:, at], weight_ref[:, at], ((1,), (1,)))
    d_input, gain_self = norm_gradient(tokens_ref[...].astype(F32), gain_ref[0:1, :], d_normed)
    dinput_ref[...] = d_input + d_stream
    sums.append(jnp.zeros((score_ref.shape[0] - len(sums), lanes), F32))
    score_ref[...] = jnp.concatenate(sums, axis=0)
    dgain_ref[...] = jnp.concatenate([gain_self, gain_cross, jnp.zeros((6, width), F32)], axis=0)


def self_back(tokens, gain_rows, bias, weight, qkv, stream, d_query, d_stream, head):
    rows, width = tokens.shape

    def whole(shape):
        return pl.BlockSpec(shape, lambda i: (0,) * len(shape))

    shapes = (
        jax.ShapeDtypeStruct(qkv.shape, BF16),
        jax.ShapeDtypeStruct(tokens.shape, BF16),
        jax.ShapeDtypeStruct(tokens.shape, F32),
        jax.ShapeDtypeStruct((-(-bias.shape[0] // 8) * 8, -(-rows // 128) * 128), F32),
        jax.ShapeDtypeStruct((8, width), F32),
    )
    return pl.pallas_call(
        partial(self_back_kernel, head),
        out_shape=shapes,
        grid=(1,),
        in_specs=[
            whole(tokens.shape),
            whole(gain_rows.shape),
            whole(bias.shape),
            whole((width, 5 * width)),
            whole(qkv.shape),
            whole(tokens.shape),
            whole(tokens.shape),
            whole(tokens.shape),
        ],
        out_specs=tuple(whole(shape.shape) for shape in shapes),
        compiler_params=pltpu.CompilerParams(vmem_limit_bytes=56 * 2**20),
        name="self_back",
    )(tokens, gain_rows, bias, weight, qkv, stream, d_query, d_stream)


def pick_chunk(full, head, rows, start):
    chunk = full.shape[1]
    first = start // rows
    lane = (lax.broadcasted_iota(jnp.int32, (head, chunk), 1) + start) // rows - first
    out = full[:head]
    for h in range(1, full.shape[0] // head):
        out = jnp.where(lane == h, full[h * head : (h + 1) * head], out)
    return out


def over_rows(value, reduce):
    rows, lanes = value.shape
    if rows % 64 == 0:
        value = reduce(value.reshape(8, rows // 8, lanes), axis=0)
    if value.shape[0] % 8 == 0:
        value = reduce(value.reshape(-1, 8, lanes), axis=0)
    return reduce(value, axis=0, keepdims=True)


def flush_queries(here_ref, queries, pack, mine_ref, other_ref):
    near = queries // 4

    def flush(at, carry):
        y = jnp.bitwise_xor(here_ref[1], at // near)
        j = at % near * 4 + 2 * y
        mine_ref[at, 0] = pack(j + here_ref[0])
        other_ref[at, 0] = pack(j + 1 - here_ref[0])
        return carry

    lax.fori_loop(0, queries // 2, flush, 0)


def either(index, a_ref, b_ref):
    count = a_ref.shape[0]
    return jnp.where(index < count, a_ref[index % count], b_ref[index % count])


def attend_kernel(plen, head, rows, asker_ref, owner_ref, here_ref, qa_ref, qb_ref, kv_ref, mine_ref, other_ref, acc, top, total):
    step = pl.program_id(1)
    queries = 2 * qa_ref.shape[0]
    width = GROUP * head

    @pl.when(step == 0)
    def _():
        acc[...] = jnp.zeros_like(acc)
        top[...] = jnp.full_like(top, FLOOR)
        total[...] = jnp.zeros_like(total)

    lanes = GROUP * rows
    chunk = min(CHUNK, lanes)

    def begin(unit):
        p, c = divmod(unit, lanes // chunk)
        if c == 0:
            spreads[p] = spread_heads(either(asker_ref[step * BLOCK + p], qa_ref, qb_ref), head)
            turned[p] = kv_ref[p * plen : (p + 1) * plen, width:].T
        keys = kv_ref[p * plen : (p + 1) * plen, :width]
        return dot(keys, spreads[p][c * chunk : (c + 1) * chunk], ((1,), (1,)))

    def finish(unit, scores):
        p, c = divmod(unit, lanes // chunk)
        owner = owner_ref[step * BLOCK + p]
        at = pl.ds(c * chunk, chunk)
        first, last = c * chunk // rows, ((c + 1) * chunk - 1) // rows
        here = over_rows(scores, jnp.max)
        raised = jnp.exp(scores - here)
        here_total = over_rows(raised, jnp.sum)
        full = dot(turned[p][first * head : (last + 1) * head], raised.astype(BF16), ((1,), (0,)))
        mixed = pick_chunk(full, head, rows, c * chunk)
        old = top[owner, :, at]
        new = jnp.maximum(old, here)
        old_scale, here_scale = jnp.exp(old - new), jnp.exp(here - new)
        top[owner, :, at] = new
        total[owner, :, at] = total[owner, :, at] * old_scale + here_total * here_scale
        acc[owner, :, at] = acc[owner, :, at] * old_scale + mixed * here_scale

    spreads, turned = {}, {}
    units = BLOCK * (lanes // chunk)
    waiting = [begin(u) for u in range(min(AHEAD, units))]
    for unit in range(units):
        if unit + AHEAD < units:
            waiting.append(begin(unit + AHEAD))
        finish(unit, waiting.pop(0))

    @pl.when(step == pl.num_programs(1) - 1)
    def _():
        def pack(j):
            parts = split_parts(top[j], 3) + split_parts(total[j], 2)
            parts.append(jnp.zeros((STAT_ROWS - len(parts), parts[0].shape[1]), F32))
            return jnp.concatenate([acc[j]] + parts, axis=0).astype(BF16)

        flush_queries(here_ref, queries, pack, mine_ref, other_ref)


def attend(asker, owner, here, plane, across, kv, plen, head):
    near, rows, columns = plane.shape
    queries = 2 * near
    width = GROUP * head
    slots = kv.shape[0] // plen
    lanes = GROUP * rows
    groups = columns // width
    block = (near, 1, head + STAT_ROWS, lanes)
    out = jax.ShapeDtypeStruct((near, groups, head + STAT_ROWS, lanes), BF16)
    q_spec = pl.BlockSpec((near, rows, width), lambda g, b, *_: (0, 0, g))
    return pl.pallas_call(
        partial(attend_kernel, plen, head, rows),
        out_shape=(out, out),
        grid_spec=pltpu.PrefetchScalarGridSpec(
            num_scalar_prefetch=3,
            grid=(groups, slots // BLOCK),
            in_specs=[
                q_spec,
                q_spec,
                pl.BlockSpec((BLOCK * plen, 2 * width), lambda g, b, *_: (b, g)),
            ],
            out_specs=(pl.BlockSpec(block, lambda g, b, *_: (0, g, 0, 0)),) * 2,
            scratch_shapes=[
                pltpu.VMEM((queries, head, lanes), F32),
                pltpu.VMEM((queries, 1, lanes), F32),
                pltpu.VMEM((queries, 1, lanes), F32),
            ],
        ),
        compiler_params=pltpu.CompilerParams(vmem_limit_bytes=60 * 2**20),
        cost_estimate=pl.CostEstimate(
            flops=16 * rows * kv.shape[0] * columns,
            bytes_accessed=4 * kv.shape[0] * columns,
            transcendentals=rows * kv.shape[0] * GROUP * groups,
        ),
        name="attend",
    )(asker, owner, here, plane, across, kv)


def read_stats(stat):
    return stat[0:1] + stat[1:2] + stat[2:3], stat[3:4] + stat[4:5]


def merge_kernel(head, a_ref, b_ref, out_ref):
    for i in range(a_ref.shape[0]):
        for g in range(a_ref.shape[1]):
            top_a, sum_a = read_stats(a_ref[i, g, head:, :].astype(F32))
            top_b, sum_b = read_stats(b_ref[i, g, head:, :].astype(F32))
            top = jnp.maximum(top_a, top_b)
            w_a, w_b = jnp.exp(top_a - top), jnp.exp(top_b - top)
            body = a_ref[i, g, :head, :].astype(F32) * w_a + b_ref[i, g, :head, :].astype(F32) * w_b
            rows = split_parts(top, 3) + split_parts(sum_a * w_a + sum_b * w_b, 2)
            rows.append(jnp.zeros((STAT_ROWS - 5, top.shape[1]), F32))
            out_ref[i, g] = jnp.concatenate([body] + rows, axis=0).astype(BF16)


def core_kernel(head, a_ref, b_ref, near_ref, far_ref):
    @pl.when(pl.program_id(0) < 2)
    def _():
        merge_kernel(head, a_ref, b_ref, far_ref)

    @pl.when(pl.program_id(0) >= 2)
    def _():
        merge_kernel(head, a_ref, b_ref, near_ref)


def core_merge(kept, came, head):
    block = (kept.shape[0] // 4,) + kept.shape[1:]
    out = jax.ShapeDtypeStruct((kept.shape[0] // 2,) + kept.shape[1:], BF16)
    return pl.pallas_call(
        partial(core_kernel, head),
        out_shape=(out, out),
        grid=(4,),
        in_specs=[pl.BlockSpec(block, lambda i: ((i + 2) % 4, 0, 0, 0))] * 2,
        out_specs=(
            pl.BlockSpec(block, lambda i: (jnp.maximum(i - 2, 0), 0, 0, 0)),
            pl.BlockSpec(block, lambda i: (jnp.minimum(i, 1), 0, 0, 0)),
        ),
        cost_estimate=pl.CostEstimate(flops=4 * kept.size, bytes_accessed=6 * kept.size, transcendentals=0),
        name="core_merge",
    )(kept, came)


def near_merge(kept, came, head):
    spec = pl.BlockSpec((kept.shape[0] // 2,) + kept.shape[1:], lambda i: (i, 0, 0, 0))
    return pl.pallas_call(
        partial(merge_kernel, head),
        out_shape=jax.ShapeDtypeStruct(kept.shape, BF16),
        grid=(2,),
        in_specs=[spec, spec],
        out_specs=spec,
        cost_estimate=pl.CostEstimate(flops=4 * kept.size, bytes_accessed=6 * kept.size, transcendentals=0),
        name="near_merge",
    )(kept, came)


def join_parts(ref, g, head):
    count = ref.shape[0]
    found = [read_stats(ref[i, g, head:, :].astype(F32)) for i in range(count)]
    top = found[0][0]
    for i in range(1, count):
        top = jnp.maximum(top, found[i][0])
    weights = [jnp.exp(found[i][0] - top) for i in range(count)]
    whole = found[0][1] * weights[0]
    mixed = ref[0, g, :head, :].astype(F32) * weights[0]
    for i in range(1, count):
        whole = whole + found[i][1] * weights[i]
        mixed = mixed + ref[i, g, :head, :].astype(F32) * weights[i]
    return mixed / whole, top + jnp.log(whole)


def ffn_kernel(head, arrived_ref, stream_ref, cot_ref, gain_ref, cross_ref, up_ref, down_ref, payload_ref, out_ref, dstream_ref, dgain_ref, mixed_ref, low_ref, normed_ref, dinner_ref, active_ref, full_ref, log_ref, total_ref, back_ref):
    rows, width = stream_ref.shape
    groups = arrived_ref.shape[1]
    wide = GROUP * head
    fold = pl.program_id(0)

    @pl.when(fold == 0)
    def _():
        for g in range(groups):
            part, log = join_parts(arrived_ref, g, head)
            log_ref[g : g + 1, :] = log
            turned = part.T
            heads = [turned[h * rows : (h + 1) * rows] for h in range(GROUP)]
            full_ref[:, g * wide : (g + 1) * wide] = jnp.concatenate(heads, axis=1)
        mixed = full_ref[...].astype(BF16)
        mixed_ref[...] = mixed
        stream = stream_ref[...] + dot(mixed, cross_ref[...], ((1,), (0,)))
        dstream_ref[...] = stream
        total_ref[...] = stream
        back_ref[...] = jnp.zeros_like(back_ref)
        normed_ref[...] = (stream * scale_rows(stream) * gain_ref[2:3, :]).astype(BF16)

    inner = dot(normed_ref[...], up_ref[...], ((1,), (0,)))
    square = inner * inner
    bent = jnp.tanh(0.7978845608028654 * (inner + 0.044715 * square * inner))
    half = 0.5 * (1.0 + bent)
    active = (inner * half).astype(BF16)
    slope = half + 0.5 * inner * (1.0 - bent * bent) * (
        0.7978845608028654 * (1.0 + 0.134145 * square)
    )
    active_ref[...] = active
    total_ref[...] += dot(active, down_ref[...], ((1,), (0,)))
    d_inner = (dot(cot_ref[...], down_ref[...], ((1,), (1,))) * slope).astype(BF16)
    dinner_ref[...] = d_inner
    back_ref[...] += dot(d_inner, up_ref[...], ((1,), (1,)))

    @pl.when(fold == pl.num_programs(0) - 1)
    def _():
        out_ref[...] = total_ref[...].astype(BF16)
        d_stream, gain = norm_gradient(dstream_ref[...], gain_ref[2:3, :], back_ref[...])
        d_stream = d_stream + cot_ref[...].astype(F32)
        dstream_ref[...] = d_stream
        dgain_ref[...] = jnp.concatenate([gain, jnp.zeros((7, width), F32)], axis=0)
        low = d_stream.astype(BF16)
        low_ref[...] = low
        d_mixed = dot(low, cross_ref[...], ((1,), (1,))).astype(BF16)
        payload_ref[:rows, :] = d_mixed
        for g in range(groups):
            columns = slice(g * wide, (g + 1) * wide)
            product = (d_mixed[:, columns].astype(F32) * full_ref[:, columns]).T
            delta = [
                jnp.sum(product[h * head : (h + 1) * head], axis=0, keepdims=True)
                for h in range(GROUP)
            ]
            parts = split_parts(log_ref[g : g + 1, :], 3) + split_parts(jnp.concatenate(delta, axis=1), 2)
            lines = [
                part[:, t * wide : (t + 1) * wide]
                for part in parts
                for t in range(GROUP * rows // wide)
            ]
            lines.append(jnp.zeros((STAT_ROWS - len(lines), wide), F32))
            payload_ref[rows:, columns] = jnp.concatenate(lines, axis=0).astype(BF16)


def feed_forward(arrived, stream, grads, gain_rows, weight, head):
    rows, width = stream.shape
    hidden = (weight.shape[1] - width) // 2
    folds = hidden // width

    def whole(shape):
        return pl.BlockSpec(shape, lambda k: (0,) * len(shape))

    low = jax.ShapeDtypeStruct((rows, width), BF16)
    long = jax.ShapeDtypeStruct((rows, hidden), BF16)
    shapes = (
        jax.ShapeDtypeStruct((rows + STAT_ROWS, width), BF16),
        low,
        jax.ShapeDtypeStruct((rows, width), F32),
        jax.ShapeDtypeStruct((8, width), F32),
        low,
        low,
        low,
    )
    fold_spec = pl.BlockSpec((rows, width), lambda k: (0, k))
    return pl.pallas_call(
        partial(ffn_kernel, head),
        out_shape=shapes + (long, long),
        grid=(folds,),
        in_specs=[whole(v.shape) for v in (arrived, stream, grads, gain_rows)]
        + [
            pl.BlockSpec((width, width), lambda k: (0, 0)),
            pl.BlockSpec((width, width), lambda k: (0, 1 + k)),
            pl.BlockSpec((width, width), lambda k: (0, 1 + folds + k)),
        ],
        out_specs=tuple(whole(shape.shape) for shape in shapes) + (fold_spec, fold_spec),
        scratch_shapes=[
            pltpu.VMEM((rows, width), F32),
            pltpu.VMEM((8, GROUP * rows), F32),
            pltpu.VMEM((rows, width), F32),
            pltpu.VMEM((rows, width), F32),
        ],
        compiler_params=pltpu.CompilerParams(vmem_limit_bytes=56 * 2**20),
        cost_estimate=pl.CostEstimate(
            flops=4 * rows * weight.size, bytes_accessed=2 * weight.size, transcendentals=rows * hidden
        ),
        name="feed_forward",
    )(arrived, stream, grads, gain_rows, weight, weight, weight)


def ffn_terms_kernel(folds, *refs):
    out_ref = refs[-1]
    tile = pl.program_id(0)
    for first, last, left, right in ((0, 1, 0, 1), (1, 1 + folds, 2, 3), (1 + folds, 1 + 2 * folds, 4, 5)):

        @pl.when((tile >= first) & (tile < last))
        def _(left=left, right=right):
            a, b = refs[2 * left : 2 * left + 2], refs[2 * right : 2 * right + 2]
            found = dot(a[0][...], b[0][...], ((0,), (0,))) + dot(a[1][...], b[1][...], ((0,), (0,)))
            out_ref[...] = found.astype(BF16)


def ffn_terms(parts, grads, hidden):
    width = grads[0].shape[1]
    folds = hidden // width

    def spec(value, start):
        if start is None:
            return pl.BlockSpec((value.shape[0], width), lambda t: (0, 0))
        return pl.BlockSpec((value.shape[0], width), lambda t: (0, jnp.clip(t - start, 0, folds - 1)))

    operands, specs = [], []
    for values, start in zip([*zip(*parts), grads], (None, None, None, 1, 1 + folds, None)):
        for value in values:
            operands.append(value)
            specs.append(spec(value, start))
    return pl.pallas_call(
        partial(ffn_terms_kernel, folds),
        out_shape=jax.ShapeDtypeStruct((width, width + 2 * hidden), BF16),
        grid=(1 + 2 * folds,),
        in_specs=specs,
        out_specs=pl.BlockSpec((width, width), lambda t: (0, t)),
        compiler_params=pltpu.CompilerParams(vmem_limit_bytes=60 * 2**20),
        cost_estimate=pl.CostEstimate(
            flops=6 * width * width * width, bytes_accessed=8 * width * hidden, transcendentals=0
        ),
        name="ffn_terms",
    )(*operands)


def attend_back_kernel(plen, head, rows, asker_ref, owner_ref, here_ref, qa_ref, qb_ref, doa_ref, dob_ref, sa_ref, sb_ref, kv_ref, *refs):
    step = pl.program_id(1)
    dkv_ref, mine_ref, other_ref, acc, log, delta = refs[-6:]
    held_ref = refs[0] if len(refs) > 6 else None
    near = qa_ref.shape[0]
    queries = 2 * near
    width = GROUP * head

    @pl.when(step == 0)
    def _():
        acc[...] = jnp.zeros_like(acc)
        third = (GROUP * rows) // width

        def fill(j, carry):
            stat = either(j, sa_ref, sb_ref).astype(F32)
            row = lax.broadcasted_iota(jnp.int32, stat.shape, 0)
            for at, ref, count in ((0, log, 3), (3 * third, delta, 2)):
                pieces = []
                for t in range(third):
                    wanted = row == at + t
                    for k in range(1, count):
                        wanted = wanted | (row == at + k * third + t)
                    pieces.append(jnp.sum(jnp.where(wanted, stat, 0.0), axis=0, keepdims=True))
                ref[j] = jnp.concatenate(pieces, axis=1)
            return carry

        lax.fori_loop(0, queries, fill, 0)

    lanes = GROUP * rows
    chunk = min(CHUNK, lanes)

    def begin(unit):
        p, c = divmod(unit, lanes // chunk)
        rows_at = slice(p * plen, (p + 1) * plen)
        if c == 0:
            asker = asker_ref[step * BLOCK + p]
            q_spread[p] = spread_heads(either(asker, qa_ref, qb_ref), head)
            do_spread[p] = spread_heads(either(asker, doa_ref, dob_ref), head)
            turned[p] = kv_ref[rows_at, :width].T
        at = slice(c * chunk, (c + 1) * chunk)
        return (
            dot(kv_ref[rows_at, :width], q_spread[p][at], ((1,), (1,))),
            dot(kv_ref[rows_at, width:], do_spread[p][at], ((1,), (1,))),
        )

    def finish(unit, found):
        scores, d_soft = found
        p, c = divmod(unit, lanes // chunk)
        owner, asker = owner_ref[step * BLOCK + p], asker_ref[step * BLOCK + p]
        at = pl.ds(c * chunk, chunk)
        cut = slice(c * chunk, (c + 1) * chunk)
        first, last = c * chunk // rows, ((c + 1) * chunk - 1) // rows
        soft = jnp.exp(scores - log[asker, :, at])
        d_score = (soft * (d_soft - delta[asker, :, at])).astype(BF16)
        d_value = dot(soft.astype(BF16), do_spread[p][cut], ((1,), (0,)))
        d_key = dot(d_score, q_spread[p][cut], ((1,), (0,)))
        sums[p] = (d_key, d_value) if c == 0 else (sums[p][0] + d_key, sums[p][1] + d_value)
        full = dot(turned[p][first * head : (last + 1) * head], d_score, ((1,), (0,)))
        acc[owner, :, at] += pick_chunk(full, head, rows, c * chunk)
        if c == lanes // chunk - 1:
            rows_at = slice(p * plen, (p + 1) * plen)
            for found, columns in zip(sums[p], (slice(0, width), slice(width, 2 * width))):
                if held_ref is not None:
                    found = found + held_ref[rows_at, columns].astype(F32)
                dkv_ref[rows_at, columns] = found.astype(BF16)

    q_spread, do_spread, turned, sums = {}, {}, {}, {}
    units = BLOCK * (lanes // chunk)
    waiting = [begin(u) for u in range(min(AHEAD, units))]
    for unit in range(units):
        if unit + AHEAD < units:
            waiting.append(begin(unit + AHEAD))
        finish(unit, waiting.pop(0))

    @pl.when(step == pl.num_programs(1) - 1)
    def _():
        flush_queries(here_ref, queries, lambda j: acc[j].astype(BF16), mine_ref, other_ref)


def attend_back(asker, owner, here, queries_in, grads_in, kv, held, plen, head):
    near, rows, columns = queries_in[0].shape
    queries = 2 * near
    width = GROUP * head
    slots = kv.shape[0] // plen
    lanes = GROUP * rows
    groups = columns // width
    block = (near, 1, head, lanes)
    out = jax.ShapeDtypeStruct((near, groups, head, lanes), BF16)
    q_spec = pl.BlockSpec((near, rows, width), lambda g, b, *_: (0, 0, g))
    stat_spec = pl.BlockSpec((near, STAT_ROWS, width), lambda g, b, *_: (0, rows // STAT_ROWS, g))
    kv_spec = pl.BlockSpec((BLOCK * plen, 2 * width), lambda g, b, *_: (b, g))
    operands = [*queries_in, *grads_in, *grads_in, kv]
    specs = [q_spec] * 4 + [stat_spec] * 2 + [kv_spec]
    if held is not None:
        operands.append(held)
        specs.append(kv_spec)
    return pl.pallas_call(
        partial(attend_back_kernel, plen, head, rows),
        out_shape=(jax.ShapeDtypeStruct(kv.shape, BF16), out, out),
        grid_spec=pltpu.PrefetchScalarGridSpec(
            num_scalar_prefetch=3,
            grid=(groups, slots // BLOCK),
            in_specs=specs,
            out_specs=(
                kv_spec,
                pl.BlockSpec(block, lambda g, b, *_: (0, g, 0, 0)),
                pl.BlockSpec(block, lambda g, b, *_: (0, g, 0, 0)),
            ),
            scratch_shapes=[
                pltpu.VMEM((queries, head, lanes), F32),
                pltpu.VMEM((queries, 1, lanes), F32),
                pltpu.VMEM((queries, 1, lanes), F32),
            ],
        ),
        input_output_aliases={} if held is None else {3 + len(operands) - 1: 0},
        compiler_params=pltpu.CompilerParams(vmem_limit_bytes=60 * 2**20),
        cost_estimate=pl.CostEstimate(
            flops=40 * rows * kv.shape[0] * columns,
            bytes_accessed=8 * kv.shape[0] * columns,
            transcendentals=rows * kv.shape[0] * GROUP * groups,
        ),
        name="attend_back",
    )(asker, owner, here, *operands)


def source_kernel(keep_ref, fetch_ref, *refs):
    weight_ref, out_ref = refs[-2:]
    for p, ref in enumerate(refs[:-2]):
        kept = keep_ref[pl.program_id(0) * (len(refs) - 2) + p]

        @pl.when(kept == 0)
        def _(p=p):
            out_ref[p] = jnp.zeros_like(out_ref[p])

        @pl.when(kept != 0)
        def _(p=p, ref=ref):
            out_ref[p] = dot(ref[...], weight_ref[...], ((1,), (1,))).astype(BF16)


def fetch_order(refresh):
    slots = refresh.shape[0]
    several = 4 if slots % 4 == 0 else 1
    order = jnp.arange(slots).reshape(-1, several)
    kept = refresh.reshape(-1, several) != 0
    fetch = lax.cummax(jnp.where(kept, order, order[:1]), axis=0)
    return several, fetch.astype(jnp.int32).reshape(-1)


def source_grads(refresh, several, fetch, dkv, weight, plen):
    slots = refresh.shape[0]
    model_width = weight.shape[0]

    def spec(p):
        return pl.BlockSpec((plen, dkv.shape[1]), lambda r, keep, fetch: (fetch[r * several + p], 0))

    return pl.pallas_call(
        source_kernel,
        out_shape=jax.ShapeDtypeStruct((slots, plen, model_width), BF16),
        grid_spec=pltpu.PrefetchScalarGridSpec(
            num_scalar_prefetch=2,
            grid=(slots // several,),
            in_specs=[spec(p) for p in range(several)] + [pl.BlockSpec(weight.shape, lambda r, *_: (0, 0))],
            out_specs=pl.BlockSpec((several, plen, model_width), lambda r, *_: (r, 0, 0)),
        ),
        compiler_params=pltpu.CompilerParams(vmem_limit_bytes=60 * 2**20),
        cost_estimate=pl.CostEstimate(
            flops=slots * plen * model_width * 2 * model_width,
            bytes_accessed=4 * slots * plen * model_width,
            transcendentals=0,
        ),
        name="source_grads",
    )(refresh, fetch, *([dkv] * several), weight)


def outer_kernel(starts, split, added, half_ref, *refs):
    count = len(starts) - 1
    outs = refs[-2:]
    tile = pl.program_id(0)
    for k in range(count):

        @pl.when((tile >= starts[k]) & (tile < starts[k + 1]))
        def _(k=k):
            found = dot(refs[2 * k][...], refs[2 * k + 1][...], ((0,), (0,)))
            side = 0 if k < split else 1
            if added:
                found = found + refs[2 * count + side][...].astype(F32)
            outs[side][...] = found.astype(BF16)


def outer(half, first, second, came=None):
    pairs = first + second
    rows, total_rows = pairs[0][0].shape
    width = total_rows // 2
    counts = [right.shape[1] // 2 // width for _, right in pairs]
    starts = [sum(counts[:k]) for k in range(len(counts) + 1)]
    edge = starts[len(first)]
    operands, specs = [], []
    for k, (left, right) in enumerate(pairs):

        def right_map(t, half_ref, start=starts[k], count=counts[k]):
            return (0, half_ref[0] * count + jnp.clip(t - start, 0, count - 1))

        operands += [left, right]
        specs += [
            pl.BlockSpec((rows, total_rows), lambda t, half_ref: (0, 0)),
            pl.BlockSpec((rows, width), right_map),
        ]
    sides = (
        pl.BlockSpec((total_rows, width), lambda t, half_ref: (0, jnp.minimum(t, edge - 1))),
        pl.BlockSpec((total_rows, width), lambda t, half_ref: (0, jnp.maximum(t - edge, 0))),
    )
    if came is not None:
        operands += came
        specs += sides
    size = total_rows * starts[-1] * width
    return pl.pallas_call(
        partial(outer_kernel, starts, len(first), came is not None),
        out_shape=(
            jax.ShapeDtypeStruct((total_rows, edge * width), BF16),
            jax.ShapeDtypeStruct((total_rows, (starts[-1] - edge) * width), BF16),
        ),
        grid_spec=pltpu.PrefetchScalarGridSpec(
            num_scalar_prefetch=1, grid=(starts[-1],), in_specs=specs, out_specs=sides
        ),
        compiler_params=pltpu.CompilerParams(vmem_limit_bytes=60 * 2**20),
        cost_estimate=pl.CostEstimate(flops=2 * rows * size, bytes_accessed=4 * size, transcendentals=0),
        name="outer",
    )(half, *operands)


def flip(value, bit):
    count = lax.axis_size("pass")
    return lax.ppermute(value, "pass", [(i, i ^ bit) for i in range(count)])


def after(value, *others):
    return lax.optimization_barrier((value,) + others)


def line_sends(block):
    count = lax.axis_size("pass")
    rings = [[(i, (i + 4 * k) % count) for i in range(count)] for k in range(1, count // 4)]
    return [lax.ppermute(block, "pass", ring) for ring in rings]


def gather_place(query, own, count):
    major = count // 4
    turn = jnp.mod(own // 4 - query // 4, major)
    return turn + major * ((own // 2) % 2 != (query // 2) % 2) + 2 * major * (own % 2 != query % 2)


def line_exchange(parts):
    count = lax.axis_size("pass")
    groups = [[r + 4 * k for k in range(count // 4)] for r in range(4)]
    return lax.all_to_all(
        parts, "pass", split_axis=0, concat_axis=0, tiled=True, axis_index_groups=groups
    )


def in_order(own, came, place, axis):
    return jnp.stack([jnp.where(place == 0, own, came), jnp.where(place == 0, came, own)], axis=axis)


def gather_rows(block):
    n_dp, count = lax.axis_size("dp"), lax.axis_size("pass")
    if n_dp != 2:
        return lax.all_gather(block, ("dp", "pass"), axis=0, tiled=True)
    own, dp = lax.axis_index("pass"), lax.axis_index("dp")
    major, core, y = count // 4, own % 2, own // 2 % 2
    pieces = [block, *line_sends(block)]
    line = jnp.zeros((major,) + block.shape, block.dtype)
    for k, piece in enumerate(pieces):
        line = lax.dynamic_update_index_in_dim(line, piece, jnp.mod(own // 4 - k, major), 0)
    cut = block.shape[1] // 256 * 128
    left, right = line[..., :cut], line[..., cut:]
    left, right = in_order(left, flip(left, 2), y, 1), in_order(right, dp_flip(right), dp, 0)
    left, right = in_order(left, dp_flip(left), dp, 0), in_order(right, flip(right, 2), y, 2)
    full = [in_order(part, flip(part, 1), core, 3) for part in (left, right)]
    return jnp.concatenate([part.reshape(-1, part.shape[-1]) for part in full], axis=1)


def line_scatter(parts):
    count = lax.axis_size("pass")
    major, place = count // 4, lax.axis_index("pass") // 4
    came = []
    for k in range(1, major):
        sent = lax.dynamic_index_in_dim(parts, jnp.mod(place + k, major), 0, keepdims=False)
        came.append(lax.ppermute(sent, "pass", [(i, (i + 4 * k) % count) for i in range(count)]))
    return lax.dynamic_index_in_dim(parts, place, 0, keepdims=False), came


def swap_send(value, place, axis, send):
    kept = lax.dynamic_index_in_dim(value, place, axis, keepdims=False)
    return kept, send(lax.dynamic_index_in_dim(value, 1 - place, axis, keepdims=False))


def add_low(kept, came):
    return (kept.astype(F32) + came.astype(F32)).astype(BF16)


def rows_by_owner(value):
    n_dp, count = lax.axis_size("dp"), lax.axis_size("pass")
    rows, columns = value.shape
    return value.reshape(n_dp, count // 4, 2, rows // (n_dp * count // 2), columns)


def dp_step(value, bit):
    pairs = [(i, i ^ bit) for i in range(lax.axis_size("dp"))]
    return lax.ppermute(value, "dp", pairs)


def dp_flip(value):
    return lax.ppermute(value, "dp", [(0, 1), (1, 0)])


def dp_send(value):
    if lax.axis_size("dp") == 2:
        return swap_send(value, lax.axis_index("dp"), 0, dp_flip)
    total = lax.psum_scatter(value, "dp", scatter_dimension=0, tiled=False)
    return total, jnp.zeros_like(total)


def near_send(value, axis):
    return swap_send(value, lax.axis_index("pass") // 2 % 2, axis, lambda v: flip(v, 2))


def over_line(value):
    return jnp.sum(line_exchange(value).astype(F32), axis=0)


def own_rows(value, core):
    shard = value.shape[0] // 2
    parts = value.reshape(2, shard, value.shape[1])
    kept = lax.dynamic_index_in_dim(parts, core, 0, keepdims=False)
    came = flip(lax.dynamic_index_in_dim(parts, 1 - core, 0, keepdims=False), 1)
    return jnp.where(core == 0, kept, came), jnp.where(core == 0, came, kept)


def on_device(
    tokens,
    cotangent,
    passages,
    refresh,
    passage_ids,
    self_query,
    self_key,
    self_value,
    self_out,
    cross_query,
    cross_key,
    cross_value,
    cross_out,
    up_weight,
    down_weight,
    gains,
    rel_table,
):
    both = ("dp", "pass")
    pass_count = lax.axis_size("pass")
    device_id = lax.axis_index(both)
    own_pass = lax.axis_index("pass")
    per_query, plen, model_width = passages.shape
    head_count = rel_table.shape[1]
    head = model_width // head_count
    rows = tokens.shape[0]
    groups = head_count // GROUP
    wide = GROUP * head
    shard = self_query.shape[0]

    def gather(value):
        return lax.all_gather(value, both, axis=0, tiled=True)

    kv_shard = jnp.stack(
        [cross_key.reshape(shard, groups, wide), cross_value.reshape(shard, groups, wide)], axis=2
    ).reshape(shard, 2 * model_width)
    gain_pad = jnp.pad(gains, ((0, 0), (0, 128 - gains.shape[1])))
    first = gather(
        jnp.concatenate([self_query, self_key, self_value, self_out, cross_query, gain_pad], axis=1)
    )
    kv_weight = lax.optimization_barrier(gather_rows(kv_shard))
    encoded = passages.reshape(per_query * plen, model_width)
    kv = matmul(encoded, kv_weight).astype(BF16)
    positions = jnp.arange(rows)
    causal = positions[:, None] >= positions[None, :]
    onehot_low = (
        bucket_of(positions[:, None] - positions[None, :], rel_table.shape[0])[:, :, None]
        == jnp.arange(rel_table.shape[0])[None, None, :]
    ).astype(BF16)
    bias = jnp.einsum("qkb,bh->hqk", onehot_low, rel_table, preferred_element_type=F32)
    bias = jnp.where(causal[None, :, :], bias, FLOOR)
    folds = up_weight.shape[1] // model_width
    total = up_weight.shape[1] // (folds * shard)
    up_fold = up_weight.reshape(shard, total, folds, shard).transpose(0, 2, 1, 3).reshape(shard, -1)
    down_fold = down_weight.reshape(folds, shard, model_width).transpose(1, 0, 2).reshape(shard, -1)
    rest = jnp.concatenate([cross_out, up_fold, down_fold], axis=1)
    several, fetch = fetch_order(refresh)
    first, kv, bias, rest, fetch = after(first, kv, bias, rest, fetch)
    gain_all = first[:, 5 * model_width : 5 * model_width + 3].astype(F32)

    row_ids = device_id * per_query + jnp.arange(per_query)
    owned = jnp.any(passage_ids[:, :, None] == row_ids[None, None, :], axis=1)
    owner = jnp.sum(
        jnp.where(owned, jnp.arange(passage_ids.shape[0])[:, None], 0), axis=0
    ).astype(jnp.int32)
    core = own_pass % 2
    half = core.astype(jnp.int32).reshape(1)
    here = jnp.stack([core, own_pass // 2 % 2]).astype(jnp.int32)
    asker = gather_place(owner, own_pass, pass_count).astype(jnp.int32)

    gain_rows = jnp.pad(gain_all.T, ((0, 5), (0, 0)))
    qkv, mixed_one, normed_self, stream_one, normed_cross, query_two = self_attend(
        tokens, gain_rows, bias, first, head
    )

    cut = rows // 192 * 128

    def merge_send(mine, came):
        near, far = core_merge(mine, came, head)
        return near, flip(far, 2)

    def rows_first(value):
        cube = value.reshape(groups, head, GROUP, -1).transpose(3, 0, 2, 1)
        return cube.reshape(-1, model_width)

    block, last_block = query_two[:cut], query_two[cut:]
    last_block, rest, *sends = after(last_block, rest, *line_sends(block))
    rest = gather(rest)
    line = jnp.stack([block, *sends])
    across, *sends = after(flip(line, 2), *line_sends(last_block))
    plane = jnp.concatenate([line, across])
    q_first = (plane, flip(plane, 1))
    line = jnp.stack([last_block, *sends])
    across = flip(line, 2)
    mine, other = attend(asker, owner, here, *q_first, kv, plen, head)
    across, mine, other = after(across, mine, other)
    came = flip(other, 1)
    plane = jnp.concatenate([line, across])
    q_second = (plane, flip(plane, 1))
    near, came = merge_send(mine, came)
    q_second, near = after(q_second, near)
    mine, other = attend(asker, owner, here, *q_second, kv, plen, head)
    came, mine, other = after(came, mine, other)
    merged, mine, other = after(near_merge(near, came, head), mine, other)
    came_next = flip(other, 1)
    arrived = line_exchange(merged)
    near, came = merge_send(mine, came_next)
    arrived, near, came = after(arrived, near, came)
    merged, arrived = after(near_merge(near, came, head), arrived)
    arrived_last = line_exchange(merged)
    payload_first, out_first, ds_first, gain_first, *terms_first = feed_forward(
        arrived, stream_one[:cut], cotangent[:cut], gain_rows, rest, head
    )
    arrived_last, payload_first = after(arrived_last, payload_first)
    sends = line_sends(payload_first)
    payload, out_last, ds_last, gain_last, *terms_last = feed_forward(
        arrived_last, stream_one[cut:], cotangent[cut:], gain_rows, rest, head
    )
    payload, *sends = after(payload, *sends)
    line_first = jnp.stack([payload_first, *sends])
    across = flip(line_first, 2)
    sends = line_sends(payload)

    block_out = jnp.concatenate([out_first, out_last])
    d_stream_two = jnp.concatenate([ds_first, ds_last])
    d_gain_ffn = gain_first[0] + gain_last[0]
    terms = ffn_terms(
        (terms_first, terms_last), (cotangent[:cut], cotangent[cut:]), up_weight.shape[1]
    )
    across, terms, *sends = after(across, terms, *sends)
    ffn_sums = lax.psum_scatter(terms, both, scatter_dimension=0, tiled=True)
    plane = jnp.concatenate([line_first, across])
    do_first = (plane, flip(plane, 1))
    line = jnp.stack([payload, *sends])
    across = flip(line, 2)

    def half_of(value, came):
        value = (value.astype(F32) + came.astype(F32)).astype(BF16)
        return value[: value.shape[0] // 2], value[value.shape[0] // 2 :]

    dkv, mine, other = attend_back(asker, owner, here, q_first, do_first, kv, None, plen, head)
    across, dkv, mine, other = after(across, dkv, mine, other)
    came = flip(other, 1)
    plane = jnp.concatenate([line, across])
    do_last = (plane, flip(plane, 1))
    near, far = half_of(mine, came)
    came = flip(far, 2)
    do_last, near = after(do_last, near)
    dkv, mine, other = attend_back(asker, owner, here, q_second, do_last, kv, dkv, plen, head)
    came, dkv, mine, other = after(came, dkv, mine, other)
    came_next = flip(other, 1)
    arrived = line_exchange((near.astype(F32) + came.astype(F32)).astype(BF16))
    near, far = half_of(mine, came_next)
    came, dkv = after(flip(far, 2), dkv)
    kept, last = line_scatter((near.astype(F32) + came.astype(F32)).astype(BF16))
    arrived, d_kv, d_stream_two, *last = after(
        arrived, left_t(encoded, dkv).astype(BF16), d_stream_two, *last
    )
    last = sum((part.astype(F32) for part in last), kept.astype(F32))
    dq_parts = [rows_first(jnp.sum(arrived.astype(F32), axis=0)), rows_first(last)]
    d_query_two = jnp.concatenate(dq_parts).astype(BF16)
    def kv_half(at):
        cube = d_kv.reshape(model_width, groups, 2, wide)
        return lax.dynamic_index_in_dim(cube, at, 2, keepdims=False).reshape(model_width, -1)

    kv_came = flip(kv_half(1 - core), 1)
    found = self_back(
        tokens, gain_rows, bias, first, qkv, stream_one, d_query_two, d_stream_two, head
    )
    kv_came, ffn_sums, *found = after(kv_came, ffn_sums, *found)
    d_qkv, grad_one, d_inputs, d_score, gain_terms = found
    late_pairs = [(normed_self, d_qkv)]
    more_pairs = [(mixed_one, grad_one), (normed_cross, d_query_two)]
    late_sent, more_sent = outer(1 - half, late_pairs, more_pairs)
    distance = jnp.mod(jnp.arange(d_score.shape[1]) - (rows - 1), d_score.shape[1])
    of_distance = bucket_of(distance, rel_table.shape[0])
    of_distance = (of_distance[:, None] == jnp.arange(rel_table.shape[0])[None, :]).astype(F32)
    d_table = jnp.dot(d_score, of_distance, precision=lax.Precision.HIGHEST)[:head_count].T
    small = jnp.concatenate([d_table.reshape(-1), gain_terms[0], gain_terms[1], d_gain_ffn])
    small = small.reshape(-1, 128)
    late_sent, more_sent, kv_came = after(late_sent, more_sent, kv_came)
    kv_part = jnp.moveaxis(rows_by_owner(add_low(kv_half(core), kv_came)), 1, 0)
    late_came, more_came, kv_part, came = after(
        flip(late_sent, 1), flip(more_sent, 1), kv_part, flip(small, 1)
    )
    small = small + came

    late, more = outer(half, late_pairs, more_pairs, [late_came, more_came])
    late, more, came = after(late, more, flip(small, 2))
    small = small + came
    late_kept, late_came = dp_send(rows_by_owner(late))
    more_kept, more_came = near_send(rows_by_owner(more), 2)
    kv_line = line_exchange(kv_part)
    passage_grad = source_grads(refresh, several, fetch, dkv, kv_weight, plen)
    for bit in range((lax.axis_size("dp") - 1).bit_length()):
        small = small + dp_step(small, 1 << bit)
    kv_line, late_came, more_came, passage_grad, small = after(
        kv_line, late_came, more_came, passage_grad, small
    )
    late_kept, late_came = near_send(add_low(late_kept, late_came), 1)
    more_kept, more_came = dp_send(add_low(more_kept, more_came))
    kv_kept, kv_came = dp_send(jnp.sum(kv_line.astype(F32), axis=0).astype(BF16))
    for bit in range(2, (pass_count - 1).bit_length() - 1):
        small = small + flip(small, 1 << bit)
    late_came, more_came, kv_came, small = after(late_came, more_came, kv_came, small)
    came = flip(small, pass_count // 2)
    kv_kept, kv_came = near_send(add_low(kv_kept, kv_came), 0)
    parts = [(late_kept, late_came), (more_kept, more_came)]
    line = line_exchange(jnp.concatenate([add_low(*part) for part in parts], axis=-1))
    ffn_sums = ffn_sums.astype(F32)
    d_up = ffn_sums[:, model_width : model_width + up_weight.shape[1]]
    d_up = d_up.reshape(shard, folds, total, shard).transpose(0, 2, 1, 3).reshape(up_weight.shape)
    d_down = ffn_sums[:, model_width + up_weight.shape[1] :].reshape(shard, folds, model_width)
    d_down = d_down.transpose(1, 0, 2).reshape(down_weight.shape)
    line, kv_came, came, d_up, d_down = after(line, kv_came, came, d_up, d_down)
    small = (small + came).reshape(-1)
    line = jnp.sum(line.astype(F32), axis=0)
    line = jnp.concatenate([line, kv_kept.astype(F32) + kv_came.astype(F32)], axis=1)
    table_grad = small[: d_table.size].reshape(d_table.shape)
    d_gains = small[d_table.size :].reshape(3, -1)
    d_gains = lax.dynamic_slice_in_dim(d_gains, device_id * shard, shard, 1)

    left, right = own_rows(line, core)
    half_width = model_width // 2

    def whole(start, stop):
        cut = slice(start * half_width, stop * half_width)
        return jnp.concatenate([left[:, cut], right[:, cut]], axis=1)

    d_first, d_out_self, d_query_cross = whole(0, 3), whole(3, 4), whole(4, 5)
    d_query_self, d_key_self, d_value_self = jnp.split(d_first, 3, axis=1)
    d_key_cross, d_value_cross = left[:, 5 * half_width :], right[:, 5 * half_width :]
    d_out_cross = ffn_sums[:, :model_width]
    return (
        block_out,
        d_inputs,
        passage_grad,
        d_query_self,
        d_key_self,
        d_value_self,
        d_out_self,
        d_query_cross,
        d_key_cross,
        d_value_cross,
        d_out_cross,
        d_up,
        d_down,
        d_gains.T,
        table_grad,
    )


def solution(mesh):
    split = P(("dp", "pass"), None)
    cube = P(("dp", "pass"), None, None)
    in_specs = (split, split, cube, P(("dp", "pass")), P("dp", None)) + (split,) * 11 + (P(),)
    out_specs = (split, split, cube) + (split,) * 11 + (P(),)
    return jax.shard_map(
        on_device, mesh=mesh, in_specs=in_specs, out_specs=out_specs, check_vma=False
    )
```

```python
from functools import partial

import jax
import jax.numpy as jnp
from jax import lax
from jax.experimental import pallas as pl
from jax.experimental.pallas import tpu as pltpu
from jax.sharding import PartitionSpec as P

F32 = jnp.float32
BF16 = jnp.bfloat16
GROUP = 4
BLOCK = 10
STAT_ROWS = 16
CHUNK = 256
AHEAD = 2
FLOOR = -1e30


def norm_rows(value, gain):
    return value * lax.rsqrt(jnp.mean(value * value, axis=-1, keepdims=True) + 1e-06) * gain


def bucket_of(spread, buckets):
    near_count = buckets // 2
    spread = jnp.maximum(spread, 0).astype(F32)
    bounds = near_count * 8.0 ** (jnp.arange(1, near_count, dtype=F32) / near_count)
    far_bucket = near_count + jnp.sum((spread[..., None] >= bounds).astype(jnp.int32), axis=-1)
    return jnp.where(spread < near_count, spread.astype(jnp.int32), far_bucket)


def matmul(left, right):
    return jnp.dot(left, right, preferred_element_type=F32)


def left_t(left, right):
    return jnp.einsum("td,te->de", left, right, preferred_element_type=F32)


def right_t(left, right):
    return jnp.einsum("te,de->td", left, right, preferred_element_type=F32)


def dot(left, right, dims):
    return lax.dot_general(left, right, (dims, ((), ())), preferred_element_type=F32)


def split_parts(value, count):
    parts = []
    for _ in range(count):
        part = value.astype(BF16).astype(F32)
        parts.append(part)
        value = value - part
    return parts


def spread_heads(rows, head):
    column = lax.broadcasted_iota(jnp.int32, rows.shape, 1) // head
    return jnp.concatenate(
        [jnp.where(column == h, rows, jnp.zeros_like(rows)) for h in range(GROUP)], axis=0
    )


def scale_rows(value):
    return lax.rsqrt(jnp.mean(value * value, axis=-1, keepdims=True) + 1e-06)


def norm_gradient(value, gain, grad):
    scale = scale_rows(value)
    unit = value * scale
    inner = grad * gain
    mean = jnp.mean(inner * unit, axis=-1, keepdims=True)
    return scale * (inner - unit * mean), jnp.sum(grad * unit, axis=0, keepdims=True)


def pair_spread(rows, head):
    first = lax.broadcasted_iota(jnp.int32, rows.shape, 1) < head
    zero = jnp.zeros_like(rows)
    return jnp.concatenate([jnp.where(first, rows, zero), jnp.where(first, zero, rows)], axis=0)


def pair_pick(full, head):
    rows = full.shape[0] // 2
    first = lax.broadcasted_iota(jnp.int32, (rows, full.shape[1]), 1) < head
    return jnp.where(first, full[:rows], full[rows:])


def pair_weights(qkv_ref, bias_ref, pair, head, width):
    at = slice(pair * 2 * head, (pair + 1) * 2 * head)
    query = pair_spread(qkv_ref[:, at], head)
    key = qkv_ref[:, width + at.start : width + at.stop]
    value = qkv_ref[:, 2 * width + at.start : 2 * width + at.stop]
    rows = key.shape[0]
    bias = bias_ref[2 * pair : 2 * pair + 2].reshape(2 * rows, rows)
    scores = dot(query, key, ((1,), (1,))) + bias
    raised = jnp.exp(scores - jnp.max(scores, axis=-1, keepdims=True))
    return query, key, value, raised / jnp.sum(raised, axis=-1, keepdims=True)


def self_kernel(head, tokens_ref, gain_ref, bias_ref, weight_ref, qkv_ref, mixed_ref, normed_ref, stream_ref, cross_ref, query_ref):
    width = tokens_ref.shape[1]
    inputs = tokens_ref[...].astype(F32)
    normed = (inputs * scale_rows(inputs) * gain_ref[0:1, :]).astype(BF16)
    normed_ref[...] = normed
    for k in range(3):
        at = slice(k * width, (k + 1) * width)
        qkv_ref[:, at] = dot(normed, weight_ref[:, at], ((1,), (0,))).astype(BF16)
    for pair in range(width // (2 * head)):
        _, _, value, weights = pair_weights(qkv_ref, bias_ref, pair, head, width)
        full = dot(weights.astype(BF16), value, ((1,), (0,)))
        mixed_ref[:, pair * 2 * head : (pair + 1) * 2 * head] = pair_pick(full, head).astype(BF16)
    stream = inputs + dot(mixed_ref[...], weight_ref[:, 3 * width : 4 * width], ((1,), (0,)))
    stream_ref[...] = stream
    cross = (stream * scale_rows(stream) * gain_ref[1:2, :]).astype(BF16)
    cross_ref[...] = cross
    query_ref[...] = dot(cross, weight_ref[:, 4 * width : 5 * width], ((1,), (0,))).astype(BF16)


def self_attend(tokens, gain_rows, bias, weight, head):
    rows, width = tokens.shape
    low = jax.ShapeDtypeStruct((rows, width), BF16)
    weight_spec = pl.BlockSpec((width, 5 * width), lambda i: (0, 0))
    return pl.pallas_call(
        partial(self_kernel, head),
        out_shape=(
            jax.ShapeDtypeStruct((rows, 3 * width), BF16),
            low,
            low,
            jax.ShapeDtypeStruct((rows, width), F32),
            low,
            low,
        ),
        grid=(1,),
        in_specs=[
            pl.BlockSpec(tokens.shape, lambda i: (0, 0)),
            pl.BlockSpec(gain_rows.shape, lambda i: (0, 0)),
            pl.BlockSpec(bias.shape, lambda i: (0, 0, 0)),
            weight_spec,
        ],
        out_specs=(pl.BlockSpec((rows, 3 * width), lambda i: (0, 0)),)
        + (pl.BlockSpec((rows, width), lambda i: (0, 0)),) * 5,
        compiler_params=pltpu.CompilerParams(vmem_limit_bytes=56 * 2**20),
        name="self_attend",
    )(tokens, gain_rows, bias, weight)


def self_back_kernel(head, tokens_ref, gain_ref, bias_ref, weight_ref, qkv_ref, stream_ref, dq_ref, dstream_ref, dqkv_ref, low_ref, dinput_ref, score_ref, dgain_ref):
    width = tokens_ref.shape[1]
    rows = tokens_ref.shape[0]
    d_cross = dot(dq_ref[...], weight_ref[:, 4 * width : 5 * width], ((1,), (1,)))
    d_stream, gain_cross = norm_gradient(stream_ref[...], gain_ref[1:2, :], d_cross)
    d_stream = d_stream + dstream_ref[...]
    low = d_stream.astype(BF16)
    low_ref[...] = low
    d_mixed = dot(low, weight_ref[:, 3 * width : 4 * width], ((1,), (1,))).astype(BF16)
    lanes = score_ref.shape[1]
    place = lax.broadcasted_iota(jnp.int32, (rows, lanes), 0) + lax.broadcasted_iota(
        jnp.int32, (rows, lanes), 1
    )
    mirror = (place == rows - 1).astype(F32).astype(BF16)
    sums = []
    for pair in range(width // (2 * head)):
        query, key, value, weights = pair_weights(qkv_ref, bias_ref, pair, head, width)
        at = slice(pair * 2 * head, (pair + 1) * 2 * head)
        spread = pair_spread(d_mixed[:, at], head)
        d_value = dot(weights.astype(BF16), spread, ((0,), (0,)))
        d_weights = dot(spread, value, ((1,), (1,)))
        inner = jnp.sum(weights * d_weights, axis=-1, keepdims=True)
        d_score = (weights * (d_weights - inner)).astype(BF16)
        reverse = dot(d_score, mirror, ((1,), (0,)))
        for h in range(2):
            turned = pltpu.roll(reverse[h * rows : (h + 1) * rows], 0, 1, stride=1, stride_axis=0)
            sums.append(jnp.sum(turned, axis=0, keepdims=True))
        d_query = pair_pick(dot(d_score, key, ((1,), (0,))), head)
        d_key = dot(d_score, query, ((0,), (0,)))
        dqkv_ref[:, at] = d_query.astype(BF16)
        dqkv_ref[:, width + at.start : width + at.stop] = d_key.astype(BF16)
        dqkv_ref[:, 2 * width + at.start : 2 * width + at.stop] = d_value.astype(BF16)
    d_normed = jnp.zeros((rows, width), F32)
    for k in range(3):
        at = slice(k * width, (k + 1) * width)
        d_normed = d_normed + dot(dqkv_ref[:, at], weight_ref[:, at], ((1,), (1,)))
    d_input, gain_self = norm_gradient(tokens_ref[...].astype(F32), gain_ref[0:1, :], d_normed)
    dinput_ref[...] = d_input + d_stream
    sums.append(jnp.zeros((score_ref.shape[0] - len(sums), lanes), F32))
    score_ref[...] = jnp.concatenate(sums, axis=0)
    dgain_ref[...] = jnp.concatenate([gain_self, gain_cross, jnp.zeros((6, width), F32)], axis=0)


def self_back(tokens, gain_rows, bias, weight, qkv, stream, d_query, d_stream, head):
    rows, width = tokens.shape

    def whole(shape):
        return pl.BlockSpec(shape, lambda i: (0,) * len(shape))

    shapes = (
        jax.ShapeDtypeStruct(qkv.shape, BF16),
        jax.ShapeDtypeStruct(tokens.shape, BF16),
        jax.ShapeDtypeStruct(tokens.shape, F32),
        jax.ShapeDtypeStruct((-(-bias.shape[0] // 8) * 8, -(-rows // 128) * 128), F32),
        jax.ShapeDtypeStruct((8, width), F32),
    )
    return pl.pallas_call(
        partial(self_back_kernel, head),
        out_shape=shapes,
        grid=(1,),
        in_specs=[
            whole(tokens.shape),
            whole(gain_rows.shape),
            whole(bias.shape),
            whole((width, 5 * width)),
            whole(qkv.shape),
            whole(tokens.shape),
            whole(tokens.shape),
            whole(tokens.shape),
        ],
        out_specs=tuple(whole(shape.shape) for shape in shapes),
        compiler_params=pltpu.CompilerParams(vmem_limit_bytes=56 * 2**20),
        name="self_back",
    )(tokens, gain_rows, bias, weight, qkv, stream, d_query, d_stream)


def pick_chunk(full, head, rows, start):
    chunk = full.shape[1]
    first = start // rows
    lane = (lax.broadcasted_iota(jnp.int32, (head, chunk), 1) + start) // rows - first
    out = full[:head]
    for h in range(1, full.shape[0] // head):
        out = jnp.where(lane == h, full[h * head : (h + 1) * head], out)
    return out


def over_rows(value, reduce):
    rows, lanes = value.shape
    if rows % 64 == 0:
        value = reduce(value.reshape(8, rows // 8, lanes), axis=0)
    if value.shape[0] % 8 == 0:
        value = reduce(value.reshape(-1, 8, lanes), axis=0)
    return reduce(value, axis=0, keepdims=True)


def each_query(here_ref, queries, store):
    near = queries // 4

    def flush(at, carry):
        y = jnp.bitwise_xor(here_ref[1], at // near)
        j = at % near * 4 + 2 * y
        store(at, j + here_ref[0], j + 1 - here_ref[0])
        return carry

    lax.fori_loop(0, queries // 2, flush, 0)


def either(index, a_ref, b_ref):
    count = a_ref.shape[0]
    return jnp.where(index < count, a_ref[index % count], b_ref[index % count])


def attend_kernel(plen, head, rows, asker_ref, owner_ref, here_ref, qa_ref, qb_ref, kv_ref, mine_ref, other_ref, acc, top, total, stat):
    step = pl.program_id(1)
    queries = 2 * qa_ref.shape[0]
    width = GROUP * head

    @pl.when(step == 0)
    def _():
        acc[...] = jnp.zeros_like(acc)
        top[...] = jnp.full_like(top, FLOOR)
        total[...] = jnp.zeros_like(total)

    @pl.when((step == 0) & (pl.program_id(0) == 0))
    def _():
        stat[...] = jnp.zeros_like(stat)

    lanes = GROUP * rows
    chunk = min(CHUNK, lanes)

    def begin(unit):
        p, c = divmod(unit, lanes // chunk)
        if c == 0:
            spreads[p] = spread_heads(either(asker_ref[step * BLOCK + p], qa_ref, qb_ref), head)
            turned[p] = kv_ref[p * plen : (p + 1) * plen, width:].T
        keys = kv_ref[p * plen : (p + 1) * plen, :width]
        return dot(keys, spreads[p][c * chunk : (c + 1) * chunk], ((1,), (1,)))

    def finish(unit, scores):
        p, c = divmod(unit, lanes // chunk)
        owner = owner_ref[step * BLOCK + p]
        at = pl.ds(c * chunk, chunk)
        first, last = c * chunk // rows, ((c + 1) * chunk - 1) // rows
        here = over_rows(scores, jnp.max)
        raised = jnp.exp(scores - here)
        here_total = over_rows(raised, jnp.sum)
        full = dot(turned[p][first * head : (last + 1) * head], raised.astype(BF16), ((1,), (0,)))
        mixed = pick_chunk(full, head, rows, c * chunk)
        old = top[owner, :, at]
        new = jnp.maximum(old, here)
        old_scale, here_scale = jnp.exp(old - new), jnp.exp(here - new)
        top[owner, :, at] = new
        total[owner, :, at] = total[owner, :, at] * old_scale + here_total * here_scale
        acc[owner, :, at] = acc[owner, :, at] * old_scale + mixed * here_scale

    spreads, turned = {}, {}
    units = BLOCK * (lanes // chunk)
    waiting = [begin(u) for u in range(min(AHEAD, units))]
    for unit in range(units):
        if unit + AHEAD < units:
            waiting.append(begin(unit + AHEAD))
        finish(unit, waiting.pop(0))

    @pl.when(step == pl.num_programs(1) - 1)
    def _():
        base = pl.program_id(0) * 5
        body = pl.ds(pl.multiple_of(pl.program_id(0) * head, head), head)

        def keep(j, carry):
            for t, part in enumerate(split_parts(top[j], 3) + split_parts(total[j], 2)):
                stat[j, pl.ds(base + t, 1), :] = part
            return carry

        def store(at, mine, other):
            mine_ref[at, body, :] = acc[mine].astype(BF16)
            other_ref[at, body, :] = acc[other].astype(BF16)

        lax.fori_loop(0, queries, keep, 0)
        each_query(here_ref, queries, store)

    @pl.when((step == pl.num_programs(1) - 1) & (pl.program_id(0) == pl.num_programs(0) - 1))
    def _():
        first = mine_ref.shape[1] - STAT_ROWS

        def store(at, mine, other):
            mine_ref[at, first:, :] = stat[mine].astype(BF16)
            other_ref[at, first:, :] = stat[other].astype(BF16)

        each_query(here_ref, queries, store)


def attend(asker, owner, here, plane, across, kv, plen, head):
    near, rows, columns = plane.shape
    queries = 2 * near
    width = GROUP * head
    slots = kv.shape[0] // plen
    lanes = GROUP * rows
    groups = columns // width
    out = jax.ShapeDtypeStruct((near, groups * head + STAT_ROWS, lanes), BF16)
    q_spec = pl.BlockSpec((near, rows, width), lambda g, b, *_: (0, 0, g))
    return pl.pallas_call(
        partial(attend_kernel, plen, head, rows),
        out_shape=(out, out),
        grid_spec=pltpu.PrefetchScalarGridSpec(
            num_scalar_prefetch=3,
            grid=(groups, slots // BLOCK),
            in_specs=[
                q_spec,
                q_spec,
                pl.BlockSpec((BLOCK * plen, 2 * width), lambda g, b, *_: (b, g)),
            ],
            out_specs=(pl.BlockSpec(out.shape, lambda g, b, *_: (0, 0, 0)),) * 2,
            scratch_shapes=[
                pltpu.VMEM((queries, head, lanes), F32),
                pltpu.VMEM((queries, 1, lanes), F32),
                pltpu.VMEM((queries, 1, lanes), F32),
                pltpu.VMEM((queries, STAT_ROWS, lanes), F32),
            ],
        ),
        compiler_params=pltpu.CompilerParams(vmem_limit_bytes=60 * 2**20),
        cost_estimate=pl.CostEstimate(
            flops=16 * rows * kv.shape[0] * columns,
            bytes_accessed=4 * kv.shape[0] * columns,
            transcendentals=rows * kv.shape[0] * GROUP * groups,
        ),
        name="attend",
    )(asker, owner, here, plane, across, kv)


def read_stats(stat, g):
    at = 5 * g
    return (
        stat[at : at + 1] + stat[at + 1 : at + 2] + stat[at + 2 : at + 3],
        stat[at + 3 : at + 4] + stat[at + 4 : at + 5],
    )


def merge_kernel(head, a_ref, b_ref, out_ref):
    body = a_ref.shape[1] - STAT_ROWS
    for i in range(a_ref.shape[0]):
        stat_a, stat_b = a_ref[i, body:, :].astype(F32), b_ref[i, body:, :].astype(F32)
        rows = []
        for g in range(body // head):
            at = slice(g * head, (g + 1) * head)
            (top_a, sum_a), (top_b, sum_b) = read_stats(stat_a, g), read_stats(stat_b, g)
            top = jnp.maximum(top_a, top_b)
            w_a, w_b = jnp.exp(top_a - top), jnp.exp(top_b - top)
            out_ref[i, at, :] = (
                a_ref[i, at, :].astype(F32) * w_a + b_ref[i, at, :].astype(F32) * w_b
            ).astype(BF16)
            rows += split_parts(top, 3) + split_parts(sum_a * w_a + sum_b * w_b, 2)
        rows.append(jnp.zeros((STAT_ROWS - len(rows), rows[0].shape[1]), F32))
        out_ref[i, body:, :] = jnp.concatenate(rows, axis=0).astype(BF16)


def core_kernel(head, a_ref, b_ref, near_ref, far_ref):
    @pl.when(pl.program_id(0) < 2)
    def _():
        merge_kernel(head, a_ref, b_ref, far_ref)

    @pl.when(pl.program_id(0) >= 2)
    def _():
        merge_kernel(head, a_ref, b_ref, near_ref)


def core_merge(kept, came, head):
    block = (kept.shape[0] // 4,) + kept.shape[1:]
    out = jax.ShapeDtypeStruct((kept.shape[0] // 2,) + kept.shape[1:], BF16)
    return pl.pallas_call(
        partial(core_kernel, head),
        out_shape=(out, out),
        grid=(4,),
        in_specs=[pl.BlockSpec(block, lambda i: ((i + 2) % 4, 0, 0))] * 2,
        out_specs=(
            pl.BlockSpec(block, lambda i: (jnp.maximum(i - 2, 0), 0, 0)),
            pl.BlockSpec(block, lambda i: (jnp.minimum(i, 1), 0, 0)),
        ),
        cost_estimate=pl.CostEstimate(flops=4 * kept.size, bytes_accessed=6 * kept.size, transcendentals=0),
        name="core_merge",
    )(kept, came)


def near_merge(kept, came, head):
    spec = pl.BlockSpec((kept.shape[0] // 2,) + kept.shape[1:], lambda i: (i, 0, 0))
    return pl.pallas_call(
        partial(merge_kernel, head),
        out_shape=jax.ShapeDtypeStruct(kept.shape, BF16),
        grid=(2,),
        in_specs=[spec, spec],
        out_specs=spec,
        cost_estimate=pl.CostEstimate(flops=4 * kept.size, bytes_accessed=6 * kept.size, transcendentals=0),
        name="near_merge",
    )(kept, came)


def join_parts(ref, g, head):
    count, rows, _ = ref.shape
    at = slice(g * head, (g + 1) * head)
    found = [read_stats(ref[i, rows - STAT_ROWS :, :].astype(F32), g) for i in range(count)]
    top = found[0][0]
    for i in range(1, count):
        top = jnp.maximum(top, found[i][0])
    weights = [jnp.exp(found[i][0] - top) for i in range(count)]
    whole = found[0][1] * weights[0]
    mixed = ref[0, at, :].astype(F32) * weights[0]
    for i in range(1, count):
        whole = whole + found[i][1] * weights[i]
        mixed = mixed + ref[i, at, :].astype(F32) * weights[i]
    return mixed / whole, top + jnp.log(whole)


def ffn_kernel(head, arrived_ref, stream_ref, cot_ref, gain_ref, cross_ref, up_ref, down_ref, payload_ref, out_ref, dstream_ref, dgain_ref, mixed_ref, low_ref, normed_ref, dinner_ref, active_ref, full_ref, log_ref, total_ref, back_ref):
    rows, width = stream_ref.shape
    groups = (arrived_ref.shape[1] - STAT_ROWS) // head
    wide = GROUP * head
    fold = pl.program_id(0)

    @pl.when(fold == 0)
    def _():
        for g in range(groups):
            part, log = join_parts(arrived_ref, g, head)
            log_ref[g : g + 1, :] = log
            turned = part.T
            heads = [turned[h * rows : (h + 1) * rows] for h in range(GROUP)]
            full_ref[:, g * wide : (g + 1) * wide] = jnp.concatenate(heads, axis=1)
        mixed = full_ref[...].astype(BF16)
        mixed_ref[...] = mixed
        stream = stream_ref[...] + dot(mixed, cross_ref[...], ((1,), (0,)))
        dstream_ref[...] = stream
        total_ref[...] = stream
        back_ref[...] = jnp.zeros_like(back_ref)
        normed_ref[...] = (stream * scale_rows(stream) * gain_ref[2:3, :]).astype(BF16)

    inner = dot(normed_ref[...], up_ref[...], ((1,), (0,)))
    square = inner * inner
    bent = jnp.tanh(0.7978845608028654 * (inner + 0.044715 * square * inner))
    half = 0.5 * (1.0 + bent)
    active = (inner * half).astype(BF16)
    slope = half + 0.5 * inner * (1.0 - bent * bent) * (
        0.7978845608028654 * (1.0 + 0.134145 * square)
    )
    active_ref[...] = active
    total_ref[...] += dot(active, down_ref[...], ((1,), (0,)))
    d_inner = (dot(cot_ref[...], down_ref[...], ((1,), (1,))) * slope).astype(BF16)
    dinner_ref[...] = d_inner
    back_ref[...] += dot(d_inner, up_ref[...], ((1,), (1,)))

    @pl.when(fold == pl.num_programs(0) - 1)
    def _():
        out_ref[...] = total_ref[...].astype(BF16)
        d_stream, gain = norm_gradient(dstream_ref[...], gain_ref[2:3, :], back_ref[...])
        d_stream = d_stream + cot_ref[...].astype(F32)
        dstream_ref[...] = d_stream
        dgain_ref[...] = jnp.concatenate([gain, jnp.zeros((7, width), F32)], axis=0)
        low = d_stream.astype(BF16)
        low_ref[...] = low
        d_mixed = dot(low, cross_ref[...], ((1,), (1,))).astype(BF16)
        payload_ref[:rows, :] = d_mixed
        for g in range(groups):
            columns = slice(g * wide, (g + 1) * wide)
            product = (d_mixed[:, columns].astype(F32) * full_ref[:, columns]).T
            delta = [
                jnp.sum(product[h * head : (h + 1) * head], axis=0, keepdims=True)
                for h in range(GROUP)
            ]
            parts = split_parts(log_ref[g : g + 1, :], 3) + split_parts(jnp.concatenate(delta, axis=1), 2)
            lines = [
                part[:, t * wide : (t + 1) * wide]
                for part in parts
                for t in range(GROUP * rows // wide)
            ]
            lines.append(jnp.zeros((STAT_ROWS - len(lines), wide), F32))
            payload_ref[rows:, columns] = jnp.concatenate(lines, axis=0).astype(BF16)


def feed_forward(arrived, stream, grads, gain_rows, weight, head):
    rows, width = stream.shape
    hidden = (weight.shape[1] - width) // 2
    folds = hidden // width

    def whole(shape):
        return pl.BlockSpec(shape, lambda k: (0,) * len(shape))

    low = jax.ShapeDtypeStruct((rows, width), BF16)
    long = jax.ShapeDtypeStruct((rows, hidden), BF16)
    shapes = (
        jax.ShapeDtypeStruct((rows + STAT_ROWS, width), BF16),
        low,
        jax.ShapeDtypeStruct((rows, width), F32),
        jax.ShapeDtypeStruct((8, width), F32),
        low,
        low,
        low,
    )
    fold_spec = pl.BlockSpec((rows, width), lambda k: (0, k))
    return pl.pallas_call(
        partial(ffn_kernel, head),
        out_shape=shapes + (long, long),
        grid=(folds,),
        in_specs=[whole(v.shape) for v in (arrived, stream, grads, gain_rows)]
        + [
            pl.BlockSpec((width, width), lambda k: (0, 0)),
            pl.BlockSpec((width, width), lambda k: (0, 1 + k)),
            pl.BlockSpec((width, width), lambda k: (0, 1 + folds + k)),
        ],
        out_specs=tuple(whole(shape.shape) for shape in shapes) + (fold_spec, fold_spec),
        scratch_shapes=[
            pltpu.VMEM((rows, width), F32),
            pltpu.VMEM((8, GROUP * rows), F32),
            pltpu.VMEM((rows, width), F32),
            pltpu.VMEM((rows, width), F32),
        ],
        compiler_params=pltpu.CompilerParams(vmem_limit_bytes=56 * 2**20),
        cost_estimate=pl.CostEstimate(
            flops=4 * rows * weight.size, bytes_accessed=2 * weight.size, transcendentals=rows * hidden
        ),
        name="feed_forward",
    )(arrived, stream, grads, gain_rows, weight, weight, weight)


def ffn_terms_kernel(folds, *refs):
    out_ref = refs[-1]
    tile = pl.program_id(0)
    for first, last, left, right in ((0, 1, 0, 1), (1, 1 + folds, 2, 3), (1 + folds, 1 + 2 * folds, 4, 5)):

        @pl.when((tile >= first) & (tile < last))
        def _(left=left, right=right):
            a, b = refs[2 * left : 2 * left + 2], refs[2 * right : 2 * right + 2]
            found = dot(a[0][...], b[0][...], ((0,), (0,))) + dot(a[1][...], b[1][...], ((0,), (0,)))
            out_ref[...] = found.astype(BF16)


def ffn_terms(parts, grads, hidden):
    width = grads[0].shape[1]
    folds = hidden // width

    def spec(value, start):
        if start is None:
            return pl.BlockSpec((value.shape[0], width), lambda t: (0, 0))
        return pl.BlockSpec((value.shape[0], width), lambda t: (0, jnp.clip(t - start, 0, folds - 1)))

    operands, specs = [], []
    for values, start in zip([*zip(*parts), grads], (None, None, None, 1, 1 + folds, None)):
        for value in values:
            operands.append(value)
            specs.append(spec(value, start))
    return pl.pallas_call(
        partial(ffn_terms_kernel, folds),
        out_shape=jax.ShapeDtypeStruct((width, width + 2 * hidden), BF16),
        grid=(1 + 2 * folds,),
        in_specs=specs,
        out_specs=pl.BlockSpec((width, width), lambda t: (0, t)),
        compiler_params=pltpu.CompilerParams(vmem_limit_bytes=60 * 2**20),
        cost_estimate=pl.CostEstimate(
            flops=6 * width * width * width, bytes_accessed=8 * width * hidden, transcendentals=0
        ),
        name="ffn_terms",
    )(*operands)


def attend_back_kernel(plen, head, rows, asker_ref, owner_ref, here_ref, qa_ref, qb_ref, doa_ref, dob_ref, sa_ref, sb_ref, kv_ref, *refs):
    step = pl.program_id(1)
    dkv_ref, mine_ref, other_ref, acc, log, delta = refs[-6:]
    held_ref = refs[0] if len(refs) > 6 else None
    near = qa_ref.shape[0]
    queries = 2 * near
    width = GROUP * head

    @pl.when(step == 0)
    def _():
        acc[...] = jnp.zeros_like(acc)
        third = (GROUP * rows) // width

        def fill(j, carry):
            stat = either(j, sa_ref, sb_ref).astype(F32)
            row = lax.broadcasted_iota(jnp.int32, stat.shape, 0)
            for at, ref, count in ((0, log, 3), (3 * third, delta, 2)):
                pieces = []
                for t in range(third):
                    wanted = row == at + t
                    for k in range(1, count):
                        wanted = wanted | (row == at + k * third + t)
                    pieces.append(jnp.sum(jnp.where(wanted, stat, 0.0), axis=0, keepdims=True))
                ref[j] = jnp.concatenate(pieces, axis=1)
            return carry

        lax.fori_loop(0, queries, fill, 0)

    lanes = GROUP * rows
    chunk = min(CHUNK, lanes)

    def begin(unit):
        p, c = divmod(unit, lanes // chunk)
        rows_at = slice(p * plen, (p + 1) * plen)
        if c == 0:
            asker = asker_ref[step * BLOCK + p]
            q_spread[p] = spread_heads(either(asker, qa_ref, qb_ref), head)
            do_spread[p] = spread_heads(either(asker, doa_ref, dob_ref), head)
            turned[p] = kv_ref[rows_at, :width].T
        at = slice(c * chunk, (c + 1) * chunk)
        return (
            dot(kv_ref[rows_at, :width], q_spread[p][at], ((1,), (1,))),
            dot(kv_ref[rows_at, width:], do_spread[p][at], ((1,), (1,))),
        )

    def finish(unit, found):
        scores, d_soft = found
        p, c = divmod(unit, lanes // chunk)
        owner, asker = owner_ref[step * BLOCK + p], asker_ref[step * BLOCK + p]
        at = pl.ds(c * chunk, chunk)
        cut = slice(c * chunk, (c + 1) * chunk)
        first, last = c * chunk // rows, ((c + 1) * chunk - 1) // rows
        soft = jnp.exp(scores - log[asker, :, at])
        d_score = (soft * (d_soft - delta[asker, :, at])).astype(BF16)
        d_value = dot(soft.astype(BF16), do_spread[p][cut], ((1,), (0,)))
        d_key = dot(d_score, q_spread[p][cut], ((1,), (0,)))
        sums[p] = (d_key, d_value) if c == 0 else (sums[p][0] + d_key, sums[p][1] + d_value)
        full = dot(turned[p][first * head : (last + 1) * head], d_score, ((1,), (0,)))
        acc[owner, :, at] += pick_chunk(full, head, rows, c * chunk)
        if c == lanes // chunk - 1:
            rows_at = slice(p * plen, (p + 1) * plen)
            for found, columns in zip(sums[p], (slice(0, width), slice(width, 2 * width))):
                if held_ref is not None:
                    found = found + held_ref[rows_at, columns].astype(F32)
                dkv_ref[rows_at, columns] = found.astype(BF16)

    q_spread, do_spread, turned, sums = {}, {}, {}, {}
    units = BLOCK * (lanes // chunk)
    waiting = [begin(u) for u in range(min(AHEAD, units))]
    for unit in range(units):
        if unit + AHEAD < units:
            waiting.append(begin(unit + AHEAD))
        finish(unit, waiting.pop(0))

    @pl.when(step == pl.num_programs(1) - 1)
    def _():
        def store(at, mine, other):
            mine_ref[at, 0] = acc[mine].astype(BF16)
            other_ref[at, 0] = acc[other].astype(BF16)

        each_query(here_ref, queries, store)


def attend_back(asker, owner, here, queries_in, grads_in, kv, held, plen, head):
    near, rows, columns = queries_in[0].shape
    queries = 2 * near
    width = GROUP * head
    slots = kv.shape[0] // plen
    lanes = GROUP * rows
    groups = columns // width
    block = (near, 1, head, lanes)
    out = jax.ShapeDtypeStruct((near, groups, head, lanes), BF16)
    q_spec = pl.BlockSpec((near, rows, width), lambda g, b, *_: (0, 0, g))
    stat_spec = pl.BlockSpec((near, STAT_ROWS, width), lambda g, b, *_: (0, rows // STAT_ROWS, g))
    kv_spec = pl.BlockSpec((BLOCK * plen, 2 * width), lambda g, b, *_: (b, g))
    operands = [*queries_in, *grads_in, *grads_in, kv]
    specs = [q_spec] * 4 + [stat_spec] * 2 + [kv_spec]
    if held is not None:
        operands.append(held)
        specs.append(kv_spec)
    return pl.pallas_call(
        partial(attend_back_kernel, plen, head, rows),
        out_shape=(jax.ShapeDtypeStruct(kv.shape, BF16), out, out),
        grid_spec=pltpu.PrefetchScalarGridSpec(
            num_scalar_prefetch=3,
            grid=(groups, slots // BLOCK),
            in_specs=specs,
            out_specs=(
                kv_spec,
                pl.BlockSpec(block, lambda g, b, *_: (0, g, 0, 0)),
                pl.BlockSpec(block, lambda g, b, *_: (0, g, 0, 0)),
            ),
            scratch_shapes=[
                pltpu.VMEM((queries, head, lanes), F32),
                pltpu.VMEM((queries, 1, lanes), F32),
                pltpu.VMEM((queries, 1, lanes), F32),
            ],
        ),
        input_output_aliases={} if held is None else {3 + len(operands) - 1: 0},
        compiler_params=pltpu.CompilerParams(vmem_limit_bytes=60 * 2**20),
        cost_estimate=pl.CostEstimate(
            flops=40 * rows * kv.shape[0] * columns,
            bytes_accessed=8 * kv.shape[0] * columns,
            transcendentals=rows * kv.shape[0] * GROUP * groups,
        ),
        name="attend_back",
    )(asker, owner, here, *operands)


def source_kernel(keep_ref, fetch_ref, *refs):
    weight_ref, out_ref = refs[-2:]
    for p, ref in enumerate(refs[:-2]):
        kept = keep_ref[pl.program_id(0) * (len(refs) - 2) + p]

        @pl.when(kept == 0)
        def _(p=p):
            out_ref[p] = jnp.zeros_like(out_ref[p])

        @pl.when(kept != 0)
        def _(p=p, ref=ref):
            out_ref[p] = dot(ref[...], weight_ref[...], ((1,), (1,))).astype(BF16)


def fetch_order(refresh):
    slots = refresh.shape[0]
    several = 4 if slots % 4 == 0 else 1
    order = jnp.arange(slots).reshape(-1, several)
    kept = refresh.reshape(-1, several) != 0
    fetch = lax.cummax(jnp.where(kept, order, order[:1]), axis=0)
    return several, fetch.astype(jnp.int32).reshape(-1)


def source_grads(refresh, several, fetch, dkv, weight, plen):
    slots = refresh.shape[0]
    model_width = weight.shape[0]

    def spec(p):
        return pl.BlockSpec((plen, dkv.shape[1]), lambda r, keep, fetch: (fetch[r * several + p], 0))

    return pl.pallas_call(
        source_kernel,
        out_shape=jax.ShapeDtypeStruct((slots, plen, model_width), BF16),
        grid_spec=pltpu.PrefetchScalarGridSpec(
            num_scalar_prefetch=2,
            grid=(slots // several,),
            in_specs=[spec(p) for p in range(several)] + [pl.BlockSpec(weight.shape, lambda r, *_: (0, 0))],
            out_specs=pl.BlockSpec((several, plen, model_width), lambda r, *_: (r, 0, 0)),
        ),
        compiler_params=pltpu.CompilerParams(vmem_limit_bytes=60 * 2**20),
        cost_estimate=pl.CostEstimate(
            flops=slots * plen * model_width * 2 * model_width,
            bytes_accessed=4 * slots * plen * model_width,
            transcendentals=0,
        ),
        name="source_grads",
    )(refresh, fetch, *([dkv] * several), weight)


def outer_kernel(starts, split, added, half_ref, *refs):
    count = len(starts) - 1
    outs = refs[-2:]
    tile = pl.program_id(0)
    for k in range(count):

        @pl.when((tile >= starts[k]) & (tile < starts[k + 1]))
        def _(k=k):
            found = dot(refs[2 * k][...], refs[2 * k + 1][...], ((0,), (0,)))
            side = 0 if k < split else 1
            if added:
                found = found + refs[2 * count + side][...].astype(F32)
            outs[side][...] = found.astype(BF16)


def outer(half, first, second, came=None):
    pairs = first + second
    rows, total_rows = pairs[0][0].shape
    width = total_rows // 2
    counts = [right.shape[1] // 2 // width for _, right in pairs]
    starts = [sum(counts[:k]) for k in range(len(counts) + 1)]
    edge = starts[len(first)]
    operands, specs = [], []
    for k, (left, right) in enumerate(pairs):

        def right_map(t, half_ref, start=starts[k], count=counts[k]):
            return (0, half_ref[0] * count + jnp.clip(t - start, 0, count - 1))

        operands += [left, right]
        specs += [
            pl.BlockSpec((rows, total_rows), lambda t, half_ref: (0, 0)),
            pl.BlockSpec((rows, width), right_map),
        ]
    sides = (
        pl.BlockSpec((total_rows, width), lambda t, half_ref: (0, jnp.minimum(t, edge - 1))),
        pl.BlockSpec((total_rows, width), lambda t, half_ref: (0, jnp.maximum(t - edge, 0))),
    )
    if came is not None:
        operands += came
        specs += sides
    size = total_rows * starts[-1] * width
    return pl.pallas_call(
        partial(outer_kernel, starts, len(first), came is not None),
        out_shape=(
            jax.ShapeDtypeStruct((total_rows, edge * width), BF16),
            jax.ShapeDtypeStruct((total_rows, (starts[-1] - edge) * width), BF16),
        ),
        grid_spec=pltpu.PrefetchScalarGridSpec(
            num_scalar_prefetch=1, grid=(starts[-1],), in_specs=specs, out_specs=sides
        ),
        compiler_params=pltpu.CompilerParams(vmem_limit_bytes=60 * 2**20),
        cost_estimate=pl.CostEstimate(flops=2 * rows * size, bytes_accessed=4 * size, transcendentals=0),
        name="outer",
    )(half, *operands)


def flip(value, bit):
    count = lax.axis_size("pass")
    return lax.ppermute(value, "pass", [(i, i ^ bit) for i in range(count)])


def after(value, *others):
    return lax.optimization_barrier((value,) + others)


def line_sends(block):
    count = lax.axis_size("pass")
    rings = [[(i, (i + 4 * k) % count) for i in range(count)] for k in range(1, count // 4)]
    return [lax.ppermute(block, "pass", ring) for ring in rings]


def gather_place(query, own, count):
    major = count // 4
    turn = jnp.mod(own // 4 - query // 4, major)
    return turn + major * ((own // 2) % 2 != (query // 2) % 2) + 2 * major * (own % 2 != query % 2)


def line_exchange(parts):
    count = lax.axis_size("pass")
    groups = [[r + 4 * k for k in range(count // 4)] for r in range(4)]
    return lax.all_to_all(
        parts, "pass", split_axis=0, concat_axis=0, tiled=True, axis_index_groups=groups
    )


def in_order(own, came, place, axis):
    return jnp.stack([jnp.where(place == 0, own, came), jnp.where(place == 0, came, own)], axis=axis)


def gather_rows(block):
    n_dp, count = lax.axis_size("dp"), lax.axis_size("pass")
    if n_dp != 2:
        return lax.all_gather(block, ("dp", "pass"), axis=0, tiled=True)
    own, dp = lax.axis_index("pass"), lax.axis_index("dp")
    major, core, y = count // 4, own % 2, own // 2 % 2
    pieces = [block, *line_sends(block)]
    line = jnp.zeros((major,) + block.shape, block.dtype)
    for k, piece in enumerate(pieces):
        line = lax.dynamic_update_index_in_dim(line, piece, jnp.mod(own // 4 - k, major), 0)
    cut = block.shape[1] // 256 * 128
    left, right = line[..., :cut], line[..., cut:]
    left, right = in_order(left, flip(left, 2), y, 1), in_order(right, dp_flip(right), dp, 0)
    left, right = in_order(left, dp_flip(left), dp, 0), in_order(right, flip(right, 2), y, 2)
    full = [in_order(part, flip(part, 1), core, 3) for part in (left, right)]
    return jnp.concatenate([part.reshape(-1, part.shape[-1]) for part in full], axis=1)


def line_scatter(parts):
    count = lax.axis_size("pass")
    major, place = count // 4, lax.axis_index("pass") // 4
    came = []
    for k in range(1, major):
        sent = lax.dynamic_index_in_dim(parts, jnp.mod(place + k, major), 0, keepdims=False)
        came.append(lax.ppermute(sent, "pass", [(i, (i + 4 * k) % count) for i in range(count)]))
    return lax.dynamic_index_in_dim(parts, place, 0, keepdims=False), came


def swap_send(value, place, axis, send):
    kept = lax.dynamic_index_in_dim(value, place, axis, keepdims=False)
    return kept, send(lax.dynamic_index_in_dim(value, 1 - place, axis, keepdims=False))


def add_low(kept, came):
    return (kept.astype(F32) + came.astype(F32)).astype(BF16)


def rows_by_owner(value):
    n_dp, count = lax.axis_size("dp"), lax.axis_size("pass")
    rows, columns = value.shape
    return value.reshape(n_dp, count // 4, 2, rows // (n_dp * count // 2), columns)


def dp_step(value, bit):
    pairs = [(i, i ^ bit) for i in range(lax.axis_size("dp"))]
    return lax.ppermute(value, "dp", pairs)


def dp_flip(value):
    return lax.ppermute(value, "dp", [(0, 1), (1, 0)])


def dp_send(value):
    if lax.axis_size("dp") == 2:
        return swap_send(value, lax.axis_index("dp"), 0, dp_flip)
    total = lax.psum_scatter(value, "dp", scatter_dimension=0, tiled=False)
    return total, jnp.zeros_like(total)


def near_send(value, axis):
    return swap_send(value, lax.axis_index("pass") // 2 % 2, axis, lambda v: flip(v, 2))


def over_line(value):
    return jnp.sum(line_exchange(value).astype(F32), axis=0)


def own_rows(value, core):
    shard = value.shape[0] // 2
    parts = value.reshape(2, shard, value.shape[1])
    kept = lax.dynamic_index_in_dim(parts, core, 0, keepdims=False)
    came = flip(lax.dynamic_index_in_dim(parts, 1 - core, 0, keepdims=False), 1)
    return jnp.where(core == 0, kept, came), jnp.where(core == 0, came, kept)


def on_device(
    tokens,
    cotangent,
    passages,
    refresh,
    passage_ids,
    self_query,
    self_key,
    self_value,
    self_out,
    cross_query,
    cross_key,
    cross_value,
    cross_out,
    up_weight,
    down_weight,
    gains,
    rel_table,
):
    both = ("dp", "pass")
    pass_count = lax.axis_size("pass")
    device_id = lax.axis_index(both)
    own_pass = lax.axis_index("pass")
    per_query, plen, model_width = passages.shape
    head_count = rel_table.shape[1]
    head = model_width // head_count
    rows = tokens.shape[0]
    groups = head_count // GROUP
    wide = GROUP * head
    shard = self_query.shape[0]

    def gather(value):
        return lax.all_gather(value, both, axis=0, tiled=True)

    kv_shard = jnp.stack(
        [cross_key.reshape(shard, groups, wide), cross_value.reshape(shard, groups, wide)], axis=2
    ).reshape(shard, 2 * model_width)
    gain_pad = jnp.pad(gains, ((0, 0), (0, 128 - gains.shape[1])))
    first = gather(
        jnp.concatenate([self_query, self_key, self_value, self_out, cross_query, gain_pad], axis=1)
    )
    kv_weight = lax.optimization_barrier(gather_rows(kv_shard))
    encoded = passages.reshape(per_query * plen, model_width)
    kv = matmul(encoded, kv_weight).astype(BF16)
    positions = jnp.arange(rows)
    causal = positions[:, None] >= positions[None, :]
    onehot_low = (
        bucket_of(positions[:, None] - positions[None, :], rel_table.shape[0])[:, :, None]
        == jnp.arange(rel_table.shape[0])[None, None, :]
    ).astype(BF16)
    bias = jnp.einsum("qkb,bh->hqk", onehot_low, rel_table, preferred_element_type=F32)
    bias = jnp.where(causal[None, :, :], bias, FLOOR)
    folds = up_weight.shape[1] // model_width
    total = up_weight.shape[1] // (folds * shard)
    up_fold = up_weight.reshape(shard, total, folds, shard).transpose(0, 2, 1, 3).reshape(shard, -1)
    down_fold = down_weight.reshape(folds, shard, model_width).transpose(1, 0, 2).reshape(shard, -1)
    rest = jnp.concatenate([cross_out, up_fold, down_fold], axis=1)
    several, fetch = fetch_order(refresh)
    first, kv, bias, rest, fetch = after(first, kv, bias, rest, fetch)
    gain_all = first[:, 5 * model_width : 5 * model_width + 3].astype(F32)

    row_ids = device_id * per_query + jnp.arange(per_query)
    owned = jnp.any(passage_ids[:, :, None] == row_ids[None, None, :], axis=1)
    owner = jnp.sum(
        jnp.where(owned, jnp.arange(passage_ids.shape[0])[:, None], 0), axis=0
    ).astype(jnp.int32)
    core = own_pass % 2
    half = core.astype(jnp.int32).reshape(1)
    here = jnp.stack([core, own_pass // 2 % 2]).astype(jnp.int32)
    asker = gather_place(owner, own_pass, pass_count).astype(jnp.int32)

    gain_rows = jnp.pad(gain_all.T, ((0, 5), (0, 0)))
    qkv, mixed_one, normed_self, stream_one, normed_cross, query_two = self_attend(
        tokens, gain_rows, bias, first, head
    )

    cut = rows // 192 * 128

    def merge_send(mine, came):
        near, far = core_merge(mine, came, head)
        return near, flip(far, 2)

    def rows_first(value):
        cube = value.reshape(groups, head, GROUP, -1).transpose(3, 0, 2, 1)
        return cube.reshape(-1, model_width)

    block, last_block = query_two[:cut], query_two[cut:]
    last_block, rest, *sends = after(last_block, rest, *line_sends(block))
    rest = gather(rest)
    line = jnp.stack([block, *sends])
    across, *sends = after(flip(line, 2), *line_sends(last_block))
    plane = jnp.concatenate([line, across])
    q_first = (plane, flip(plane, 1))
    line = jnp.stack([last_block, *sends])
    across = flip(line, 2)
    mine, other = attend(asker, owner, here, *q_first, kv, plen, head)
    across, mine, other = after(across, mine, other)
    came = flip(other, 1)
    plane = jnp.concatenate([line, across])
    q_second = (plane, flip(plane, 1))
    near, came = merge_send(mine, came)
    q_second, near = after(q_second, near)
    mine, other = attend(asker, owner, here, *q_second, kv, plen, head)
    came, mine, other = after(came, mine, other)
    merged, mine, other = after(near_merge(near, came, head), mine, other)
    came_next = flip(other, 1)
    arrived = line_exchange(merged)
    near, came = merge_send(mine, came_next)
    arrived, near, came = after(arrived, near, came)
    merged, arrived = after(near_merge(near, came, head), arrived)
    arrived_last = line_exchange(merged)
    payload_first, out_first, ds_first, gain_first, *terms_first = feed_forward(
        arrived, stream_one[:cut], cotangent[:cut], gain_rows, rest, head
    )
    arrived_last, payload_first = after(arrived_last, payload_first)
    sends = line_sends(payload_first)
    payload, out_last, ds_last, gain_last, *terms_last = feed_forward(
        arrived_last, stream_one[cut:], cotangent[cut:], gain_rows, rest, head
    )
    payload, *sends = after(payload, *sends)
    line_first = jnp.stack([payload_first, *sends])
    across = flip(line_first, 2)
    sends = line_sends(payload)

    block_out = jnp.concatenate([out_first, out_last])
    d_stream_two = jnp.concatenate([ds_first, ds_last])
    d_gain_ffn = gain_first[0] + gain_last[0]
    terms = ffn_terms(
        (terms_first, terms_last), (cotangent[:cut], cotangent[cut:]), up_weight.shape[1]
    )
    across, terms, *sends = after(across, terms, *sends)
    ffn_sums = lax.psum_scatter(terms, both, scatter_dimension=0, tiled=True)
    plane = jnp.concatenate([line_first, across])
    do_first = (plane, flip(plane, 1))
    line = jnp.stack([payload, *sends])
    across = flip(line, 2)

    def half_of(value, came):
        value = (value.astype(F32) + came.astype(F32)).astype(BF16)
        return value[: value.shape[0] // 2], value[value.shape[0] // 2 :]

    dkv, mine, other = attend_back(asker, owner, here, q_first, do_first, kv, None, plen, head)
    across, dkv, mine, other = after(across, dkv, mine, other)
    came = flip(other, 1)
    plane = jnp.concatenate([line, across])
    do_last = (plane, flip(plane, 1))
    near, far = half_of(mine, came)
    came = flip(far, 2)
    do_last, near = after(do_last, near)
    dkv, mine, other = attend_back(asker, owner, here, q_second, do_last, kv, dkv, plen, head)
    came, dkv, mine, other = after(came, dkv, mine, other)
    came_next = flip(other, 1)
    arrived = line_exchange((near.astype(F32) + came.astype(F32)).astype(BF16))
    near, far = half_of(mine, came_next)
    came, dkv = after(flip(far, 2), dkv)
    kept, last = line_scatter((near.astype(F32) + came.astype(F32)).astype(BF16))
    arrived, d_kv, d_stream_two, *last = after(
        arrived, left_t(encoded, dkv).astype(BF16), d_stream_two, *last
    )
    last = sum((part.astype(F32) for part in last), kept.astype(F32))
    dq_parts = [rows_first(jnp.sum(arrived.astype(F32), axis=0)), rows_first(last)]
    d_query_two = jnp.concatenate(dq_parts).astype(BF16)
    def kv_half(at):
        cube = d_kv.reshape(model_width, groups, 2, wide)
        return lax.dynamic_index_in_dim(cube, at, 2, keepdims=False).reshape(model_width, -1)

    kv_came = flip(kv_half(1 - core), 1)
    found = self_back(
        tokens, gain_rows, bias, first, qkv, stream_one, d_query_two, d_stream_two, head
    )
    kv_came, ffn_sums, *found = after(kv_came, ffn_sums, *found)
    d_qkv, grad_one, d_inputs, d_score, gain_terms = found
    late_pairs = [(normed_self, d_qkv)]
    more_pairs = [(mixed_one, grad_one), (normed_cross, d_query_two)]
    late_sent, more_sent = outer(1 - half, late_pairs, more_pairs)
    distance = jnp.mod(jnp.arange(d_score.shape[1]) - (rows - 1), d_score.shape[1])
    of_distance = bucket_of(distance, rel_table.shape[0])
    of_distance = (of_distance[:, None] == jnp.arange(rel_table.shape[0])[None, :]).astype(F32)
    d_table = jnp.dot(d_score, of_distance, precision=lax.Precision.HIGHEST)[:head_count].T
    small = jnp.concatenate([d_table.reshape(-1), gain_terms[0], gain_terms[1], d_gain_ffn])
    small = small.reshape(-1, 128)
    late_sent, more_sent, kv_came = after(late_sent, more_sent, kv_came)
    kv_part = jnp.moveaxis(rows_by_owner(add_low(kv_half(core), kv_came)), 1, 0)
    late_came, more_came, kv_part, came = after(
        flip(late_sent, 1), flip(more_sent, 1), kv_part, flip(small, 1)
    )
    small = small + came

    late, more = outer(half, late_pairs, more_pairs, [late_came, more_came])
    late, more, came, kv_part = after(late, more, flip(small, 2), kv_part)
    small = small + came
    late_kept, late_came = dp_send(rows_by_owner(late))
    more_kept, more_came = near_send(rows_by_owner(more), 2)
    kv_line = line_exchange(kv_part)
    passage_grad = source_grads(refresh, several, fetch, dkv, kv_weight, plen)
    for bit in range((lax.axis_size("dp") - 1).bit_length()):
        small = small + dp_step(small, 1 << bit)
    kv_line, late_came, more_came, passage_grad, small = after(
        kv_line, late_came, more_came, passage_grad, small
    )
    late_kept, late_came = near_send(add_low(late_kept, late_came), 1)
    more_kept, more_came = dp_send(add_low(more_kept, more_came))
    kv_kept, kv_came = dp_send(jnp.sum(kv_line.astype(F32), axis=0).astype(BF16))
    for bit in range(2, (pass_count - 1).bit_length() - 1):
        small = small + flip(small, 1 << bit)
    late_came, more_came, kv_came, small = after(late_came, more_came, kv_came, small)
    came = flip(small, pass_count // 2)
    kv_kept, kv_came = near_send(add_low(kv_kept, kv_came), 0)
    parts = [(late_kept, late_came), (more_kept, more_came)]
    line = line_exchange(jnp.concatenate([add_low(*part) for part in parts], axis=-1))
    ffn_sums = ffn_sums.astype(F32)
    d_up = ffn_sums[:, model_width : model_width + up_weight.shape[1]]
    d_up = d_up.reshape(shard, folds, total, shard).transpose(0, 2, 1, 3).reshape(up_weight.shape)
    d_down = ffn_sums[:, model_width + up_weight.shape[1] :].reshape(shard, folds, model_width)
    d_down = d_down.transpose(1, 0, 2).reshape(down_weight.shape)
    line, kv_came, came, d_up, d_down = after(line, kv_came, came, d_up, d_down)
    small = (small + came).reshape(-1)
    line = jnp.sum(line.astype(F32), axis=0)
    line = jnp.concatenate([line, kv_kept.astype(F32) + kv_came.astype(F32)], axis=1)
    table_grad = small[: d_table.size].reshape(d_table.shape)
    d_gains = small[d_table.size :].reshape(3, -1)
    d_gains = lax.dynamic_slice_in_dim(d_gains, device_id * shard, shard, 1)

    left, right = own_rows(line, core)
    half_width = model_width // 2

    def whole(start, stop):
        cut = slice(start * half_width, stop * half_width)
        return jnp.concatenate([left[:, cut], right[:, cut]], axis=1)

    d_first, d_out_self, d_query_cross = whole(0, 3), whole(3, 4), whole(4, 5)
    d_query_self, d_key_self, d_value_self = jnp.split(d_first, 3, axis=1)
    d_key_cross, d_value_cross = left[:, 5 * half_width :], right[:, 5 * half_width :]
    d_out_cross = ffn_sums[:, :model_width]
    return (
        block_out,
        d_inputs,
        passage_grad,
        d_query_self,
        d_key_self,
        d_value_self,
        d_out_self,
        d_query_cross,
        d_key_cross,
        d_value_cross,
        d_out_cross,
        d_up,
        d_down,
        d_gains.T,
        table_grad,
    )


def solution(mesh):
    split = P(("dp", "pass"), None)
    cube = P(("dp", "pass"), None, None)
    in_specs = (split, split, cube, P(("dp", "pass")), P("dp", None)) + (split,) * 11 + (P(),)
    out_specs = (split, split, cube) + (split,) * 11 + (P(),)
    return jax.shard_map(
        on_device, mesh=mesh, in_specs=in_specs, out_specs=out_specs, check_vma=False
    )
```

```python
from functools import partial

import jax
import jax.numpy as jnp
from jax import lax
from jax.experimental import pallas as pl
from jax.experimental.pallas import tpu as pltpu
from jax.sharding import PartitionSpec as P

F32 = jnp.float32
BF16 = jnp.bfloat16
GROUP = 4
BLOCK = 10
STAT_ROWS = 16
CHUNK = 256
AHEAD = 2
FLOOR = -1e30


def norm_rows(value, gain):
    return value * lax.rsqrt(jnp.mean(value * value, axis=-1, keepdims=True) + 1e-06) * gain


def bucket_of(spread, buckets):
    near_count = buckets // 2
    spread = jnp.maximum(spread, 0).astype(F32)
    bounds = near_count * 8.0 ** (jnp.arange(1, near_count, dtype=F32) / near_count)
    far_bucket = near_count + jnp.sum((spread[..., None] >= bounds).astype(jnp.int32), axis=-1)
    return jnp.where(spread < near_count, spread.astype(jnp.int32), far_bucket)


def matmul(left, right):
    return jnp.dot(left, right, preferred_element_type=F32)


def left_t(left, right):
    return jnp.einsum("td,te->de", left, right, preferred_element_type=F32)


def right_t(left, right):
    return jnp.einsum("te,de->td", left, right, preferred_element_type=F32)


def dot(left, right, dims):
    return lax.dot_general(left, right, (dims, ((), ())), preferred_element_type=F32)


def split_parts(value, count):
    parts = []
    for _ in range(count):
        part = value.astype(BF16).astype(F32)
        parts.append(part)
        value = value - part
    return parts


def spread_heads(rows, head):
    column = lax.broadcasted_iota(jnp.int32, rows.shape, 1) // head
    return jnp.concatenate(
        [jnp.where(column == h, rows, jnp.zeros_like(rows)) for h in range(GROUP)], axis=0
    )


def scale_rows(value):
    return lax.rsqrt(jnp.mean(value * value, axis=-1, keepdims=True) + 1e-06)


def norm_gradient(value, gain, grad):
    scale = scale_rows(value)
    unit = value * scale
    inner = grad * gain
    mean = jnp.mean(inner * unit, axis=-1, keepdims=True)
    return scale * (inner - unit * mean), jnp.sum(grad * unit, axis=0, keepdims=True)


def pair_spread(rows, head):
    first = lax.broadcasted_iota(jnp.int32, rows.shape, 1) < head
    zero = jnp.zeros_like(rows)
    return jnp.concatenate([jnp.where(first, rows, zero), jnp.where(first, zero, rows)], axis=0)


def pair_pick(full, head):
    rows = full.shape[0] // 2
    first = lax.broadcasted_iota(jnp.int32, (rows, full.shape[1]), 1) < head
    return jnp.where(first, full[:rows], full[rows:])


def pair_weights(qkv_ref, bias_ref, pair, head, width):
    at = slice(pair * 2 * head, (pair + 1) * 2 * head)
    query = pair_spread(qkv_ref[:, at], head)
    key = qkv_ref[:, width + at.start : width + at.stop]
    value = qkv_ref[:, 2 * width + at.start : 2 * width + at.stop]
    rows = key.shape[0]
    bias = bias_ref[2 * pair : 2 * pair + 2].reshape(2 * rows, rows)
    scores = dot(query, key, ((1,), (1,))) + bias
    raised = jnp.exp(scores - jnp.max(scores, axis=-1, keepdims=True))
    return query, key, value, raised / jnp.sum(raised, axis=-1, keepdims=True)


def self_kernel(head, tokens_ref, gain_ref, bias_ref, weight_ref, qkv_ref, mixed_ref, normed_ref, stream_ref, cross_ref, query_ref):
    width = tokens_ref.shape[1]
    inputs = tokens_ref[...].astype(F32)
    normed = (inputs * scale_rows(inputs) * gain_ref[0:1, :]).astype(BF16)
    normed_ref[...] = normed
    for k in range(3):
        at = slice(k * width, (k + 1) * width)
        qkv_ref[:, at] = dot(normed, weight_ref[:, at], ((1,), (0,))).astype(BF16)
    for pair in range(width // (2 * head)):
        _, _, value, weights = pair_weights(qkv_ref, bias_ref, pair, head, width)
        full = dot(weights.astype(BF16), value, ((1,), (0,)))
        mixed_ref[:, pair * 2 * head : (pair + 1) * 2 * head] = pair_pick(full, head).astype(BF16)
    stream = inputs + dot(mixed_ref[...], weight_ref[:, 3 * width : 4 * width], ((1,), (0,)))
    stream_ref[...] = stream
    cross = (stream * scale_rows(stream) * gain_ref[1:2, :]).astype(BF16)
    cross_ref[...] = cross
    query_ref[...] = dot(cross, weight_ref[:, 4 * width : 5 * width], ((1,), (0,))).astype(BF16)


def self_attend(tokens, gain_rows, bias, weight, head):
    rows, width = tokens.shape
    low = jax.ShapeDtypeStruct((rows, width), BF16)
    weight_spec = pl.BlockSpec((width, 5 * width), lambda i: (0, 0))
    return pl.pallas_call(
        partial(self_kernel, head),
        out_shape=(
            jax.ShapeDtypeStruct((rows, 3 * width), BF16),
            low,
            low,
            jax.ShapeDtypeStruct((rows, width), F32),
            low,
            low,
        ),
        grid=(1,),
        in_specs=[
            pl.BlockSpec(tokens.shape, lambda i: (0, 0)),
            pl.BlockSpec(gain_rows.shape, lambda i: (0, 0)),
            pl.BlockSpec(bias.shape, lambda i: (0, 0, 0)),
            weight_spec,
        ],
        out_specs=(pl.BlockSpec((rows, 3 * width), lambda i: (0, 0)),)
        + (pl.BlockSpec((rows, width), lambda i: (0, 0)),) * 5,
        compiler_params=pltpu.CompilerParams(vmem_limit_bytes=56 * 2**20),
        name="self_attend",
    )(tokens, gain_rows, bias, weight)


def self_back_kernel(head, tokens_ref, gain_ref, bias_ref, weight_ref, qkv_ref, stream_ref, dq_ref, dstream_ref, dqkv_ref, low_ref, dinput_ref, score_ref, dgain_ref):
    width = tokens_ref.shape[1]
    rows = tokens_ref.shape[0]
    d_cross = dot(dq_ref[...], weight_ref[:, 4 * width : 5 * width], ((1,), (1,)))
    d_stream, gain_cross = norm_gradient(stream_ref[...], gain_ref[1:2, :], d_cross)
    d_stream = d_stream + dstream_ref[...]
    low = d_stream.astype(BF16)
    low_ref[...] = low
    d_mixed = dot(low, weight_ref[:, 3 * width : 4 * width], ((1,), (1,))).astype(BF16)
    lanes = score_ref.shape[1]
    place = lax.broadcasted_iota(jnp.int32, (rows, lanes), 0) + lax.broadcasted_iota(
        jnp.int32, (rows, lanes), 1
    )
    mirror = (place == rows - 1).astype(F32).astype(BF16)
    sums = []
    for pair in range(width // (2 * head)):
        query, key, value, weights = pair_weights(qkv_ref, bias_ref, pair, head, width)
        at = slice(pair * 2 * head, (pair + 1) * 2 * head)
        spread = pair_spread(d_mixed[:, at], head)
        d_value = dot(weights.astype(BF16), spread, ((0,), (0,)))
        d_weights = dot(spread, value, ((1,), (1,)))
        inner = jnp.sum(weights * d_weights, axis=-1, keepdims=True)
        d_score = (weights * (d_weights - inner)).astype(BF16)
        reverse = dot(d_score, mirror, ((1,), (0,)))
        for h in range(2):
            turned = pltpu.roll(reverse[h * rows : (h + 1) * rows], 0, 1, stride=1, stride_axis=0)
            sums.append(jnp.sum(turned, axis=0, keepdims=True))
        d_query = pair_pick(dot(d_score, key, ((1,), (0,))), head)
        d_key = dot(d_score, query, ((0,), (0,)))
        dqkv_ref[:, at] = d_query.astype(BF16)
        dqkv_ref[:, width + at.start : width + at.stop] = d_key.astype(BF16)
        dqkv_ref[:, 2 * width + at.start : 2 * width + at.stop] = d_value.astype(BF16)
    d_normed = jnp.zeros((rows, width), F32)
    for k in range(3):
        at = slice(k * width, (k + 1) * width)
        d_normed = d_normed + dot(dqkv_ref[:, at], weight_ref[:, at], ((1,), (1,)))
    d_input, gain_self = norm_gradient(tokens_ref[...].astype(F32), gain_ref[0:1, :], d_normed)
    dinput_ref[...] = d_input + d_stream
    sums.append(jnp.zeros((score_ref.shape[0] - len(sums), lanes), F32))
    score_ref[...] = jnp.concatenate(sums, axis=0)
    dgain_ref[...] = jnp.concatenate([gain_self, gain_cross, jnp.zeros((6, width), F32)], axis=0)


def self_back(tokens, gain_rows, bias, weight, qkv, stream, d_query, d_stream, head):
    rows, width = tokens.shape

    def whole(shape):
        return pl.BlockSpec(shape, lambda i: (0,) * len(shape))

    shapes = (
        jax.ShapeDtypeStruct(qkv.shape, BF16),
        jax.ShapeDtypeStruct(tokens.shape, BF16),
        jax.ShapeDtypeStruct(tokens.shape, F32),
        jax.ShapeDtypeStruct((-(-bias.shape[0] // 8) * 8, -(-rows // 128) * 128), F32),
        jax.ShapeDtypeStruct((8, width), F32),
    )
    return pl.pallas_call(
        partial(self_back_kernel, head),
        out_shape=shapes,
        grid=(1,),
        in_specs=[
            whole(tokens.shape),
            whole(gain_rows.shape),
            whole(bias.shape),
            whole((width, 5 * width)),
            whole(qkv.shape),
            whole(tokens.shape),
            whole(tokens.shape),
            whole(tokens.shape),
        ],
        out_specs=tuple(whole(shape.shape) for shape in shapes),
        compiler_params=pltpu.CompilerParams(vmem_limit_bytes=56 * 2**20),
        name="self_back",
    )(tokens, gain_rows, bias, weight, qkv, stream, d_query, d_stream)


def pick_chunk(full, head, rows, start):
    chunk = full.shape[1]
    first = start // rows
    lane = (lax.broadcasted_iota(jnp.int32, (head, chunk), 1) + start) // rows - first
    out = full[:head]
    for h in range(1, full.shape[0] // head):
        out = jnp.where(lane == h, full[h * head : (h + 1) * head], out)
    return out


def over_rows(value, reduce):
    rows, lanes = value.shape
    if rows % 64 == 0:
        value = reduce(value.reshape(8, rows // 8, lanes), axis=0)
    if value.shape[0] % 8 == 0:
        value = reduce(value.reshape(-1, 8, lanes), axis=0)
    return reduce(value, axis=0, keepdims=True)


def each_query(here_ref, queries, store):
    near = queries // 4

    def flush(at, carry):
        y = jnp.bitwise_xor(here_ref[1], at // near)
        j = at % near * 4 + 2 * y
        store(at, j + here_ref[0], j + 1 - here_ref[0])
        return carry

    lax.fori_loop(0, queries // 2, flush, 0)


def either(index, a_ref, b_ref):
    count = a_ref.shape[0]
    return jnp.where(index < count, a_ref[index % count], b_ref[index % count])


def attend_kernel(plen, head, rows, asker_ref, owner_ref, here_ref, qa_ref, qb_ref, kv_ref, mine_ref, other_ref, acc, top, total, stat):
    step = pl.program_id(1)
    queries = 2 * qa_ref.shape[0]
    width = GROUP * head

    @pl.when(step == 0)
    def _():
        acc[...] = jnp.zeros_like(acc)
        top[...] = jnp.full_like(top, FLOOR)
        total[...] = jnp.zeros_like(total)

    @pl.when((step == 0) & (pl.program_id(0) == 0))
    def _():
        stat[...] = jnp.zeros_like(stat)

    lanes = GROUP * rows
    chunk = min(CHUNK, lanes)

    def begin(unit):
        p, c = divmod(unit, lanes // chunk)
        if c == 0:
            spreads[p] = spread_heads(either(asker_ref[step * BLOCK + p], qa_ref, qb_ref), head)
            turned[p] = kv_ref[p * plen : (p + 1) * plen, width:].T
        keys = kv_ref[p * plen : (p + 1) * plen, :width]
        return dot(keys, spreads[p][c * chunk : (c + 1) * chunk], ((1,), (1,)))

    def finish(unit, scores):
        p, c = divmod(unit, lanes // chunk)
        owner = owner_ref[step * BLOCK + p]
        at = pl.ds(c * chunk, chunk)
        first, last = c * chunk // rows, ((c + 1) * chunk - 1) // rows
        here = over_rows(scores, jnp.max)
        raised = jnp.exp(scores - here)
        here_total = over_rows(raised, jnp.sum)
        full = dot(turned[p][first * head : (last + 1) * head], raised.astype(BF16), ((1,), (0,)))
        mixed = pick_chunk(full, head, rows, c * chunk)
        old = top[owner, :, at]
        new = jnp.maximum(old, here)
        old_scale, here_scale = jnp.exp(old - new), jnp.exp(here - new)
        top[owner, :, at] = new
        total[owner, :, at] = total[owner, :, at] * old_scale + here_total * here_scale
        acc[owner, :, at] = acc[owner, :, at] * old_scale + mixed * here_scale

    spreads, turned = {}, {}
    units = BLOCK * (lanes // chunk)
    waiting = [begin(u) for u in range(min(AHEAD, units))]
    for unit in range(units):
        if unit + AHEAD < units:
            waiting.append(begin(unit + AHEAD))
        finish(unit, waiting.pop(0))

    @pl.when(step == pl.num_programs(1) - 1)
    def _():
        base = pl.program_id(0) * 5
        body = pl.ds(pl.multiple_of(pl.program_id(0) * head, head), head)

        def keep(j, carry):
            for t, part in enumerate(split_parts(top[j], 3) + split_parts(total[j], 2)):
                stat[j, pl.ds(base + t, 1), :] = part
            return carry

        def store(at, mine, other):
            mine_ref[at, body, :] = acc[mine].astype(BF16)
            other_ref[at, body, :] = acc[other].astype(BF16)

        lax.fori_loop(0, queries, keep, 0)
        each_query(here_ref, queries, store)

    @pl.when((step == pl.num_programs(1) - 1) & (pl.program_id(0) == pl.num_programs(0) - 1))
    def _():
        first = mine_ref.shape[1] - STAT_ROWS

        def store(at, mine, other):
            mine_ref[at, first:, :] = stat[mine].astype(BF16)
            other_ref[at, first:, :] = stat[other].astype(BF16)

        each_query(here_ref, queries, store)


def attend(asker, owner, here, plane, across, kv, plen, head):
    near, rows, columns = plane.shape
    queries = 2 * near
    width = GROUP * head
    slots = kv.shape[0] // plen
    lanes = GROUP * rows
    groups = columns // width
    out = jax.ShapeDtypeStruct((near, groups * head + STAT_ROWS, lanes), BF16)
    q_spec = pl.BlockSpec((near, rows, width), lambda g, b, *_: (0, 0, g))
    return pl.pallas_call(
        partial(attend_kernel, plen, head, rows),
        out_shape=(out, out),
        grid_spec=pltpu.PrefetchScalarGridSpec(
            num_scalar_prefetch=3,
            grid=(groups, slots // BLOCK),
            in_specs=[
                q_spec,
                q_spec,
                pl.BlockSpec((BLOCK * plen, 2 * width), lambda g, b, *_: (b, g)),
            ],
            out_specs=(pl.BlockSpec(out.shape, lambda g, b, *_: (0, 0, 0)),) * 2,
            scratch_shapes=[
                pltpu.VMEM((queries, head, lanes), F32),
                pltpu.VMEM((queries, 1, lanes), F32),
                pltpu.VMEM((queries, 1, lanes), F32),
                pltpu.VMEM((queries, STAT_ROWS, lanes), F32),
            ],
        ),
        compiler_params=pltpu.CompilerParams(vmem_limit_bytes=60 * 2**20),
        cost_estimate=pl.CostEstimate(
            flops=16 * rows * kv.shape[0] * columns,
            bytes_accessed=4 * kv.shape[0] * columns,
            transcendentals=rows * kv.shape[0] * GROUP * groups,
        ),
        name="attend",
    )(asker, owner, here, plane, across, kv)


def read_stats(stat, g):
    at = 5 * g
    return (
        stat[at : at + 1] + stat[at + 1 : at + 2] + stat[at + 2 : at + 3],
        stat[at + 3 : at + 4] + stat[at + 4 : at + 5],
    )


def merge_kernel(head, a_ref, b_ref, out_ref):
    body = a_ref.shape[1] - STAT_ROWS
    for i in range(a_ref.shape[0]):
        stat_a, stat_b = a_ref[i, body:, :].astype(F32), b_ref[i, body:, :].astype(F32)
        rows = []
        for g in range(body // head):
            at = slice(g * head, (g + 1) * head)
            (top_a, sum_a), (top_b, sum_b) = read_stats(stat_a, g), read_stats(stat_b, g)
            top = jnp.maximum(top_a, top_b)
            w_a, w_b = jnp.exp(top_a - top), jnp.exp(top_b - top)
            out_ref[i, at, :] = (
                a_ref[i, at, :].astype(F32) * w_a + b_ref[i, at, :].astype(F32) * w_b
            ).astype(BF16)
            rows += split_parts(top, 3) + split_parts(sum_a * w_a + sum_b * w_b, 2)
        rows.append(jnp.zeros((STAT_ROWS - len(rows), rows[0].shape[1]), F32))
        out_ref[i, body:, :] = jnp.concatenate(rows, axis=0).astype(BF16)


def core_kernel(head, a_ref, b_ref, near_ref, far_ref):
    @pl.when(pl.program_id(0) < 2)
    def _():
        merge_kernel(head, a_ref, b_ref, far_ref)

    @pl.when(pl.program_id(0) >= 2)
    def _():
        merge_kernel(head, a_ref, b_ref, near_ref)


def core_merge(kept, came, head):
    block = (kept.shape[0] // 4,) + kept.shape[1:]
    out = jax.ShapeDtypeStruct((kept.shape[0] // 2,) + kept.shape[1:], BF16)
    return pl.pallas_call(
        partial(core_kernel, head),
        out_shape=(out, out),
        grid=(4,),
        in_specs=[pl.BlockSpec(block, lambda i: ((i + 2) % 4, 0, 0))] * 2,
        out_specs=(
            pl.BlockSpec(block, lambda i: (jnp.maximum(i - 2, 0), 0, 0)),
            pl.BlockSpec(block, lambda i: (jnp.minimum(i, 1), 0, 0)),
        ),
        cost_estimate=pl.CostEstimate(flops=4 * kept.size, bytes_accessed=6 * kept.size, transcendentals=0),
        name="core_merge",
    )(kept, came)


def near_merge(kept, came, head):
    spec = pl.BlockSpec((kept.shape[0] // 2,) + kept.shape[1:], lambda i: (i, 0, 0))
    return pl.pallas_call(
        partial(merge_kernel, head),
        out_shape=jax.ShapeDtypeStruct(kept.shape, BF16),
        grid=(2,),
        in_specs=[spec, spec],
        out_specs=spec,
        cost_estimate=pl.CostEstimate(flops=4 * kept.size, bytes_accessed=6 * kept.size, transcendentals=0),
        name="near_merge",
    )(kept, came)


def join_parts(ref, g, head):
    count, rows, _ = ref.shape
    at = slice(g * head, (g + 1) * head)
    found = [read_stats(ref[i, rows - STAT_ROWS :, :].astype(F32), g) for i in range(count)]
    top = found[0][0]
    for i in range(1, count):
        top = jnp.maximum(top, found[i][0])
    weights = [jnp.exp(found[i][0] - top) for i in range(count)]
    whole = found[0][1] * weights[0]
    mixed = ref[0, at, :].astype(F32) * weights[0]
    for i in range(1, count):
        whole = whole + found[i][1] * weights[i]
        mixed = mixed + ref[i, at, :].astype(F32) * weights[i]
    return mixed / whole, top + jnp.log(whole)


def ffn_kernel(head, arrived_ref, stream_ref, cot_ref, gain_ref, cross_ref, up_ref, down_ref, payload_ref, out_ref, dstream_ref, dgain_ref, mixed_ref, low_ref, normed_ref, dinner_ref, active_ref, full_ref, log_ref, total_ref, back_ref):
    rows, width = stream_ref.shape
    groups = (arrived_ref.shape[1] - STAT_ROWS) // head
    wide = GROUP * head
    fold = pl.program_id(0)

    @pl.when(fold == 0)
    def _():
        for g in range(groups):
            part, log = join_parts(arrived_ref, g, head)
            log_ref[g : g + 1, :] = log
            turned = part.T
            heads = [turned[h * rows : (h + 1) * rows] for h in range(GROUP)]
            full_ref[:, g * wide : (g + 1) * wide] = jnp.concatenate(heads, axis=1)
        mixed = full_ref[...].astype(BF16)
        mixed_ref[...] = mixed
        stream = stream_ref[...] + dot(mixed, cross_ref[...], ((1,), (0,)))
        dstream_ref[...] = stream
        total_ref[...] = stream
        back_ref[...] = jnp.zeros_like(back_ref)
        normed_ref[...] = (stream * scale_rows(stream) * gain_ref[2:3, :]).astype(BF16)

    inner = dot(normed_ref[...], up_ref[...], ((1,), (0,)))
    square = inner * inner
    bent = jnp.tanh(0.7978845608028654 * (inner + 0.044715 * square * inner))
    half = 0.5 * (1.0 + bent)
    active = (inner * half).astype(BF16)
    slope = half + 0.5 * inner * (1.0 - bent * bent) * (
        0.7978845608028654 * (1.0 + 0.134145 * square)
    )
    active_ref[...] = active
    total_ref[...] += dot(active, down_ref[...], ((1,), (0,)))
    d_inner = (dot(cot_ref[...], down_ref[...], ((1,), (1,))) * slope).astype(BF16)
    dinner_ref[...] = d_inner
    back_ref[...] += dot(d_inner, up_ref[...], ((1,), (1,)))

    @pl.when(fold == pl.num_programs(0) - 1)
    def _():
        out_ref[...] = total_ref[...].astype(BF16)
        d_stream, gain = norm_gradient(dstream_ref[...], gain_ref[2:3, :], back_ref[...])
        d_stream = d_stream + cot_ref[...].astype(F32)
        dstream_ref[...] = d_stream
        dgain_ref[...] = jnp.concatenate([gain, jnp.zeros((7, width), F32)], axis=0)
        low = d_stream.astype(BF16)
        low_ref[...] = low
        d_mixed = dot(low, cross_ref[...], ((1,), (1,))).astype(BF16)
        payload_ref[:rows, :] = d_mixed
        for g in range(groups):
            columns = slice(g * wide, (g + 1) * wide)
            product = (d_mixed[:, columns].astype(F32) * full_ref[:, columns]).T
            delta = [
                jnp.sum(product[h * head : (h + 1) * head], axis=0, keepdims=True)
                for h in range(GROUP)
            ]
            parts = split_parts(log_ref[g : g + 1, :], 3) + split_parts(jnp.concatenate(delta, axis=1), 2)
            lines = [
                part[:, t * wide : (t + 1) * wide]
                for part in parts
                for t in range(GROUP * rows // wide)
            ]
            lines.append(jnp.zeros((STAT_ROWS - len(lines), wide), F32))
            payload_ref[rows:, columns] = jnp.concatenate(lines, axis=0).astype(BF16)


def feed_forward(arrived, stream, grads, gain_rows, weight, head):
    rows, width = stream.shape
    hidden = (weight.shape[1] - width) // 2
    folds = hidden // width

    def whole(shape):
        return pl.BlockSpec(shape, lambda k: (0,) * len(shape))

    low = jax.ShapeDtypeStruct((rows, width), BF16)
    long = jax.ShapeDtypeStruct((rows, hidden), BF16)
    shapes = (
        jax.ShapeDtypeStruct((rows + STAT_ROWS, width), BF16),
        low,
        jax.ShapeDtypeStruct((rows, width), F32),
        jax.ShapeDtypeStruct((8, width), F32),
        low,
        low,
        low,
    )
    fold_spec = pl.BlockSpec((rows, width), lambda k: (0, k))
    return pl.pallas_call(
        partial(ffn_kernel, head),
        out_shape=shapes + (long, long),
        grid=(folds,),
        in_specs=[whole(v.shape) for v in (arrived, stream, grads, gain_rows)]
        + [
            pl.BlockSpec((width, width), lambda k: (0, 0)),
            pl.BlockSpec((width, width), lambda k: (0, 1 + k)),
            pl.BlockSpec((width, width), lambda k: (0, 1 + folds + k)),
        ],
        out_specs=tuple(whole(shape.shape) for shape in shapes) + (fold_spec, fold_spec),
        scratch_shapes=[
            pltpu.VMEM((rows, width), F32),
            pltpu.VMEM((8, GROUP * rows), F32),
            pltpu.VMEM((rows, width), F32),
            pltpu.VMEM((rows, width), F32),
        ],
        compiler_params=pltpu.CompilerParams(vmem_limit_bytes=56 * 2**20),
        cost_estimate=pl.CostEstimate(
            flops=4 * rows * weight.size, bytes_accessed=2 * weight.size, transcendentals=rows * hidden
        ),
        name="feed_forward",
    )(arrived, stream, grads, gain_rows, weight, weight, weight)


def ffn_terms_kernel(folds, *refs):
    out_ref = refs[-1]
    tile = pl.program_id(0)
    for first, last, left, right in ((0, 1, 0, 1), (1, 1 + folds, 2, 3), (1 + folds, 1 + 2 * folds, 4, 5)):

        @pl.when((tile >= first) & (tile < last))
        def _(left=left, right=right):
            a, b = refs[2 * left : 2 * left + 2], refs[2 * right : 2 * right + 2]
            found = dot(a[0][...], b[0][...], ((0,), (0,))) + dot(a[1][...], b[1][...], ((0,), (0,)))
            out_ref[...] = found.astype(BF16)


def ffn_terms(parts, grads, hidden):
    width = grads[0].shape[1]
    folds = hidden // width

    def spec(value, start):
        if start is None:
            return pl.BlockSpec((value.shape[0], width), lambda t: (0, 0))
        return pl.BlockSpec((value.shape[0], width), lambda t: (0, jnp.clip(t - start, 0, folds - 1)))

    operands, specs = [], []
    for values, start in zip([*zip(*parts), grads], (None, None, None, 1, 1 + folds, None)):
        for value in values:
            operands.append(value)
            specs.append(spec(value, start))
    return pl.pallas_call(
        partial(ffn_terms_kernel, folds),
        out_shape=jax.ShapeDtypeStruct((width, width + 2 * hidden), BF16),
        grid=(1 + 2 * folds,),
        in_specs=specs,
        out_specs=pl.BlockSpec((width, width), lambda t: (0, t)),
        compiler_params=pltpu.CompilerParams(vmem_limit_bytes=60 * 2**20),
        cost_estimate=pl.CostEstimate(
            flops=6 * width * width * width, bytes_accessed=8 * width * hidden, transcendentals=0
        ),
        name="ffn_terms",
    )(*operands)


def attend_back_kernel(plen, head, rows, asker_ref, owner_ref, here_ref, qa_ref, qb_ref, doa_ref, dob_ref, sa_ref, sb_ref, kv_ref, *refs):
    step = pl.program_id(1)
    dkv_ref, mine_ref, other_ref, acc, log, delta = refs[-6:]
    held_ref = refs[0] if len(refs) > 6 else None
    near = qa_ref.shape[0]
    queries = 2 * near
    width = GROUP * head

    @pl.when(step == 0)
    def _():
        acc[...] = jnp.zeros_like(acc)
        third = (GROUP * rows) // width

        def fill(j, carry):
            stat = either(j, sa_ref, sb_ref).astype(F32)
            row = lax.broadcasted_iota(jnp.int32, stat.shape, 0)
            for at, ref, count in ((0, log, 3), (3 * third, delta, 2)):
                pieces = []
                for t in range(third):
                    wanted = row == at + t
                    for k in range(1, count):
                        wanted = wanted | (row == at + k * third + t)
                    pieces.append(jnp.sum(jnp.where(wanted, stat, 0.0), axis=0, keepdims=True))
                ref[j] = jnp.concatenate(pieces, axis=1)
            return carry

        lax.fori_loop(0, queries, fill, 0)

    lanes = GROUP * rows
    chunk = min(CHUNK, lanes)

    def begin(unit):
        p, c = divmod(unit, lanes // chunk)
        rows_at = slice(p * plen, (p + 1) * plen)
        if c == 0:
            asker = asker_ref[step * BLOCK + p]
            q_spread[p] = spread_heads(either(asker, qa_ref, qb_ref), head)
            do_spread[p] = spread_heads(either(asker, doa_ref, dob_ref), head)
            turned[p] = kv_ref[rows_at, :width].T
        at = slice(c * chunk, (c + 1) * chunk)
        return (
            dot(kv_ref[rows_at, :width], q_spread[p][at], ((1,), (1,))),
            dot(kv_ref[rows_at, width:], do_spread[p][at], ((1,), (1,))),
        )

    def finish(unit, found):
        scores, d_soft = found
        p, c = divmod(unit, lanes // chunk)
        owner, asker = owner_ref[step * BLOCK + p], asker_ref[step * BLOCK + p]
        at = pl.ds(c * chunk, chunk)
        cut = slice(c * chunk, (c + 1) * chunk)
        first, last = c * chunk // rows, ((c + 1) * chunk - 1) // rows
        soft = jnp.exp(scores - log[asker, :, at])
        d_score = (soft * (d_soft - delta[asker, :, at])).astype(BF16)
        d_value = dot(soft.astype(BF16), do_spread[p][cut], ((1,), (0,)))
        d_key = dot(d_score, q_spread[p][cut], ((1,), (0,)))
        sums[p] = (d_key, d_value) if c == 0 else (sums[p][0] + d_key, sums[p][1] + d_value)
        full = dot(turned[p][first * head : (last + 1) * head], d_score, ((1,), (0,)))
        acc[owner, :, at] += pick_chunk(full, head, rows, c * chunk)
        if c == lanes // chunk - 1:
            rows_at = slice(p * plen, (p + 1) * plen)
            for found, columns in zip(sums[p], (slice(0, width), slice(width, 2 * width))):
                if held_ref is not None:
                    found = found + held_ref[rows_at, columns].astype(F32)
                dkv_ref[rows_at, columns] = found.astype(BF16)

    q_spread, do_spread, turned, sums = {}, {}, {}, {}
    units = BLOCK * (lanes // chunk)
    waiting = [begin(u) for u in range(min(AHEAD, units))]
    for unit in range(units):
        if unit + AHEAD < units:
            waiting.append(begin(unit + AHEAD))
        finish(unit, waiting.pop(0))

    @pl.when(step == pl.num_programs(1) - 1)
    def _():
        def store(at, mine, other):
            mine_ref[at, 0] = acc[mine].astype(BF16)
            other_ref[at, 0] = acc[other].astype(BF16)

        each_query(here_ref, queries, store)


def attend_back(asker, owner, here, queries_in, grads_in, kv, held, plen, head):
    near, rows, columns = queries_in[0].shape
    queries = 2 * near
    width = GROUP * head
    slots = kv.shape[0] // plen
    lanes = GROUP * rows
    groups = columns // width
    block = (near, 1, head, lanes)
    out = jax.ShapeDtypeStruct((near, groups, head, lanes), BF16)
    q_spec = pl.BlockSpec((near, rows, width), lambda g, b, *_: (0, 0, g))
    stat_spec = pl.BlockSpec((near, STAT_ROWS, width), lambda g, b, *_: (0, rows // STAT_ROWS, g))
    kv_spec = pl.BlockSpec((BLOCK * plen, 2 * width), lambda g, b, *_: (b, g))
    operands = [*queries_in, *grads_in, *grads_in, kv]
    specs = [q_spec] * 4 + [stat_spec] * 2 + [kv_spec]
    if held is not None:
        operands.append(held)
        specs.append(kv_spec)
    return pl.pallas_call(
        partial(attend_back_kernel, plen, head, rows),
        out_shape=(jax.ShapeDtypeStruct(kv.shape, BF16), out, out),
        grid_spec=pltpu.PrefetchScalarGridSpec(
            num_scalar_prefetch=3,
            grid=(groups, slots // BLOCK),
            in_specs=specs,
            out_specs=(
                kv_spec,
                pl.BlockSpec(block, lambda g, b, *_: (0, g, 0, 0)),
                pl.BlockSpec(block, lambda g, b, *_: (0, g, 0, 0)),
            ),
            scratch_shapes=[
                pltpu.VMEM((queries, head, lanes), F32),
                pltpu.VMEM((queries, 1, lanes), F32),
                pltpu.VMEM((queries, 1, lanes), F32),
            ],
        ),
        input_output_aliases={} if held is None else {3 + len(operands) - 1: 0},
        compiler_params=pltpu.CompilerParams(vmem_limit_bytes=60 * 2**20),
        cost_estimate=pl.CostEstimate(
            flops=40 * rows * kv.shape[0] * columns,
            bytes_accessed=8 * kv.shape[0] * columns,
            transcendentals=rows * kv.shape[0] * GROUP * groups,
        ),
        name="attend_back",
    )(asker, owner, here, *operands)


def source_kernel(keep_ref, fetch_ref, *refs):
    weight_ref, out_ref = refs[-2:]
    for p, ref in enumerate(refs[:-2]):
        kept = keep_ref[pl.program_id(0) * (len(refs) - 2) + p]

        @pl.when(kept == 0)
        def _(p=p):
            out_ref[p] = jnp.zeros_like(out_ref[p])

        @pl.when(kept != 0)
        def _(p=p, ref=ref):
            out_ref[p] = dot(ref[...], weight_ref[...], ((1,), (1,))).astype(BF16)


def fetch_order(refresh):
    slots = refresh.shape[0]
    several = 4 if slots % 4 == 0 else 1
    order = jnp.arange(slots).reshape(-1, several)
    kept = refresh.reshape(-1, several) != 0
    fetch = lax.cummax(jnp.where(kept, order, order[:1]), axis=0)
    return several, fetch.astype(jnp.int32).reshape(-1)


def source_grads(refresh, several, fetch, dkv, weight, plen):
    slots = refresh.shape[0]
    model_width = weight.shape[0]

    def spec(p):
        return pl.BlockSpec((plen, dkv.shape[1]), lambda r, keep, fetch: (fetch[r * several + p], 0))

    return pl.pallas_call(
        source_kernel,
        out_shape=jax.ShapeDtypeStruct((slots, plen, model_width), BF16),
        grid_spec=pltpu.PrefetchScalarGridSpec(
            num_scalar_prefetch=2,
            grid=(slots // several,),
            in_specs=[spec(p) for p in range(several)] + [pl.BlockSpec(weight.shape, lambda r, *_: (0, 0))],
            out_specs=pl.BlockSpec((several, plen, model_width), lambda r, *_: (r, 0, 0)),
        ),
        compiler_params=pltpu.CompilerParams(vmem_limit_bytes=60 * 2**20),
        cost_estimate=pl.CostEstimate(
            flops=slots * plen * model_width * 2 * model_width,
            bytes_accessed=4 * slots * plen * model_width,
            transcendentals=0,
        ),
        name="source_grads",
    )(refresh, fetch, *([dkv] * several), weight)


def outer_kernel(starts, split, added, half_ref, *refs):
    count = len(starts) - 1
    outs = refs[-2:]
    tile = pl.program_id(0)
    for k in range(count):

        @pl.when((tile >= starts[k]) & (tile < starts[k + 1]))
        def _(k=k):
            found = dot(refs[2 * k][...], refs[2 * k + 1][...], ((0,), (0,)))
            side = 0 if k < split else 1
            if added:
                found = found + refs[2 * count + side][...].astype(F32)
            outs[side][...] = found.astype(BF16)


def outer(half, first, second, came=None):
    pairs = first + second
    rows, total_rows = pairs[0][0].shape
    width = total_rows // 2
    counts = [right.shape[1] // 2 // width for _, right in pairs]
    starts = [sum(counts[:k]) for k in range(len(counts) + 1)]
    edge = starts[len(first)]
    operands, specs = [], []
    for k, (left, right) in enumerate(pairs):

        def right_map(t, half_ref, start=starts[k], count=counts[k]):
            return (0, half_ref[0] * count + jnp.clip(t - start, 0, count - 1))

        operands += [left, right]
        specs += [
            pl.BlockSpec((rows, total_rows), lambda t, half_ref: (0, 0)),
            pl.BlockSpec((rows, width), right_map),
        ]
    sides = (
        pl.BlockSpec((total_rows, width), lambda t, half_ref: (0, jnp.minimum(t, edge - 1))),
        pl.BlockSpec((total_rows, width), lambda t, half_ref: (0, jnp.maximum(t - edge, 0))),
    )
    if came is not None:
        operands += came
        specs += sides
    size = total_rows * starts[-1] * width
    return pl.pallas_call(
        partial(outer_kernel, starts, len(first), came is not None),
        out_shape=(
            jax.ShapeDtypeStruct((total_rows, edge * width), BF16),
            jax.ShapeDtypeStruct((total_rows, (starts[-1] - edge) * width), BF16),
        ),
        grid_spec=pltpu.PrefetchScalarGridSpec(
            num_scalar_prefetch=1, grid=(starts[-1],), in_specs=specs, out_specs=sides
        ),
        compiler_params=pltpu.CompilerParams(vmem_limit_bytes=60 * 2**20),
        cost_estimate=pl.CostEstimate(flops=2 * rows * size, bytes_accessed=4 * size, transcendentals=0),
        name="outer",
    )(half, *operands)


def flip(value, bit):
    count = lax.axis_size("pass")
    return lax.ppermute(value, "pass", [(i, i ^ bit) for i in range(count)])


def after(value, *others):
    return lax.optimization_barrier((value,) + others)


def line_sends(block):
    count = lax.axis_size("pass")
    rings = [[(i, (i + 4 * k) % count) for i in range(count)] for k in range(1, count // 4)]
    return [lax.ppermute(block, "pass", ring) for ring in rings]


def gather_place(query, own, count):
    major = count // 4
    turn = jnp.mod(own // 4 - query // 4, major)
    return turn + major * ((own // 2) % 2 != (query // 2) % 2) + 2 * major * (own % 2 != query % 2)


def line_exchange(parts):
    count = lax.axis_size("pass")
    groups = [[r + 4 * k for k in range(count // 4)] for r in range(4)]
    return lax.all_to_all(
        parts, "pass", split_axis=0, concat_axis=0, tiled=True, axis_index_groups=groups
    )


def in_order(own, came, place, axis):
    return jnp.stack([jnp.where(place == 0, own, came), jnp.where(place == 0, came, own)], axis=axis)


def gather_rows(block):
    n_dp, count = lax.axis_size("dp"), lax.axis_size("pass")
    if n_dp != 2:
        return lax.all_gather(block, ("dp", "pass"), axis=0, tiled=True)
    own, dp = lax.axis_index("pass"), lax.axis_index("dp")
    major, core, y = count // 4, own % 2, own // 2 % 2
    pieces = [block, *line_sends(block)]
    line = jnp.zeros((major,) + block.shape, block.dtype)
    for k, piece in enumerate(pieces):
        line = lax.dynamic_update_index_in_dim(line, piece, jnp.mod(own // 4 - k, major), 0)
    cut = block.shape[1] // 256 * 128
    left, right = line[..., :cut], line[..., cut:]
    left, right = in_order(left, flip(left, 2), y, 1), in_order(right, dp_flip(right), dp, 0)
    left, right = in_order(left, dp_flip(left), dp, 0), in_order(right, flip(right, 2), y, 2)
    full = [in_order(part, flip(part, 1), core, 3) for part in (left, right)]
    return jnp.concatenate([part.reshape(-1, part.shape[-1]) for part in full], axis=1)


def line_scatter(parts):
    count = lax.axis_size("pass")
    major, place = count // 4, lax.axis_index("pass") // 4
    came = []
    for k in range(1, major):
        sent = lax.dynamic_index_in_dim(parts, jnp.mod(place + k, major), 0, keepdims=False)
        came.append(lax.ppermute(sent, "pass", [(i, (i + 4 * k) % count) for i in range(count)]))
    return lax.dynamic_index_in_dim(parts, place, 0, keepdims=False), came


def swap_send(value, place, axis, send):
    kept = lax.dynamic_index_in_dim(value, place, axis, keepdims=False)
    return kept, send(lax.dynamic_index_in_dim(value, 1 - place, axis, keepdims=False))


def add_low(kept, came):
    return (kept.astype(F32) + came.astype(F32)).astype(BF16)


def rows_by_owner(value):
    n_dp, count = lax.axis_size("dp"), lax.axis_size("pass")
    rows, columns = value.shape
    return value.reshape(n_dp, count // 4, 2, rows // (n_dp * count // 2), columns)


def dp_step(value, bit):
    pairs = [(i, i ^ bit) for i in range(lax.axis_size("dp"))]
    return lax.ppermute(value, "dp", pairs)


def dp_flip(value):
    return lax.ppermute(value, "dp", [(0, 1), (1, 0)])


def dp_send(value):
    if lax.axis_size("dp") == 2:
        return swap_send(value, lax.axis_index("dp"), 0, dp_flip)
    total = lax.psum_scatter(value, "dp", scatter_dimension=0, tiled=False)
    return total, jnp.zeros_like(total)


def near_send(value, axis):
    return swap_send(value, lax.axis_index("pass") // 2 % 2, axis, lambda v: flip(v, 2))


def over_line(value):
    return jnp.sum(line_exchange(value).astype(F32), axis=0)


def own_rows(value, core):
    shard = value.shape[0] // 2
    parts = value.reshape(2, shard, value.shape[1])
    kept = lax.dynamic_index_in_dim(parts, core, 0, keepdims=False)
    came = flip(lax.dynamic_index_in_dim(parts, 1 - core, 0, keepdims=False), 1)
    return jnp.where(core == 0, kept, came), jnp.where(core == 0, came, kept)


def on_device(
    tokens,
    cotangent,
    passages,
    refresh,
    passage_ids,
    self_query,
    self_key,
    self_value,
    self_out,
    cross_query,
    cross_key,
    cross_value,
    cross_out,
    up_weight,
    down_weight,
    gains,
    rel_table,
):
    both = ("dp", "pass")
    pass_count = lax.axis_size("pass")
    device_id = lax.axis_index(both)
    own_pass = lax.axis_index("pass")
    per_query, plen, model_width = passages.shape
    head_count = rel_table.shape[1]
    head = model_width // head_count
    rows = tokens.shape[0]
    groups = head_count // GROUP
    wide = GROUP * head
    shard = self_query.shape[0]

    def gather(value):
        return lax.all_gather(value, both, axis=0, tiled=True)

    kv_shard = jnp.stack(
        [cross_key.reshape(shard, groups, wide), cross_value.reshape(shard, groups, wide)], axis=2
    ).reshape(shard, 2 * model_width)
    gain_pad = jnp.pad(gains, ((0, 0), (0, 128 - gains.shape[1])))
    first = gather(
        jnp.concatenate([self_query, self_key, self_value, self_out, cross_query, gain_pad], axis=1)
    )
    kv_weight = lax.optimization_barrier(gather_rows(kv_shard))
    encoded = passages.reshape(per_query * plen, model_width)
    kv = matmul(encoded, kv_weight).astype(BF16)
    positions = jnp.arange(rows)
    causal = positions[:, None] >= positions[None, :]
    onehot_low = (
        bucket_of(positions[:, None] - positions[None, :], rel_table.shape[0])[:, :, None]
        == jnp.arange(rel_table.shape[0])[None, None, :]
    ).astype(BF16)
    bias = jnp.einsum("qkb,bh->hqk", onehot_low, rel_table, preferred_element_type=F32)
    bias = jnp.where(causal[None, :, :], bias, FLOOR)
    folds = up_weight.shape[1] // model_width
    total = up_weight.shape[1] // (folds * shard)
    up_fold = up_weight.reshape(shard, total, folds, shard).transpose(0, 2, 1, 3).reshape(shard, -1)
    down_fold = down_weight.reshape(folds, shard, model_width).transpose(1, 0, 2).reshape(shard, -1)
    rest = jnp.concatenate([cross_out, up_fold, down_fold], axis=1)
    several, fetch = fetch_order(refresh)
    first, kv, bias, rest, fetch = after(first, kv, bias, rest, fetch)
    gain_all = first[:, 5 * model_width : 5 * model_width + 3].astype(F32)

    row_ids = device_id * per_query + jnp.arange(per_query)
    owned = jnp.any(passage_ids[:, :, None] == row_ids[None, None, :], axis=1)
    owner = jnp.sum(
        jnp.where(owned, jnp.arange(passage_ids.shape[0])[:, None], 0), axis=0
    ).astype(jnp.int32)
    core = own_pass % 2
    half = core.astype(jnp.int32).reshape(1)
    here = jnp.stack([core, own_pass // 2 % 2]).astype(jnp.int32)
    asker = gather_place(owner, own_pass, pass_count).astype(jnp.int32)

    gain_rows = jnp.pad(gain_all.T, ((0, 5), (0, 0)))
    qkv, mixed_one, normed_self, stream_one, normed_cross, query_two = self_attend(
        tokens, gain_rows, bias, first, head
    )

    cut = rows // 192 * 128

    def merge_send(mine, came):
        near, far = core_merge(mine, came, head)
        return near, flip(far, 2)

    def rows_first(value):
        cube = value.reshape(groups, head, GROUP, -1).transpose(3, 0, 2, 1)
        return cube.reshape(-1, model_width)

    block, last_block = query_two[:cut], query_two[cut:]
    last_block, rest, *sends = after(last_block, rest, *line_sends(block))
    rest = gather(rest)
    line = jnp.stack([block, *sends])
    across, *sends = after(flip(line, 2), *line_sends(last_block))
    plane = jnp.concatenate([line, across])
    q_first = (plane, flip(plane, 1))
    line = jnp.stack([last_block, *sends])
    across = flip(line, 2)
    mine, other = attend(asker, owner, here, *q_first, kv, plen, head)
    across, mine, other = after(across, mine, other)
    came = flip(other, 1)
    plane = jnp.concatenate([line, across])
    q_second = (plane, flip(plane, 1))
    near, came = merge_send(mine, came)
    q_second, near = after(q_second, near)
    mine, other = attend(asker, owner, here, *q_second, kv, plen, head)
    came, mine, other = after(came, mine, other)
    merged, mine, other = after(near_merge(near, came, head), mine, other)
    came_next = flip(other, 1)
    arrived = line_exchange(merged)
    near, came = merge_send(mine, came_next)
    arrived, near, came = after(arrived, near, came)
    merged, arrived = after(near_merge(near, came, head), arrived)
    arrived_last = line_exchange(merged)
    payload_first, out_first, ds_first, gain_first, *terms_first = feed_forward(
        arrived, stream_one[:cut], cotangent[:cut], gain_rows, rest, head
    )
    arrived_last, payload_first = after(arrived_last, payload_first)
    sends = line_sends(payload_first)
    payload, out_last, ds_last, gain_last, *terms_last = feed_forward(
        arrived_last, stream_one[cut:], cotangent[cut:], gain_rows, rest, head
    )
    payload, *sends = after(payload, *sends)
    line_first = jnp.stack([payload_first, *sends])
    across = flip(line_first, 2)
    sends = line_sends(payload)

    block_out = jnp.concatenate([out_first, out_last])
    d_stream_two = jnp.concatenate([ds_first, ds_last])
    d_gain_ffn = gain_first[0] + gain_last[0]
    terms = ffn_terms(
        (terms_first, terms_last), (cotangent[:cut], cotangent[cut:]), up_weight.shape[1]
    )
    across, terms, *sends = after(across, terms, *sends)
    ffn_sums = lax.psum_scatter(terms, both, scatter_dimension=0, tiled=True)
    plane = jnp.concatenate([line_first, across])
    do_first = (plane, flip(plane, 1))
    line = jnp.stack([payload, *sends])
    across = flip(line, 2)

    def half_of(value, came):
        value = (value.astype(F32) + came.astype(F32)).astype(BF16)
        return value[: value.shape[0] // 2], value[value.shape[0] // 2 :]

    dkv, mine, other = attend_back(asker, owner, here, q_first, do_first, kv, None, plen, head)
    across, dkv, mine, other = after(across, dkv, mine, other)
    came = flip(other, 1)
    plane = jnp.concatenate([line, across])
    do_last = (plane, flip(plane, 1))
    near, far = half_of(mine, came)
    came = flip(far, 2)
    do_last, near = after(do_last, near)
    dkv, mine, other = attend_back(asker, owner, here, q_second, do_last, kv, dkv, plen, head)
    came, dkv, mine, other = after(came, dkv, mine, other)
    merged, mine, other = after(add_low(near, came), mine, other)
    arrived = line_exchange(merged)
    near, far = half_of(mine, flip(other, 1))
    came, dkv = after(flip(far, 2), dkv)
    kept, last = line_scatter((near.astype(F32) + came.astype(F32)).astype(BF16))
    arrived, d_kv, d_stream_two, *last = after(
        arrived, left_t(encoded, dkv).astype(BF16), d_stream_two, *last
    )
    last = sum((part.astype(F32) for part in last), kept.astype(F32))
    dq_parts = [rows_first(jnp.sum(arrived.astype(F32), axis=0)), rows_first(last)]
    d_query_two = jnp.concatenate(dq_parts).astype(BF16)
    def kv_half(at):
        cube = d_kv.reshape(model_width, groups, 2, wide)
        return lax.dynamic_index_in_dim(cube, at, 2, keepdims=False).reshape(model_width, -1)

    kv_came = flip(kv_half(1 - core), 1)
    found = self_back(
        tokens, gain_rows, bias, first, qkv, stream_one, d_query_two, d_stream_two, head
    )
    kv_came, ffn_sums, *found = after(kv_came, ffn_sums, *found)
    d_qkv, grad_one, d_inputs, d_score, gain_terms = found
    late_pairs = [(normed_self, d_qkv)]
    more_pairs = [(mixed_one, grad_one), (normed_cross, d_query_two)]
    late_sent, more_sent = outer(1 - half, late_pairs, more_pairs)
    distance = jnp.mod(jnp.arange(d_score.shape[1]) - (rows - 1), d_score.shape[1])
    of_distance = bucket_of(distance, rel_table.shape[0])
    of_distance = (of_distance[:, None] == jnp.arange(rel_table.shape[0])[None, :]).astype(F32)
    d_table = jnp.dot(d_score, of_distance, precision=lax.Precision.HIGHEST)[:head_count].T
    small = jnp.concatenate([d_table.reshape(-1), gain_terms[0], gain_terms[1], d_gain_ffn])
    small = small.reshape(-1, 128)
    late_sent, more_sent, kv_came = after(late_sent, more_sent, kv_came)
    kv_part = jnp.moveaxis(rows_by_owner(add_low(kv_half(core), kv_came)), 1, 0)
    late_came, more_came, kv_part, came = after(
        flip(late_sent, 1), flip(more_sent, 1), kv_part, flip(small, 1)
    )
    small = small + came

    late, more = outer(half, late_pairs, more_pairs, [late_came, more_came])
    late, more, came, kv_part = after(late, more, flip(small, 2), kv_part)
    small = small + came
    late_kept, late_came = dp_send(rows_by_owner(late))
    more_kept, more_came = near_send(rows_by_owner(more), 2)
    kv_line = line_exchange(kv_part)
    passage_grad = source_grads(refresh, several, fetch, dkv, kv_weight, plen)
    for bit in range((lax.axis_size("dp") - 1).bit_length()):
        small = small + dp_step(small, 1 << bit)
    kv_line, late_came, more_came, passage_grad, small = after(
        kv_line, late_came, more_came, passage_grad, small
    )
    late_kept, late_came = near_send(add_low(late_kept, late_came), 1)
    more_kept, more_came = dp_send(add_low(more_kept, more_came))
    kv_kept, kv_came = dp_send(jnp.sum(kv_line.astype(F32), axis=0).astype(BF16))
    for bit in range(2, (pass_count - 1).bit_length() - 1):
        small = small + flip(small, 1 << bit)
    late_came, more_came, kv_came, small = after(late_came, more_came, kv_came, small)
    came = flip(small, pass_count // 2)
    kv_kept, kv_came = near_send(add_low(kv_kept, kv_came), 0)
    parts = [(late_kept, late_came), (more_kept, more_came)]
    line = line_exchange(jnp.concatenate([add_low(*part) for part in parts], axis=-1))
    ffn_sums = ffn_sums.astype(F32)
    d_up = ffn_sums[:, model_width : model_width + up_weight.shape[1]]
    d_up = d_up.reshape(shard, folds, total, shard).transpose(0, 2, 1, 3).reshape(up_weight.shape)
    d_down = ffn_sums[:, model_width + up_weight.shape[1] :].reshape(shard, folds, model_width)
    d_down = d_down.transpose(1, 0, 2).reshape(down_weight.shape)
    line, kv_came, came, d_up, d_down = after(line, kv_came, came, d_up, d_down)
    small = (small + came).reshape(-1)
    line = jnp.sum(line.astype(F32), axis=0)
    line = jnp.concatenate([line, kv_kept.astype(F32) + kv_came.astype(F32)], axis=1)
    table_grad = small[: d_table.size].reshape(d_table.shape)
    d_gains = small[d_table.size :].reshape(3, -1)
    d_gains = lax.dynamic_slice_in_dim(d_gains, device_id * shard, shard, 1)

    left, right = own_rows(line, core)
    half_width = model_width // 2

    def whole(start, stop):
        cut = slice(start * half_width, stop * half_width)
        return jnp.concatenate([left[:, cut], right[:, cut]], axis=1)

    d_first, d_out_self, d_query_cross = whole(0, 3), whole(3, 4), whole(4, 5)
    d_query_self, d_key_self, d_value_self = jnp.split(d_first, 3, axis=1)
    d_key_cross, d_value_cross = left[:, 5 * half_width :], right[:, 5 * half_width :]
    d_out_cross = ffn_sums[:, :model_width]
    return (
        block_out,
        d_inputs,
        passage_grad,
        d_query_self,
        d_key_self,
        d_value_self,
        d_out_self,
        d_query_cross,
        d_key_cross,
        d_value_cross,
        d_out_cross,
        d_up,
        d_down,
        d_gains.T,
        table_grad,
    )


def solution(mesh):
    split = P(("dp", "pass"), None)
    cube = P(("dp", "pass"), None, None)
    in_specs = (split, split, cube, P(("dp", "pass")), P("dp", None)) + (split,) * 11 + (P(),)
    out_specs = (split, split, cube) + (split,) * 11 + (P(),)
    return jax.shard_map(
        on_device, mesh=mesh, in_specs=in_specs, out_specs=out_specs, check_vma=False
    )
```
